32 devices in a mesh: lat: 8 (over y, x, core), lon: 4 (over z).
Axes of the slice: x: 2, y: 2, z: 4, core: 2. Of those that a mesh axis runs over, the one named last changes fastest.
Arguments:
- fields: bfloat16 [32, 64, 1024], P(None, 'lat', 'lon'), may hold values from -6 to 6
- cotangent: bfloat16 [32, 64, 1024], P(None, 'lat', 'lon'), may hold values from -0.0234375 to 0.0234375
- kernel_in: bfloat16 [9, 128, 32], replicated, may hold values from -0.375 to 0.375
- kernel_mid: bfloat16 [9, 128, 128], replicated, may hold values from -0.1875 to 0.1875
- kernel_out: bfloat16 [9, 32, 128], replicated, may hold values from -0.1875 to 0.1875
- patch_anchors: int32 [8, 4, 4, 2], P('lat', 'lon'), may hold values from 0 to 8
- blend_weights: int32 [4, 64, 1024], P(None, 'lat', 'lon'), may hold values from 1 to 8
- tile_counts: int32 [8, 4], P('lat', 'lon'), may hold values from 0 to 4, as said below
Outputs:
- blended: float32 [32, 64, 1024], P(None, 'lat', 'lon')
- grad_in: float32 [9, 128, 32], replicated
- grad_mid: float32 [9, 128, 128], replicated
- grad_out: float32 [9, 32, 128], replicated
The draws below stay inside these ranges and needn't reach their ends.
Inputs may be any that keep to these rules, and one draw needn't show every extreme that they name: `tile_counts`: the counts of the tiles in lat rows i and i + 4 at the same lon sum to exactly 4; tile (1, 0) holds 4 patches and tile (5, 0) none.
All inputs are finite; a program needn't handle non-finite values.
Results may differ from the reference program's by a relative error of at most 0.005.
Values may be sent and summed in bfloat16 or wider, within the bound.
No kernel may reach another device: no remote copies, remote signals or barrier semaphores. Data moves between devices by JAX's collectives and lax.ppermute only.
A program may use at most 64 MiB of HBM per device.

```python
import jax
import jax.numpy as jnp
from jax import lax

CHANNELS = 32
WIDTH = 128
TILE_ROWS = 8
TILE_COLS = 256
MARGIN = 4
SLOTS = 4
LAT_TILES = 8
LON_TILES = 4
ROWS = 64
COLS = 1024


def draw_tile_counts(key, part):
    first_half = jax.random.randint(key, (LAT_TILES // 2, LON_TILES), 1, SLOTS)
    first_half = first_half.at[1, 0].set(SLOTS)
    return jnp.concatenate([first_half, SLOTS - first_half], axis=0).astype(jnp.int32)


def with_ends(entries, stream_key, smallest, largest):
    longest = entries.shape.index(max(entries.shape))
    spots = []
    for shift in (0, 1):
        where = [jax.random.randint(jax.random.fold_in(stream_key, axis), (), 0, length) for axis, length in enumerate(entries.shape)]
        where[longest] = (where[longest] + shift) % entries.shape[longest]
        spots.append(tuple(where))
    return entries.at[spots[0]].set(smallest).at[spots[1]].set(largest)


def block_scale(stream_key, dims, shards, smallest, high):
    def one(axis_at, blocks):
        draws = jax.random.uniform(jax.random.fold_in(jax.random.fold_in(stream_key, 6), axis_at), (blocks,), jnp.float32, smallest / len(shards), high / len(shards))
        return jnp.repeat(jnp.exp(draws), dims[axis_at] // blocks).reshape((-1,) + (1,) * (len(dims) - axis_at - 1))

    gain = one(*shards[0])
    for cut in shards[1:]:
        gain = gain * one(*cut)
    return gain


def normal_values(key, shape, scale, most, shards=(), held_as=jnp.bfloat16):
    entries = jax.random.normal(key, shape, jnp.float32) * scale
    if len(shards) > 0:
        entries = block_scale(key, shape, shards, -0.22, 0.18) * entries
    return jnp.clip(entries, min=-most, max=most).astype(held_as)


def setup_inputs(seed: int = 0) -> dict:
    splits = jax.random.split(jax.random.key(seed), 9)
    fields = normal_values(splits[0], (CHANNELS, ROWS, COLS), 1.0, 6.0, ((1, 8), (2, 4)))
    cotangent = normal_values(splits[1], (CHANNELS, ROWS, COLS), ((ROWS * COLS) ** -0.5), 0.0234375, ((1, 8), (2, 4)))
    kernel_in = normal_values(splits[2], (9, WIDTH, CHANNELS), (9 * CHANNELS) ** -0.5, 0.375)
    kernel_mid = normal_values(splits[3], (9, WIDTH, WIDTH), (9 * WIDTH) ** -0.5, 0.1875)
    kernel_out = normal_values(splits[4], (9, CHANNELS, WIDTH), (9 * WIDTH) ** -0.5, 0.1875)
    patch_anchors = with_ends(jax.random.randint(splits[5], (LAT_TILES, LON_TILES, SLOTS, 2), 0, 2 * MARGIN + 1), jax.random.fold_in(splits[5], 1), 0, 2 * MARGIN).astype(jnp.int32)
    blend_weights = with_ends(jax.random.randint(splits[6], (SLOTS, ROWS, COLS), 1, 9), jax.random.fold_in(splits[6], 1), 1, 8).astype(jnp.int32)
    tile_counts = draw_tile_counts(jax.random.fold_in(splits[8], 71), 0)
    return {"fields": fields, "cotangent": cotangent, "kernel_in": kernel_in, "kernel_mid": kernel_mid, "kernel_out": kernel_out, "patch_anchors": patch_anchors, "blend_weights": blend_weights, "tile_counts": tile_counts}


KERNEL_TAPS = ((0, 0), (0, 1), (0, 2), (1, 0), (1, 1), (1, 2), (2, 0), (2, 1), (2, 2))

def contract(form, left_side, right_side):
    return jnp.einsum(form, left_side.astype(jnp.float32), right_side.astype(jnp.float32), precision=lax.Precision.HIGHEST)

def forward_conv(values, kernel):
    height, breadth = (values.shape[1], values.shape[2])
    padded = jnp.pad(values, ((0, 0), (1, 1), (1, 1)))
    summed = jnp.zeros((kernel.shape[1], height, breadth), jnp.float32)
    for tap_index, (tap_row, tap_col) in enumerate(KERNEL_TAPS):
        summed = summed + contract('ok,khw->ohw', kernel[tap_index], padded[:, tap_row:tap_row + height, tap_col:tap_col + breadth])
    return summed

def backward_conv(cotangent, kernel):
    height, breadth = (cotangent.shape[1], cotangent.shape[2])
    padded = jnp.pad(cotangent, ((0, 0), (1, 1), (1, 1)))
    summed = jnp.zeros((kernel.shape[2], height, breadth), jnp.float32)
    for tap_index, (tap_row, tap_col) in enumerate(KERNEL_TAPS):
        summed = summed + contract('ok,ohw->khw', kernel[tap_index], padded[:, 2 - tap_row:2 - tap_row + height, 2 - tap_col:2 - tap_col + breadth])
    return summed

def kernel_grad(cotangent, values):
    height, breadth = (values.shape[1], values.shape[2])
    padded = jnp.pad(values, ((0, 0), (1, 1), (1, 1)))
    pieces = [contract('ohw,khw->ok', cotangent, padded[:, tap_row:tap_row + height, tap_col:tap_col + breadth]) for tap_row, tap_col in KERNEL_TAPS]
    return jnp.stack(pieces)

def silu_slope(pre_act):
    sigmoid = jax.nn.sigmoid(pre_act)
    return sigmoid * (1.0 + pre_act * (1.0 - sigmoid))

def patch_pass(inputs, out_grad, kernel_in, kernel_mid, kernel_out):
    pre_one = forward_conv(inputs, kernel_in)
    hidden_one = jax.nn.silu(pre_one).astype(jnp.bfloat16)
    pre_two = forward_conv(hidden_one, kernel_mid)
    hidden_two = (hidden_one.astype(jnp.float32) + jax.nn.silu(pre_two)).astype(jnp.bfloat16)
    result = forward_conv(hidden_two, kernel_out)
    grad_two = backward_conv(out_grad, kernel_out)
    delta_two = (grad_two * silu_slope(pre_two)).astype(jnp.bfloat16)
    grad_one = grad_two + backward_conv(delta_two, kernel_mid)
    delta_one = (grad_one * silu_slope(pre_one)).astype(jnp.bfloat16)
    return (result, kernel_grad(delta_one, inputs), kernel_grad(delta_two, hidden_one), kernel_grad(out_grad, hidden_two))

def extend_field(values):
    wrapped = jnp.concatenate([values[:, :, COLS - MARGIN:], values, values[:, :, :MARGIN]], axis=2)
    return jnp.pad(wrapped, ((0, 0), (MARGIN, MARGIN), (0, 0)))

def fold_field(extended):
    center_part = extended[:, MARGIN:MARGIN + ROWS, MARGIN:MARGIN + COLS]
    left_rim = extended[:, MARGIN:MARGIN + ROWS, :MARGIN]
    right_rim = extended[:, MARGIN:MARGIN + ROWS, MARGIN + COLS:]
    center_part = center_part.at[:, :, :MARGIN].add(right_rim)
    center_part = center_part.at[:, :, COLS - MARGIN:].add(left_rim)
    return center_part

def reference(fields, cotangent, kernel_in, kernel_mid, kernel_out, patch_anchors, blend_weights, tile_counts):
    total_slots = LAT_TILES * LON_TILES * SLOTS
    slot_ids = jnp.arange(total_slots, dtype=jnp.int32)
    flat_counts = tile_counts.reshape(-1).astype(jnp.int32)
    alive_flags = (slot_ids % SLOTS < flat_counts[slot_ids // SLOTS]).astype(jnp.int32)
    live_order = jnp.argsort(1 - alive_flags, stable=True)[:total_slots // 2].astype(jnp.int32)

    def patch_info(flat_index):
        tile_id = flat_index // SLOTS
        slot_id = flat_index % SLOTS
        lat_id = tile_id // LON_TILES
        lon_id = tile_id % LON_TILES
        row_start = (lat_id * TILE_ROWS + patch_anchors[lat_id, lon_id, slot_id, 0]).astype(jnp.int32)
        col_start = (lon_id * TILE_COLS + patch_anchors[lat_id, lon_id, slot_id, 1]).astype(jnp.int32)
        weight = lax.dynamic_slice(blend_weights, (slot_id.astype(jnp.int32), (lat_id * TILE_ROWS).astype(jnp.int32), (lon_id * TILE_COLS).astype(jnp.int32)), (1, TILE_ROWS, TILE_COLS)).astype(jnp.float32)
        return (row_start, col_start, weight)

    def add_weight(canvas, flat_index):
        row_start, col_start, weight = patch_info(flat_index)
        corner = (jnp.int32(0), row_start, col_start)
        current = lax.dynamic_slice(canvas, corner, (1, TILE_ROWS, TILE_COLS))
        return (lax.dynamic_update_slice(canvas, current + weight, corner), None)
    weight_canvas = lax.scan(add_weight, jnp.zeros((1, ROWS + 2 * MARGIN, COLS + 2 * MARGIN), jnp.float32), live_order)[0]
    total_weight = jnp.maximum(fold_field(weight_canvas), 1.0)
    scaled = (cotangent.astype(jnp.float32) / total_weight).astype(jnp.bfloat16)
    wide_fields = extend_field(fields)
    wide_scaled = extend_field(scaled)

    def add_patch(running, flat_index):
        row_start, col_start, weight = patch_info(flat_index)
        corner = (jnp.int32(0), row_start, col_start)
        inputs = lax.dynamic_slice(wide_fields, corner, (CHANNELS, TILE_ROWS, TILE_COLS))
        out_grad = (weight * lax.dynamic_slice(wide_scaled, corner, (CHANNELS, TILE_ROWS, TILE_COLS)).astype(jnp.float32)).astype(jnp.bfloat16)
        result, part_in, part_mid, part_out = patch_pass(inputs, out_grad, kernel_in, kernel_mid, kernel_out)
        current = lax.dynamic_slice(running[0], corner, (CHANNELS, TILE_ROWS, TILE_COLS))
        numerator = lax.dynamic_update_slice(running[0], current + weight * result, corner)
        return ((numerator, running[1] + part_in, running[2] + part_mid, running[3] + part_out), None)
    initial = (jnp.zeros((CHANNELS, ROWS + 2 * MARGIN, COLS + 2 * MARGIN), jnp.float32), jnp.zeros(kernel_in.shape, jnp.float32), jnp.zeros(kernel_mid.shape, jnp.float32), jnp.zeros(kernel_out.shape, jnp.float32))
    finals = lax.scan(add_patch, initial, live_order)[0]
    blended = fold_field(finals[0]) / total_weight
    return (blended, finals[1], finals[2], finals[3])
```

```python
import functools

import jax
import jax.numpy as jnp
from jax import lax
from jax.experimental import pallas as pl
from jax.experimental.pallas import tpu as pltpu
from jax.sharding import PartitionSpec as P

MARGIN = 4
SLOTS = 4
LANES = 128
F32 = jnp.float32
BF16 = jnp.bfloat16
VMEM_LIMIT = 48 * 1024 * 1024


def vmem():
    return pl.BlockSpec(memory_space=pltpu.VMEM)


def smem():
    return pl.BlockSpec(memory_space=pltpu.SMEM)


def lane_ids(shape):
    return lax.broadcasted_iota(jnp.int32, shape, len(shape) - 1)


def roll(value, shift, axis):
    size = value.shape[axis]
    if isinstance(shift, int):
        shift = shift % size
        if shift == 0:
            return value
    return pltpu.roll(value, shift, axis)


def pack_kernel(anchors, counts, fields, cotangent, weights, center, to_up, to_down, edges, canvas, spread):
    channels, rows, cols = fields.shape
    wide = cols + LANES
    spread[...] = jnp.zeros_like(spread)
    for slot in range(SLOTS):

        @pl.when(slot < counts[0, 0])
        def _():
            row = anchors[0, 0, slot, 0]
            col = anchors[0, 0, slot, 1]
            values = weights[slot].astype(F32)
            values = jnp.concatenate([values, jnp.zeros((rows, LANES), F32)], axis=1)
            values = jnp.concatenate([values, jnp.zeros((2 * MARGIN, wide), F32)], axis=0)
            values = roll(values, lax.rem(col + (wide - MARGIN), wide), 1)
            values = roll(values, row, 0)
            spread[...] += values

    total = spread[...]
    canvas[...] = total
    both = []
    for source in (fields, cotangent):
        both.append(jnp.swapaxes(source[...].astype(F32), 0, 1))
    tile = jnp.concatenate(both, axis=1)
    center[...] = tile.astype(BF16)
    to_up[0:MARGIN] = tile[:MARGIN].astype(BF16)
    to_down[0:MARGIN] = tile[rows - MARGIN :].astype(BF16)
    lanes = lane_ids((2 * channels, LANES))
    packed = jnp.zeros((2 * channels, LANES), F32)
    for row in range(rows):
        first = jnp.where(lanes < MARGIN, tile[row, :, :LANES], 0.0)
        last = jnp.where(lanes >= LANES - MARGIN, tile[row, :, cols - LANES :], 0.0)
        packed = packed + roll(first, MARGIN * row, 1) + roll(last, -MARGIN * row, 1)
    edges[0 : 2 * channels] = packed.astype(BF16)
    first = total[:, :LANES]
    last = total[:, cols - LANES : cols]
    margin = total[:, cols:]
    lanes = lane_ids(margin.shape)
    height = margin.shape[0]
    to_left = jnp.where(lanes < LANES // 2, first, margin)
    to_right = jnp.where(lanes < LANES // 2, margin, last)
    edges[2 * channels : 2 * channels + height] = to_left.astype(BF16)
    edges[2 * channels + height : 2 * channels + 2 * height] = to_right.astype(BF16)
    half = height // 2
    pad = jnp.zeros((2 * channels - height, cols), F32)
    for target, part in ((to_up, total[:half]), (to_down, total[half:])):
        beside = jnp.concatenate([part[:, cols:], jnp.zeros((half, cols - LANES), F32)], axis=1)
        extra = jnp.concatenate([part[:, :cols], beside, pad], axis=0)
        target[MARGIN] = extra.astype(BF16)


def dot(left, right):
    return jnp.dot(left, right, preferred_element_type=F32)


def dot_lanes(left, right):
    return lax.dot_general(left, right, (((1,), (1,)), ((), ())), preferred_element_type=F32)


def patch_kernel(
    anchors, counts, center, up, down, left, right, up_left, up_right, down_left, down_right, canvas, weights,
    w_in, w_mid, w_mid_back, w_out, w_out_back,
    grads, inner, to_up, to_down, edges, den_out,
    window, numer, x_s, d_s, h_s, z_s, slope_s, dh_s, h2_s, dz_s, y_s,
):
    rows = center.shape[0]
    channels = center.shape[1] // 2
    cols = center.shape[2]
    wide = cols + LANES
    width = w_mid.shape[0]
    full = rows * cols
    height = rows + 2 * MARGIN
    half = height // 2
    lanes = lane_ids((2 * channels, LANES))

    total = canvas[...]
    upper = up[MARGIN].astype(F32)
    lower = down[MARGIN].astype(F32)

    def stretch(block):
        return jnp.concatenate([block[:half], block[half:height, :LANES]], axis=1)

    total = total + jnp.concatenate([stretch(upper), stretch(lower)], axis=0)
    base = 2 * channels
    left_part = left[base + height : base + 2 * height].astype(F32)
    left_part = left_part + jnp.concatenate(
        [
            up_left[base + height : base + 2 * height].astype(F32)[half:],
            down_left[base + height : base + 2 * height].astype(F32)[:half],
        ],
        axis=0,
    )
    right_part = right[base : base + height].astype(F32)
    right_part = right_part + jnp.concatenate(
        [
            up_right[base : base + height].astype(F32)[half:],
            down_right[base : base + height].astype(F32)[:half],
        ],
        axis=0,
    )
    edge_lanes = lane_ids((height, LANES))
    low = edge_lanes < MARGIN
    high = edge_lanes >= LANES - MARGIN
    zero = jnp.zeros((height, LANES), F32)
    pieces = [jnp.where(low, left_part, zero)]
    for _ in range(cols // LANES - 2):
        pieces.append(zero)
    pieces.append(jnp.where(high, right_part, zero))
    pieces.append(jnp.where(high, left_part, zero) + jnp.where(low, right_part, zero))
    den = jnp.maximum(total + jnp.concatenate(pieces, axis=1), 1.0)
    den_out[...] = den[MARGIN : MARGIN + rows, :cols]
    inverse = 1.0 / den

    left_e = left[0:base].astype(F32)
    right_e = right[0:base].astype(F32)
    up_left_e = up_left[0:base].astype(F32)
    up_right_e = up_right[0:base].astype(F32)
    down_left_e = down_left[0:base].astype(F32)
    down_right_e = down_right[0:base].astype(F32)
    for row in range(height):
        if row < MARGIN:
            body, from_left, from_right, at = up[row], up_left_e, up_right_e, rows - MARGIN + row
        elif row < MARGIN + rows:
            body, from_left, from_right, at = center[row - MARGIN], left_e, right_e, row - MARGIN
        else:
            body, from_left, from_right, at = down[row - MARGIN - rows], down_left_e, down_right_e, row - MARGIN - rows
        beside = jnp.where(
            lanes < LANES // 2, roll(from_right, -MARGIN * at, 1), roll(from_left, MARGIN * at, 1)
        )
        line = jnp.concatenate([body.astype(F32), beside], axis=1)
        scaled = line[channels:] * inverse[row : row + 1]
        window[row, 0:channels] = line[:channels]
        window[row, channels : 2 * channels] = scaled.astype(BF16).astype(F32)

    numer[...] = jnp.zeros_like(numer)
    grads[...] = jnp.zeros_like(grads)
    for ref in (x_s, d_s, h_s, z_s):
        ref[:, 0:cols] = jnp.zeros((ref.shape[0], cols), BF16)
        ref[:, cols + full : 2 * cols + full] = jnp.zeros((ref.shape[0], cols), BF16)
    y_s[:, 0:cols] = jnp.zeros((y_s.shape[0], cols), F32)
    y_s[:, cols + full : 2 * cols + full] = jnp.zeros((y_s.shape[0], cols), F32)

    def before(value):
        ids = lane_ids(value.shape)
        return jnp.where(ids == 0, 0.0, roll(value, 1, 1))

    def after(value):
        ids = lane_ids(value.shape)
        return jnp.where(ids == cols - 1, 0.0, roll(value, cols - 1, 1))

    def spread(ref, value, row, flip):
        count = value.shape[0]
        at = slice((row + 1) * cols, (row + 2) * cols)
        first, last = before(value), after(value)
        if flip:
            first, last = last, first
        ref[0:count, at] = first.astype(BF16)
        ref[count : 2 * count, at] = value.astype(BF16)
        ref[2 * count : 3 * count, at] = last.astype(BF16)

    def stack(ref, row, flip):
        starts = [(row + (2 - tap if flip else tap)) * cols for tap in range(3)]
        return jnp.concatenate([ref[:, start : start + cols] for start in starts], axis=0)

    def one_patch(slot, carry):
        row0 = anchors[0, 0, slot, 0]
        col0 = anchors[0, 0, slot, 1]
        patch_weights = weights[slot].astype(F32)
        back_shift = lax.rem(wide + MARGIN - col0, wide)
        for row in range(rows):
            line = roll(window[row0 + row], back_shift, 1)[:, :cols]
            spread(x_s, line[:channels], row, False)
            grad = line[channels:] * patch_weights[row : row + 1]
            spread(d_s, grad.astype(BF16).astype(F32), row, True)
        for row in range(rows):
            at = slice(row * cols, (row + 1) * cols)
            z1 = dot(w_in[...], stack(x_s, row, False))
            sig = 0.5 * jnp.tanh(0.5 * z1) + 0.5
            h1 = (z1 * sig).astype(BF16).astype(F32)
            slope_s[:, at] = sig * (1.0 + z1 * (1.0 - sig))
            spread(h_s, h1, row, False)
        for row in range(rows):
            at = slice(row * cols, (row + 1) * cols)
            dh2 = dot(w_out_back[...], stack(d_s, row, True))
            z2 = dot(w_mid[...], stack(h_s, row, False))
            sig = 0.5 * jnp.tanh(0.5 * z2) + 0.5
            h1 = h_s[width : 2 * width, (row + 1) * cols : (row + 2) * cols].astype(F32)
            h2 = (h1 + z2 * sig).astype(BF16)
            h2_s[:, at] = h2
            dz2 = (dh2 * (sig * (1.0 + z2 * (1.0 - sig)))).astype(BF16).astype(F32)
            dh_s[:, at] = dh2
            spread(z_s, dz2, row, True)
            y_s[:, (row + 1) * cols : (row + 2) * cols] = dot(w_out[...], h2)
        for row in range(rows):
            at = slice(row * cols, (row + 1) * cols)
            dh1 = dh_s[:, at] + dot(w_mid_back[...], stack(z_s, row, True))
            dz_s[:, at] = (dh1 * slope_s[:, at]).astype(BF16)
        small = 9 * channels
        for tap in range(3):
            ahead = slice(tap * cols, tap * cols + full)
            behind = slice((2 - tap) * cols, (2 - tap) * cols + full)
            at = slice(tap * 3 * channels, (tap + 1) * 3 * channels)
            grads[at] += dot_lanes(x_s[:, ahead], dz_s[...])
            part = dot_lanes(z_s[width : 2 * width, cols : cols + full], h_s[:, ahead])
            for tap_col in range(3):
                start = small + (3 * tap + tap_col) * width
                grads[start : start + width] += part[:, tap_col * width : (tap_col + 1) * width]
            at = slice(small + 9 * width + tap * 3 * channels, small + 9 * width + (tap + 1) * 3 * channels)
            grads[at] += dot_lanes(d_s[:, behind], h2_s[...])
        for row in range(rows):
            sums = []
            for tap_col in range(3):
                terms = [
                    y_s[
                        (3 * tap + tap_col) * channels : (3 * tap + tap_col + 1) * channels,
                        (row + tap) * cols : (row + tap + 1) * cols,
                    ]
                    for tap in range(3)
                ]
                sums.append(terms[0] + terms[1] + terms[2])
            result = before(sums[0]) + sums[1] + after(sums[2])
            result = result * patch_weights[row : row + 1]
            result = jnp.concatenate([result, jnp.zeros((channels, LANES), F32)], axis=1)
            numer[row0 + row] += roll(result, lax.rem(col0 + (wide - MARGIN), wide), 1)
        return carry

    lax.fori_loop(0, counts[0, 0], one_patch, 0)

    lanes = lane_ids((channels, LANES))
    packed = jnp.zeros((channels, LANES), F32)
    for row in range(height):
        beside = numer[row, :, cols:]
        first = jnp.where(lanes < MARGIN, beside, 0.0)
        last = jnp.where(lanes >= LANES - MARGIN, beside, 0.0)
        packed = packed + roll(first, MARGIN * row, 1) + roll(last, -MARGIN * row, 1)
    edges[...] = packed
    to_up[...] = numer[0:MARGIN, :, :cols]
    inner[...] = numer[MARGIN : MARGIN + rows, :, :cols]
    to_down[...] = numer[MARGIN + rows :, :, :cols]


def fold_kernel(
    inner, up, down, left, right, up_left, up_right, down_left, down_right, den, blended
):
    rows, channels, cols = inner.shape
    lanes = lane_ids((channels, LANES))
    inverse = 1.0 / den[...]
    lines = []
    for row in range(rows):
        line = inner[row]
        from_left = jnp.where(lanes < MARGIN, roll(left[...], -MARGIN * (row + MARGIN), 1), 0.0)
        from_right = jnp.where(lanes >= LANES - MARGIN, roll(right[...], MARGIN * (row + MARGIN), 1), 0.0)
        if row < MARGIN:
            line = line + up[row]
            at = MARGIN * (row + MARGIN + rows)
            more_left, more_right = up_left, up_right
        else:
            line = line + down[row - (rows - MARGIN)]
            at = MARGIN * (row - (rows - MARGIN))
            more_left, more_right = down_left, down_right
        from_left = from_left + jnp.where(lanes < MARGIN, roll(more_left[...], -at, 1), 0.0)
        from_right = from_right + jnp.where(lanes >= LANES - MARGIN, roll(more_right[...], at, 1), 0.0)
        beside = [from_left]
        for _ in range(cols // LANES - 2):
            beside.append(jnp.zeros((channels, LANES), F32))
        beside.append(from_right)
        line = line + jnp.concatenate(beside, axis=1)
        lines.append((line * inverse[row : row + 1])[None])
    blended[...] = jnp.swapaxes(jnp.concatenate(lines, axis=0), 0, 1)


def split_kernel(summed, grad_in, grad_mid, grad_out):
    taps, width, channels = grad_in.shape
    for tap in range(taps):
        grad_in[tap] = summed[tap * channels : (tap + 1) * channels].astype(F32).T
        start = taps * channels + tap * width
        grad_mid[tap] = summed[start : start + width].astype(F32)
        start = taps * (channels + width) + tap * channels
        grad_out[tap] = summed[start : start + channels].astype(F32)


def params():
    return pltpu.CompilerParams(vmem_limit_bytes=VMEM_LIMIT)


def shift(value, lat_step, lon_step):
    lat_size, lon_size = lax.axis_size("lat"), lax.axis_size("lon")
    pairs = []
    for lat in range(lat_size):
        for lon in range(lon_size):
            if 0 <= lat + lat_step < lat_size:
                target = (lat + lat_step) * lon_size + (lon + lon_step) % lon_size
                pairs.append((lat * lon_size + lon, target))
    return lax.ppermute(value, ("lat", "lon"), pairs)


def neighbours(to_up, to_down, edges):
    up = shift(to_down, 1, 0)
    down = shift(to_up, -1, 0)
    left = shift(edges, 0, 1)
    right = shift(edges, 0, -1)
    up_left = shift(edges, 1, 1)
    down_right = shift(edges, -1, -1)
    up_right = shift(edges, 1, -1)
    down_left = shift(edges, -1, 1)
    return up, down, left, right, up_left, up_right, down_left, down_right


def reduce_all(grads):
    lat_size, lon_size = lax.axis_size("lat"), lax.axis_size("lon")
    length = grads.shape[0]
    parts = grads.astype(BF16).reshape(lat_size, length // lat_size, LANES)
    parts = lax.all_to_all(parts, "lat", 0, 0)
    mine = jnp.sum(parts.astype(F32), axis=0)
    parts = mine.reshape(lon_size, length // (lat_size * lon_size), LANES)
    parts = lax.all_to_all(parts, "lon", 0, 0)
    mine = jnp.sum(parts, axis=0).astype(BF16)
    parts = jnp.broadcast_to(mine[None], (lon_size,) + mine.shape)
    parts = lax.all_to_all(parts, "lon", 0, 0)
    mine = parts.reshape(length // lat_size, LANES)
    parts = jnp.broadcast_to(mine[None], (lat_size,) + mine.shape)
    parts = lax.all_to_all(parts, "lat", 0, 0)
    return parts.reshape(length, LANES)


def shards(
    fields, cotangent, kernel_in, kernel_mid, kernel_out, patch_anchors, blend_weights, tile_counts
):
    channels, rows, cols = fields.shape
    taps, width, _ = kernel_in.shape
    height = rows + 2 * MARGIN
    wide = cols + LANES
    full = rows * cols
    padded = full + 2 * cols
    shape = jax.ShapeDtypeStruct
    center, to_up, to_down, edges, canvas = pl.pallas_call(
        pack_kernel,
        out_shape=(
            shape((rows, 2 * channels, cols), BF16),
            shape((MARGIN + 1, 2 * channels, cols), BF16),
            shape((MARGIN + 1, 2 * channels, cols), BF16),
            shape((2 * channels + 2 * height, LANES), BF16),
            shape((height, wide), F32),
        ),
        in_specs=[smem(), smem(), vmem(), vmem(), vmem()],
        out_specs=(vmem(),) * 5,
        scratch_shapes=[pltpu.VMEM((height, wide), F32)],
        compiler_params=params(),
        name="pack",
    )(patch_anchors, tile_counts, fields, cotangent, blend_weights)
    received = neighbours(to_up, to_down, edges)

    w_in = jnp.transpose(kernel_in, (1, 0, 2)).reshape(width, taps * channels)
    w_mid = jnp.transpose(kernel_mid, (1, 0, 2)).reshape(width, taps * width)
    w_mid_back = jnp.transpose(kernel_mid, (2, 0, 1)).reshape(width, taps * width)
    w_out = kernel_out.reshape(taps * channels, width)
    w_out_back = jnp.transpose(kernel_out, (2, 0, 1)).reshape(width, taps * channels)

    length = taps * (2 * channels + width)
    unit = 8 * lax.axis_size("lat") * lax.axis_size("lon")
    length = (length + unit - 1) // unit * unit
    grads, inner, out_up, out_down, out_edges, den = pl.pallas_call(
        patch_kernel,
        out_shape=(
            shape((length, LANES), F32),
            shape((rows, channels, cols), F32),
            shape((MARGIN, channels, cols), F32),
            shape((MARGIN, channels, cols), F32),
            shape((channels, LANES), F32),
            shape((rows, cols), F32),
        ),
        in_specs=[smem(), smem()] + [vmem()] * 16,
        out_specs=(vmem(),) * 6,
        scratch_shapes=[
            pltpu.VMEM((height, 2 * channels, wide), F32),
            pltpu.VMEM((height, channels, wide), F32),
            pltpu.VMEM((3 * channels, padded), BF16),
            pltpu.VMEM((3 * channels, padded), BF16),
            pltpu.VMEM((3 * width, padded), BF16),
            pltpu.VMEM((3 * width, padded), BF16),
            pltpu.VMEM((width, full), F32),
            pltpu.VMEM((width, full), F32),
            pltpu.VMEM((width, full), BF16),
            pltpu.VMEM((width, full), BF16),
            pltpu.VMEM((taps * channels, padded), F32),
        ],
        compiler_params=params(),
        name="patches",
    )(
        patch_anchors, tile_counts, center, *received, canvas, blend_weights,
        w_in, w_mid, w_mid_back, w_out, w_out_back,
    )
    summed = reduce_all(grads)
    returned = neighbours(out_up, out_down, out_edges)
    blended = pl.pallas_call(
        fold_kernel,
        out_shape=shape((channels, rows, cols), F32),
        in_specs=[vmem()] * 10,
        out_specs=vmem(),
        compiler_params=params(),
        name="fold",
    )(inner, *returned, den)
    grad_in, grad_mid, grad_out = pl.pallas_call(
        split_kernel,
        out_shape=(
            shape((taps, width, channels), F32),
            shape((taps, width, width), F32),
            shape((taps, channels, width), F32),
        ),
        in_specs=[vmem()],
        out_specs=(vmem(),) * 3,
        compiler_params=params(),
        name="split",
    )(summed)
    return blended, grad_in, grad_mid, grad_out


def solution(mesh):
    return jax.shard_map(
        shards,
        mesh=mesh,
        in_specs=(
            P(None, "lat", "lon"),
            P(None, "lat", "lon"),
            P(),
            P(),
            P(),
            P("lat", "lon", None, None),
            P(None, "lat", "lon"),
            P("lat", "lon"),
        ),
        out_specs=(P(None, "lat", "lon"), P(), P(), P()),
        check_vma=False,
    )
```

```python
import functools

import jax
import jax.numpy as jnp
from jax import lax
from jax.experimental import pallas as pl
from jax.experimental.pallas import tpu as pltpu
from jax.sharding import PartitionSpec as P

MARGIN = 4
SLOTS = 4
LANES = 128
F32 = jnp.float32
BF16 = jnp.bfloat16
VMEM_LIMIT = 48 * 1024 * 1024


def vmem():
    return pl.BlockSpec(memory_space=pltpu.VMEM)


def smem():
    return pl.BlockSpec(memory_space=pltpu.SMEM)


def lane_ids(shape):
    return lax.broadcasted_iota(jnp.int32, shape, len(shape) - 1)


def roll(value, shift, axis):
    size = value.shape[axis]
    if isinstance(shift, int):
        shift = shift % size
        if shift == 0:
            return value
    return pltpu.roll(value, shift, axis)


def choose(odd, when_odd, when_even):
    return jnp.where(odd, when_odd, when_even)


def pack_kernel(
    anchors, counts, fields_in, cotangent_in, weights_in, center, first_out, second_out, canvas,
    fields, cotangent, weights, spread, sems,
):
    copies = []
    for index, (source, target) in enumerate(
        ((weights_in, weights), (fields_in, fields), (cotangent_in, cotangent))
    ):
        copy = pltpu.make_async_copy(source, target, sems.at[index])
        copy.start()
        copies.append(copy)
    channels, rows, cols = fields.shape
    wide = cols + LANES
    odd = lax.rem(lax.axis_index("lat"), 2) == 1
    spread[...] = jnp.zeros_like(spread)
    copies[0].wait()
    for slot in range(SLOTS):

        @pl.when(slot < counts[0, 0])
        def _():
            row = anchors[0, 0, slot, 0]
            col = anchors[0, 0, slot, 1]
            values = weights[slot].astype(F32)
            values = jnp.concatenate([values, jnp.zeros((rows, LANES), F32)], axis=1)
            values = jnp.concatenate([values, jnp.zeros((2 * MARGIN, wide), F32)], axis=0)
            values = roll(values, lax.rem(col + (wide - MARGIN), wide), 1)
            values = roll(values, row, 0)
            spread[...] += values

    total = spread[...]
    canvas[...] = total
    copies[1].wait()
    copies[2].wait()
    both = []
    for source in (fields, cotangent):
        both.append(jnp.swapaxes(source[...].astype(F32), 0, 1))
    tile = jnp.concatenate(both, axis=1).astype(BF16)
    center[...] = tile
    half = total.shape[0] // 2
    pad = jnp.zeros((2 * channels - 2 * half, cols), F32)
    extras = []
    for part in (total[:half], total[half:]):
        beside = jnp.concatenate([part[:, cols:], jnp.zeros((half, cols - LANES), F32)], axis=1)
        extras.append(jnp.concatenate([part[:, :cols], beside, pad], axis=0).astype(BF16))
    top, bottom = tile[:MARGIN], tile[rows - MARGIN :]
    first_out[0:MARGIN] = choose(odd, top, bottom)
    first_out[MARGIN] = choose(odd, extras[0], extras[1])
    second_out[0:MARGIN] = choose(odd, bottom, top)
    second_out[MARGIN] = choose(odd, extras[1], extras[0])


def edge_kernel(center, first, second, canvas, edges, total_out):
    rows = center.shape[0]
    channels = center.shape[1] // 2
    cols = center.shape[2]
    height = rows + 2 * MARGIN
    half = height // 2
    odd = lax.rem(lax.axis_index("lat"), 2) == 1

    def stretch(block):
        block = block.astype(F32)
        return jnp.concatenate([block[:half], block[half:height, :LANES]], axis=1)

    upper = stretch(choose(odd, first[MARGIN], second[MARGIN]))
    lower = stretch(choose(odd, second[MARGIN], first[MARGIN]))
    total = canvas[...] + jnp.concatenate([upper, lower], axis=0)
    total_out[...] = total
    lanes = lane_ids((2 * channels, LANES))
    packed = jnp.zeros((2 * channels, LANES), F32)
    for row in range(height):
        if row < MARGIN:
            line = choose(odd, first[row], second[row])
        elif row < MARGIN + rows:
            line = center[row - MARGIN]
        else:
            line = choose(odd, second[row - MARGIN - rows], first[row - MARGIN - rows])
        line = line.astype(F32)
        low = jnp.where(lanes < MARGIN, line[:, :LANES], 0.0)
        high = jnp.where(lanes >= LANES - MARGIN, line[:, cols - LANES :], 0.0)
        packed = packed + roll(low, MARGIN * row, 1) + roll(high, -MARGIN * row, 1)
    edges[0 : 2 * channels] = packed.astype(BF16)
    margin = total[:, cols:]
    lanes = lane_ids(margin.shape)
    to_left = jnp.where(lanes < LANES // 2, total[:, :LANES], margin)
    to_right = jnp.where(lanes < LANES // 2, margin, total[:, cols - LANES : cols])
    edges[2 * channels : 2 * channels + height] = to_left.astype(BF16)
    edges[2 * channels + height : 2 * channels + 2 * height] = to_right.astype(BF16)


def dot(left, right):
    return jnp.dot(left, right, preferred_element_type=F32)


def dot_lanes(left, right):
    return lax.dot_general(left, right, (((1,), (1,)), ((), ())), preferred_element_type=F32)


def patch_kernel(
    anchors, counts, center, first, second, third, fourth, total_in, weights,
    w_in, w_mid, w_mid_back, w_out, w_out_back,
    grads, numer, edges, den_out,
    window, x_s, d_s, h_s, z_s, slope_s, dh_s, h2_s, dz_s, y_s,
):
    rows = center.shape[0]
    channels = center.shape[1] // 2
    cols = center.shape[2]
    wide = cols + LANES
    width = w_mid.shape[0]
    full = rows * cols
    height = rows + 2 * MARGIN
    lanes = lane_ids((2 * channels, LANES))
    lat_odd = lax.rem(lax.axis_index("lat"), 2) == 1
    lon_odd = lax.rem(lax.axis_index("lon"), 2) == 1

    left = choose(lon_odd, third[...], fourth[...]).astype(F32)
    right = choose(lon_odd, fourth[...], third[...]).astype(F32)
    base = 2 * channels
    left_part = left[base + height : base + 2 * height]
    right_part = right[base : base + height]
    edge_lanes = lane_ids((height, LANES))
    low = edge_lanes < MARGIN
    high = edge_lanes >= LANES - MARGIN
    zero = jnp.zeros((height, LANES), F32)
    pieces = [jnp.where(low, left_part, zero)]
    for _ in range(cols // LANES - 2):
        pieces.append(zero)
    pieces.append(jnp.where(high, right_part, zero))
    pieces.append(jnp.where(high, left_part, zero) + jnp.where(low, right_part, zero))
    den = jnp.maximum(total_in[...] + jnp.concatenate(pieces, axis=1), 1.0)
    den_out[...] = den[MARGIN : MARGIN + rows, :cols]
    inverse = 1.0 / den

    left = left[:base]
    right = right[:base]
    for row in range(height):
        if row < MARGIN:
            body = choose(lat_odd, first[row], second[row])
        elif row < MARGIN + rows:
            body = center[row - MARGIN]
        else:
            body = choose(lat_odd, second[row - MARGIN - rows], first[row - MARGIN - rows])
        beside = jnp.where(
            lanes < LANES // 2, roll(right, -MARGIN * row, 1), roll(left, MARGIN * row, 1)
        )
        line = jnp.concatenate([body.astype(F32), beside], axis=1)
        scaled = line[channels:] * inverse[row : row + 1]
        window[row, 0:channels] = line[:channels]
        window[row, channels : 2 * channels] = scaled.astype(BF16).astype(F32)

    numer[...] = jnp.zeros_like(numer)
    grads[...] = jnp.zeros_like(grads)
    for ref in (x_s, d_s, h_s, z_s):
        ref[:, 0:cols] = jnp.zeros((ref.shape[0], cols), BF16)
        ref[:, cols + full : 2 * cols + full] = jnp.zeros((ref.shape[0], cols), BF16)
    y_s[:, 0:cols] = jnp.zeros((y_s.shape[0], cols), F32)
    y_s[:, cols + full : 2 * cols + full] = jnp.zeros((y_s.shape[0], cols), F32)

    def before(value):
        ids = lane_ids(value.shape)
        return jnp.where(ids == 0, 0.0, roll(value, 1, 1))

    def after(value):
        ids = lane_ids(value.shape)
        return jnp.where(ids == cols - 1, 0.0, roll(value, cols - 1, 1))

    def spread(ref, value, row, flip):
        count = value.shape[0]
        at = slice((row + 1) * cols, (row + 2) * cols)
        first, last = before(value), after(value)
        if flip:
            first, last = last, first
        ref[0:count, at] = first.astype(BF16)
        ref[count : 2 * count, at] = value.astype(BF16)
        ref[2 * count : 3 * count, at] = last.astype(BF16)

    def stack(ref, row, flip):
        starts = [(row + (2 - tap if flip else tap)) * cols for tap in range(3)]
        return jnp.concatenate([ref[:, start : start + cols] for start in starts], axis=0)

    def one_patch(slot, carry):
        row0 = anchors[0, 0, slot, 0]
        col0 = anchors[0, 0, slot, 1]
        patch_weights = weights[slot].astype(F32)
        back_shift = lax.rem(wide + MARGIN - col0, wide)
        for row in range(rows):
            line = roll(window[row0 + row], back_shift, 1)[:, :cols]
            spread(x_s, line[:channels], row, False)
            grad = line[channels:] * patch_weights[row : row + 1]
            spread(d_s, grad.astype(BF16).astype(F32), row, True)
        for row in range(rows):
            at = slice(row * cols, (row + 1) * cols)
            z1 = dot(w_in[...], stack(x_s, row, False))
            sig = 0.5 * jnp.tanh(0.5 * z1) + 0.5
            h1 = (z1 * sig).astype(BF16).astype(F32)
            slope_s[:, at] = sig * (1.0 + z1 * (1.0 - sig))
            spread(h_s, h1, row, False)
        for row in range(rows):
            at = slice(row * cols, (row + 1) * cols)
            dh2 = dot(w_out_back[...], stack(d_s, row, True))
            z2 = dot(w_mid[...], stack(h_s, row, False))
            sig = 0.5 * jnp.tanh(0.5 * z2) + 0.5
            h1 = h_s[width : 2 * width, (row + 1) * cols : (row + 2) * cols].astype(F32)
            h2 = (h1 + z2 * sig).astype(BF16)
            h2_s[:, at] = h2
            dz2 = (dh2 * (sig * (1.0 + z2 * (1.0 - sig)))).astype(BF16).astype(F32)
            dh_s[:, at] = dh2
            spread(z_s, dz2, row, True)
            y_s[:, (row + 1) * cols : (row + 2) * cols] = dot(w_out[...], h2)
        for row in range(rows):
            at = slice(row * cols, (row + 1) * cols)
            dh1 = dh_s[:, at] + dot(w_mid_back[...], stack(z_s, row, True))
            dz_s[:, at] = (dh1 * slope_s[:, at]).astype(BF16)
        small = 9 * channels
        for tap in range(3):
            ahead = slice(tap * cols, tap * cols + full)
            behind = slice((2 - tap) * cols, (2 - tap) * cols + full)
            at = slice(tap * 3 * channels, (tap + 1) * 3 * channels)
            grads[at] += dot_lanes(x_s[:, ahead], dz_s[...])
            part = dot_lanes(z_s[width : 2 * width, cols : cols + full], h_s[:, ahead])
            for tap_col in range(3):
                start = small + (3 * tap + tap_col) * width
                grads[start : start + width] += part[:, tap_col * width : (tap_col + 1) * width]
            at = slice(small + 9 * width + tap * 3 * channels, small + 9 * width + (tap + 1) * 3 * channels)
            grads[at] += dot_lanes(d_s[:, behind], h2_s[...])
        for row in range(rows):
            sums = []
            for tap_col in range(3):
                terms = [
                    y_s[
                        (3 * tap + tap_col) * channels : (3 * tap + tap_col + 1) * channels,
                        (row + tap) * cols : (row + tap + 1) * cols,
                    ]
                    for tap in range(3)
                ]
                sums.append(terms[0] + terms[1] + terms[2])
            result = before(sums[0]) + sums[1] + after(sums[2])
            result = result * patch_weights[row : row + 1]
            result = jnp.concatenate([result, jnp.zeros((channels, LANES), F32)], axis=1)
            numer[row0 + row] += roll(result, lax.rem(col0 + (wide - MARGIN), wide), 1)
        return carry

    lax.fori_loop(0, counts[0, 0], one_patch, 0)

    lanes = lane_ids((channels, LANES))
    packed = jnp.zeros((channels, LANES), F32)
    for row in range(height):
        beside = numer[row, :, cols:]
        first = jnp.where(lanes < MARGIN, beside, 0.0)
        last = jnp.where(lanes >= LANES - MARGIN, beside, 0.0)
        packed = packed + roll(first, MARGIN * row, 1) + roll(last, -MARGIN * row, 1)
    edges[...] = packed


def beside_kernel(numer, third, fourth, inner, first_out, second_out):
    height, channels, wide = numer.shape
    cols = wide - LANES
    rows = height - 2 * MARGIN
    lanes = lane_ids((channels, LANES))
    lat_odd = lax.rem(lax.axis_index("lat"), 2) == 1
    lon_odd = lax.rem(lax.axis_index("lon"), 2) == 1
    left = choose(lon_odd, third[...], fourth[...])
    right = choose(lon_odd, fourth[...], third[...])
    lines = []
    for row in range(height):
        from_left = jnp.where(lanes < MARGIN, roll(left, -MARGIN * row, 1), 0.0)
        from_right = jnp.where(lanes >= LANES - MARGIN, roll(right, MARGIN * row, 1), 0.0)
        beside = [from_left]
        for _ in range(cols // LANES - 2):
            beside.append(jnp.zeros((channels, LANES), F32))
        beside.append(from_right)
        lines.append(numer[row, :, :cols] + jnp.concatenate(beside, axis=1))
    for row in range(MARGIN):
        upper, lower = lines[row], lines[MARGIN + rows + row]
        first_out[row] = choose(lat_odd, upper, lower)
        second_out[row] = choose(lat_odd, lower, upper)
    for row in range(rows):
        inner[row] = lines[MARGIN + row]


def fold_kernel(inner, first, second, den, blended):
    rows = inner.shape[0]
    lat_odd = lax.rem(lax.axis_index("lat"), 2) == 1
    inverse = 1.0 / den[...]
    lines = []
    for row in range(rows):
        if row < MARGIN:
            other = choose(lat_odd, first[row], second[row])
        else:
            at = row - (rows - MARGIN)
            other = choose(lat_odd, second[at], first[at])
        lines.append(((inner[row] + other) * inverse[row : row + 1])[None])
    blended[...] = jnp.swapaxes(jnp.concatenate(lines, axis=0), 0, 1)


def split_kernel(summed, grad_in, grad_mid, grad_out):
    taps, width, channels = grad_in.shape
    for tap in range(taps):
        grad_in[tap] = summed[tap * channels : (tap + 1) * channels].astype(F32).T
        start = taps * channels + tap * width
        grad_mid[tap] = summed[start : start + width].astype(F32)
        start = taps * (channels + width) + tap * channels
        grad_out[tap] = summed[start : start + channels].astype(F32)


def params():
    return pltpu.CompilerParams(vmem_limit_bytes=VMEM_LIMIT)


def swap(value, axis, first, wrap):
    size = lax.axis_size(axis)
    pairs = []
    for index in range(first, size, 2):
        other = (index + 1) % size
        if other > index or wrap:
            pairs.extend([(index, other), (other, index)])
    return lax.ppermute(value, axis, pairs)


def swap_lat(first, second):
    return swap(first, "lat", 0, False), swap(second, "lat", 1, False)


def swap_lon(edges):
    return swap(edges, "lon", 0, True), swap(edges, "lon", 1, True)


def reduce_all(grads):
    lat_size, lon_size = lax.axis_size("lat"), lax.axis_size("lon")
    length = grads.shape[0]
    parts = grads.astype(BF16).reshape(lat_size, length // lat_size, LANES)
    parts = lax.all_to_all(parts, "lat", 0, 0)
    mine = jnp.sum(parts.astype(F32), axis=0)
    parts = mine.reshape(lon_size, length // (lat_size * lon_size), LANES)
    parts = lax.all_to_all(parts, "lon", 0, 0)
    mine = jnp.sum(parts, axis=0).astype(BF16)
    parts = jnp.broadcast_to(mine[None], (lon_size,) + mine.shape)
    parts = lax.all_to_all(parts, "lon", 0, 0)
    mine = parts.reshape(length // lat_size, LANES)
    parts = jnp.broadcast_to(mine[None], (lat_size,) + mine.shape)
    parts = lax.all_to_all(parts, "lat", 0, 0)
    return parts.reshape(length, LANES)


def shards(
    fields, cotangent, kernel_in, kernel_mid, kernel_out, patch_anchors, blend_weights, tile_counts
):
    channels, rows, cols = fields.shape
    taps, width, _ = kernel_in.shape
    height = rows + 2 * MARGIN
    wide = cols + LANES
    full = rows * cols
    padded = full + 2 * cols
    shape = jax.ShapeDtypeStruct
    center, first, second, canvas = pl.pallas_call(
        pack_kernel,
        out_shape=(
            shape((rows, 2 * channels, cols), BF16),
            shape((MARGIN + 1, 2 * channels, cols), BF16),
            shape((MARGIN + 1, 2 * channels, cols), BF16),
            shape((height, wide), F32),
        ),
        in_specs=[smem(), smem()] + [pl.BlockSpec(memory_space=pl.ANY)] * 3,
        out_specs=(vmem(),) * 4,
        scratch_shapes=[
            pltpu.VMEM(fields.shape, BF16),
            pltpu.VMEM(cotangent.shape, BF16),
            pltpu.VMEM(blend_weights.shape, jnp.int32),
            pltpu.VMEM((height, wide), F32),
            pltpu.SemaphoreType.DMA((3,)),
        ],
        compiler_params=params(),
        name="pack",
    )(patch_anchors, tile_counts, fields, cotangent, blend_weights)
    first, second = swap_lat(first, second)
    edges, total = pl.pallas_call(
        edge_kernel,
        out_shape=(shape((2 * channels + 2 * height, LANES), BF16), shape((height, wide), F32)),
        in_specs=[vmem()] * 4,
        out_specs=(vmem(),) * 2,
        compiler_params=params(),
        name="edges",
    )(center, first, second, canvas)
    third, fourth = swap_lon(edges)

    w_in = jnp.transpose(kernel_in, (1, 0, 2)).reshape(width, taps * channels)
    w_mid = jnp.transpose(kernel_mid, (1, 0, 2)).reshape(width, taps * width)
    w_mid_back = jnp.transpose(kernel_mid, (2, 0, 1)).reshape(width, taps * width)
    w_out = kernel_out.reshape(taps * channels, width)
    w_out_back = jnp.transpose(kernel_out, (2, 0, 1)).reshape(width, taps * channels)

    length = taps * (2 * channels + width)
    unit = 8 * lax.axis_size("lat") * lax.axis_size("lon")
    length = (length + unit - 1) // unit * unit
    grads, numer, edges, den = pl.pallas_call(
        patch_kernel,
        out_shape=(
            shape((length, LANES), F32),
            shape((height, channels, wide), F32),
            shape((channels, LANES), F32),
            shape((rows, cols), F32),
        ),
        in_specs=[smem(), smem()] + [vmem()] * 12,
        out_specs=(vmem(),) * 4,
        scratch_shapes=[
            pltpu.VMEM((height, 2 * channels, wide), F32),
            pltpu.VMEM((3 * channels, padded), BF16),
            pltpu.VMEM((3 * channels, padded), BF16),
            pltpu.VMEM((3 * width, padded), BF16),
            pltpu.VMEM((3 * width, padded), BF16),
            pltpu.VMEM((width, full), F32),
            pltpu.VMEM((width, full), F32),
            pltpu.VMEM((width, full), BF16),
            pltpu.VMEM((width, full), BF16),
            pltpu.VMEM((taps * channels, padded), F32),
        ],
        compiler_params=params(),
        name="patches",
    )(
        patch_anchors, tile_counts, center, first, second, third, fourth, total, blend_weights,
        w_in, w_mid, w_mid_back, w_out, w_out_back,
    )
    third, fourth = swap_lon(edges)
    inner, first, second = pl.pallas_call(
        beside_kernel,
        out_shape=(
            shape((rows, channels, cols), F32),
            shape((MARGIN, channels, cols), F32),
            shape((MARGIN, channels, cols), F32),
        ),
        in_specs=[vmem()] * 3,
        out_specs=(vmem(),) * 3,
        compiler_params=params(),
        name="beside",
    )(numer, third, fourth)
    first, second = swap_lat(first, second)
    blended = pl.pallas_call(
        fold_kernel,
        out_shape=shape((channels, rows, cols), F32),
        in_specs=[vmem()] * 4,
        out_specs=vmem(),
        compiler_params=params(),
        name="fold",
    )(inner, first, second, den)
    summed = reduce_all(grads)
    grad_in, grad_mid, grad_out = pl.pallas_call(
        split_kernel,
        out_shape=(
            shape((taps, width, channels), F32),
            shape((taps, width, width), F32),
            shape((taps, channels, width), F32),
        ),
        in_specs=[vmem()],
        out_specs=(vmem(),) * 3,
        compiler_params=params(),
        name="split",
    )(summed)
    return blended, grad_in, grad_mid, grad_out


def solution(mesh):
    return jax.shard_map(
        shards,
        mesh=mesh,
        in_specs=(
            P(None, "lat", "lon"),
            P(None, "lat", "lon"),
            P(),
            P(),
            P(),
            P("lat", "lon", None, None),
            P(None, "lat", "lon"),
            P("lat", "lon"),
        ),
        out_specs=(P(None, "lat", "lon"), P(), P(), P()),
        check_vma=False,
    )
```

```python
import functools

import jax
import jax.numpy as jnp
from jax import lax
from jax.experimental import pallas as pl
from jax.experimental.pallas import tpu as pltpu
from jax.sharding import PartitionSpec as P

MARGIN = 4
SLOTS = 4
LANES = 128
F32 = jnp.float32
BF16 = jnp.bfloat16
VMEM_LIMIT = 48 * 1024 * 1024


def vmem():
    return pl.BlockSpec(memory_space=pltpu.VMEM)


def smem():
    return pl.BlockSpec(memory_space=pltpu.SMEM)


def lane_ids(shape):
    return lax.broadcasted_iota(jnp.int32, shape, len(shape) - 1)


def roll(value, shift, axis):
    size = value.shape[axis]
    if isinstance(shift, int):
        shift = shift % size
        if shift == 0:
            return value
    return pltpu.roll(value, shift, axis)


def choose(odd, when_odd, when_even):
    return jnp.where(odd, when_odd, when_even)


def pack_kernel(
    anchors, counts, fields_in, cotangent_in, weights_in, center, first_out, second_out, canvas,
    fields, cotangent, weights, spread, sems,
):
    copies = []
    for index, (source, target) in enumerate(
        ((weights_in, weights), (fields_in, fields), (cotangent_in, cotangent))
    ):
        copy = pltpu.make_async_copy(source, target, sems.at[index])
        copy.start()
        copies.append(copy)
    channels, rows, cols = fields.shape
    wide = cols + LANES
    odd = lax.rem(lax.axis_index("lat"), 2) == 1
    spread[...] = jnp.zeros_like(spread)
    copies[0].wait()
    for slot in range(SLOTS):

        @pl.when(slot < counts[0, 0])
        def _():
            row = anchors[0, 0, slot, 0]
            col = anchors[0, 0, slot, 1]
            values = weights[slot].astype(F32)
            values = jnp.concatenate([values, jnp.zeros((rows, LANES), F32)], axis=1)
            values = jnp.concatenate([values, jnp.zeros((2 * MARGIN, wide), F32)], axis=0)
            values = roll(values, lax.rem(col + (wide - MARGIN), wide), 1)
            values = roll(values, row, 0)
            spread[...] += values

    total = spread[...]
    canvas[...] = total
    copies[1].wait()
    copies[2].wait()
    both = []
    for source in (fields, cotangent):
        both.append(jnp.swapaxes(source[...].astype(F32), 0, 1))
    tile = jnp.concatenate(both, axis=1).astype(BF16)
    center[...] = tile
    half = total.shape[0] // 2
    pad = jnp.zeros((2 * channels - 2 * half, cols), F32)
    extras = []
    for part in (total[:half], total[half:]):
        beside = jnp.concatenate([part[:, cols:], jnp.zeros((half, cols - LANES), F32)], axis=1)
        extras.append(jnp.concatenate([part[:, :cols], beside, pad], axis=0).astype(BF16))
    top, bottom = tile[:MARGIN], tile[rows - MARGIN :]
    first_out[0:MARGIN] = choose(odd, top, bottom)
    first_out[MARGIN] = choose(odd, extras[0], extras[1])
    second_out[0:MARGIN] = choose(odd, bottom, top)
    second_out[MARGIN] = choose(odd, extras[1], extras[0])


def edge_kernel(center, first, second, canvas, edges, total_out):
    rows = center.shape[0]
    channels = center.shape[1] // 2
    cols = center.shape[2]
    height = rows + 2 * MARGIN
    half = height // 2
    odd = lax.rem(lax.axis_index("lat"), 2) == 1

    def stretch(block):
        block = block.astype(F32)
        return jnp.concatenate([block[:half], block[half:height, :LANES]], axis=1)

    upper = stretch(choose(odd, first[MARGIN], second[MARGIN]))
    lower = stretch(choose(odd, second[MARGIN], first[MARGIN]))
    total = canvas[...] + jnp.concatenate([upper, lower], axis=0)
    total_out[...] = total
    lanes = lane_ids((2 * channels, LANES))
    packed = jnp.zeros((2 * channels, LANES), F32)
    for row in range(height):
        if row < MARGIN:
            line = choose(odd, first[row], second[row])
        elif row < MARGIN + rows:
            line = center[row - MARGIN]
        else:
            line = choose(odd, second[row - MARGIN - rows], first[row - MARGIN - rows])
        line = line.astype(F32)
        low = jnp.where(lanes < MARGIN, line[:, :LANES], 0.0)
        high = jnp.where(lanes >= LANES - MARGIN, line[:, cols - LANES :], 0.0)
        packed = packed + roll(low, MARGIN * row, 1) + roll(high, -MARGIN * row, 1)
    edges[0 : 2 * channels] = packed.astype(BF16)
    margin = total[:, cols:]
    lanes = lane_ids(margin.shape)
    to_left = jnp.where(lanes < LANES // 2, total[:, :LANES], margin)
    to_right = jnp.where(lanes < LANES // 2, margin, total[:, cols - LANES : cols])
    edges[2 * channels : 2 * channels + height] = to_left.astype(BF16)
    edges[2 * channels + height : 2 * channels + 2 * height] = to_right.astype(BF16)


def dot(left, right):
    return jnp.dot(left, right, preferred_element_type=F32)


def dot_lanes(left, right):
    return lax.dot_general(left, right, (((1,), (1,)), ((), ())), preferred_element_type=F32)


def patch_kernel(
    anchors, counts, center, first, second, third, fourth, total_in, weights,
    w_in, w_mid, w_mid_back, w_out, w_out_back,
    send, keep, second_out, numer, den_out,
    grads, window, x_s, d_s, h_s, z_s, slope_s, dh_s, h2_s, dz_s, y_s,
):
    rows = center.shape[0]
    channels = center.shape[1] // 2
    cols = center.shape[2]
    wide = cols + LANES
    width = w_mid.shape[0]
    full = rows * cols
    height = rows + 2 * MARGIN
    lanes = lane_ids((2 * channels, LANES))
    lat_odd = lax.rem(lax.axis_index("lat"), 2) == 1
    lon_odd = lax.rem(lax.axis_index("lon"), 2) == 1

    left = choose(lon_odd, third[...], fourth[...]).astype(F32)
    right = choose(lon_odd, fourth[...], third[...]).astype(F32)
    base = 2 * channels
    left_part = left[base + height : base + 2 * height]
    right_part = right[base : base + height]
    edge_lanes = lane_ids((height, LANES))
    low = edge_lanes < MARGIN
    high = edge_lanes >= LANES - MARGIN
    zero = jnp.zeros((height, LANES), F32)
    pieces = [jnp.where(low, left_part, zero)]
    for _ in range(cols // LANES - 2):
        pieces.append(zero)
    pieces.append(jnp.where(high, right_part, zero))
    pieces.append(jnp.where(high, left_part, zero) + jnp.where(low, right_part, zero))
    den = jnp.maximum(total_in[...] + jnp.concatenate(pieces, axis=1), 1.0)
    den_out[...] = den[MARGIN : MARGIN + rows, :cols]
    inverse = 1.0 / den

    left = left[:base]
    right = right[:base]
    for row in range(height):
        if row < MARGIN:
            body = choose(lat_odd, first[row], second[row])
        elif row < MARGIN + rows:
            body = center[row - MARGIN]
        else:
            body = choose(lat_odd, second[row - MARGIN - rows], first[row - MARGIN - rows])
        beside = jnp.where(
            lanes < LANES // 2, roll(right, -MARGIN * row, 1), roll(left, MARGIN * row, 1)
        )
        line = jnp.concatenate([body.astype(F32), beside], axis=1)
        scaled = line[channels:] * inverse[row : row + 1]
        window[row, 0:channels] = line[:channels]
        window[row, channels : 2 * channels] = scaled.astype(BF16).astype(F32)

    numer[...] = jnp.zeros_like(numer)
    grads[...] = jnp.zeros_like(grads)
    for ref in (x_s, d_s, h_s, z_s):
        ref[:, 0:cols] = jnp.zeros((ref.shape[0], cols), BF16)
        ref[:, cols + full : 2 * cols + full] = jnp.zeros((ref.shape[0], cols), BF16)
    y_s[:, 0:cols] = jnp.zeros((y_s.shape[0], cols), F32)
    y_s[:, cols + full : 2 * cols + full] = jnp.zeros((y_s.shape[0], cols), F32)

    def before(value):
        ids = lane_ids(value.shape)
        return jnp.where(ids == 0, jnp.zeros_like(value), roll(value, 1, 1))

    def after(value):
        ids = lane_ids(value.shape)
        return jnp.where(ids == cols - 1, jnp.zeros_like(value), roll(value, cols - 1, 1))

    def spread(ref, value, row, flip):
        count = value.shape[0]
        at = slice((row + 1) * cols, (row + 2) * cols)
        first, last = before(value), after(value)
        if flip:
            first, last = last, first
        ref[0:count, at] = first
        ref[count : 2 * count, at] = value
        ref[2 * count : 3 * count, at] = last

    def stack(ref, row, flip):
        starts = [(row + (2 - tap if flip else tap)) * cols for tap in range(3)]
        return jnp.concatenate([ref[:, start : start + cols] for start in starts], axis=0)

    def one_patch(slot, carry):
        row0 = anchors[0, 0, slot, 0]
        col0 = anchors[0, 0, slot, 1]
        patch_weights = weights[slot].astype(F32)
        back_shift = lax.rem(wide + MARGIN - col0, wide)
        for row in range(rows):
            line = roll(window[row0 + row], back_shift, 1)[:, :cols]
            spread(x_s, line[:channels].astype(BF16), row, False)
            grad = line[channels:] * patch_weights[row : row + 1]
            spread(d_s, grad.astype(BF16), row, True)
        for row in range(rows):
            at = slice(row * cols, (row + 1) * cols)
            z1 = dot(w_in[...], stack(x_s, row, False))
            sig = 0.5 * jnp.tanh(0.5 * z1) + 0.5
            h1 = (z1 * sig).astype(BF16)
            slope_s[:, at] = sig * (1.0 + z1 * (1.0 - sig))
            spread(h_s, h1, row, False)
        for row in range(rows):
            at = slice(row * cols, (row + 1) * cols)
            dh2 = dot(w_out_back[...], stack(d_s, row, True))
            z2 = dot(w_mid[...], stack(h_s, row, False))
            sig = 0.5 * jnp.tanh(0.5 * z2) + 0.5
            h1 = h_s[width : 2 * width, (row + 1) * cols : (row + 2) * cols].astype(F32)
            h2 = (h1 + z2 * sig).astype(BF16)
            h2_s[:, at] = h2
            dz2 = (dh2 * (sig * (1.0 + z2 * (1.0 - sig)))).astype(BF16)
            dh_s[:, at] = dh2
            spread(z_s, dz2, row, True)
            y_s[:, (row + 1) * cols : (row + 2) * cols] = dot(w_out[...], h2)
        for row in range(rows):
            at = slice(row * cols, (row + 1) * cols)
            dh1 = dh_s[:, at] + dot(w_mid_back[...], stack(z_s, row, True))
            dz_s[:, at] = (dh1 * slope_s[:, at]).astype(BF16)
        small = 9 * channels
        for tap in range(3):
            ahead = slice(tap * cols, tap * cols + full)
            behind = slice((2 - tap) * cols, (2 - tap) * cols + full)
            at = slice(tap * 3 * channels, (tap + 1) * 3 * channels)
            grads[at] += dot_lanes(x_s[:, ahead], dz_s[...])
            part = dot_lanes(z_s[width : 2 * width, cols : cols + full], h_s[:, ahead])
            for tap_col in range(3):
                start = small + (3 * tap + tap_col) * width
                grads[start : start + width] += part[:, tap_col * width : (tap_col + 1) * width]
            at = slice(small + 9 * width + tap * 3 * channels, small + 9 * width + (tap + 1) * 3 * channels)
            grads[at] += dot_lanes(d_s[:, behind], h2_s[...])
        for row in range(rows):
            sums = []
            for tap_col in range(3):
                terms = [
                    y_s[
                        (3 * tap + tap_col) * channels : (3 * tap + tap_col + 1) * channels,
                        (row + tap) * cols : (row + tap + 1) * cols,
                    ]
                    for tap in range(3)
                ]
                sums.append(terms[0] + terms[1] + terms[2])
            result = before(sums[0]) + sums[1] + after(sums[2])
            result = result * patch_weights[row : row + 1]
            result = jnp.concatenate([result, jnp.zeros((channels, LANES), F32)], axis=1)
            numer[row0 + row] += roll(result, lax.rem(col0 + (wide - MARGIN), wide), 1)
        return carry

    lax.fori_loop(0, counts[0, 0], one_patch, 0)

    half = grads.shape[0] // 2
    odd_index = lax.rem(lax.axis_index("lat"), 2)
    send[0:half] = grads[pl.ds(pl.multiple_of((1 - odd_index) * half, half), half)].astype(BF16)
    keep[...] = grads[pl.ds(pl.multiple_of(odd_index * half, half), half)]
    blocks = wide // LANES
    for row in range(MARGIN):
        upper, lower = numer[row], numer[MARGIN + rows + row]
        near = choose(lat_odd, upper, lower).astype(BF16)
        far = choose(lat_odd, lower, upper).astype(BF16)
        for block in range(blocks):
            at = (row * blocks + block) * channels
            send[half + at : half + at + channels] = near[:, block * LANES : (block + 1) * LANES]
            second_out[at : at + channels] = far[:, block * LANES : (block + 1) * LANES]


def beside_kernel(numer, first, second, inner, edges):
    height, channels, wide = numer.shape
    cols = wide - LANES
    rows = height - 2 * MARGIN
    blocks = wide // LANES
    base = first.shape[0] - second.shape[0]
    lanes = lane_ids((channels, LANES))
    lat_odd = lax.rem(lax.axis_index("lat"), 2) == 1
    packed = jnp.zeros((channels, LANES), F32)
    for row in range(rows):
        parts = []
        for block in range(blocks):
            at = ((row % MARGIN) * blocks + block) * channels
            near = first[base + at : base + at + channels].astype(F32)
            far = second[at : at + channels].astype(F32)
            other = choose(lat_odd, near, far) if row < MARGIN else choose(lat_odd, far, near)
            parts.append(numer[MARGIN + row, :, block * LANES : (block + 1) * LANES] + other)
        inner[row] = jnp.concatenate(parts[:-1], axis=1)
        low = jnp.where(lanes < MARGIN, parts[-1], 0.0)
        high = jnp.where(lanes >= LANES - MARGIN, parts[-1], 0.0)
        packed = packed + roll(low, MARGIN * row, 1) + roll(high, -MARGIN * row, 1)
    edges[...] = packed.astype(BF16)


def fold_kernel(inner, third, fourth, den, blended):
    rows, channels, cols = inner.shape
    lanes = lane_ids((channels, LANES))
    lon_odd = lax.rem(lax.axis_index("lon"), 2) == 1
    left = choose(lon_odd, third[...], fourth[...]).astype(F32)
    right = choose(lon_odd, fourth[...], third[...]).astype(F32)
    inverse = 1.0 / den[...]
    lines = []
    for row in range(rows):
        from_left = jnp.where(lanes < MARGIN, roll(left, -MARGIN * row, 1), 0.0)
        from_right = jnp.where(lanes >= LANES - MARGIN, roll(right, MARGIN * row, 1), 0.0)
        beside = [from_left]
        for _ in range(cols // LANES - 2):
            beside.append(jnp.zeros((channels, LANES), F32))
        beside.append(from_right)
        line = inner[row] + jnp.concatenate(beside, axis=1)
        lines.append((line * inverse[row : row + 1])[None])
    blended[...] = jnp.swapaxes(jnp.concatenate(lines, axis=0), 0, 1)


def split_kernel(own, other, grad_in, grad_mid, grad_out):
    taps, channels, width = grad_in.shape
    half = own.shape[0]
    odd = lax.rem(lax.axis_index("lat"), 2) == 1
    own, other = own[...], other[...]
    summed = (choose(odd, other, own), choose(odd, own, other))

    def rows_of(start, count):
        pieces = []
        stop = start + count
        if start < half:
            pieces.append(summed[0][start : min(stop, half)])
        if stop > half:
            pieces.append(summed[1][max(start, half) - half : stop - half])
        return jnp.concatenate(pieces, axis=0).astype(F32) if len(pieces) > 1 else pieces[0].astype(F32)

    for tap in range(taps):
        grad_in[tap] = rows_of(tap * channels, channels)
        grad_mid[tap] = rows_of(taps * channels + tap * width, width)
        grad_out[tap] = rows_of(taps * (channels + width) + tap * channels, channels)


def params():
    return pltpu.CompilerParams(vmem_limit_bytes=VMEM_LIMIT)


def swap(value, axis, first, wrap):
    size = lax.axis_size(axis)
    pairs = []
    for index in range(first, size, 2):
        other = (index + 1) % size
        if other > index or wrap:
            pairs.extend([(index, other), (other, index)])
    return lax.ppermute(value, axis, pairs)


def swap_lat(first, second):
    return swap(first, "lat", 0, False), swap(second, "lat", 1, False)


def swap_lon(edges):
    return swap(edges, "lon", 0, True), swap(edges, "lon", 1, True)


def exchange(value, axis, step):
    pairs = [(index, index ^ step) for index in range(lax.axis_size(axis))]
    return lax.ppermute(value, axis, pairs)


def halves(value, bit):
    half = value.shape[0] // 2
    own = lax.dynamic_slice_in_dim(value, bit * half, half, 0)
    other = lax.dynamic_slice_in_dim(value, (1 - bit) * half, half, 0)
    return own, other


def ordered(own, other, bit):
    return jnp.concatenate([jnp.where(bit == 0, own, other), jnp.where(bit == 0, other, own)], axis=0)


def shards(
    fields, cotangent, kernel_in, kernel_mid, kernel_out, patch_anchors, blend_weights, tile_counts
):
    channels, rows, cols = fields.shape
    taps, width, _ = kernel_in.shape
    height = rows + 2 * MARGIN
    wide = cols + LANES
    full = rows * cols
    padded = full + 2 * cols
    shape = jax.ShapeDtypeStruct
    center, first, second, canvas = pl.pallas_call(
        pack_kernel,
        out_shape=(
            shape((rows, 2 * channels, cols), BF16),
            shape((MARGIN + 1, 2 * channels, cols), BF16),
            shape((MARGIN + 1, 2 * channels, cols), BF16),
            shape((height, wide), F32),
        ),
        in_specs=[smem(), smem()] + [pl.BlockSpec(memory_space=pltpu.HBM)] * 3,
        out_specs=(vmem(),) * 4,
        scratch_shapes=[
            pltpu.VMEM(fields.shape, BF16),
            pltpu.VMEM(cotangent.shape, BF16),
            pltpu.VMEM(blend_weights.shape, jnp.int32),
            pltpu.VMEM((height, wide), F32),
            pltpu.SemaphoreType.DMA((3,)),
        ],
        compiler_params=params(),
        name="pack",
    )(patch_anchors, tile_counts, fields, cotangent, blend_weights)
    first, second = swap_lat(first, second)
    edges, total = pl.pallas_call(
        edge_kernel,
        out_shape=(shape((2 * channels + 2 * height, LANES), BF16), shape((height, wide), F32)),
        in_specs=[vmem()] * 4,
        out_specs=(vmem(),) * 2,
        compiler_params=params(),
        name="edges",
    )(center, first, second, canvas)
    third, fourth = swap_lon(edges)

    w_in = jnp.transpose(kernel_in, (1, 0, 2)).reshape(width, taps * channels)
    w_mid = jnp.transpose(kernel_mid, (1, 0, 2)).reshape(width, taps * width)
    w_mid_back = jnp.transpose(kernel_mid, (2, 0, 1)).reshape(width, taps * width)
    w_out = kernel_out.reshape(taps * channels, width)
    w_out_back = jnp.transpose(kernel_out, (2, 0, 1)).reshape(width, taps * channels)

    lat_size, lon_size = lax.axis_size("lat"), lax.axis_size("lon")
    length = taps * (2 * channels + width)
    unit = 16 * lat_size
    length = (length + unit - 1) // unit * unit
    half = length // 2
    edge_rows = MARGIN * channels * (wide // LANES)
    send, keep, second, numer, den = pl.pallas_call(
        patch_kernel,
        out_shape=(
            shape((half + edge_rows, LANES), BF16),
            shape((half, LANES), F32),
            shape((edge_rows, LANES), BF16),
            shape((height, channels, wide), F32),
            shape((rows, cols), F32),
        ),
        in_specs=[smem(), smem()] + [vmem()] * 12,
        out_specs=(vmem(),) * 5,
        scratch_shapes=[
            pltpu.VMEM((length, LANES), F32),
            pltpu.VMEM((height, 2 * channels, wide), F32),
            pltpu.VMEM((3 * channels, padded), BF16),
            pltpu.VMEM((3 * channels, padded), BF16),
            pltpu.VMEM((3 * width, padded), BF16),
            pltpu.VMEM((3 * width, padded), BF16),
            pltpu.VMEM((width, full), F32),
            pltpu.VMEM((width, full), F32),
            pltpu.VMEM((width, full), BF16),
            pltpu.VMEM((width, full), BF16),
            pltpu.VMEM((taps * channels, padded), F32),
        ],
        compiler_params=params(),
        name="patches",
    )(
        patch_anchors, tile_counts, center, first, second, third, fourth, total, blend_weights,
        w_in, w_mid, w_mid_back, w_out, w_out_back,
    )

    lat = lax.axis_index("lat")
    first = exchange(send, "lat", 1)
    second = swap(second, "lat", 1, False)
    mine = keep + first[:half].astype(F32)
    step = 2
    while step < lat_size:
        own, other = halves(mine, (lat // step) % 2)
        mine = own + exchange(other.astype(BF16), "lat", step).astype(F32)
        step *= 2
    inner, edges = pl.pallas_call(
        beside_kernel,
        out_shape=(shape((rows, channels, cols), F32), shape((channels, LANES), BF16)),
        in_specs=[vmem()] * 3,
        out_specs=(vmem(),) * 2,
        compiler_params=params(),
        name="beside",
    )(numer, first, second)
    count = mine.shape[0]
    mine = mine.astype(BF16)
    if lon_size == 4:
        received = []
        for start in (0, 1):
            other = swap(jnp.concatenate([mine, edges], axis=0), "lon", start, True)
            received.append(other[count:])
            mine = (mine.astype(F32) + other[:count].astype(F32)).astype(BF16)
        third, fourth = received
    else:
        third, fourth = swap_lon(edges)
        step = 1
        while step < lon_size:
            mine = (mine.astype(F32) + exchange(mine, "lon", step).astype(F32)).astype(BF16)
            step *= 2
    blended = pl.pallas_call(
        fold_kernel,
        out_shape=shape((channels, rows, cols), F32),
        in_specs=[vmem()] * 4,
        out_specs=vmem(),
        compiler_params=params(),
        name="fold",
    )(inner, third, fourth, den)
    step = lat_size // 2
    while step > 1:
        mine = ordered(mine, exchange(mine, "lat", step), (lat // step) % 2)
        step //= 2
    grad_in, grad_mid, grad_out = pl.pallas_call(
        split_kernel,
        out_shape=(
            shape((taps, channels, width), F32),
            shape((taps, width, width), F32),
            shape((taps, channels, width), F32),
        ),
        in_specs=[vmem()] * 2,
        out_specs=(vmem(),) * 3,
        compiler_params=params(),
        name="split",
    )(mine, exchange(mine, "lat", 1))
    return blended, jnp.transpose(grad_in, (0, 2, 1)), grad_mid, grad_out


def solution(mesh):
    return jax.shard_map(
        shards,
        mesh=mesh,
        in_specs=(
            P(None, "lat", "lon"),
            P(None, "lat", "lon"),
            P(),
            P(),
            P(),
            P("lat", "lon", None, None),
            P(None, "lat", "lon"),
            P("lat", "lon"),
        ),
        out_specs=(P(None, "lat", "lon"), P(), P(), P()),
        check_vma=False,
    )
```

```python
import functools

import jax
import jax.numpy as jnp
from jax import lax
from jax.experimental import pallas as pl
from jax.experimental.pallas import tpu as pltpu
from jax.sharding import PartitionSpec as P

MARGIN = 4
SLOTS = 4
LANES = 128
F32 = jnp.float32
BF16 = jnp.bfloat16
VMEM_LIMIT = 48 * 1024 * 1024


def vmem():
    return pl.BlockSpec(memory_space=pltpu.VMEM)


def smem():
    return pl.BlockSpec(memory_space=pltpu.SMEM)


def lane_ids(shape):
    return lax.broadcasted_iota(jnp.int32, shape, len(shape) - 1)


def roll(value, shift, axis):
    size = value.shape[axis]
    if isinstance(shift, int):
        shift = shift % size
        if shift == 0:
            return value
    return pltpu.roll(value, shift, axis)


def choose(odd, when_odd, when_even):
    return jnp.where(odd, when_odd, when_even)


def pack_kernel(
    anchors, counts, fields_in, cotangent_in, weights_in, center, first_out, second_out, canvas,
    fields, cotangent, weights, spread, sems,
):
    copies = []
    for index, (source, target) in enumerate(
        ((weights_in, weights), (fields_in, fields), (cotangent_in, cotangent))
    ):
        copy = pltpu.make_async_copy(source, target, sems.at[index])
        copy.start()
        copies.append(copy)
    channels, rows, cols = fields.shape
    wide = cols + LANES
    odd = lax.rem(lax.axis_index("lat"), 2) == 1
    spread[...] = jnp.zeros_like(spread)
    copies[0].wait()
    for slot in range(SLOTS):

        @pl.when(slot < counts[0, 0])
        def _():
            row = anchors[0, 0, 0, slot]
            col = anchors[0, 0, 1, slot]
            values = weights[slot].astype(F32)
            values = jnp.concatenate([values, jnp.zeros((rows, LANES), F32)], axis=1)
            values = jnp.concatenate([values, jnp.zeros((2 * MARGIN, wide), F32)], axis=0)
            values = roll(values, lax.rem(col + (wide - MARGIN), wide), 1)
            values = roll(values, row, 0)
            spread[...] += values

    total = spread[...]
    canvas[...] = total
    copies[1].wait()
    copies[2].wait()
    both = []
    for source in (fields, cotangent):
        both.append(jnp.swapaxes(source[...].astype(F32), 0, 1))
    tile = jnp.concatenate(both, axis=1).astype(BF16)
    center[...] = tile
    half = total.shape[0] // 2
    pad = jnp.zeros((2 * channels - 2 * half, cols), F32)
    extras = []
    for part in (total[:half], total[half:]):
        beside = jnp.concatenate([part[:, cols:], jnp.zeros((half, cols - LANES), F32)], axis=1)
        extras.append(jnp.concatenate([part[:, :cols], beside, pad], axis=0).astype(BF16))
    top, bottom = tile[:MARGIN], tile[rows - MARGIN :]
    first_out[0:MARGIN] = choose(odd, top, bottom)
    first_out[MARGIN] = choose(odd, extras[0], extras[1])
    second_out[0:MARGIN] = choose(odd, bottom, top)
    second_out[MARGIN] = choose(odd, extras[1], extras[0])


def edge_kernel(center, first, second, canvas, edges, total_out):
    rows = center.shape[0]
    channels = center.shape[1] // 2
    cols = center.shape[2]
    height = rows + 2 * MARGIN
    half = height // 2
    odd = lax.rem(lax.axis_index("lat"), 2) == 1

    def stretch(block):
        block = block.astype(F32)
        return jnp.concatenate([block[:half], block[half:height, :LANES]], axis=1)

    upper = stretch(choose(odd, first[MARGIN], second[MARGIN]))
    lower = stretch(choose(odd, second[MARGIN], first[MARGIN]))
    total = canvas[...] + jnp.concatenate([upper, lower], axis=0)
    total_out[...] = total
    lanes = lane_ids((2 * channels, LANES))
    packed = jnp.zeros((2 * channels, LANES), F32)
    for row in range(height):
        if row < MARGIN:
            line = choose(odd, first[row], second[row])
        elif row < MARGIN + rows:
            line = center[row - MARGIN]
        else:
            line = choose(odd, second[row - MARGIN - rows], first[row - MARGIN - rows])
        line = line.astype(F32)
        low = jnp.where(lanes < MARGIN, line[:, :LANES], 0.0)
        high = jnp.where(lanes >= LANES - MARGIN, line[:, cols - LANES :], 0.0)
        packed = packed + roll(low, MARGIN * row, 1) + roll(high, -MARGIN * row, 1)
    edges[0 : 2 * channels] = packed.astype(BF16)
    margin = total[:, cols:]
    lanes = lane_ids(margin.shape)
    to_left = jnp.where(lanes < LANES // 2, total[:, :LANES], margin)
    to_right = jnp.where(lanes < LANES // 2, margin, total[:, cols - LANES : cols])
    edges[2 * channels : 2 * channels + height] = to_left.astype(BF16)
    edges[2 * channels + height : 2 * channels + 2 * height] = to_right.astype(BF16)


def dot(left, right):
    return jnp.dot(left, right, preferred_element_type=F32)


def dot_lanes(left, right):
    return lax.dot_general(left, right, (((1,), (1,)), ((), ())), preferred_element_type=F32)


def patch_kernel(
    anchors, counts, center, first, second, third, fourth, total_in, weights,
    w_in, w_mid, w_mid_back, w_out, w_out_back,
    send, keep, second_out, numer, den_out,
    grads, window, x_s, d_s, h_s, z_s, h2_s, slope_s, dh_s, dz_s,
):
    rows = center.shape[0]
    channels = center.shape[1] // 2
    cols = center.shape[2]
    wide = cols + LANES
    width = w_in.shape[0]
    full = rows * cols
    height = rows + 2 * MARGIN
    lanes = lane_ids((2 * channels, LANES))
    lat_odd = lax.rem(lax.axis_index("lat"), 2) == 1
    lon_odd = lax.rem(lax.axis_index("lon"), 2) == 1

    left = choose(lon_odd, third[...], fourth[...]).astype(F32)
    right = choose(lon_odd, fourth[...], third[...]).astype(F32)
    base = 2 * channels
    left_part = left[base + height : base + 2 * height]
    right_part = right[base : base + height]
    edge_lanes = lane_ids((height, LANES))
    low = edge_lanes < MARGIN
    high = edge_lanes >= LANES - MARGIN
    zero = jnp.zeros((height, LANES), F32)
    pieces = [jnp.where(low, left_part, zero)]
    for _ in range(cols // LANES - 2):
        pieces.append(zero)
    pieces.append(jnp.where(high, right_part, zero))
    pieces.append(jnp.where(high, left_part, zero) + jnp.where(low, right_part, zero))
    den = jnp.maximum(total_in[...] + jnp.concatenate(pieces, axis=1), 1.0)
    den_out[...] = den[MARGIN : MARGIN + rows, :cols]
    inverse = 1.0 / den

    left = left[:base]
    right = right[:base]
    for row in range(height):
        if row < MARGIN:
            body = choose(lat_odd, first[row], second[row])
        elif row < MARGIN + rows:
            body = center[row - MARGIN]
        else:
            body = choose(lat_odd, second[row - MARGIN - rows], first[row - MARGIN - rows])
        beside = jnp.where(
            lanes < LANES // 2, roll(right, -MARGIN * row, 1), roll(left, MARGIN * row, 1)
        )
        line = jnp.concatenate([body.astype(F32), beside], axis=1)
        scaled = line[channels:] * inverse[row : row + 1]
        window[row, 0:channels] = line[:channels]
        window[row, channels : 2 * channels] = scaled.astype(BF16).astype(F32)

    numer[...] = jnp.zeros_like(numer)
    grads[...] = jnp.zeros_like(grads)
    for ref in (x_s, d_s, h_s, z_s, h2_s):
        ref[:, 0:cols] = jnp.zeros((ref.shape[0], cols), BF16)
        ref[:, cols + full : 2 * cols + full] = jnp.zeros((ref.shape[0], cols), BF16)

    def before(value):
        ids = lane_ids(value.shape)
        return jnp.where(ids == 0, jnp.zeros_like(value), roll(value, 1, 1))

    def after(value):
        ids = lane_ids(value.shape)
        return jnp.where(ids == cols - 1, jnp.zeros_like(value), roll(value, cols - 1, 1))

    def spread(ref, value, row, flip):
        count = value.shape[0]
        at = slice((row + 1) * cols, (row + 2) * cols)
        first, last = before(value), after(value)
        if flip:
            first, last = last, first
        ref[0:count, at] = first
        ref[count : 2 * count, at] = value
        ref[2 * count : 3 * count, at] = last

    def stack(ref, row, flip):
        starts = [(row + (2 - tap if flip else tap)) * cols for tap in range(3)]
        return jnp.concatenate([ref[:, start : start + cols] for start in starts], axis=0)

    def across(parts, flip):
        count = parts.shape[0] // 3
        first, last = parts[:count], parts[2 * count :]
        if flip:
            first, last = last, first
        return before(first) + parts[count : 2 * count] + after(last)

    def all_rows(ref, flip):
        starts = [(2 - tap if flip else tap) * cols for tap in range(3)]
        return jnp.concatenate([ref[:, start : start + full] for start in starts], axis=0)

    def one_patch(slot, carry):
        row0 = anchors[0, 0, 0, slot]
        col0 = anchors[0, 0, 1, slot]
        patch_weights = weights[slot].astype(F32)
        back_shift = lax.rem(wide + MARGIN - col0, wide)
        for row in range(rows):
            line = roll(window[row0 + row], back_shift, 1)[:, :cols]
            spread(x_s, line[:channels].astype(BF16), row, False)
            grad = line[channels:] * patch_weights[row : row + 1]
            spread(d_s, grad.astype(BF16), row, True)
        for row in range(rows):
            at = slice(row * cols, (row + 1) * cols)
            z1 = dot(w_in[...], stack(x_s, row, False))
            sig = 0.5 * jnp.tanh(0.5 * z1) + 0.5
            slope_s[:, at] = sig * (1.0 + z1 * (1.0 - sig))
            h_s[:, (row + 1) * cols : (row + 2) * cols] = (z1 * sig).astype(BF16)
        for row in range(rows):
            at = slice(row * cols, (row + 1) * cols)
            ahead = slice((row + 1) * cols, (row + 2) * cols)
            dh2 = dot(w_out_back[...], stack(d_s, row, True))
            z2 = across(dot(w_mid[...], stack(h_s, row, False)), False)
            sig = 0.5 * jnp.tanh(0.5 * z2) + 0.5
            h2_s[:, ahead] = (h_s[:, ahead].astype(F32) + z2 * sig).astype(BF16)
            dz2 = (dh2 * (sig * (1.0 + z2 * (1.0 - sig)))).astype(BF16)
            dh_s[:, at] = dh2
            spread(z_s, dz2, row, True)
        for row in range(rows):
            at = slice(row * cols, (row + 1) * cols)
            back = across(dot(w_mid_back[...], stack(z_s.at[width : 2 * width], row, True)), True)
            dz_s[:, at] = ((dh_s[:, at] + back) * slope_s[:, at]).astype(BF16)
        for row in range(rows):
            result = across(dot(w_out[...], stack(h2_s, row, False)), False)
            result = result * patch_weights[row : row + 1]
            result = jnp.concatenate([result, jnp.zeros((channels, LANES), F32)], axis=1)
            numer[row0 + row] += roll(result, lax.rem(col0 + (wide - MARGIN), wide), 1)
        inside = slice(cols, cols + full)
        small = 9 * channels
        part = dot_lanes(z_s[:, inside], all_rows(h_s, False))
        for tap in range(3):
            for tap_col in range(3):
                start = small + (3 * tap + tap_col) * width
                grads[start : start + width] += part[
                    tap_col * width : (tap_col + 1) * width, tap * width : (tap + 1) * width
                ]
        grads[0:small] += dot_lanes(all_rows(x_s, False), dz_s[...])
        start = small + 9 * width
        grads[start : start + small] += dot_lanes(all_rows(d_s, True), h2_s[:, inside])
        return carry

    lax.fori_loop(0, counts[0, 0], one_patch, 0)

    half = grads.shape[0] // 2
    odd_index = lax.rem(lax.axis_index("lat"), 2)
    send[0:half] = grads[pl.ds(pl.multiple_of((1 - odd_index) * half, half), half)].astype(BF16)
    keep[...] = grads[pl.ds(pl.multiple_of(odd_index * half, half), half)]
    blocks = wide // LANES
    for row in range(MARGIN):
        upper, lower = numer[row], numer[MARGIN + rows + row]
        near = choose(lat_odd, upper, lower).astype(BF16)
        far = choose(lat_odd, lower, upper).astype(BF16)
        for block in range(blocks):
            at = (row * blocks + block) * channels
            send[half + at : half + at + channels] = near[:, block * LANES : (block + 1) * LANES]
            second_out[at : at + channels] = far[:, block * LANES : (block + 1) * LANES]


def beside_kernel(numer, first, second, inner, edges):
    height, channels, wide = numer.shape
    cols = wide - LANES
    rows = height - 2 * MARGIN
    blocks = wide // LANES
    base = first.shape[0] - second.shape[0]
    lanes = lane_ids((channels, LANES))
    lat_odd = lax.rem(lax.axis_index("lat"), 2) == 1
    packed = jnp.zeros((channels, LANES), F32)
    for row in range(rows):
        parts = []
        for block in range(blocks):
            at = ((row % MARGIN) * blocks + block) * channels
            near = first[base + at : base + at + channels].astype(F32)
            far = second[at : at + channels].astype(F32)
            other = choose(lat_odd, near, far) if row < MARGIN else choose(lat_odd, far, near)
            parts.append(numer[MARGIN + row, :, block * LANES : (block + 1) * LANES] + other)
        inner[row] = jnp.concatenate(parts[:-1], axis=1)
        low = jnp.where(lanes < MARGIN, parts[-1], 0.0)
        high = jnp.where(lanes >= LANES - MARGIN, parts[-1], 0.0)
        packed = packed + roll(low, MARGIN * row, 1) + roll(high, -MARGIN * row, 1)
    edges[...] = packed.astype(BF16)


def fold_kernel(inner, third, fourth, den, blended):
    rows, channels, cols = inner.shape
    lanes = lane_ids((channels, LANES))
    lon_odd = lax.rem(lax.axis_index("lon"), 2) == 1
    left = choose(lon_odd, third[...], fourth[...]).astype(F32)
    right = choose(lon_odd, fourth[...], third[...]).astype(F32)
    inverse = 1.0 / den[...]
    lines = []
    for row in range(rows):
        from_left = jnp.where(lanes < MARGIN, roll(left, -MARGIN * row, 1), 0.0)
        from_right = jnp.where(lanes >= LANES - MARGIN, roll(right, MARGIN * row, 1), 0.0)
        beside = [from_left]
        for _ in range(cols // LANES - 2):
            beside.append(jnp.zeros((channels, LANES), F32))
        beside.append(from_right)
        line = inner[row] + jnp.concatenate(beside, axis=1)
        lines.append((line * inverse[row : row + 1])[None])
    blended[...] = jnp.swapaxes(jnp.concatenate(lines, axis=0), 0, 1)


def split_kernel(own, other, grad_in, grad_mid, grad_out):
    taps, channels, width = grad_in.shape
    half = own.shape[0]
    odd = lax.rem(lax.axis_index("lat"), 2) == 1
    own, other = own[...], other[...]
    summed = (choose(odd, other, own), choose(odd, own, other))

    def rows_of(start, count):
        pieces = []
        stop = start + count
        if start < half:
            pieces.append(summed[0][start : min(stop, half)])
        if stop > half:
            pieces.append(summed[1][max(start, half) - half : stop - half])
        return jnp.concatenate(pieces, axis=0).astype(F32) if len(pieces) > 1 else pieces[0].astype(F32)

    for tap in range(taps):
        grad_in[tap] = rows_of(tap * channels, channels)
        grad_mid[tap] = rows_of(taps * channels + tap * width, width)
        grad_out[tap] = rows_of(taps * (channels + width) + tap * channels, channels)


def params():
    return pltpu.CompilerParams(vmem_limit_bytes=VMEM_LIMIT)


def swap(value, axis, first, wrap):
    size = lax.axis_size(axis)
    pairs = []
    for index in range(first, size, 2):
        other = (index + 1) % size
        if other > index or wrap:
            pairs.extend([(index, other), (other, index)])
    return lax.ppermute(value, axis, pairs)


def swap_lat(first, second):
    return swap(first, "lat", 0, False), swap(second, "lat", 1, False)


def swap_lon(edges):
    return swap(edges, "lon", 0, True), swap(edges, "lon", 1, True)


def exchange(value, axis, step):
    pairs = [(index, index ^ step) for index in range(lax.axis_size(axis))]
    return lax.ppermute(value, axis, pairs)


def shards(
    fields, cotangent, kernel_in, kernel_mid, kernel_out, patch_anchors, blend_weights, tile_counts
):
    channels, rows, cols = fields.shape
    taps, width, _ = kernel_in.shape
    patch_anchors = jnp.transpose(patch_anchors, (0, 1, 3, 2))
    height = rows + 2 * MARGIN
    wide = cols + LANES
    full = rows * cols
    padded = full + 2 * cols
    shape = jax.ShapeDtypeStruct
    center, first, second, canvas = pl.pallas_call(
        pack_kernel,
        out_shape=(
            shape((rows, 2 * channels, cols), BF16),
            shape((MARGIN + 1, 2 * channels, cols), BF16),
            shape((MARGIN + 1, 2 * channels, cols), BF16),
            shape((height, wide), F32),
        ),
        in_specs=[smem(), smem()] + [pl.BlockSpec(memory_space=pltpu.HBM)] * 3,
        out_specs=(vmem(),) * 4,
        scratch_shapes=[
            pltpu.VMEM(fields.shape, BF16),
            pltpu.VMEM(cotangent.shape, BF16),
            pltpu.VMEM(blend_weights.shape, jnp.int32),
            pltpu.VMEM((height, wide), F32),
            pltpu.SemaphoreType.DMA((3,)),
        ],
        compiler_params=params(),
        name="pack",
    )(patch_anchors, tile_counts, fields, cotangent, blend_weights)
    first, second = swap_lat(first, second)
    edges, total = pl.pallas_call(
        edge_kernel,
        out_shape=(shape((2 * channels + 2 * height, LANES), BF16), shape((height, wide), F32)),
        in_specs=[vmem()] * 4,
        out_specs=(vmem(),) * 2,
        compiler_params=params(),
        name="edges",
    )(center, first, second, canvas)
    third, fourth = swap_lon(edges)

    w_in = jnp.transpose(kernel_in, (1, 0, 2)).reshape(width, taps * channels)
    kernel_mid = kernel_mid.reshape(3, 3, width, width)
    kernel_out = kernel_out.reshape(3, 3, channels, width)
    w_mid = jnp.transpose(kernel_mid, (1, 2, 0, 3)).reshape(3 * width, 3 * width)
    w_mid_back = jnp.transpose(kernel_mid, (1, 3, 0, 2)).reshape(3 * width, 3 * width)
    w_out = jnp.transpose(kernel_out, (1, 2, 0, 3)).reshape(3 * channels, 3 * width)
    w_out_back = jnp.transpose(kernel_out, (3, 0, 1, 2)).reshape(width, taps * channels)

    lat_size, lon_size = lax.axis_size("lat"), lax.axis_size("lon")
    length = taps * (2 * channels + width)
    unit = 16 * lat_size
    length = (length + unit - 1) // unit * unit
    half = length // 2
    edge_rows = MARGIN * channels * (wide // LANES)
    send, keep, second, numer, den = pl.pallas_call(
        patch_kernel,
        out_shape=(
            shape((half + edge_rows, LANES), BF16),
            shape((half, LANES), F32),
            shape((edge_rows, LANES), BF16),
            shape((height, channels, wide), F32),
            shape((rows, cols), F32),
        ),
        in_specs=[smem(), smem()] + [vmem()] * 12,
        out_specs=(vmem(),) * 5,
        scratch_shapes=[
            pltpu.VMEM((length, LANES), F32),
            pltpu.VMEM((height, 2 * channels, wide), F32),
            pltpu.VMEM((3 * channels, padded), BF16),
            pltpu.VMEM((3 * channels, padded), BF16),
            pltpu.VMEM((width, padded), BF16),
            pltpu.VMEM((3 * width, padded), BF16),
            pltpu.VMEM((width, padded), BF16),
            pltpu.VMEM((width, full), F32),
            pltpu.VMEM((width, full), F32),
            pltpu.VMEM((width, full), BF16),
        ],
        compiler_params=params(),
        name="patches",
    )(
        patch_anchors, tile_counts, center, first, second, third, fourth, total, blend_weights,
        w_in, w_mid, w_mid_back, w_out, w_out_back,
    )

    first = exchange(send, "lat", 1)
    second = swap(second, "lat", 1, False)
    mine = keep + first[:half].astype(F32)
    planes = [list(range(start, lat_size, 2)) for start in (0, 1)]
    parts = mine.astype(BF16).reshape(lat_size // 2, length // lat_size, LANES)
    parts = lax.all_to_all(parts, "lat", 0, 0, axis_index_groups=planes)
    mine = jnp.sum(parts.astype(F32), axis=0)
    inner, edges = pl.pallas_call(
        beside_kernel,
        out_shape=(shape((rows, channels, cols), F32), shape((channels, LANES), BF16)),
        in_specs=[vmem()] * 3,
        out_specs=(vmem(),) * 2,
        compiler_params=params(),
        name="beside",
    )(numer, first, second)
    count = mine.shape[0]
    mine = mine.astype(BF16)
    if lon_size == 4:
        received = []
        for start in (0, 1):
            other = swap(jnp.concatenate([mine, edges], axis=0), "lon", start, True)
            received.append(other[count:])
            mine = (mine.astype(F32) + other[:count].astype(F32)).astype(BF16)
        third, fourth = received
    else:
        third, fourth = swap_lon(edges)
        step = 1
        while step < lon_size:
            mine = (mine.astype(F32) + exchange(mine, "lon", step).astype(F32)).astype(BF16)
            step *= 2
    blended = pl.pallas_call(
        fold_kernel,
        out_shape=shape((channels, rows, cols), F32),
        in_specs=[vmem()] * 4,
        out_specs=vmem(),
        compiler_params=params(),
        name="fold",
    )(inner, third, fourth, den)
    parts = jnp.broadcast_to(mine[None], (lat_size // 2,) + mine.shape)
    mine = lax.all_to_all(parts, "lat", 0, 0, axis_index_groups=planes).reshape(half, LANES)
    grad_in, grad_mid, grad_out = pl.pallas_call(
        split_kernel,
        out_shape=(
            shape((taps, channels, width), F32),
            shape((taps, width, width), F32),
            shape((taps, channels, width), F32),
        ),
        in_specs=[vmem()] * 2,
        out_specs=(vmem(),) * 3,
        compiler_params=params(),
        name="split",
    )(mine, exchange(mine, "lat", 1))
    return blended, jnp.transpose(grad_in, (0, 2, 1)), grad_mid, grad_out


def solution(mesh):
    return jax.shard_map(
        shards,
        mesh=mesh,
        in_specs=(
            P(None, "lat", "lon"),
            P(None, "lat", "lon"),
            P(),
            P(),
            P(),
            P("lat", "lon", None, None),
            P(None, "lat", "lon"),
            P("lat", "lon"),
        ),
        out_specs=(P(None, "lat", "lon"), P(), P(), P()),
        check_vma=False,
    )
```

```python
import functools

import jax
import jax.numpy as jnp
from jax import lax
from jax.experimental import pallas as pl
from jax.experimental.pallas import tpu as pltpu
from jax.sharding import PartitionSpec as P

MARGIN = 4
SLOTS = 4
LANES = 128
F32 = jnp.float32
BF16 = jnp.bfloat16
VMEM_LIMIT = 48 * 1024 * 1024


def vmem():
    return pl.BlockSpec(memory_space=pltpu.VMEM)


def smem():
    return pl.BlockSpec(memory_space=pltpu.SMEM)


def lane_ids(shape):
    return lax.broadcasted_iota(jnp.int32, shape, len(shape) - 1)


def roll(value, shift, axis):
    size = value.shape[axis]
    if isinstance(shift, int):
        shift = shift % size
        if shift == 0:
            return value
    return pltpu.roll(value, shift, axis)


def choose(odd, when_odd, when_even):
    return jnp.where(odd, when_odd, when_even)


def pack_kernel(
    anchors, counts, fields_in, cotangent_in, weights_in, center, first_out, second_out, canvas,
    fields, cotangent, weights, spread, sems,
):
    copies = []
    for index, (source, target) in enumerate(
        ((weights_in, weights), (fields_in, fields), (cotangent_in, cotangent))
    ):
        copy = pltpu.make_async_copy(source, target, sems.at[index])
        copy.start()
        copies.append(copy)
    channels, rows, cols = fields.shape
    wide = cols + LANES
    odd = lax.rem(lax.axis_index("lat"), 2) == 1
    spread[...] = jnp.zeros_like(spread)
    copies[0].wait()
    for slot in range(SLOTS):

        @pl.when(slot < counts[0, 0])
        def _():
            row = anchors[0, 0, 0, slot]
            col = anchors[0, 0, 1, slot]
            values = weights[slot].astype(F32)
            values = jnp.concatenate([values, jnp.zeros((rows, LANES), F32)], axis=1)
            values = jnp.concatenate([values, jnp.zeros((2 * MARGIN, wide), F32)], axis=0)
            values = roll(values, lax.rem(col + (wide - MARGIN), wide), 1)
            values = roll(values, row, 0)
            spread[...] += values

    total = spread[...]
    canvas[...] = total
    copies[1].wait()
    copies[2].wait()
    both = []
    for source in (fields, cotangent):
        both.append(jnp.swapaxes(source[...].astype(F32), 0, 1))
    tile = jnp.concatenate(both, axis=1).astype(BF16)
    center[...] = tile
    half = total.shape[0] // 2
    pad = jnp.zeros((2 * channels - 2 * half, cols), F32)
    extras = []
    for part in (total[:half], total[half:]):
        beside = jnp.concatenate([part[:, cols:], jnp.zeros((half, cols - LANES), F32)], axis=1)
        extras.append(jnp.concatenate([part[:, :cols], beside, pad], axis=0).astype(BF16))
    top, bottom = tile[:MARGIN], tile[rows - MARGIN :]
    first_out[0:MARGIN] = choose(odd, top, bottom)
    first_out[MARGIN] = choose(odd, extras[0], extras[1])
    second_out[0:MARGIN] = choose(odd, bottom, top)
    second_out[MARGIN] = choose(odd, extras[1], extras[0])


def edge_kernel(center, first, second, canvas, edges, total_out):
    rows = center.shape[0]
    channels = center.shape[1] // 2
    cols = center.shape[2]
    height = rows + 2 * MARGIN
    half = height // 2
    odd = lax.rem(lax.axis_index("lat"), 2) == 1

    def stretch(block):
        block = block.astype(F32)
        return jnp.concatenate([block[:half], block[half:height, :LANES]], axis=1)

    upper = stretch(choose(odd, first[MARGIN], second[MARGIN]))
    lower = stretch(choose(odd, second[MARGIN], first[MARGIN]))
    total = canvas[...] + jnp.concatenate([upper, lower], axis=0)
    total_out[...] = total
    lanes = lane_ids((2 * channels, LANES))
    packed = jnp.zeros((2 * channels, LANES), F32)
    for row in range(height):
        if row < MARGIN:
            line = choose(odd, first[row], second[row])
        elif row < MARGIN + rows:
            line = center[row - MARGIN]
        else:
            line = choose(odd, second[row - MARGIN - rows], first[row - MARGIN - rows])
        line = line.astype(F32)
        low = jnp.where(lanes < MARGIN, line[:, :LANES], 0.0)
        high = jnp.where(lanes >= LANES - MARGIN, line[:, cols - LANES :], 0.0)
        packed = packed + roll(low, MARGIN * row, 1) + roll(high, -MARGIN * row, 1)
    edges[0 : 2 * channels] = packed.astype(BF16)
    margin = total[:, cols:]
    lanes = lane_ids(margin.shape)
    to_left = jnp.where(lanes < LANES // 2, total[:, :LANES], margin)
    to_right = jnp.where(lanes < LANES // 2, margin, total[:, cols - LANES : cols])
    edges[2 * channels : 2 * channels + height] = to_left.astype(BF16)
    edges[2 * channels + height : 2 * channels + 2 * height] = to_right.astype(BF16)


def dot(left, right):
    return jnp.dot(left, right, preferred_element_type=F32)


def dot_lanes(left, right):
    return lax.dot_general(left, right, (((1,), (1,)), ((), ())), preferred_element_type=F32)


def patch_kernel(
    anchors, counts, center, first, second, third, fourth, total_in, weights,
    w_in, w_mid, w_mid_back, w_out, w_out_back,
    send, keep, second_out, numer, den_out,
    grads, window, x_s, d_s, h_s, z_s, h2_s, slope_s, dh_s, dz_s,
):
    rows = center.shape[0]
    channels = center.shape[1] // 2
    cols = center.shape[2]
    wide = cols + LANES
    width = w_in.shape[0]
    full = rows * cols
    height = rows + 2 * MARGIN
    lanes = lane_ids((2 * channels, LANES))
    lat_odd = lax.rem(lax.axis_index("lat"), 2) == 1
    lon_odd = lax.rem(lax.axis_index("lon"), 2) == 1

    left = choose(lon_odd, third[...], fourth[...]).astype(F32)
    right = choose(lon_odd, fourth[...], third[...]).astype(F32)
    base = 2 * channels
    left_part = left[base + height : base + 2 * height]
    right_part = right[base : base + height]
    edge_lanes = lane_ids((height, LANES))
    low = edge_lanes < MARGIN
    high = edge_lanes >= LANES - MARGIN
    zero = jnp.zeros((height, LANES), F32)
    pieces = [jnp.where(low, left_part, zero)]
    for _ in range(cols // LANES - 2):
        pieces.append(zero)
    pieces.append(jnp.where(high, right_part, zero))
    pieces.append(jnp.where(high, left_part, zero) + jnp.where(low, right_part, zero))
    den = jnp.maximum(total_in[...] + jnp.concatenate(pieces, axis=1), 1.0)
    den_out[...] = den[MARGIN : MARGIN + rows, :cols]
    inverse = 1.0 / den

    left = left[:base]
    right = right[:base]
    for row in range(height):
        if row < MARGIN:
            body = choose(lat_odd, first[row], second[row])
        elif row < MARGIN + rows:
            body = center[row - MARGIN]
        else:
            body = choose(lat_odd, second[row - MARGIN - rows], first[row - MARGIN - rows])
        beside = jnp.where(
            lanes < LANES // 2, roll(right, -MARGIN * row, 1), roll(left, MARGIN * row, 1)
        )
        line = jnp.concatenate([body.astype(F32), beside], axis=1)
        scaled = line[channels:] * inverse[row : row + 1]
        window[row, 0:channels] = line[:channels]
        window[row, channels : 2 * channels] = scaled.astype(BF16).astype(F32)

    numer[...] = jnp.zeros_like(numer)
    grads[...] = jnp.zeros_like(grads)
    for ref in (x_s, d_s, h_s, z_s, h2_s):
        ref[:, 0:cols] = jnp.zeros((ref.shape[0], cols), BF16)
        ref[:, cols + full : 2 * cols + full] = jnp.zeros((ref.shape[0], cols), BF16)

    def shifted(value, step):
        blocks = [value[:, at : at + LANES] for at in range(0, cols, LANES)]
        turned = [roll(block, step, 1) for block in blocks]
        ids = lane_ids(blocks[0].shape)
        zero = jnp.zeros_like(blocks[0])
        if step > 0:
            ends = [zero] + turned[:-1]
            at_end = ids == 0
        else:
            ends = turned[1:] + [zero]
            at_end = ids == LANES - 1
        return jnp.concatenate([jnp.where(at_end, end, own) for end, own in zip(ends, turned)], axis=1)

    def before(value):
        return shifted(value, 1)

    def after(value):
        return shifted(value, -1)

    def spread(ref, value, row, flip):
        count = value.shape[0]
        at = slice((row + 1) * cols, (row + 2) * cols)
        first, last = before(value), after(value)
        if flip:
            first, last = last, first
        ref[0:count, at] = first
        ref[count : 2 * count, at] = value
        ref[2 * count : 3 * count, at] = last

    def stack(ref, row, flip):
        starts = [(row + (2 - tap if flip else tap)) * cols for tap in range(3)]
        return jnp.concatenate([ref[:, start : start + cols] for start in starts], axis=0)

    def across(parts, flip):
        count = parts.shape[0] // 3
        first, last = parts[:count], parts[2 * count :]
        if flip:
            first, last = last, first
        return before(first) + parts[count : 2 * count] + after(last)

    def all_rows(ref, flip):
        starts = [(2 - tap if flip else tap) * cols for tap in range(3)]
        return jnp.concatenate([ref[:, start : start + full] for start in starts], axis=0)

    def one_patch(slot, carry):
        row0 = anchors[0, 0, 0, slot]
        col0 = anchors[0, 0, 1, slot]
        patch_weights = weights[slot].astype(F32)
        back_shift = lax.rem(wide + MARGIN - col0, wide)
        for row in range(rows):
            line = roll(window[row0 + row], back_shift, 1)[:, :cols]
            spread(x_s, line[:channels].astype(BF16), row, False)
            grad = line[channels:] * patch_weights[row : row + 1]
            spread(d_s, grad.astype(BF16), row, True)
        for row in range(rows):
            at = slice(row * cols, (row + 1) * cols)
            z1 = dot(w_in[...], stack(x_s, row, False))
            sig = 0.5 * jnp.tanh(0.5 * z1) + 0.5
            slope_s[:, at] = sig * (1.0 + z1 * (1.0 - sig))
            h_s[:, (row + 1) * cols : (row + 2) * cols] = (z1 * sig).astype(BF16)
        for row in range(rows):
            at = slice(row * cols, (row + 1) * cols)
            ahead = slice((row + 1) * cols, (row + 2) * cols)
            dh2 = dot(w_out_back[...], stack(d_s, row, True))
            z2 = across(dot(w_mid[...], stack(h_s, row, False)), False)
            sig = 0.5 * jnp.tanh(0.5 * z2) + 0.5
            h2_s[:, ahead] = (h_s[:, ahead].astype(F32) + z2 * sig).astype(BF16)
            dz2 = (dh2 * (sig * (1.0 + z2 * (1.0 - sig)))).astype(BF16)
            dh_s[:, at] = dh2
            spread(z_s, dz2, row, True)
        for row in range(rows):
            at = slice(row * cols, (row + 1) * cols)
            back = across(dot(w_mid_back[...], stack(z_s.at[width : 2 * width], row, True)), True)
            dz_s[:, at] = ((dh_s[:, at] + back) * slope_s[:, at]).astype(BF16)
        for row in range(rows):
            result = across(dot(w_out[...], stack(h2_s, row, False)), False)
            result = result * patch_weights[row : row + 1]
            result = jnp.concatenate([result, jnp.zeros((channels, LANES), F32)], axis=1)
            numer[row0 + row] += roll(result, lax.rem(col0 + (wide - MARGIN), wide), 1)
        inside = slice(cols, cols + full)
        small = 9 * channels
        part = dot_lanes(z_s[:, inside], all_rows(h_s, False))
        for tap in range(3):
            for tap_col in range(3):
                start = small + (3 * tap + tap_col) * width
                grads[start : start + width] += part[
                    tap_col * width : (tap_col + 1) * width, tap * width : (tap + 1) * width
                ]
        grads[0:small] += dot_lanes(all_rows(x_s, False), dz_s[...])
        start = small + 9 * width
        grads[start : start + small] += dot_lanes(all_rows(d_s, True), h2_s[:, inside])
        return carry

    lax.fori_loop(0, counts[0, 0], one_patch, 0)

    half = grads.shape[0] // 2
    odd_index = lax.rem(lax.axis_index("lat"), 2)
    send[0:half] = grads[pl.ds(pl.multiple_of((1 - odd_index) * half, half), half)].astype(BF16)
    keep[...] = grads[pl.ds(pl.multiple_of(odd_index * half, half), half)]
    blocks = wide // LANES
    for row in range(MARGIN):
        upper, lower = numer[row], numer[MARGIN + rows + row]
        near = choose(lat_odd, upper, lower).astype(BF16)
        far = choose(lat_odd, lower, upper).astype(BF16)
        for block in range(blocks):
            at = (row * blocks + block) * channels
            send[half + at : half + at + channels] = near[:, block * LANES : (block + 1) * LANES]
            second_out[at : at + channels] = far[:, block * LANES : (block + 1) * LANES]


def beside_kernel(numer, first, second, inner, edges):
    height, channels, wide = numer.shape
    cols = wide - LANES
    rows = height - 2 * MARGIN
    blocks = wide // LANES
    base = first.shape[0] - second.shape[0]
    lanes = lane_ids((channels, LANES))
    lat_odd = lax.rem(lax.axis_index("lat"), 2) == 1
    packed = jnp.zeros((channels, LANES), F32)
    for row in range(rows):
        parts = []
        for block in range(blocks):
            at = ((row % MARGIN) * blocks + block) * channels
            near = first[base + at : base + at + channels].astype(F32)
            far = second[at : at + channels].astype(F32)
            other = choose(lat_odd, near, far) if row < MARGIN else choose(lat_odd, far, near)
            parts.append(numer[MARGIN + row, :, block * LANES : (block + 1) * LANES] + other)
        inner[row] = jnp.concatenate(parts[:-1], axis=1)
        low = jnp.where(lanes < MARGIN, parts[-1], 0.0)
        high = jnp.where(lanes >= LANES - MARGIN, parts[-1], 0.0)
        packed = packed + roll(low, MARGIN * row, 1) + roll(high, -MARGIN * row, 1)
    edges[...] = packed.astype(BF16)


def fold_kernel(inner, third, fourth, den, blended):
    rows, channels, cols = inner.shape
    lanes = lane_ids((channels, LANES))
    lon_odd = lax.rem(lax.axis_index("lon"), 2) == 1
    left = choose(lon_odd, third[...], fourth[...]).astype(F32)
    right = choose(lon_odd, fourth[...], third[...]).astype(F32)
    inverse = 1.0 / den[...]
    lines = []
    for row in range(rows):
        from_left = jnp.where(lanes < MARGIN, roll(left, -MARGIN * row, 1), 0.0)
        from_right = jnp.where(lanes >= LANES - MARGIN, roll(right, MARGIN * row, 1), 0.0)
        beside = [from_left]
        for _ in range(cols // LANES - 2):
            beside.append(jnp.zeros((channels, LANES), F32))
        beside.append(from_right)
        line = inner[row] + jnp.concatenate(beside, axis=1)
        lines.append((line * inverse[row : row + 1])[None])
    blended[...] = jnp.swapaxes(jnp.concatenate(lines, axis=0), 0, 1)


def split_kernel(own, other, grad_in, grad_mid, grad_out):
    taps, channels, width = grad_in.shape
    half = own.shape[0]
    odd = lax.rem(lax.axis_index("lat"), 2) == 1
    own, other = own[...], other[...]
    summed = (choose(odd, other, own), choose(odd, own, other))

    def rows_of(start, count):
        pieces = []
        stop = start + count
        if start < half:
            pieces.append(summed[0][start : min(stop, half)])
        if stop > half:
            pieces.append(summed[1][max(start, half) - half : stop - half])
        return jnp.concatenate(pieces, axis=0).astype(F32) if len(pieces) > 1 else pieces[0].astype(F32)

    for tap in range(taps):
        grad_in[tap] = rows_of(tap * channels, channels)
        grad_mid[tap] = rows_of(taps * channels + tap * width, width)
        grad_out[tap] = rows_of(taps * (channels + width) + tap * channels, channels)


def params():
    return pltpu.CompilerParams(vmem_limit_bytes=VMEM_LIMIT)


def swap(value, axis, first, wrap):
    size = lax.axis_size(axis)
    pairs = []
    for index in range(first, size, 2):
        other = (index + 1) % size
        if other > index or wrap:
            pairs.extend([(index, other), (other, index)])
    return lax.ppermute(value, axis, pairs)


def swap_lat(first, second):
    return swap(first, "lat", 0, False), swap(second, "lat", 1, False)


def swap_lon(edges):
    return swap(edges, "lon", 0, True), swap(edges, "lon", 1, True)


def exchange(value, axis, step):
    pairs = [(index, index ^ step) for index in range(lax.axis_size(axis))]
    return lax.ppermute(value, axis, pairs)


def halves(value, bit):
    half = value.shape[0] // 2
    own = lax.dynamic_slice_in_dim(value, bit * half, half, 0)
    other = lax.dynamic_slice_in_dim(value, (1 - bit) * half, half, 0)
    return own, other


def ordered(own, other, bit):
    return jnp.concatenate([jnp.where(bit == 0, own, other), jnp.where(bit == 0, other, own)], axis=0)


def shards(
    fields, cotangent, kernel_in, kernel_mid, kernel_out, patch_anchors, blend_weights, tile_counts
):
    channels, rows, cols = fields.shape
    taps, width, _ = kernel_in.shape
    patch_anchors = jnp.transpose(patch_anchors, (0, 1, 3, 2))
    height = rows + 2 * MARGIN
    wide = cols + LANES
    full = rows * cols
    padded = full + 2 * cols
    shape = jax.ShapeDtypeStruct
    center, first, second, canvas = pl.pallas_call(
        pack_kernel,
        out_shape=(
            shape((rows, 2 * channels, cols), BF16),
            shape((MARGIN + 1, 2 * channels, cols), BF16),
            shape((MARGIN + 1, 2 * channels, cols), BF16),
            shape((height, wide), F32),
        ),
        in_specs=[smem(), smem()] + [pl.BlockSpec(memory_space=pltpu.HBM)] * 3,
        out_specs=(vmem(),) * 4,
        scratch_shapes=[
            pltpu.VMEM(fields.shape, BF16),
            pltpu.VMEM(cotangent.shape, BF16),
            pltpu.VMEM(blend_weights.shape, jnp.int32),
            pltpu.VMEM((height, wide), F32),
            pltpu.SemaphoreType.DMA((3,)),
        ],
        compiler_params=params(),
        name="pack",
    )(
        patch_anchors,
        tile_counts,
        *(pltpu.with_memory_space_constraint(value, pltpu.HBM) for value in (fields, cotangent, blend_weights)),
    )
    first, second = swap_lat(first, second)
    edges, total = pl.pallas_call(
        edge_kernel,
        out_shape=(shape((2 * channels + 2 * height, LANES), BF16), shape((height, wide), F32)),
        in_specs=[vmem()] * 4,
        out_specs=(vmem(),) * 2,
        compiler_params=params(),
        name="edges",
    )(center, first, second, canvas)
    third, fourth = swap_lon(edges)

    w_in = jnp.transpose(kernel_in, (1, 0, 2)).reshape(width, taps * channels)
    kernel_mid = kernel_mid.reshape(3, 3, width, width)
    kernel_out = kernel_out.reshape(3, 3, channels, width)
    w_mid = jnp.transpose(kernel_mid, (1, 2, 0, 3)).reshape(3 * width, 3 * width)
    w_mid_back = jnp.transpose(kernel_mid, (1, 3, 0, 2)).reshape(3 * width, 3 * width)
    w_out = jnp.transpose(kernel_out, (1, 2, 0, 3)).reshape(3 * channels, 3 * width)
    w_out_back = jnp.transpose(kernel_out, (3, 0, 1, 2)).reshape(width, taps * channels)

    lat_size, lon_size = lax.axis_size("lat"), lax.axis_size("lon")
    length = taps * (2 * channels + width)
    unit = 16 * lat_size
    length = (length + unit - 1) // unit * unit
    half = length // 2
    edge_rows = MARGIN * channels * (wide // LANES)
    send, keep, second, numer, den = pl.pallas_call(
        patch_kernel,
        out_shape=(
            shape((half + edge_rows, LANES), BF16),
            shape((half, LANES), F32),
            shape((edge_rows, LANES), BF16),
            shape((height, channels, wide), F32),
            shape((rows, cols), F32),
        ),
        in_specs=[smem(), smem()] + [vmem()] * 12,
        out_specs=(vmem(),) * 5,
        scratch_shapes=[
            pltpu.VMEM((length, LANES), F32),
            pltpu.VMEM((height, 2 * channels, wide), F32),
            pltpu.VMEM((3 * channels, padded), BF16),
            pltpu.VMEM((3 * channels, padded), BF16),
            pltpu.VMEM((width, padded), BF16),
            pltpu.VMEM((3 * width, padded), BF16),
            pltpu.VMEM((width, padded), BF16),
            pltpu.VMEM((width, full), F32),
            pltpu.VMEM((width, full), F32),
            pltpu.VMEM((width, full), BF16),
        ],
        compiler_params=params(),
        name="patches",
    )(
        patch_anchors, tile_counts, center, first, second, third, fourth, total, blend_weights,
        w_in, w_mid, w_mid_back, w_out, w_out_back,
    )

    lat = lax.axis_index("lat")
    first = exchange(send, "lat", 1)
    second = swap(second, "lat", 1, False)
    mine = keep + first[:half].astype(F32)
    steps = [2 << bit for bit in range(lat_size.bit_length() - 2)]
    parts = jnp.split(mine, 2)
    orders = (steps, steps[1:] + steps[:1])
    for turn in range(len(steps)):
        for index in (0, 1):
            step = orders[index][turn]
            own, other = halves(parts[index], (lat // step) % 2)
            parts[index] = own + exchange(other.astype(BF16), "lat", step).astype(F32)
    mine = jnp.concatenate(parts, axis=0)
    inner, edges = pl.pallas_call(
        beside_kernel,
        out_shape=(shape((rows, channels, cols), F32), shape((channels, LANES), BF16)),
        in_specs=[vmem()] * 3,
        out_specs=(vmem(),) * 2,
        compiler_params=params(),
        name="beside",
    )(numer, first, second)
    count = mine.shape[0]
    mine = mine.astype(BF16)
    if lon_size == 4:
        received = []
        for start in (0, 1):
            other = swap(jnp.concatenate([mine, edges], axis=0), "lon", start, True)
            received.append(other[count:])
            mine = (mine.astype(F32) + other[:count].astype(F32)).astype(BF16)
        third, fourth = received
    else:
        third, fourth = swap_lon(edges)
        step = 1
        while step < lon_size:
            mine = (mine.astype(F32) + exchange(mine, "lon", step).astype(F32)).astype(BF16)
            step *= 2
    blended = pl.pallas_call(
        fold_kernel,
        out_shape=shape((channels, rows, cols), F32),
        in_specs=[vmem()] * 4,
        out_specs=vmem(),
        compiler_params=params(),
        name="fold",
    )(inner, third, fourth, den)
    parts = jnp.split(mine, 2)
    for turn in reversed(range(len(steps))):
        for index in (0, 1):
            step = orders[index][turn]
            parts[index] = ordered(parts[index], exchange(parts[index], "lat", step), (lat // step) % 2)
    mine = jnp.concatenate(parts, axis=0)
    grad_in, grad_mid, grad_out = pl.pallas_call(
        split_kernel,
        out_shape=(
            shape((taps, channels, width), F32),
            shape((taps, width, width), F32),
            shape((taps, channels, width), F32),
        ),
        in_specs=[vmem()] * 2,
        out_specs=(vmem(),) * 3,
        compiler_params=params(),
        name="split",
    )(mine, exchange(mine, "lat", 1))
    return blended, jnp.transpose(grad_in, (0, 2, 1)), grad_mid, grad_out


def solution(mesh):
    return jax.shard_map(
        shards,
        mesh=mesh,
        in_specs=(
            P(None, "lat", "lon"),
            P(None, "lat", "lon"),
            P(),
            P(),
            P(),
            P("lat", "lon", None, None),
            P(None, "lat", "lon"),
            P("lat", "lon"),
        ),
        out_specs=(P(None, "lat", "lon"), P(), P(), P()),
        check_vma=False,
    )
```

```python
import functools

import jax
import jax.numpy as jnp
from jax import lax
from jax.experimental import pallas as pl
from jax.experimental.pallas import tpu as pltpu
from jax.sharding import PartitionSpec as P

MARGIN = 4
SLOTS = 4
LANES = 128
F32 = jnp.float32
BF16 = jnp.bfloat16
VMEM_LIMIT = 48 * 1024 * 1024


def vmem():
    return pl.BlockSpec(memory_space=pltpu.VMEM)


def smem():
    return pl.BlockSpec(memory_space=pltpu.SMEM)


def lane_ids(shape):
    return lax.broadcasted_iota(jnp.int32, shape, len(shape) - 1)


def roll(value, shift, axis):
    size = value.shape[axis]
    if isinstance(shift, int):
        shift = shift % size
        if shift == 0:
            return value
    return pltpu.roll(value, shift, axis)


def choose(odd, when_odd, when_even):
    return jnp.where(odd, when_odd, when_even)


def pack_kernel(
    anchors, counts, fields_in, cotangent_in, weights_in, center, first_out, second_out, canvas,
    fields, cotangent, weights, spread, sems,
):
    copies = []
    for index, (source, target) in enumerate(
        ((weights_in, weights), (fields_in, fields), (cotangent_in, cotangent))
    ):
        copy = pltpu.make_async_copy(source, target, sems.at[index])
        copy.start()
        copies.append(copy)
    channels, rows, cols = fields.shape
    wide = cols + LANES
    odd = lax.rem(lax.axis_index("lat"), 2) == 1
    spread[...] = jnp.zeros_like(spread)
    copies[0].wait()
    for slot in range(SLOTS):

        @pl.when(slot < counts[0, 0])
        def _():
            row = anchors[0, 0, 0, slot]
            col = anchors[0, 0, 1, slot]
            values = weights[slot].astype(F32)
            values = jnp.concatenate([values, jnp.zeros((rows, LANES), F32)], axis=1)
            values = jnp.concatenate([values, jnp.zeros((2 * MARGIN, wide), F32)], axis=0)
            values = roll(values, lax.rem(col + (wide - MARGIN), wide), 1)
            values = roll(values, row, 0)
            spread[...] += values

    total = spread[...]
    canvas[...] = total
    copies[1].wait()
    copies[2].wait()
    both = []
    for source in (fields, cotangent):
        both.append(jnp.swapaxes(source[...].astype(F32), 0, 1))
    tile = jnp.concatenate(both, axis=1).astype(BF16)
    center[...] = tile
    half = total.shape[0] // 2
    pad = jnp.zeros((2 * channels - 2 * half, cols), F32)
    extras = []
    for part in (total[:half], total[half:]):
        beside = jnp.concatenate([part[:, cols:], jnp.zeros((half, cols - LANES), F32)], axis=1)
        extras.append(jnp.concatenate([part[:, :cols], beside, pad], axis=0).astype(BF16))
    top, bottom = tile[:MARGIN], tile[rows - MARGIN :]
    first_out[0:MARGIN] = choose(odd, top, bottom)
    first_out[MARGIN] = choose(odd, extras[0], extras[1])
    second_out[0:MARGIN] = choose(odd, bottom, top)
    second_out[MARGIN] = choose(odd, extras[1], extras[0])


def edge_kernel(center, first, second, canvas, edges, total_out):
    rows = center.shape[0]
    channels = center.shape[1] // 2
    cols = center.shape[2]
    height = rows + 2 * MARGIN
    half = height // 2
    odd = lax.rem(lax.axis_index("lat"), 2) == 1

    def stretch(block):
        block = block.astype(F32)
        return jnp.concatenate([block[:half], block[half:height, :LANES]], axis=1)

    upper = stretch(choose(odd, first[MARGIN], second[MARGIN]))
    lower = stretch(choose(odd, second[MARGIN], first[MARGIN]))
    total = canvas[...] + jnp.concatenate([upper, lower], axis=0)
    total_out[...] = total
    lanes = lane_ids((2 * channels, LANES))
    packed = jnp.zeros((2 * channels, LANES), F32)
    for row in range(height):
        if row < MARGIN:
            line = choose(odd, first[row], second[row])
        elif row < MARGIN + rows:
            line = center[row - MARGIN]
        else:
            line = choose(odd, second[row - MARGIN - rows], first[row - MARGIN - rows])
        line = line.astype(F32)
        low = jnp.where(lanes < MARGIN, line[:, :LANES], 0.0)
        high = jnp.where(lanes >= LANES - MARGIN, line[:, cols - LANES :], 0.0)
        packed = packed + roll(low, MARGIN * row, 1) + roll(high, -MARGIN * row, 1)
    edges[0 : 2 * channels] = packed.astype(BF16)
    margin = total[:, cols:]
    lanes = lane_ids(margin.shape)
    to_left = jnp.where(lanes < LANES // 2, total[:, :LANES], margin)
    to_right = jnp.where(lanes < LANES // 2, margin, total[:, cols - LANES : cols])
    edges[2 * channels : 2 * channels + height] = to_left.astype(BF16)
    edges[2 * channels + height : 2 * channels + 2 * height] = to_right.astype(BF16)


def dot(left, right):
    return jnp.dot(left, right, preferred_element_type=F32)


def dot_lanes(left, right):
    return lax.dot_general(left, right, (((1,), (1,)), ((), ())), preferred_element_type=F32)


def patch_kernel(
    anchors, counts, center, first, second, third, fourth, total_in, weights,
    w_in, w_mid, w_mid_back, w_out, w_out_back,
    send, keep, second_out, numer, den_out,
    grads, window, x_s, d_s, h_s, z_s, h2_s, slope_s, dh_s, dz_s,
):
    rows = center.shape[0]
    channels = center.shape[1] // 2
    cols = center.shape[2]
    wide = cols + LANES
    width = w_in.shape[0]
    full = rows * cols
    height = rows + 2 * MARGIN
    lanes = lane_ids((2 * channels, LANES))
    lat_odd = lax.rem(lax.axis_index("lat"), 2) == 1
    lon_odd = lax.rem(lax.axis_index("lon"), 2) == 1

    left = choose(lon_odd, third[...], fourth[...]).astype(F32)
    right = choose(lon_odd, fourth[...], third[...]).astype(F32)
    base = 2 * channels
    left_part = left[base + height : base + 2 * height]
    right_part = right[base : base + height]
    edge_lanes = lane_ids((height, LANES))
    low = edge_lanes < MARGIN
    high = edge_lanes >= LANES - MARGIN
    zero = jnp.zeros((height, LANES), F32)
    pieces = [jnp.where(low, left_part, zero)]
    for _ in range(cols // LANES - 2):
        pieces.append(zero)
    pieces.append(jnp.where(high, right_part, zero))
    pieces.append(jnp.where(high, left_part, zero) + jnp.where(low, right_part, zero))
    den = jnp.maximum(total_in[...] + jnp.concatenate(pieces, axis=1), 1.0)
    den_out[...] = den[MARGIN : MARGIN + rows, :cols]
    inverse = 1.0 / den

    left = left[:base]
    right = right[:base]
    for row in range(height):
        if row < MARGIN:
            body = choose(lat_odd, first[row], second[row])
        elif row < MARGIN + rows:
            body = center[row - MARGIN]
        else:
            body = choose(lat_odd, second[row - MARGIN - rows], first[row - MARGIN - rows])
        beside = jnp.where(
            lanes < LANES // 2, roll(right, -MARGIN * row, 1), roll(left, MARGIN * row, 1)
        )
        line = jnp.concatenate([body.astype(F32), beside], axis=1)
        scaled = line[channels:] * inverse[row : row + 1]
        window[row, 0:channels] = line[:channels]
        window[row, channels : 2 * channels] = scaled.astype(BF16).astype(F32)

    numer[...] = jnp.zeros_like(numer)
    grads[...] = jnp.zeros_like(grads)
    for ref in (x_s, d_s, h_s, z_s, h2_s):
        ref[:, 0:cols] = jnp.zeros((ref.shape[0], cols), BF16)
        ref[:, cols + full : 2 * cols + full] = jnp.zeros((ref.shape[0], cols), BF16)

    def shifted(value, step):
        blocks = [value[:, at : at + LANES] for at in range(0, cols, LANES)]
        turned = [roll(block, step, 1) for block in blocks]
        ids = lane_ids(blocks[0].shape)
        zero = jnp.zeros_like(blocks[0])
        if step > 0:
            ends = [zero] + turned[:-1]
            at_end = ids == 0
        else:
            ends = turned[1:] + [zero]
            at_end = ids == LANES - 1
        return jnp.concatenate([jnp.where(at_end, end, own) for end, own in zip(ends, turned)], axis=1)

    def before(value):
        return shifted(value, 1)

    def after(value):
        return shifted(value, -1)

    def spread(ref, value, row, flip):
        count = value.shape[0]
        at = slice((row + 1) * cols, (row + 2) * cols)
        first, last = before(value), after(value)
        if flip:
            first, last = last, first
        ref[0:count, at] = first
        ref[count : 2 * count, at] = value
        ref[2 * count : 3 * count, at] = last

    def stack(ref, row, flip):
        starts = [(row + (2 - tap if flip else tap)) * cols for tap in range(3)]
        return jnp.concatenate([ref[:, start : start + cols] for start in starts], axis=0)

    def across(parts, flip):
        count = parts.shape[0] // 3
        first, last = parts[:count], parts[2 * count :]
        if flip:
            first, last = last, first
        return before(first) + parts[count : 2 * count] + after(last)

    def all_rows(ref, flip):
        starts = [(2 - tap if flip else tap) * cols for tap in range(3)]
        return jnp.concatenate([ref[:, start : start + full] for start in starts], axis=0)

    def one_patch(slot, carry):
        row0 = anchors[0, 0, 0, slot]
        col0 = anchors[0, 0, 1, slot]
        patch_weights = weights[slot].astype(F32)
        back_shift = lax.rem(wide + MARGIN - col0, wide)
        for row in range(rows):
            line = roll(window[row0 + row], back_shift, 1)[:, :cols]
            spread(x_s, line[:channels].astype(BF16), row, False)
            grad = line[channels:] * patch_weights[row : row + 1]
            spread(d_s, grad.astype(BF16), row, True)
        for row in range(rows):
            at = slice(row * cols, (row + 1) * cols)
            z1 = dot(w_in[...], stack(x_s, row, False))
            sig = 0.5 * jnp.tanh(0.5 * z1) + 0.5
            h1 = z1 * sig
            slope_s[:, at] = sig + h1 * (1.0 - sig)
            h_s[:, (row + 1) * cols : (row + 2) * cols] = h1.astype(BF16)
        for row in range(rows):
            at = slice(row * cols, (row + 1) * cols)
            ahead = slice((row + 1) * cols, (row + 2) * cols)
            dh2 = dot(w_out_back[...], stack(d_s, row, True))
            z2 = across(dot(w_mid[...], stack(h_s, row, False)), False)
            sig = 0.5 * jnp.tanh(0.5 * z2) + 0.5
            added = z2 * sig
            h2_s[:, ahead] = (h_s[:, ahead].astype(F32) + added).astype(BF16)
            dz2 = (dh2 * (sig + added * (1.0 - sig))).astype(BF16)
            dh_s[:, at] = dh2
            spread(z_s, dz2, row, True)
        for row in range(rows):
            at = slice(row * cols, (row + 1) * cols)
            back = across(dot(w_mid_back[...], stack(z_s.at[width : 2 * width], row, True)), True)
            dz_s[:, at] = ((dh_s[:, at] + back) * slope_s[:, at]).astype(BF16)
        for row in range(rows):
            result = across(dot(w_out[...], stack(h2_s, row, False)), False)
            result = result * patch_weights[row : row + 1]
            result = jnp.concatenate([result, jnp.zeros((channels, LANES), F32)], axis=1)
            numer[row0 + row] += roll(result, lax.rem(col0 + (wide - MARGIN), wide), 1)
        inside = slice(cols, cols + full)
        small = 9 * channels
        part = dot_lanes(z_s[:, inside], all_rows(h_s, False))
        for tap in range(3):
            for tap_col in range(3):
                start = small + (3 * tap + tap_col) * width
                grads[start : start + width] += part[
                    tap_col * width : (tap_col + 1) * width, tap * width : (tap + 1) * width
                ]
        grads[0:small] += dot_lanes(all_rows(x_s, False), dz_s[...])
        start = small + 9 * width
        grads[start : start + small] += dot_lanes(all_rows(d_s, True), h2_s[:, inside])
        return carry

    lax.fori_loop(0, counts[0, 0], one_patch, 0)

    half = grads.shape[0] // 2
    odd_index = lax.rem(lax.axis_index("lat"), 2)
    send[0:half] = grads[pl.ds(pl.multiple_of((1 - odd_index) * half, half), half)].astype(BF16)
    keep[...] = grads[pl.ds(pl.multiple_of(odd_index * half, half), half)]
    blocks = wide // LANES
    for row in range(MARGIN):
        upper, lower = numer[row], numer[MARGIN + rows + row]
        near = choose(lat_odd, upper, lower).astype(BF16)
        far = choose(lat_odd, lower, upper).astype(BF16)
        for block in range(blocks):
            at = (row * blocks + block) * channels
            send[half + at : half + at + channels] = near[:, block * LANES : (block + 1) * LANES]
            second_out[at : at + channels] = far[:, block * LANES : (block + 1) * LANES]


def beside_kernel(numer, first, second, inner, edges):
    height, channels, wide = numer.shape
    cols = wide - LANES
    rows = height - 2 * MARGIN
    blocks = wide // LANES
    base = first.shape[0] - second.shape[0]
    lanes = lane_ids((channels, LANES))
    lat_odd = lax.rem(lax.axis_index("lat"), 2) == 1
    packed = jnp.zeros((channels, LANES), F32)
    for row in range(rows):
        parts = []
        for block in range(blocks):
            at = ((row % MARGIN) * blocks + block) * channels
            near = first[base + at : base + at + channels].astype(F32)
            far = second[at : at + channels].astype(F32)
            other = choose(lat_odd, near, far) if row < MARGIN else choose(lat_odd, far, near)
            parts.append(numer[MARGIN + row, :, block * LANES : (block + 1) * LANES] + other)
        inner[row] = jnp.concatenate(parts[:-1], axis=1)
        low = jnp.where(lanes < MARGIN, parts[-1], 0.0)
        high = jnp.where(lanes >= LANES - MARGIN, parts[-1], 0.0)
        packed = packed + roll(low, MARGIN * row, 1) + roll(high, -MARGIN * row, 1)
    edges[...] = packed.astype(BF16)


def fold_kernel(inner, third, fourth, den, blended):
    rows, channels, cols = inner.shape
    lanes = lane_ids((channels, LANES))
    lon_odd = lax.rem(lax.axis_index("lon"), 2) == 1
    left = choose(lon_odd, third[...], fourth[...]).astype(F32)
    right = choose(lon_odd, fourth[...], third[...]).astype(F32)
    inverse = 1.0 / den[...]
    lines = []
    for row in range(rows):
        from_left = jnp.where(lanes < MARGIN, roll(left, -MARGIN * row, 1), 0.0)
        from_right = jnp.where(lanes >= LANES - MARGIN, roll(right, MARGIN * row, 1), 0.0)
        beside = [from_left]
        for _ in range(cols // LANES - 2):
            beside.append(jnp.zeros((channels, LANES), F32))
        beside.append(from_right)
        line = inner[row] + jnp.concatenate(beside, axis=1)
        lines.append((line * inverse[row : row + 1])[None])
    blended[...] = jnp.swapaxes(jnp.concatenate(lines, axis=0), 0, 1)


def split_kernel(own, other, grad_in, grad_mid, grad_out):
    taps, channels, width = grad_in.shape
    half = own.shape[0]
    odd = lax.rem(lax.axis_index("lat"), 2) == 1
    own, other = own[...], other[...]
    summed = (choose(odd, other, own), choose(odd, own, other))

    def rows_of(start, count):
        pieces = []
        stop = start + count
        if start < half:
            pieces.append(summed[0][start : min(stop, half)])
        if stop > half:
            pieces.append(summed[1][max(start, half) - half : stop - half])
        return jnp.concatenate(pieces, axis=0).astype(F32) if len(pieces) > 1 else pieces[0].astype(F32)

    for tap in range(taps):
        grad_in[tap] = rows_of(tap * channels, channels)
        grad_mid[tap] = rows_of(taps * channels + tap * width, width)
        grad_out[tap] = rows_of(taps * (channels + width) + tap * channels, channels)


def params():
    return pltpu.CompilerParams(vmem_limit_bytes=VMEM_LIMIT)


def swap(value, axis, first, wrap):
    size = lax.axis_size(axis)
    pairs = []
    for index in range(first, size, 2):
        other = (index + 1) % size
        if other > index or wrap:
            pairs.extend([(index, other), (other, index)])
    return lax.ppermute(value, axis, pairs)


def swap_lat(first, second):
    return swap(first, "lat", 0, False), swap(second, "lat", 1, False)


def swap_lon(edges):
    return swap(edges, "lon", 0, True), swap(edges, "lon", 1, True)


def exchange(value, axis, order):
    pairs = [(index, index ^ order[index % 2]) for index in range(lax.axis_size(axis))]
    return lax.ppermute(value, axis, pairs)


def order_bit(lat, order):
    step = jnp.where(lat % 2 == 0, order[0], order[1])
    return (lat // step) % 2


def halves(value, bit):
    half = value.shape[0] // 2
    own = lax.dynamic_slice_in_dim(value, bit * half, half, 0)
    other = lax.dynamic_slice_in_dim(value, (1 - bit) * half, half, 0)
    return own, other


def ordered(own, other, bit):
    return jnp.concatenate([jnp.where(bit == 0, own, other), jnp.where(bit == 0, other, own)], axis=0)


def shards(
    fields, cotangent, kernel_in, kernel_mid, kernel_out, patch_anchors, blend_weights, tile_counts
):
    channels, rows, cols = fields.shape
    taps, width, _ = kernel_in.shape
    patch_anchors = jnp.transpose(patch_anchors, (0, 1, 3, 2))
    height = rows + 2 * MARGIN
    wide = cols + LANES
    full = rows * cols
    padded = full + 2 * cols
    shape = jax.ShapeDtypeStruct
    center, first, second, canvas = pl.pallas_call(
        pack_kernel,
        out_shape=(
            shape((rows, 2 * channels, cols), BF16),
            shape((MARGIN + 1, 2 * channels, cols), BF16),
            shape((MARGIN + 1, 2 * channels, cols), BF16),
            shape((height, wide), F32),
        ),
        in_specs=[smem(), smem()] + [pl.BlockSpec(memory_space=pltpu.HBM)] * 3,
        out_specs=(vmem(),) * 4,
        scratch_shapes=[
            pltpu.VMEM(fields.shape, BF16),
            pltpu.VMEM(cotangent.shape, BF16),
            pltpu.VMEM(blend_weights.shape, jnp.int32),
            pltpu.VMEM((height, wide), F32),
            pltpu.SemaphoreType.DMA((3,)),
        ],
        compiler_params=params(),
        name="pack",
    )(
        patch_anchors,
        tile_counts,
        *(pltpu.with_memory_space_constraint(value, pltpu.HBM) for value in (fields, cotangent, blend_weights)),
    )
    first, second = swap_lat(first, second)
    w_in = jnp.transpose(kernel_in, (1, 0, 2)).reshape(width, taps * channels)
    kernel_mid = kernel_mid.reshape(3, 3, width, width)
    kernel_out = kernel_out.reshape(3, 3, channels, width)
    w_mid = jnp.transpose(kernel_mid, (1, 2, 0, 3)).reshape(3 * width, 3 * width)
    w_mid_back = jnp.transpose(kernel_mid, (1, 3, 0, 2)).reshape(3 * width, 3 * width)
    w_out = jnp.transpose(kernel_out, (1, 2, 0, 3)).reshape(3 * channels, 3 * width)
    w_out_back = jnp.transpose(kernel_out, (3, 0, 1, 2)).reshape(width, taps * channels)
    first, second, w_in, w_mid, w_mid_back, w_out, w_out_back = lax.optimization_barrier(
        (first, second, w_in, w_mid, w_mid_back, w_out, w_out_back)
    )
    edges, total = pl.pallas_call(
        edge_kernel,
        out_shape=(shape((2 * channels + 2 * height, LANES), BF16), shape((height, wide), F32)),
        in_specs=[vmem()] * 4,
        out_specs=(vmem(),) * 2,
        compiler_params=params(),
        name="edges",
    )(center, first, second, canvas)
    third, fourth = swap_lon(edges)

    lat_size, lon_size = lax.axis_size("lat"), lax.axis_size("lon")
    length = taps * (2 * channels + width)
    unit = 16 * lat_size
    length = (length + unit - 1) // unit * unit
    half = length // 2
    edge_rows = MARGIN * channels * (wide // LANES)
    send, keep, second, numer, den = pl.pallas_call(
        patch_kernel,
        out_shape=(
            shape((half + edge_rows, LANES), BF16),
            shape((half, LANES), F32),
            shape((edge_rows, LANES), BF16),
            shape((height, channels, wide), F32),
            shape((rows, cols), F32),
        ),
        in_specs=[smem(), smem()] + [vmem()] * 12,
        out_specs=(vmem(),) * 5,
        scratch_shapes=[
            pltpu.VMEM((length, LANES), F32),
            pltpu.VMEM((height, 2 * channels, wide), F32),
            pltpu.VMEM((3 * channels, padded), BF16),
            pltpu.VMEM((3 * channels, padded), BF16),
            pltpu.VMEM((width, padded), BF16),
            pltpu.VMEM((3 * width, padded), BF16),
            pltpu.VMEM((width, padded), BF16),
            pltpu.VMEM((width, full), F32),
            pltpu.VMEM((width, full), F32),
            pltpu.VMEM((width, full), BF16),
        ],
        compiler_params=params(),
        name="patches",
    )(
        patch_anchors, tile_counts, center, first, second, third, fourth, total, blend_weights,
        w_in, w_mid, w_mid_back, w_out, w_out_back,
    )

    lat = lax.axis_index("lat")
    first = exchange(send, "lat", (1, 1))
    second = swap(second, "lat", 1, False)
    mine = keep + first[:half].astype(F32)
    steps = [2 << bit for bit in range(lat_size.bit_length() - 2)]
    orders = list(zip(steps, steps[1:] + steps[:1]))
    for order in orders:
        own, other = halves(mine, order_bit(lat, order))
        mine = own + exchange(other.astype(BF16), "lat", order).astype(F32)
    mine = mine.astype(BF16)
    second, mine = lax.optimization_barrier((second, mine))
    inner, edges = pl.pallas_call(
        beside_kernel,
        out_shape=(shape((rows, channels, cols), F32), shape((channels, LANES), BF16)),
        in_specs=[vmem()] * 3,
        out_specs=(vmem(),) * 2,
        compiler_params=params(),
        name="beside",
    )(numer, first, second)
    count = mine.shape[0]
    if lon_size == 4:
        received = []
        for start in (0, 1):
            other = swap(jnp.concatenate([mine, edges], axis=0), "lon", start, True)
            received.append(other[count:])
            mine = (mine.astype(F32) + other[:count].astype(F32)).astype(BF16)
        third, fourth = received
    else:
        third, fourth = swap_lon(edges)
        step = 1
        while step < lon_size:
            mine = (mine.astype(F32) + exchange(mine, "lon", (step, step)).astype(F32)).astype(BF16)
            step *= 2
    blended = pl.pallas_call(
        fold_kernel,
        out_shape=shape((channels, rows, cols), F32),
        in_specs=[vmem()] * 4,
        out_specs=vmem(),
        compiler_params=params(),
        name="fold",
    )(inner, third, fourth, den)
    for order in reversed(orders):
        mine = ordered(mine, exchange(mine, "lat", order), order_bit(lat, order))
    grad_in, grad_mid, grad_out = pl.pallas_call(
        split_kernel,
        out_shape=(
            shape((taps, channels, width), F32),
            shape((taps, width, width), F32),
            shape((taps, channels, width), F32),
        ),
        in_specs=[vmem()] * 2,
        out_specs=(vmem(),) * 3,
        compiler_params=params(),
        name="split",
    )(mine, exchange(mine, "lat", (1, 1)))
    return blended, jnp.transpose(grad_in, (0, 2, 1)), grad_mid, grad_out


def solution(mesh):
    return jax.shard_map(
        shards,
        mesh=mesh,
        in_specs=(
            P(None, "lat", "lon"),
            P(None, "lat", "lon"),
            P(),
            P(),
            P(),
            P("lat", "lon", None, None),
            P(None, "lat", "lon"),
            P("lat", "lon"),
        ),
        out_specs=(P(None, "lat", "lon"), P(), P(), P()),
        check_vma=False,
    )
```

```python
import functools

import jax
import jax.numpy as jnp
from jax import lax
from jax.experimental import pallas as pl
from jax.experimental.pallas import tpu as pltpu
from jax.sharding import PartitionSpec as P

MARGIN = 4
SLOTS = 4
LANES = 128
F32 = jnp.float32
BF16 = jnp.bfloat16
VMEM_LIMIT = 48 * 1024 * 1024


def vmem():
    return pl.BlockSpec(memory_space=pltpu.VMEM)


def smem():
    return pl.BlockSpec(memory_space=pltpu.SMEM)


def lane_ids(shape):
    return lax.broadcasted_iota(jnp.int32, shape, len(shape) - 1)


def roll(value, shift, axis):
    size = value.shape[axis]
    if isinstance(shift, int):
        shift = shift % size
        if shift == 0:
            return value
    return pltpu.roll(value, shift, axis)


def choose(odd, when_odd, when_even):
    return jnp.where(odd, when_odd, when_even)


def pack_kernel(
    anchors, counts, fields_in, cotangent_in, weights_in, center, first_out, second_out, canvas,
    fields, cotangent, weights, spread, sems,
):
    copies = []
    for index, (source, target) in enumerate(
        ((weights_in, weights), (fields_in, fields), (cotangent_in, cotangent))
    ):
        copy = pltpu.make_async_copy(source, target, sems.at[index])
        copy.start()
        copies.append(copy)
    channels, rows, cols = fields.shape
    wide = cols + LANES
    odd = lax.rem(lax.axis_index("lat"), 2) == 1
    spread[...] = jnp.zeros_like(spread)
    copies[0].wait()
    for slot in range(SLOTS):

        @pl.when(slot < counts[0, 0])
        def _():
            row = anchors[0, 0, 0, slot]
            col = anchors[0, 0, 1, slot]
            values = weights[slot].astype(F32)
            values = jnp.concatenate([values, jnp.zeros((rows, LANES), F32)], axis=1)
            values = jnp.concatenate([values, jnp.zeros((2 * MARGIN, wide), F32)], axis=0)
            values = roll(values, lax.rem(col + (wide - MARGIN), wide), 1)
            values = roll(values, row, 0)
            spread[...] += values

    total = spread[...]
    canvas[...] = total
    copies[1].wait()
    copies[2].wait()
    both = []
    for source in (fields, cotangent):
        both.append(jnp.swapaxes(source[...].astype(F32), 0, 1))
    tile = jnp.concatenate(both, axis=1).astype(BF16)
    center[...] = tile
    half = total.shape[0] // 2
    pad = jnp.zeros((2 * channels - 2 * half, cols), F32)
    extras = []
    for part in (total[:half], total[half:]):
        beside = jnp.concatenate([part[:, cols:], jnp.zeros((half, cols - LANES), F32)], axis=1)
        extras.append(jnp.concatenate([part[:, :cols], beside, pad], axis=0).astype(BF16))
    top, bottom = tile[:MARGIN], tile[rows - MARGIN :]
    first_out[0:MARGIN] = choose(odd, top, bottom)
    first_out[MARGIN] = choose(odd, extras[0], extras[1])
    second_out[0:MARGIN] = choose(odd, bottom, top)
    second_out[MARGIN] = choose(odd, extras[1], extras[0])


def edge_kernel(center, first, second, canvas, edges, total_out):
    rows = center.shape[0]
    channels = center.shape[1] // 2
    cols = center.shape[2]
    height = rows + 2 * MARGIN
    half = height // 2
    odd = lax.rem(lax.axis_index("lat"), 2) == 1

    def stretch(block):
        block = block.astype(F32)
        return jnp.concatenate([block[:half], block[half:height, :LANES]], axis=1)

    upper = stretch(choose(odd, first[MARGIN], second[MARGIN]))
    lower = stretch(choose(odd, second[MARGIN], first[MARGIN]))
    total = canvas[...] + jnp.concatenate([upper, lower], axis=0)
    total_out[...] = total
    lanes = lane_ids((2 * channels, LANES))
    packed = jnp.zeros((2 * channels, LANES), F32)
    for row in range(height):
        if row < MARGIN:
            line = choose(odd, first[row], second[row])
        elif row < MARGIN + rows:
            line = center[row - MARGIN]
        else:
            line = choose(odd, second[row - MARGIN - rows], first[row - MARGIN - rows])
        line = line.astype(F32)
        low = jnp.where(lanes < MARGIN, line[:, :LANES], 0.0)
        high = jnp.where(lanes >= LANES - MARGIN, line[:, cols - LANES :], 0.0)
        packed = packed + roll(low, MARGIN * row, 1) + roll(high, -MARGIN * row, 1)
    edges[0 : 2 * channels] = packed.astype(BF16)
    margin = total[:, cols:]
    lanes = lane_ids(margin.shape)
    to_left = jnp.where(lanes < LANES // 2, total[:, :LANES], margin)
    to_right = jnp.where(lanes < LANES // 2, margin, total[:, cols - LANES : cols])
    edges[2 * channels : 2 * channels + height] = to_left.astype(BF16)
    edges[2 * channels + height : 2 * channels + 2 * height] = to_right.astype(BF16)


def dot(left, right):
    return jnp.dot(left, right, preferred_element_type=F32)


def dot_lanes(left, right):
    return lax.dot_general(left, right, (((1,), (1,)), ((), ())), preferred_element_type=F32)


def patch_kernel(
    anchors, counts, center, first, second, third, fourth, total_in, weights,
    w_in, w_mid, w_mid_back, w_out, w_out_back,
    send, keep, numer, den_out,
    grads, window, x_s, d_s, h_s, z_s, h2_s, slope_s, dh_s, dz_s,
):
    rows = center.shape[0]
    channels = center.shape[1] // 2
    cols = center.shape[2]
    wide = cols + LANES
    width = w_in.shape[0]
    full = rows * cols
    height = rows + 2 * MARGIN
    lanes = lane_ids((2 * channels, LANES))
    lat_odd = lax.rem(lax.axis_index("lat"), 2) == 1
    lon_odd = lax.rem(lax.axis_index("lon"), 2) == 1

    left = choose(lon_odd, third[...], fourth[...]).astype(F32)
    right = choose(lon_odd, fourth[...], third[...]).astype(F32)
    base = 2 * channels
    left_part = left[base + height : base + 2 * height]
    right_part = right[base : base + height]
    edge_lanes = lane_ids((height, LANES))
    low = edge_lanes < MARGIN
    high = edge_lanes >= LANES - MARGIN
    zero = jnp.zeros((height, LANES), F32)
    pieces = [jnp.where(low, left_part, zero)]
    for _ in range(cols // LANES - 2):
        pieces.append(zero)
    pieces.append(jnp.where(high, right_part, zero))
    pieces.append(jnp.where(high, left_part, zero) + jnp.where(low, right_part, zero))
    den = jnp.maximum(total_in[...] + jnp.concatenate(pieces, axis=1), 1.0)
    den_out[...] = den[MARGIN : MARGIN + rows, :cols]
    inverse = 1.0 / den

    left = left[:base]
    right = right[:base]
    for row in range(height):
        if row < MARGIN:
            body = choose(lat_odd, first[row], second[row])
        elif row < MARGIN + rows:
            body = center[row - MARGIN]
        else:
            body = choose(lat_odd, second[row - MARGIN - rows], first[row - MARGIN - rows])
        beside = jnp.where(
            lanes < LANES // 2, roll(right, -MARGIN * row, 1), roll(left, MARGIN * row, 1)
        )
        line = jnp.concatenate([body.astype(F32), beside], axis=1)
        scaled = line[channels:] * inverse[row : row + 1]
        window[row, 0:channels] = line[:channels]
        window[row, channels : 2 * channels] = scaled.astype(BF16).astype(F32)

    numer[...] = jnp.zeros_like(numer)
    grads[...] = jnp.zeros_like(grads)
    for ref in (x_s, d_s, h_s, z_s, h2_s):
        ref[:, 0:cols] = jnp.zeros((ref.shape[0], cols), BF16)
        ref[:, cols + full : 2 * cols + full] = jnp.zeros((ref.shape[0], cols), BF16)

    def shifted(value, step):
        blocks = [value[:, at : at + LANES] for at in range(0, cols, LANES)]
        turned = [roll(block, step, 1) for block in blocks]
        ids = lane_ids(blocks[0].shape)
        zero = jnp.zeros_like(blocks[0])
        if step > 0:
            ends = [zero] + turned[:-1]
            at_end = ids == 0
        else:
            ends = turned[1:] + [zero]
            at_end = ids == LANES - 1
        return jnp.concatenate([jnp.where(at_end, end, own) for end, own in zip(ends, turned)], axis=1)

    def before(value):
        return shifted(value, 1)

    def after(value):
        return shifted(value, -1)

    def spread(ref, value, row, flip):
        count = value.shape[0]
        at = slice((row + 1) * cols, (row + 2) * cols)
        first, last = before(value), after(value)
        if flip:
            first, last = last, first
        ref[0:count, at] = first
        ref[count : 2 * count, at] = value
        ref[2 * count : 3 * count, at] = last

    def stack(ref, row, flip):
        starts = [(row + (2 - tap if flip else tap)) * cols for tap in range(3)]
        return jnp.concatenate([ref[:, start : start + cols] for start in starts], axis=0)

    def across(parts, flip):
        count = parts.shape[0] // 3
        first, last = parts[:count], parts[2 * count :]
        if flip:
            first, last = last, first
        return before(first) + parts[count : 2 * count] + after(last)

    def all_rows(ref, flip):
        starts = [(2 - tap if flip else tap) * cols for tap in range(3)]
        return jnp.concatenate([ref[:, start : start + full] for start in starts], axis=0)

    def one_patch(slot, carry):
        row0 = anchors[0, 0, 0, slot]
        col0 = anchors[0, 0, 1, slot]
        patch_weights = weights[slot].astype(F32)
        back_shift = lax.rem(wide + MARGIN - col0, wide)
        for row in range(rows):
            line = roll(window[row0 + row], back_shift, 1)[:, :cols]
            spread(x_s, line[:channels].astype(BF16), row, False)
            grad = line[channels:] * patch_weights[row : row + 1]
            spread(d_s, grad.astype(BF16), row, True)
        for row in range(rows):
            at = slice(row * cols, (row + 1) * cols)
            z1 = dot(w_in[...], stack(x_s, row, False))
            sig = 0.5 * jnp.tanh(0.5 * z1) + 0.5
            h1 = z1 * sig
            slope_s[:, at] = sig + h1 * (1.0 - sig)
            h_s[:, (row + 1) * cols : (row + 2) * cols] = h1.astype(BF16)
        for row in range(rows):
            at = slice(row * cols, (row + 1) * cols)
            ahead = slice((row + 1) * cols, (row + 2) * cols)
            dh2 = dot(w_out_back[...], stack(d_s, row, True))
            z2 = across(dot(w_mid[...], stack(h_s, row, False)), False)
            sig = 0.5 * jnp.tanh(0.5 * z2) + 0.5
            added = z2 * sig
            h2_s[:, ahead] = (h_s[:, ahead].astype(F32) + added).astype(BF16)
            dz2 = (dh2 * (sig + added * (1.0 - sig))).astype(BF16)
            dh_s[:, at] = dh2
            spread(z_s, dz2, row, True)
        for row in range(rows):
            at = slice(row * cols, (row + 1) * cols)
            back = across(dot(w_mid_back[...], stack(z_s.at[width : 2 * width], row, True)), True)
            dz_s[:, at] = ((dh_s[:, at] + back) * slope_s[:, at]).astype(BF16)
        for row in range(rows):
            result = across(dot(w_out[...], stack(h2_s, row, False)), False)
            result = result * patch_weights[row : row + 1]
            result = jnp.concatenate([result, jnp.zeros((channels, LANES), F32)], axis=1)
            numer[row0 + row] += roll(result, lax.rem(col0 + (wide - MARGIN), wide), 1)
        inside = slice(cols, cols + full)
        small = 9 * channels
        part = dot_lanes(z_s[:, inside], all_rows(h_s, False))
        for tap in range(3):
            for tap_col in range(3):
                start = small + (3 * tap + tap_col) * width
                grads[start : start + width] += part[
                    tap_col * width : (tap_col + 1) * width, tap * width : (tap + 1) * width
                ]
        grads[0:small] += dot_lanes(all_rows(x_s, False), dz_s[...])
        start = small + 9 * width
        grads[start : start + small] += dot_lanes(all_rows(d_s, True), h2_s[:, inside])
        return carry

    lax.fori_loop(0, counts[0, 0], one_patch, 0)

    half = grads.shape[0] // 2
    odd_index = lax.rem(lax.axis_index("lat"), 2)
    send[0:half] = grads[pl.ds(pl.multiple_of((1 - odd_index) * half, half), half)].astype(BF16)
    keep[...] = grads[pl.ds(pl.multiple_of(odd_index * half, half), half)]
    lanes = lane_ids((channels, LANES))
    blocks = cols // LANES
    base = half
    upper = [numer[row] for row in range(MARGIN)]
    lower = [numer[MARGIN + rows + row] for row in range(MARGIN)]
    for when_odd, when_even in ((upper, lower), (lower, upper)):
        packed = jnp.zeros((channels, LANES), F32)
        for row in range(MARGIN):
            line = choose(lat_odd, when_odd[row], when_even[row])
            for block in range(blocks):
                send[base : base + channels] = line[:, block * LANES : (block + 1) * LANES].astype(BF16)
                base += channels
            low = jnp.where(lanes < MARGIN, line[:, cols:], 0.0)
            high = jnp.where(lanes >= LANES - MARGIN, line[:, cols:], 0.0)
            packed = packed + roll(low, MARGIN * row, 1) + roll(high, -MARGIN * row, 1)
        send[base : base + channels] = packed.astype(BF16)
        base += channels


def beside_kernel(numer, first, held, inner, edges):
    height, channels, wide = numer.shape
    cols = wide - LANES
    rows = height - 2 * MARGIN
    blocks = cols // LANES
    edge_rows = held.shape[0]
    base = first.shape[0] - 2 * edge_rows
    lanes = lane_ids((channels, LANES))
    lat = lax.axis_index("lat")
    odd = lax.rem(lat, 2) == 1
    inside = jnp.logical_and(lat > 0, lat < lax.axis_size("lat") - 1)
    packed = jnp.zeros((channels, LANES), F32)
    for row in range(rows):
        at = row % MARGIN
        parts = []
        for block in range(blocks + 1):
            start = (at * blocks + block if block < blocks else MARGIN * blocks) * channels
            near = first[base + start : base + start + channels].astype(F32)
            far = choose(inside, held[start : start + channels].astype(F32), 0.0)
            other = choose(odd, near, far) if row < MARGIN else choose(odd, far, near)
            if block == blocks:
                low = jnp.where(lanes < MARGIN, roll(other, -MARGIN * at, 1), 0.0)
                other = low + jnp.where(lanes >= LANES - MARGIN, roll(other, MARGIN * at, 1), 0.0)
            parts.append(numer[MARGIN + row, :, block * LANES : (block + 1) * LANES] + other)
        inner[row] = jnp.concatenate(parts[:-1], axis=1)
        low = jnp.where(lanes < MARGIN, parts[-1], 0.0)
        high = jnp.where(lanes >= LANES - MARGIN, parts[-1], 0.0)
        packed = packed + roll(low, MARGIN * row, 1) + roll(high, -MARGIN * row, 1)
    edges[...] = packed.astype(BF16)


def fold_kernel(inner, parts, den, blended):
    rows, channels, cols = inner.shape
    lanes = lane_ids((channels, LANES))
    lon, lon_size = lax.axis_index("lon"), lax.axis_size("lon")
    base = parts.shape[1] - channels
    left = parts[lax.rem(lon + lon_size - 1, lon_size), base : base + channels].astype(F32)
    right = parts[lax.rem(lon + 1, lon_size), base : base + channels].astype(F32)
    inverse = 1.0 / den[...]
    lines = []
    for row in range(rows):
        from_left = jnp.where(lanes < MARGIN, roll(left, -MARGIN * row, 1), 0.0)
        from_right = jnp.where(lanes >= LANES - MARGIN, roll(right, MARGIN * row, 1), 0.0)
        beside = [from_left]
        for _ in range(cols // LANES - 2):
            beside.append(jnp.zeros((channels, LANES), F32))
        beside.append(from_right)
        line = inner[row] + jnp.concatenate(beside, axis=1)
        lines.append((line * inverse[row : row + 1])[None])
    blended[...] = jnp.swapaxes(jnp.concatenate(lines, axis=0), 0, 1)


def split_kernel(own, other, grad_in, grad_mid, grad_out):
    taps, channels, width = grad_in.shape
    half = own.shape[0]
    odd = lax.rem(lax.axis_index("lat"), 2) == 1
    own, other = own[...], other[...]
    summed = (choose(odd, other, own), choose(odd, own, other))

    def rows_of(start, count):
        pieces = []
        stop = start + count
        if start < half:
            pieces.append(summed[0][start : min(stop, half)])
        if stop > half:
            pieces.append(summed[1][max(start, half) - half : stop - half])
        return jnp.concatenate(pieces, axis=0).astype(F32) if len(pieces) > 1 else pieces[0].astype(F32)

    for tap in range(taps):
        grad_in[tap] = rows_of(tap * channels, channels)
        grad_mid[tap] = rows_of(taps * channels + tap * width, width)
        grad_out[tap] = rows_of(taps * (channels + width) + tap * channels, channels)


def params():
    return pltpu.CompilerParams(vmem_limit_bytes=VMEM_LIMIT)


def swap(value, axis, first, wrap):
    size = lax.axis_size(axis)
    pairs = []
    for index in range(first, size, 2):
        other = (index + 1) % size
        if other > index or wrap:
            pairs.extend([(index, other), (other, index)])
    return lax.ppermute(value, axis, pairs)


def swap_lat(first, second):
    return swap(first, "lat", 0, False), swap(second, "lat", 1, False)


def swap_lon(edges):
    return swap(edges, "lon", 0, True), swap(edges, "lon", 1, True)


def exchange(value, axis, order):
    pairs = [(index, index ^ order[index % 2]) for index in range(lax.axis_size(axis))]
    return lax.ppermute(value, axis, pairs)


def order_bit(lat, order):
    step = jnp.where(lat % 2 == 0, order[0], order[1])
    return (lat // step) % 2


def halves(value, bit):
    half = value.shape[0] // 2
    own = lax.dynamic_slice_in_dim(value, bit * half, half, 0)
    other = lax.dynamic_slice_in_dim(value, (1 - bit) * half, half, 0)
    return own, other


def ordered(own, other, bit):
    return jnp.concatenate([jnp.where(bit == 0, own, other), jnp.where(bit == 0, other, own)], axis=0)


def shards(
    fields, cotangent, kernel_in, kernel_mid, kernel_out, patch_anchors, blend_weights, tile_counts
):
    channels, rows, cols = fields.shape
    taps, width, _ = kernel_in.shape
    patch_anchors = jnp.transpose(patch_anchors, (0, 1, 3, 2))
    height = rows + 2 * MARGIN
    wide = cols + LANES
    full = rows * cols
    padded = full + 2 * cols
    shape = jax.ShapeDtypeStruct
    center, first, second, canvas = pl.pallas_call(
        pack_kernel,
        out_shape=(
            shape((rows, 2 * channels, cols), BF16),
            shape((MARGIN + 1, 2 * channels, cols), BF16),
            shape((MARGIN + 1, 2 * channels, cols), BF16),
            shape((height, wide), F32),
        ),
        in_specs=[smem(), smem()] + [pl.BlockSpec(memory_space=pltpu.HBM)] * 3,
        out_specs=(vmem(),) * 4,
        scratch_shapes=[
            pltpu.VMEM(fields.shape, BF16),
            pltpu.VMEM(cotangent.shape, BF16),
            pltpu.VMEM(blend_weights.shape, jnp.int32),
            pltpu.VMEM((height, wide), F32),
            pltpu.SemaphoreType.DMA((3,)),
        ],
        compiler_params=params(),
        name="pack",
    )(
        patch_anchors,
        tile_counts,
        *(pltpu.with_memory_space_constraint(value, pltpu.HBM) for value in (fields, cotangent, blend_weights)),
    )
    first, second = swap_lat(first, second)
    w_in = jnp.transpose(kernel_in, (1, 0, 2)).reshape(width, taps * channels)
    kernel_mid = kernel_mid.reshape(3, 3, width, width)
    kernel_out = kernel_out.reshape(3, 3, channels, width)
    w_mid = jnp.transpose(kernel_mid, (1, 2, 0, 3)).reshape(3 * width, 3 * width)
    w_mid_back = jnp.transpose(kernel_mid, (1, 3, 0, 2)).reshape(3 * width, 3 * width)
    w_out = jnp.transpose(kernel_out, (1, 2, 0, 3)).reshape(3 * channels, 3 * width)
    w_out_back = jnp.transpose(kernel_out, (3, 0, 1, 2)).reshape(width, taps * channels)
    first, second, w_in, w_mid, w_mid_back, w_out, w_out_back = lax.optimization_barrier(
        (first, second, w_in, w_mid, w_mid_back, w_out, w_out_back)
    )
    edges, total = pl.pallas_call(
        edge_kernel,
        out_shape=(shape((2 * channels + 2 * height, LANES), BF16), shape((height, wide), F32)),
        in_specs=[vmem()] * 4,
        out_specs=(vmem(),) * 2,
        compiler_params=params(),
        name="edges",
    )(center, first, second, canvas)
    third, fourth = swap_lon(edges)

    lat_size, lon_size = lax.axis_size("lat"), lax.axis_size("lon")
    length = taps * (2 * channels + width)
    unit = 16 * lat_size
    length = (length + unit - 1) // unit * unit
    half = length // 2
    edge_rows = channels * (MARGIN * (cols // LANES) + 1)
    send, keep, numer, den = pl.pallas_call(
        patch_kernel,
        out_shape=(
            shape((half + 2 * edge_rows, LANES), BF16),
            shape((half, LANES), F32),
            shape((height, channels, wide), F32),
            shape((rows, cols), F32),
        ),
        in_specs=[smem(), smem()] + [vmem()] * 12,
        out_specs=(vmem(),) * 4,
        scratch_shapes=[
            pltpu.VMEM((length, LANES), F32),
            pltpu.VMEM((height, 2 * channels, wide), F32),
            pltpu.VMEM((3 * channels, padded), BF16),
            pltpu.VMEM((3 * channels, padded), BF16),
            pltpu.VMEM((width, padded), BF16),
            pltpu.VMEM((3 * width, padded), BF16),
            pltpu.VMEM((width, padded), BF16),
            pltpu.VMEM((width, full), F32),
            pltpu.VMEM((width, full), F32),
            pltpu.VMEM((width, full), BF16),
        ],
        compiler_params=params(),
        name="patches",
    )(
        patch_anchors, tile_counts, center, first, second, third, fourth, total, blend_weights,
        w_in, w_mid, w_mid_back, w_out, w_out_back,
    )

    lat = lax.axis_index("lat")
    even = lat % 2 == 0
    first = exchange(send, "lat", (1, 1))
    mine = keep + first[:half].astype(F32)
    held = first[half + edge_rows :]
    steps = [2 << bit for bit in range(lat_size.bit_length() - 2)]
    orders = list(zip(steps, steps[1:] + steps[:1]))
    for turn, order in enumerate(orders):
        own, other = halves(mine, order_bit(lat, order))
        payload = jnp.concatenate([other.astype(BF16), held], axis=0)
        payload = exchange(payload, "lat", order)
        count = own.shape[0]
        mine = own + payload[:count].astype(F32)
        moves = []
        for side in (0, 1):
            done = [orders[before][side] for before in range(turn)]
            move = jnp.bool_(True)
            for step in steps:
                if step < order[side]:
                    carries = 1 if (step in done) == (side == 1) else 0
                    move = jnp.logical_and(move, (lat // step) % 2 == carries)
            moves.append(move)
        held = jnp.where(jnp.where(even, moves[0], moves[1]), payload[count:], held)
    inner, edges = pl.pallas_call(
        beside_kernel,
        out_shape=(shape((rows, channels, cols), F32), shape((channels, LANES), BF16)),
        in_specs=[vmem()] * 3,
        out_specs=(vmem(),) * 2,
        compiler_params=params(),
        name="beside",
    )(numer, first, held)
    count = mine.shape[0]
    payload = jnp.concatenate([mine.astype(BF16), edges], axis=0)
    payload = jnp.broadcast_to(payload[None], (lon_size,) + payload.shape)
    payload = lax.all_to_all(payload, "lon", 0, 0)
    mine = jnp.sum(payload[:, :count].astype(F32), axis=0).astype(BF16)
    blended = pl.pallas_call(
        fold_kernel,
        out_shape=shape((channels, rows, cols), F32),
        in_specs=[vmem()] * 3,
        out_specs=vmem(),
        compiler_params=params(),
        name="fold",
    )(inner, payload, den)
    for order in reversed(orders):
        mine = ordered(mine, exchange(mine, "lat", order), order_bit(lat, order))
    grad_in, grad_mid, grad_out = pl.pallas_call(
        split_kernel,
        out_shape=(
            shape((taps, channels, width), F32),
            shape((taps, width, width), F32),
            shape((taps, channels, width), F32),
        ),
        in_specs=[vmem()] * 2,
        out_specs=(vmem(),) * 3,
        compiler_params=params(),
        name="split",
    )(mine, exchange(mine, "lat", (1, 1)))
    return blended, jnp.transpose(grad_in, (0, 2, 1)), grad_mid, grad_out


def solution(mesh):
    return jax.shard_map(
        shards,
        mesh=mesh,
        in_specs=(
            P(None, "lat", "lon"),
            P(None, "lat", "lon"),
            P(),
            P(),
            P(),
            P("lat", "lon", None, None),
            P(None, "lat", "lon"),
            P("lat", "lon"),
        ),
        out_specs=(P(None, "lat", "lon"), P(), P(), P()),
        check_vma=False,
    )
```

```python
import functools

import jax
import jax.numpy as jnp
from jax import lax
from jax.experimental import pallas as pl
from jax.experimental.pallas import tpu as pltpu
from jax.sharding import PartitionSpec as P

MARGIN = 4
SLOTS = 4
LANES = 128
F32 = jnp.float32
BF16 = jnp.bfloat16
VMEM_LIMIT = 48 * 1024 * 1024


def vmem():
    return pl.BlockSpec(memory_space=pltpu.VMEM)


def smem():
    return pl.BlockSpec(memory_space=pltpu.SMEM)


def lane_ids(shape):
    return lax.broadcasted_iota(jnp.int32, shape, len(shape) - 1)


def roll(value, shift, axis):
    size = value.shape[axis]
    if isinstance(shift, int):
        shift = shift % size
        if shift == 0:
            return value
    return pltpu.roll(value, shift, axis)


def choose(odd, when_odd, when_even):
    return jnp.where(odd, when_odd, when_even)


def pack_kernel(
    anchors, counts, fields_in, cotangent_in, weights_in, center, first_out, second_out, canvas,
    fields, cotangent, weights, spread, sems,
):
    copies = []
    for index, (source, target) in enumerate(
        ((weights_in, weights), (fields_in, fields), (cotangent_in, cotangent))
    ):
        copy = pltpu.make_async_copy(source, target, sems.at[index])
        copy.start()
        copies.append(copy)
    channels, rows, cols = fields.shape
    wide = cols + LANES
    odd = lax.rem(lax.axis_index("lat"), 2) == 1
    spread[...] = jnp.zeros_like(spread)
    copies[0].wait()
    for slot in range(SLOTS):

        @pl.when(slot < counts[0, 0])
        def _():
            row = anchors[0, 0, 0, slot]
            col = anchors[0, 0, 1, slot]
            values = weights[slot].astype(F32)
            values = jnp.concatenate([values, jnp.zeros((rows, LANES), F32)], axis=1)
            values = jnp.concatenate([values, jnp.zeros((2 * MARGIN, wide), F32)], axis=0)
            values = roll(values, lax.rem(col + (wide - MARGIN), wide), 1)
            values = roll(values, row, 0)
            spread[...] += values

    total = spread[...]
    canvas[...] = total
    copies[1].wait()
    copies[2].wait()
    both = []
    for source in (fields, cotangent):
        both.append(jnp.swapaxes(source[...].astype(F32), 0, 1))
    tile = jnp.concatenate(both, axis=1).astype(BF16)
    center[...] = tile
    half = total.shape[0] // 2
    pad = jnp.zeros((2 * channels - 2 * half, cols), F32)
    extras = []
    for part in (total[:half], total[half:]):
        beside = jnp.concatenate([part[:, cols:], jnp.zeros((half, cols - LANES), F32)], axis=1)
        extras.append(jnp.concatenate([part[:, :cols], beside, pad], axis=0).astype(BF16))
    top, bottom = tile[:MARGIN], tile[rows - MARGIN :]
    first_out[0:MARGIN] = choose(odd, top, bottom)
    first_out[MARGIN] = choose(odd, extras[0], extras[1])
    second_out[0:MARGIN] = choose(odd, bottom, top)
    second_out[MARGIN] = choose(odd, extras[1], extras[0])


def edge_kernel(center, first, second, canvas, edges, total_out):
    rows = center.shape[0]
    channels = center.shape[1] // 2
    cols = center.shape[2]
    height = rows + 2 * MARGIN
    half = height // 2
    odd = lax.rem(lax.axis_index("lat"), 2) == 1

    def stretch(block):
        block = block.astype(F32)
        return jnp.concatenate([block[:half], block[half:height, :LANES]], axis=1)

    upper = stretch(choose(odd, first[MARGIN], second[MARGIN]))
    lower = stretch(choose(odd, second[MARGIN], first[MARGIN]))
    total = canvas[...] + jnp.concatenate([upper, lower], axis=0)
    total_out[...] = total
    lanes = lane_ids((2 * channels, LANES))
    packed = jnp.zeros((2 * channels, LANES), F32)
    for row in range(height):
        if row < MARGIN:
            line = choose(odd, first[row], second[row])
        elif row < MARGIN + rows:
            line = center[row - MARGIN]
        else:
            line = choose(odd, second[row - MARGIN - rows], first[row - MARGIN - rows])
        line = line.astype(F32)
        low = jnp.where(lanes < MARGIN, line[:, :LANES], 0.0)
        high = jnp.where(lanes >= LANES - MARGIN, line[:, cols - LANES :], 0.0)
        packed = packed + roll(low, MARGIN * row, 1) + roll(high, -MARGIN * row, 1)
    edges[0 : 2 * channels] = packed.astype(BF16)
    margin = total[:, cols:]
    lanes = lane_ids(margin.shape)
    to_left = jnp.where(lanes < LANES // 2, total[:, :LANES], margin)
    to_right = jnp.where(lanes < LANES // 2, margin, total[:, cols - LANES : cols])
    edges[2 * channels : 2 * channels + height] = to_left.astype(BF16)
    edges[2 * channels + height : 2 * channels + 2 * height] = to_right.astype(BF16)


def dot(left, right):
    return jnp.dot(left, right, preferred_element_type=F32)


def dot_lanes(left, right):
    return lax.dot_general(left, right, (((1,), (1,)), ((), ())), preferred_element_type=F32)


def patch_kernel(
    anchors, counts, center, first, second, third, fourth, total_in, weights,
    w_in, w_mid, w_mid_back, w_out, w_out_back,
    send, keep, numer, den_out,
    grads, window, x_s, d_s, h_s, z_s, h2_s, slope_s, dh_s, dz_s,
):
    rows = center.shape[0]
    channels = center.shape[1] // 2
    cols = center.shape[2]
    wide = cols + LANES
    width = w_in.shape[0]
    full = rows * cols
    height = rows + 2 * MARGIN
    lanes = lane_ids((2 * channels, LANES))
    lat_odd = lax.rem(lax.axis_index("lat"), 2) == 1
    lon_odd = lax.rem(lax.axis_index("lon"), 2) == 1

    left = choose(lon_odd, third[...], fourth[...]).astype(F32)
    right = choose(lon_odd, fourth[...], third[...]).astype(F32)
    base = 2 * channels
    left_part = left[base + height : base + 2 * height]
    right_part = right[base : base + height]
    edge_lanes = lane_ids((height, LANES))
    low = edge_lanes < MARGIN
    high = edge_lanes >= LANES - MARGIN
    zero = jnp.zeros((height, LANES), F32)
    pieces = [jnp.where(low, left_part, zero)]
    for _ in range(cols // LANES - 2):
        pieces.append(zero)
    pieces.append(jnp.where(high, right_part, zero))
    pieces.append(jnp.where(high, left_part, zero) + jnp.where(low, right_part, zero))
    den = jnp.maximum(total_in[...] + jnp.concatenate(pieces, axis=1), 1.0)
    den_out[...] = den[MARGIN : MARGIN + rows, :cols]
    inverse = 1.0 / den

    left = left[:base]
    right = right[:base]
    for row in range(height):
        if row < MARGIN:
            body = choose(lat_odd, first[row], second[row])
        elif row < MARGIN + rows:
            body = center[row - MARGIN]
        else:
            body = choose(lat_odd, second[row - MARGIN - rows], first[row - MARGIN - rows])
        beside = jnp.where(
            lanes < LANES // 2, roll(right, -MARGIN * row, 1), roll(left, MARGIN * row, 1)
        )
        line = jnp.concatenate([body.astype(F32), beside], axis=1)
        scaled = line[channels:] * inverse[row : row + 1]
        window[row, 0:channels] = line[:channels]
        window[row, channels : 2 * channels] = scaled.astype(BF16).astype(F32)

    numer[...] = jnp.zeros_like(numer)
    grads[...] = jnp.zeros_like(grads)
    for ref in (x_s, d_s, h_s, z_s, h2_s):
        ref[:, 0:cols] = jnp.zeros((ref.shape[0], cols), BF16)
        ref[:, cols + full : 2 * cols + full] = jnp.zeros((ref.shape[0], cols), BF16)

    def shifted(value, step):
        blocks = [value[:, at : at + LANES] for at in range(0, cols, LANES)]
        turned = [roll(block, step, 1) for block in blocks]
        ids = lane_ids(blocks[0].shape)
        zero = jnp.zeros_like(blocks[0])
        if step > 0:
            ends = [zero] + turned[:-1]
            at_end = ids == 0
        else:
            ends = turned[1:] + [zero]
            at_end = ids == LANES - 1
        return jnp.concatenate([jnp.where(at_end, end, own) for end, own in zip(ends, turned)], axis=1)

    def before(value):
        return shifted(value, 1)

    def after(value):
        return shifted(value, -1)

    def spread(ref, value, row, flip):
        count = value.shape[0]
        at = slice((row + 1) * cols, (row + 2) * cols)
        first, last = before(value), after(value)
        if flip:
            first, last = last, first
        ref[0:count, at] = first
        ref[count : 2 * count, at] = value
        ref[2 * count : 3 * count, at] = last

    def stack(ref, row, flip):
        starts = [(row + (2 - tap if flip else tap)) * cols for tap in range(3)]
        return jnp.concatenate([ref[:, start : start + cols] for start in starts], axis=0)

    def across(parts, flip):
        count = parts.shape[0] // 3
        first, last = parts[:count], parts[2 * count :]
        if flip:
            first, last = last, first
        return before(first) + parts[count : 2 * count] + after(last)

    def all_rows(ref, flip):
        starts = [(2 - tap if flip else tap) * cols for tap in range(3)]
        return jnp.concatenate([ref[:, start : start + full] for start in starts], axis=0)

    def one_patch(slot, carry):
        row0 = anchors[0, 0, 0, slot]
        col0 = anchors[0, 0, 1, slot]
        patch_weights = weights[slot].astype(F32)
        back_shift = lax.rem(wide + MARGIN - col0, wide)
        for row in range(rows):
            line = roll(window[row0 + row], back_shift, 1)[:, :cols]
            spread(x_s, line[:channels].astype(BF16), row, False)
            grad = line[channels:] * patch_weights[row : row + 1]
            spread(d_s, grad.astype(BF16), row, True)
        for row in range(rows):
            at = slice(row * cols, (row + 1) * cols)
            z1 = dot(w_in[...], stack(x_s, row, False))
            sig = 0.5 * jnp.tanh(0.5 * z1) + 0.5
            h1 = z1 * sig
            slope_s[:, at] = sig + h1 * (1.0 - sig)
            h_s[:, (row + 1) * cols : (row + 2) * cols] = h1.astype(BF16)
        for row in range(rows):
            at = slice(row * cols, (row + 1) * cols)
            ahead = slice((row + 1) * cols, (row + 2) * cols)
            dh2 = dot(w_out_back[...], stack(d_s, row, True))
            z2 = across(dot(w_mid[...], stack(h_s, row, False)), False)
            sig = 0.5 * jnp.tanh(0.5 * z2) + 0.5
            added = z2 * sig
            h2_s[:, ahead] = (h_s[:, ahead].astype(F32) + added).astype(BF16)
            dz2 = (dh2 * (sig + added * (1.0 - sig))).astype(BF16)
            dh_s[:, at] = dh2
            spread(z_s, dz2, row, True)
        for row in range(rows):
            at = slice(row * cols, (row + 1) * cols)
            back = dot(w_mid_back[...], stack(z_s, row, True))
            dz_s[:, at] = ((dh_s[:, at] + back) * slope_s[:, at]).astype(BF16)
        for row in range(rows):
            result = across(dot(w_out[...], stack(h2_s, row, False)), False)
            result = result * patch_weights[row : row + 1]
            result = jnp.concatenate([result, jnp.zeros((channels, LANES), F32)], axis=1)
            numer[row0 + row] += roll(result, lax.rem(col0 + (wide - MARGIN), wide), 1)
        inside = slice(cols, cols + full)
        small = 9 * channels
        part = dot_lanes(z_s[:, inside], all_rows(h_s, False))
        for tap in range(3):
            for tap_col in range(3):
                start = small + (3 * tap + tap_col) * width
                grads[start : start + width] += part[
                    tap_col * width : (tap_col + 1) * width, tap * width : (tap + 1) * width
                ]
        grads[0:small] += dot_lanes(all_rows(x_s, False), dz_s[...])
        start = small + 9 * width
        grads[start : start + small] += dot_lanes(all_rows(d_s, True), h2_s[:, inside])
        return carry

    lax.fori_loop(0, counts[0, 0], one_patch, 0)

    half = grads.shape[0] // 2
    odd_index = lax.rem(lax.axis_index("lat"), 2)
    send[0:half] = grads[pl.ds(pl.multiple_of((1 - odd_index) * half, half), half)].astype(BF16)
    keep[...] = grads[pl.ds(pl.multiple_of(odd_index * half, half), half)]
    lanes = lane_ids((channels, LANES))
    blocks = cols // LANES
    base = half
    upper = [numer[row] for row in range(MARGIN)]
    lower = [numer[MARGIN + rows + row] for row in range(MARGIN)]
    for when_odd, when_even in ((upper, lower), (lower, upper)):
        packed = jnp.zeros((channels, LANES), F32)
        for row in range(MARGIN):
            line = choose(lat_odd, when_odd[row], when_even[row])
            for block in range(blocks):
                send[base : base + channels] = line[:, block * LANES : (block + 1) * LANES].astype(BF16)
                base += channels
            low = jnp.where(lanes < MARGIN, line[:, cols:], 0.0)
            high = jnp.where(lanes >= LANES - MARGIN, line[:, cols:], 0.0)
            packed = packed + roll(low, MARGIN * row, 1) + roll(high, -MARGIN * row, 1)
        send[base : base + channels] = packed.astype(BF16)
        base += channels


def beside_kernel(numer, first, held, inner, edges):
    height, channels, wide = numer.shape
    cols = wide - LANES
    rows = height - 2 * MARGIN
    blocks = cols // LANES
    edge_rows = held.shape[0]
    base = first.shape[0] - 2 * edge_rows
    lanes = lane_ids((channels, LANES))
    lat = lax.axis_index("lat")
    odd = lax.rem(lat, 2) == 1
    inside = jnp.logical_and(lat > 0, lat < lax.axis_size("lat") - 1)
    packed = jnp.zeros((channels, LANES), F32)
    for row in range(rows):
        at = row % MARGIN
        parts = []
        for block in range(blocks + 1):
            start = (at * blocks + block if block < blocks else MARGIN * blocks) * channels
            near = first[base + start : base + start + channels].astype(F32)
            far = choose(inside, held[start : start + channels].astype(F32), 0.0)
            other = choose(odd, near, far) if row < MARGIN else choose(odd, far, near)
            if block == blocks:
                low = jnp.where(lanes < MARGIN, roll(other, -MARGIN * at, 1), 0.0)
                other = low + jnp.where(lanes >= LANES - MARGIN, roll(other, MARGIN * at, 1), 0.0)
            parts.append(numer[MARGIN + row, :, block * LANES : (block + 1) * LANES] + other)
        inner[row] = jnp.concatenate(parts[:-1], axis=1)
        low = jnp.where(lanes < MARGIN, parts[-1], 0.0)
        high = jnp.where(lanes >= LANES - MARGIN, parts[-1], 0.0)
        packed = packed + roll(low, MARGIN * row, 1) + roll(high, -MARGIN * row, 1)
    edges[...] = packed.astype(BF16)


def fold_kernel(inner, parts, den, blended):
    rows, channels, cols = inner.shape
    lanes = lane_ids((channels, LANES))
    lon, lon_size = lax.axis_index("lon"), lax.axis_size("lon")
    base = parts.shape[1] - channels
    left = parts[lax.rem(lon + lon_size - 1, lon_size), base : base + channels].astype(F32)
    right = parts[lax.rem(lon + 1, lon_size), base : base + channels].astype(F32)
    inverse = 1.0 / den[...]
    lines = []
    for row in range(rows):
        from_left = jnp.where(lanes < MARGIN, roll(left, -MARGIN * row, 1), 0.0)
        from_right = jnp.where(lanes >= LANES - MARGIN, roll(right, MARGIN * row, 1), 0.0)
        beside = [from_left]
        for _ in range(cols // LANES - 2):
            beside.append(jnp.zeros((channels, LANES), F32))
        beside.append(from_right)
        line = inner[row] + jnp.concatenate(beside, axis=1)
        lines.append((line * inverse[row : row + 1])[None])
    blended[...] = jnp.swapaxes(jnp.concatenate(lines, axis=0), 0, 1)


def split_kernel(own, other, grad_in, grad_mid, grad_out):
    taps, channels, width = grad_in.shape
    half = own.shape[0]
    odd = lax.rem(lax.axis_index("lat"), 2) == 1
    own, other = own[...], other[...]
    summed = (choose(odd, other, own), choose(odd, own, other))

    def rows_of(start, count):
        pieces = []
        stop = start + count
        if start < half:
            pieces.append(summed[0][start : min(stop, half)])
        if stop > half:
            pieces.append(summed[1][max(start, half) - half : stop - half])
        return jnp.concatenate(pieces, axis=0).astype(F32) if len(pieces) > 1 else pieces[0].astype(F32)

    for tap in range(taps):
        grad_in[tap] = rows_of(tap * channels, channels)
        grad_mid[tap] = rows_of(taps * channels + tap * width, width)
        grad_out[tap] = rows_of(taps * (channels + width) + tap * channels, channels)


def params():
    return pltpu.CompilerParams(vmem_limit_bytes=VMEM_LIMIT)


def swap(value, axis, first, wrap):
    size = lax.axis_size(axis)
    pairs = []
    for index in range(first, size, 2):
        other = (index + 1) % size
        if other > index or wrap:
            pairs.extend([(index, other), (other, index)])
    return lax.ppermute(value, axis, pairs)


def swap_lat(first, second):
    return swap(first, "lat", 0, False), swap(second, "lat", 1, False)


def swap_lon(edges):
    return swap(edges, "lon", 0, True), swap(edges, "lon", 1, True)


def exchange(value, axis, order):
    pairs = [(index, index ^ order[index % 2]) for index in range(lax.axis_size(axis))]
    return lax.ppermute(value, axis, pairs)


def order_bit(lat, order):
    step = jnp.where(lat % 2 == 0, order[0], order[1])
    return (lat // step) % 2


def halves(value, bit):
    half = value.shape[0] // 2
    own = lax.dynamic_slice_in_dim(value, bit * half, half, 0)
    other = lax.dynamic_slice_in_dim(value, (1 - bit) * half, half, 0)
    return own, other


def ordered(own, other, bit):
    return jnp.concatenate([jnp.where(bit == 0, own, other), jnp.where(bit == 0, other, own)], axis=0)


def shards(
    fields, cotangent, kernel_in, kernel_mid, kernel_out, patch_anchors, blend_weights, tile_counts
):
    channels, rows, cols = fields.shape
    taps, width, _ = kernel_in.shape
    patch_anchors = jnp.transpose(patch_anchors, (0, 1, 3, 2))
    height = rows + 2 * MARGIN
    wide = cols + LANES
    full = rows * cols
    padded = full + 2 * cols
    shape = jax.ShapeDtypeStruct
    center, first, second, canvas = pl.pallas_call(
        pack_kernel,
        out_shape=(
            shape((rows, 2 * channels, cols), BF16),
            shape((MARGIN + 1, 2 * channels, cols), BF16),
            shape((MARGIN + 1, 2 * channels, cols), BF16),
            shape((height, wide), F32),
        ),
        in_specs=[smem(), smem()] + [pl.BlockSpec(memory_space=pltpu.HBM)] * 3,
        out_specs=(vmem(),) * 4,
        scratch_shapes=[
            pltpu.VMEM(fields.shape, BF16),
            pltpu.VMEM(cotangent.shape, BF16),
            pltpu.VMEM(blend_weights.shape, jnp.int32),
            pltpu.VMEM((height, wide), F32),
            pltpu.SemaphoreType.DMA((3,)),
        ],
        compiler_params=params(),
        name="pack",
    )(
        patch_anchors,
        tile_counts,
        *(pltpu.with_memory_space_constraint(value, pltpu.HBM) for value in (fields, cotangent, blend_weights)),
    )
    first, second = swap_lat(first, second)
    w_in = jnp.transpose(kernel_in, (1, 0, 2)).reshape(width, taps * channels)
    kernel_mid = kernel_mid.reshape(3, 3, width, width)
    kernel_out = kernel_out.reshape(3, 3, channels, width)
    w_mid = jnp.transpose(kernel_mid, (1, 2, 0, 3)).reshape(3 * width, 3 * width)
    w_mid_back = jnp.transpose(kernel_mid, (3, 0, 1, 2)).reshape(width, taps * width)
    w_out = jnp.transpose(kernel_out, (1, 2, 0, 3)).reshape(3 * channels, 3 * width)
    w_out_back = jnp.transpose(kernel_out, (3, 0, 1, 2)).reshape(width, taps * channels)
    first, second, w_in, w_mid, w_mid_back, w_out, w_out_back = lax.optimization_barrier(
        (first, second, w_in, w_mid, w_mid_back, w_out, w_out_back)
    )
    edges, total = pl.pallas_call(
        edge_kernel,
        out_shape=(shape((2 * channels + 2 * height, LANES), BF16), shape((height, wide), F32)),
        in_specs=[vmem()] * 4,
        out_specs=(vmem(),) * 2,
        compiler_params=params(),
        name="edges",
    )(center, first, second, canvas)
    third, fourth = swap_lon(edges)

    lat_size, lon_size = lax.axis_size("lat"), lax.axis_size("lon")
    length = taps * (2 * channels + width)
    unit = 16 * lat_size
    length = (length + unit - 1) // unit * unit
    half = length // 2
    edge_rows = channels * (MARGIN * (cols // LANES) + 1)
    send, keep, numer, den = pl.pallas_call(
        patch_kernel,
        out_shape=(
            shape((half + 2 * edge_rows, LANES), BF16),
            shape((half, LANES), F32),
            shape((height, channels, wide), F32),
            shape((rows, cols), F32),
        ),
        in_specs=[smem(), smem()] + [vmem()] * 12,
        out_specs=(vmem(),) * 4,
        scratch_shapes=[
            pltpu.VMEM((length, LANES), F32),
            pltpu.VMEM((height, 2 * channels, wide), F32),
            pltpu.VMEM((3 * channels, padded), BF16),
            pltpu.VMEM((3 * channels, padded), BF16),
            pltpu.VMEM((width, padded), BF16),
            pltpu.VMEM((3 * width, padded), BF16),
            pltpu.VMEM((width, padded), BF16),
            pltpu.VMEM((width, full), F32),
            pltpu.VMEM((width, full), F32),
            pltpu.VMEM((width, full), BF16),
        ],
        compiler_params=params(),
        name="patches",
    )(
        patch_anchors, tile_counts, center, first, second, third, fourth, total, blend_weights,
        w_in, w_mid, w_mid_back, w_out, w_out_back,
    )

    lat = lax.axis_index("lat")
    even = lat % 2 == 0
    first = exchange(send, "lat", (1, 1))
    mine = keep + first[:half].astype(F32)
    held = first[half + edge_rows :]
    steps = [2 << bit for bit in range(lat_size.bit_length() - 2)]
    orders = list(zip(steps, steps[1:] + steps[:1]))
    for turn, order in enumerate(orders):
        own, other = halves(mine, order_bit(lat, order))
        payload = jnp.concatenate([other.astype(BF16), held], axis=0)
        payload = exchange(payload, "lat", order)
        count = own.shape[0]
        mine = own + payload[:count].astype(F32)
        moves = []
        for side in (0, 1):
            done = [orders[before][side] for before in range(turn)]
            move = jnp.bool_(True)
            for step in steps:
                if step < order[side]:
                    carries = 1 if (step in done) == (side == 1) else 0
                    move = jnp.logical_and(move, (lat // step) % 2 == carries)
            moves.append(move)
        held = jnp.where(jnp.where(even, moves[0], moves[1]), payload[count:], held)
    inner, edges = pl.pallas_call(
        beside_kernel,
        out_shape=(shape((rows, channels, cols), F32), shape((channels, LANES), BF16)),
        in_specs=[vmem()] * 3,
        out_specs=(vmem(),) * 2,
        compiler_params=params(),
        name="beside",
    )(numer, first, held)
    count = mine.shape[0]
    payload = jnp.concatenate([mine.astype(BF16), edges], axis=0)
    payload = lax.all_gather(payload, "lon")
    mine = jnp.sum(payload[:, :count].astype(F32), axis=0).astype(BF16)
    blended = pl.pallas_call(
        fold_kernel,
        out_shape=shape((channels, rows, cols), F32),
        in_specs=[vmem()] * 3,
        out_specs=vmem(),
        compiler_params=params(),
        name="fold",
    )(inner, payload, den)
    for order in reversed(orders):
        mine = ordered(mine, exchange(mine, "lat", order), order_bit(lat, order))
    grad_in, grad_mid, grad_out = pl.pallas_call(
        split_kernel,
        out_shape=(
            shape((taps, channels, width), F32),
            shape((taps, width, width), F32),
            shape((taps, channels, width), F32),
        ),
        in_specs=[vmem()] * 2,
        out_specs=(vmem(),) * 3,
        compiler_params=params(),
        name="split",
    )(mine, exchange(mine, "lat", (1, 1)))
    return blended, jnp.transpose(grad_in, (0, 2, 1)), grad_mid, grad_out


def solution(mesh):
    return jax.shard_map(
        shards,
        mesh=mesh,
        in_specs=(
            P(None, "lat", "lon"),
            P(None, "lat", "lon"),
            P(),
            P(),
            P(),
            P("lat", "lon", None, None),
            P(None, "lat", "lon"),
            P("lat", "lon"),
        ),
        out_specs=(P(None, "lat", "lon"), P(), P(), P()),
        check_vma=False,
    )
```

```python
import functools

import jax
import jax.numpy as jnp
from jax import lax
from jax.experimental import pallas as pl
from jax.experimental.pallas import tpu as pltpu
from jax.sharding import PartitionSpec as P

MARGIN = 4
SLOTS = 4
LANES = 128
F32 = jnp.float32
BF16 = jnp.bfloat16
VMEM_LIMIT = 48 * 1024 * 1024


def vmem():
    return pl.BlockSpec(memory_space=pltpu.VMEM)


def smem():
    return pl.BlockSpec(memory_space=pltpu.SMEM)


def lane_ids(shape):
    return lax.broadcasted_iota(jnp.int32, shape, len(shape) - 1)


def roll(value, shift, axis):
    size = value.shape[axis]
    if isinstance(shift, int):
        shift = shift % size
        if shift == 0:
            return value
    return pltpu.roll(value, shift, axis)


def choose(odd, when_odd, when_even):
    return jnp.where(odd, when_odd, when_even)


def pack_kernel(
    counts, anchors_in, fields_in, cotangent_in, weights_in, center, first_out, second_out, canvas,
    fields, cotangent, weights, anchors, spread, sems,
):
    copies = []
    for index, (source, target) in enumerate(
        ((weights_in, weights), (fields_in, fields), (cotangent_in, cotangent), (anchors_in, anchors))
    ):
        copy = pltpu.make_async_copy(source, target, sems.at[index])
        copy.start()
        copies.append(copy)
    channels, rows, cols = fields.shape
    wide = cols + LANES
    odd = lax.rem(lax.axis_index("lat"), 2) == 1
    spread[...] = jnp.zeros_like(spread)
    copies[0].wait()
    copies[3].wait()
    for slot in range(SLOTS):

        @pl.when(slot < counts[0, 0])
        def _():
            row = anchors[0, 0, 0, slot]
            col = anchors[0, 0, 1, slot]
            values = weights[slot].astype(F32)
            values = jnp.concatenate([values, jnp.zeros((rows, LANES), F32)], axis=1)
            values = jnp.concatenate([values, jnp.zeros((2 * MARGIN, wide), F32)], axis=0)
            values = roll(values, lax.rem(col + (wide - MARGIN), wide), 1)
            values = roll(values, row, 0)
            spread[...] += values

    total = spread[...]
    canvas[...] = total
    copies[1].wait()
    copies[2].wait()
    both = []
    for source in (fields, cotangent):
        both.append(jnp.swapaxes(source[...].astype(F32), 0, 1))
    tile = jnp.concatenate(both, axis=1).astype(BF16)
    center[...] = tile
    half = total.shape[0] // 2
    pad = jnp.zeros((2 * channels - 2 * half, cols), F32)
    extras = []
    for part in (total[:half], total[half:]):
        beside = jnp.concatenate([part[:, cols:], jnp.zeros((half, cols - LANES), F32)], axis=1)
        extras.append(jnp.concatenate([part[:, :cols], beside, pad], axis=0).astype(BF16))
    top, bottom = tile[:MARGIN], tile[rows - MARGIN :]
    first_out[0:MARGIN] = choose(odd, top, bottom)
    first_out[MARGIN] = choose(odd, extras[0], extras[1])
    second_out[0:MARGIN] = choose(odd, bottom, top)
    second_out[MARGIN] = choose(odd, extras[1], extras[0])


def edge_kernel(center, first, second, canvas, edges, total_out):
    rows = center.shape[0]
    channels = center.shape[1] // 2
    cols = center.shape[2]
    height = rows + 2 * MARGIN
    half = height // 2
    odd = lax.rem(lax.axis_index("lat"), 2) == 1

    def stretch(block):
        block = block.astype(F32)
        return jnp.concatenate([block[:half], block[half:height, :LANES]], axis=1)

    upper = stretch(choose(odd, first[MARGIN], second[MARGIN]))
    lower = stretch(choose(odd, second[MARGIN], first[MARGIN]))
    total = canvas[...] + jnp.concatenate([upper, lower], axis=0)
    total_out[...] = total
    lanes = lane_ids((2 * channels, LANES))
    packed = jnp.zeros((2 * channels, LANES), F32)
    for row in range(height):
        if row < MARGIN:
            line = choose(odd, first[row], second[row])
        elif row < MARGIN + rows:
            line = center[row - MARGIN]
        else:
            line = choose(odd, second[row - MARGIN - rows], first[row - MARGIN - rows])
        line = line.astype(F32)
        low = jnp.where(lanes < MARGIN, line[:, :LANES], 0.0)
        high = jnp.where(lanes >= LANES - MARGIN, line[:, cols - LANES :], 0.0)
        packed = packed + roll(low, MARGIN * row, 1) + roll(high, -MARGIN * row, 1)
    edges[0 : 2 * channels] = packed.astype(BF16)
    margin = total[:, cols:]
    lanes = lane_ids(margin.shape)
    to_left = jnp.where(lanes < LANES // 2, total[:, :LANES], margin)
    to_right = jnp.where(lanes < LANES // 2, margin, total[:, cols - LANES : cols])
    edges[2 * channels : 2 * channels + height] = to_left.astype(BF16)
    edges[2 * channels + height : 2 * channels + 2 * height] = to_right.astype(BF16)


def dot(left, right):
    return jnp.dot(left, right, preferred_element_type=F32)


def dot_lanes(left, right):
    return lax.dot_general(left, right, (((1,), (1,)), ((), ())), preferred_element_type=F32)


def patch_kernel(
    anchors, counts, center, first, second, third, fourth, total_in, weights,
    w_in, w_mid, w_mid_back, w_out, w_out_back,
    send, keep, numer, den_out,
    grads, window, *sets,
):
    rows = center.shape[0]
    channels = center.shape[1] // 2
    cols = center.shape[2]
    wide = cols + LANES
    width = w_in.shape[0]
    full = rows * cols
    height = rows + 2 * MARGIN
    lanes = lane_ids((2 * channels, LANES))
    lat_odd = lax.rem(lax.axis_index("lat"), 2) == 1
    lon_odd = lax.rem(lax.axis_index("lon"), 2) == 1

    left = choose(lon_odd, third[...], fourth[...]).astype(F32)
    right = choose(lon_odd, fourth[...], third[...]).astype(F32)
    base = 2 * channels
    left_part = left[base + height : base + 2 * height]
    right_part = right[base : base + height]
    edge_lanes = lane_ids((height, LANES))
    low = edge_lanes < MARGIN
    high = edge_lanes >= LANES - MARGIN
    zero = jnp.zeros((height, LANES), F32)
    pieces = [jnp.where(low, left_part, zero)]
    for _ in range(cols // LANES - 2):
        pieces.append(zero)
    pieces.append(jnp.where(high, right_part, zero))
    pieces.append(jnp.where(high, left_part, zero) + jnp.where(low, right_part, zero))
    den = jnp.maximum(total_in[...] + jnp.concatenate(pieces, axis=1), 1.0)
    den_out[...] = den[MARGIN : MARGIN + rows, :cols]
    inverse = 1.0 / den

    left = left[:base]
    right = right[:base]
    for row in range(height):
        if row < MARGIN:
            body = choose(lat_odd, first[row], second[row])
        elif row < MARGIN + rows:
            body = center[row - MARGIN]
        else:
            body = choose(lat_odd, second[row - MARGIN - rows], first[row - MARGIN - rows])
        beside = jnp.where(
            lanes < LANES // 2, roll(right, -MARGIN * row, 1), roll(left, MARGIN * row, 1)
        )
        line = jnp.concatenate([body.astype(F32), beside], axis=1)
        scaled = line[channels:] * inverse[row : row + 1]
        window[row, 0:channels] = line[:channels]
        window[row, channels : 2 * channels] = scaled.astype(BF16).astype(F32)

    numer[...] = jnp.zeros_like(numer)
    grads[...] = jnp.zeros_like(grads)
    sets = (sets[: len(sets) // 2], sets[len(sets) // 2 :])
    for ref in sets[0][:5] + sets[1][:5]:
        ref[:, 0:cols] = jnp.zeros((ref.shape[0], cols), BF16)
        ref[:, cols + full : 2 * cols + full] = jnp.zeros((ref.shape[0], cols), BF16)

    def shifted(value, step):
        blocks = [value[:, at : at + LANES] for at in range(0, cols, LANES)]
        turned = [roll(block, step, 1) for block in blocks]
        ids = lane_ids(blocks[0].shape)
        zero = jnp.zeros_like(blocks[0])
        if step > 0:
            ends = [zero] + turned[:-1]
            at_end = ids == 0
        else:
            ends = turned[1:] + [zero]
            at_end = ids == LANES - 1
        return jnp.concatenate([jnp.where(at_end, end, own) for end, own in zip(ends, turned)], axis=1)

    def before(value):
        return shifted(value, 1)

    def after(value):
        return shifted(value, -1)

    def spread(ref, value, row, flip):
        count = value.shape[0]
        at = slice((row + 1) * cols, (row + 2) * cols)
        first, last = before(value), after(value)
        if flip:
            first, last = last, first
        ref[0:count, at] = first
        ref[count : 2 * count, at] = value
        ref[2 * count : 3 * count, at] = last

    def stack(ref, row, flip):
        starts = [(row + (2 - tap if flip else tap)) * cols for tap in range(3)]
        return jnp.concatenate([ref[:, start : start + cols] for start in starts], axis=0)

    def across(parts, flip):
        count = parts.shape[0] // 3
        first, last = parts[:count], parts[2 * count :]
        if flip:
            first, last = last, first
        return before(first) + parts[count : 2 * count] + after(last)

    def all_rows(ref, flip):
        starts = [(2 - tap if flip else tap) * cols for tap in range(3)]
        return jnp.concatenate([ref[:, start : start + full] for start in starts], axis=0)

    def weights_of(slot):
        return weights[slot].astype(F32) * (slot < counts[0, 0]).astype(F32)

    def first_part(slot, x_s, d_s, h_s, z_s, h2_s, slope_s, dh_s, dz_s):
        row0 = anchors[0, 0, 0, slot]
        col0 = anchors[0, 0, 1, slot]
        patch_weights = weights_of(slot)
        back_shift = lax.rem(wide + MARGIN - col0, wide)

        def cut(row):
            line = roll(window[row0 + row], back_shift, 1)[:, :cols]
            spread(x_s, line[:channels].astype(BF16), row, False)
            grad = line[channels:] * patch_weights[row : row + 1]
            spread(d_s, grad.astype(BF16), row, True)

        def conv_in(row):
            at = slice(row * cols, (row + 1) * cols)
            z1 = dot(w_in[...], stack(x_s, row, False))
            sig = 0.5 * jnp.tanh(0.5 * z1) + 0.5
            h1 = z1 * sig
            slope_s[:, at] = sig + h1 * (1.0 - sig)
            h_s[:, (row + 1) * cols : (row + 2) * cols] = h1.astype(BF16)

        def conv_mid(row):
            at = slice(row * cols, (row + 1) * cols)
            ahead = slice((row + 1) * cols, (row + 2) * cols)
            dh2 = dot(w_out_back[...], stack(d_s, row, True))
            z2 = across(dot(w_mid[...], stack(h_s, row, False)), False)
            sig = 0.5 * jnp.tanh(0.5 * z2) + 0.5
            added = z2 * sig
            h2_s[:, ahead] = (h_s[:, ahead].astype(F32) + added).astype(BF16)
            dz2 = (dh2 * (sig + added * (1.0 - sig))).astype(BF16)
            dh_s[:, at] = dh2
            spread(z_s, dz2, row, True)

        return [functools.partial(step, row) for step in (cut, conv_in, conv_mid) for row in range(rows)]

    def second_part(slot, x_s, d_s, h_s, z_s, h2_s, slope_s, dh_s, dz_s):
        row0 = anchors[0, 0, 0, slot]
        col0 = anchors[0, 0, 1, slot]
        patch_weights = weights_of(slot)
        inside = slice(cols, cols + full)
        small = 9 * channels

        def conv_back(row):
            at = slice(row * cols, (row + 1) * cols)
            back = dot(w_mid_back[...], stack(z_s, row, True))
            dz_s[:, at] = ((dh_s[:, at] + back) * slope_s[:, at]).astype(BF16)

        def conv_out(row):
            result = across(dot(w_out[...], stack(h2_s, row, False)), False)
            result = result * patch_weights[row : row + 1]
            result = jnp.concatenate([result, jnp.zeros((channels, LANES), F32)], axis=1)
            numer[row0 + row] += roll(result, lax.rem(col0 + (wide - MARGIN), wide), 1)

        def grad_mid():
            part = dot_lanes(z_s[:, inside], all_rows(h_s, False))
            for tap in range(3):
                for tap_col in range(3):
                    start = small + (3 * tap + tap_col) * width
                    grads[start : start + width] += part[
                        tap_col * width : (tap_col + 1) * width, tap * width : (tap + 1) * width
                    ]

        def grad_out():
            start = small + 9 * width
            grads[start : start + small] += dot_lanes(all_rows(d_s, True), h2_s[:, inside])

        def grad_in():
            grads[0:small] += dot_lanes(all_rows(x_s, False), dz_s[...])

        backs = [functools.partial(conv_back, row) for row in range(rows)]
        outs = [functools.partial(conv_out, row) for row in range(rows)]
        return [grad_mid, grad_out] + backs + [grad_in] + outs

    def merged(left, right):
        left = [((at + 0.5) / len(left), step) for at, step in enumerate(left)]
        right = [((at + 0.5) / len(right), step) for at, step in enumerate(right)]
        for _, step in sorted(left + right, key=lambda pair: pair[0]):
            step()

    for slot in range(SLOTS + 1):
        ahead = first_part(slot, *sets[slot % 2]) if slot < SLOTS else []
        behind = second_part(slot - 1, *sets[(slot - 1) % 2]) if slot > 0 else []
        merged(behind, ahead)

    half = grads.shape[0] // 2
    odd_index = lax.rem(lax.axis_index("lat"), 2)
    send[0:half] = grads[pl.ds(pl.multiple_of((1 - odd_index) * half, half), half)].astype(BF16)
    keep[...] = grads[pl.ds(pl.multiple_of(odd_index * half, half), half)]
    lanes = lane_ids((channels, LANES))
    blocks = cols // LANES
    base = half
    upper = [numer[row] for row in range(MARGIN)]
    lower = [numer[MARGIN + rows + row] for row in range(MARGIN)]
    for when_odd, when_even in ((upper, lower), (lower, upper)):
        packed = jnp.zeros((channels, LANES), F32)
        for row in range(MARGIN):
            line = choose(lat_odd, when_odd[row], when_even[row])
            for block in range(blocks):
                send[base : base + channels] = line[:, block * LANES : (block + 1) * LANES].astype(BF16)
                base += channels
            low = jnp.where(lanes < MARGIN, line[:, cols:], 0.0)
            high = jnp.where(lanes >= LANES - MARGIN, line[:, cols:], 0.0)
            packed = packed + roll(low, MARGIN * row, 1) + roll(high, -MARGIN * row, 1)
        send[base : base + channels] = packed.astype(BF16)
        base += channels


def beside_kernel(numer, first, held, inner, edges):
    height, channels, wide = numer.shape
    cols = wide - LANES
    rows = height - 2 * MARGIN
    blocks = cols // LANES
    edge_rows = held.shape[0]
    base = first.shape[0] - 2 * edge_rows
    lanes = lane_ids((channels, LANES))
    lat = lax.axis_index("lat")
    odd = lax.rem(lat, 2) == 1
    inside = jnp.logical_and(lat > 0, lat < lax.axis_size("lat") - 1)
    packed = jnp.zeros((channels, LANES), F32)
    for row in range(rows):
        at = row % MARGIN
        parts = []
        for block in range(blocks + 1):
            start = (at * blocks + block if block < blocks else MARGIN * blocks) * channels
            near = first[base + start : base + start + channels].astype(F32)
            far = choose(inside, held[start : start + channels].astype(F32), 0.0)
            other = choose(odd, near, far) if row < MARGIN else choose(odd, far, near)
            if block == blocks:
                low = jnp.where(lanes < MARGIN, roll(other, -MARGIN * at, 1), 0.0)
                other = low + jnp.where(lanes >= LANES - MARGIN, roll(other, MARGIN * at, 1), 0.0)
            parts.append(numer[MARGIN + row, :, block * LANES : (block + 1) * LANES] + other)
        inner[row] = jnp.concatenate(parts[:-1], axis=1)
        low = jnp.where(lanes < MARGIN, parts[-1], 0.0)
        high = jnp.where(lanes >= LANES - MARGIN, parts[-1], 0.0)
        packed = packed + roll(low, MARGIN * row, 1) + roll(high, -MARGIN * row, 1)
    edges[...] = packed.astype(BF16)


def fold_kernel(inner, parts, den, blended):
    rows, channels, cols = inner.shape
    lanes = lane_ids((channels, LANES))
    lon, lon_size = lax.axis_index("lon"), lax.axis_size("lon")
    base = parts.shape[1] - channels
    left = parts[lax.rem(lon + lon_size - 1, lon_size), base : base + channels].astype(F32)
    right = parts[lax.rem(lon + 1, lon_size), base : base + channels].astype(F32)
    inverse = 1.0 / den[...]
    lines = []
    for row in range(rows):
        from_left = jnp.where(lanes < MARGIN, roll(left, -MARGIN * row, 1), 0.0)
        from_right = jnp.where(lanes >= LANES - MARGIN, roll(right, MARGIN * row, 1), 0.0)
        beside = [from_left]
        for _ in range(cols // LANES - 2):
            beside.append(jnp.zeros((channels, LANES), F32))
        beside.append(from_right)
        line = inner[row] + jnp.concatenate(beside, axis=1)
        lines.append((line * inverse[row : row + 1])[None])
    blended[...] = jnp.swapaxes(jnp.concatenate(lines, axis=0), 0, 1)


def split_kernel(own, other, grad_in, grad_mid, grad_out):
    taps, channels, width = grad_in.shape
    half = own.shape[0]
    odd = lax.rem(lax.axis_index("lat"), 2) == 1
    own, other = own[...], other[...]
    summed = (choose(odd, other, own), choose(odd, own, other))

    def rows_of(start, count):
        pieces = []
        stop = start + count
        if start < half:
            pieces.append(summed[0][start : min(stop, half)])
        if stop > half:
            pieces.append(summed[1][max(start, half) - half : stop - half])
        return jnp.concatenate(pieces, axis=0).astype(F32) if len(pieces) > 1 else pieces[0].astype(F32)

    for tap in range(taps):
        grad_in[tap] = rows_of(tap * channels, channels)
        grad_mid[tap] = rows_of(taps * channels + tap * width, width)
        grad_out[tap] = rows_of(taps * (channels + width) + tap * channels, channels)


def params():
    return pltpu.CompilerParams(vmem_limit_bytes=VMEM_LIMIT)


def swap(value, axis, first, wrap):
    size = lax.axis_size(axis)
    pairs = []
    for index in range(first, size, 2):
        other = (index + 1) % size
        if other > index or wrap:
            pairs.extend([(index, other), (other, index)])
    return lax.ppermute(value, axis, pairs)


def swap_lat(first, second):
    return swap(first, "lat", 0, False), swap(second, "lat", 1, False)


def swap_lon(edges):
    return swap(edges, "lon", 0, True), swap(edges, "lon", 1, True)


def exchange(value, axis, order):
    pairs = [(index, index ^ order[index % 2]) for index in range(lax.axis_size(axis))]
    return lax.ppermute(value, axis, pairs)


def order_bit(lat, order):
    step = jnp.where(lat % 2 == 0, order[0], order[1])
    return (lat // step) % 2


def halves(value, bit):
    half = value.shape[0] // 2
    own = lax.dynamic_slice_in_dim(value, bit * half, half, 0)
    other = lax.dynamic_slice_in_dim(value, (1 - bit) * half, half, 0)
    return own, other


def ordered(own, other, bit):
    return jnp.concatenate([jnp.where(bit == 0, own, other), jnp.where(bit == 0, other, own)], axis=0)


def shards(
    fields, cotangent, kernel_in, kernel_mid, kernel_out, patch_anchors, blend_weights, tile_counts
):
    channels, rows, cols = fields.shape
    taps, width, _ = kernel_in.shape
    patch_anchors = jnp.transpose(patch_anchors, (0, 1, 3, 2))
    height = rows + 2 * MARGIN
    wide = cols + LANES
    full = rows * cols
    padded = full + 2 * cols
    shape = jax.ShapeDtypeStruct
    center, first, second, canvas = pl.pallas_call(
        pack_kernel,
        out_shape=(
            shape((rows, 2 * channels, cols), BF16),
            shape((MARGIN + 1, 2 * channels, cols), BF16),
            shape((MARGIN + 1, 2 * channels, cols), BF16),
            shape((height, wide), F32),
        ),
        in_specs=[smem()] + [pl.BlockSpec(memory_space=pltpu.HBM)] * 4,
        out_specs=(vmem(),) * 4,
        scratch_shapes=[
            pltpu.VMEM(fields.shape, BF16),
            pltpu.VMEM(cotangent.shape, BF16),
            pltpu.VMEM(blend_weights.shape, jnp.int32),
            pltpu.SMEM(patch_anchors.shape, jnp.int32),
            pltpu.VMEM((height, wide), F32),
            pltpu.SemaphoreType.DMA((4,)),
        ],
        compiler_params=params(),
        name="pack",
    )(
        tile_counts,
        *(
            pltpu.with_memory_space_constraint(value, pltpu.HBM)
            for value in (patch_anchors, fields, cotangent, blend_weights)
        ),
    )
    first, second = swap_lat(first, second)
    w_in = jnp.transpose(kernel_in, (1, 0, 2)).reshape(width, taps * channels)
    kernel_mid = kernel_mid.reshape(3, 3, width, width)
    kernel_out = kernel_out.reshape(3, 3, channels, width)
    w_mid = jnp.transpose(kernel_mid, (1, 2, 0, 3)).reshape(3 * width, 3 * width)
    w_mid_back = jnp.transpose(kernel_mid, (3, 0, 1, 2)).reshape(width, taps * width)
    w_out = jnp.transpose(kernel_out, (1, 2, 0, 3)).reshape(3 * channels, 3 * width)
    w_out_back = jnp.transpose(kernel_out, (3, 0, 1, 2)).reshape(width, taps * channels)
    first, second, w_in, w_mid, w_mid_back, w_out, w_out_back = lax.optimization_barrier(
        (first, second, w_in, w_mid, w_mid_back, w_out, w_out_back)
    )
    edges, total = pl.pallas_call(
        edge_kernel,
        out_shape=(shape((2 * channels + 2 * height, LANES), BF16), shape((height, wide), F32)),
        in_specs=[vmem()] * 4,
        out_specs=(vmem(),) * 2,
        compiler_params=params(),
        name="edges",
    )(center, first, second, canvas)
    third, fourth = swap_lon(edges)

    lat_size, lon_size = lax.axis_size("lat"), lax.axis_size("lon")
    length = taps * (2 * channels + width)
    unit = 16 * lat_size
    length = (length + unit - 1) // unit * unit
    half = length // 2
    edge_rows = channels * (MARGIN * (cols // LANES) + 1)
    send, keep, numer, den = pl.pallas_call(
        patch_kernel,
        out_shape=(
            shape((half + 2 * edge_rows, LANES), BF16),
            shape((half, LANES), F32),
            shape((height, channels, wide), F32),
            shape((rows, cols), F32),
        ),
        in_specs=[smem(), smem()] + [vmem()] * 12,
        out_specs=(vmem(),) * 4,
        scratch_shapes=[
            pltpu.VMEM((length, LANES), F32),
            pltpu.VMEM((height, 2 * channels, wide), F32),
        ]
        + 2
        * [
            pltpu.VMEM((3 * channels, padded), BF16),
            pltpu.VMEM((3 * channels, padded), BF16),
            pltpu.VMEM((width, padded), BF16),
            pltpu.VMEM((3 * width, padded), BF16),
            pltpu.VMEM((width, padded), BF16),
            pltpu.VMEM((width, full), F32),
            pltpu.VMEM((width, full), F32),
            pltpu.VMEM((width, full), BF16),
        ],
        compiler_params=params(),
        name="patches",
    )(
        patch_anchors, tile_counts, center, first, second, third, fourth, total, blend_weights,
        w_in, w_mid, w_mid_back, w_out, w_out_back,
    )

    lat = lax.axis_index("lat")
    even = lat % 2 == 0
    first = exchange(send, "lat", (1, 1))
    mine = keep + first[:half].astype(F32)
    held = first[half + edge_rows :]
    steps = [2 << bit for bit in range(lat_size.bit_length() - 2)]
    orders = list(zip(steps, steps[1:] + steps[:1]))
    for turn, order in enumerate(orders):
        own, other = halves(mine, order_bit(lat, order))
        payload = jnp.concatenate([other.astype(BF16), held], axis=0)
        payload = exchange(payload, "lat", order)
        count = own.shape[0]
        mine = own + payload[:count].astype(F32)
        moves = []
        for side in (0, 1):
            done = [orders[before][side] for before in range(turn)]
            move = jnp.bool_(True)
            for step in steps:
                if step < order[side]:
                    carries = 1 if (step in done) == (side == 1) else 0
                    move = jnp.logical_and(move, (lat // step) % 2 == carries)
            moves.append(move)
        held = jnp.where(jnp.where(even, moves[0], moves[1]), payload[count:], held)
    inner, edges = pl.pallas_call(
        beside_kernel,
        out_shape=(shape((rows, channels, cols), F32), shape((channels, LANES), BF16)),
        in_specs=[vmem()] * 3,
        out_specs=(vmem(),) * 2,
        compiler_params=params(),
        name="beside",
    )(numer, first, held)
    count = mine.shape[0]
    payload = jnp.concatenate([mine.astype(BF16), edges], axis=0)
    payload = jnp.broadcast_to(payload[None], (lon_size,) + payload.shape)
    payload = lax.all_to_all(payload, "lon", 0, 0)
    mine = jnp.sum(payload[:, :count].astype(F32), axis=0).astype(BF16)
    blended = pl.pallas_call(
        fold_kernel,
        out_shape=shape((channels, rows, cols), F32),
        in_specs=[vmem()] * 3,
        out_specs=vmem(),
        compiler_params=params(),
        name="fold",
    )(inner, payload, den)
    for order in reversed(orders):
        mine = ordered(mine, exchange(mine, "lat", order), order_bit(lat, order))
    grad_in, grad_mid, grad_out = pl.pallas_call(
        split_kernel,
        out_shape=(
            shape((taps, channels, width), F32),
            shape((taps, width, width), F32),
            shape((taps, channels, width), F32),
        ),
        in_specs=[vmem()] * 2,
        out_specs=(vmem(),) * 3,
        compiler_params=params(),
        name="split",
    )(mine, exchange(mine, "lat", (1, 1)))
    return blended, jnp.transpose(grad_in, (0, 2, 1)), grad_mid, grad_out


def solution(mesh):
    return jax.shard_map(
        shards,
        mesh=mesh,
        in_specs=(
            P(None, "lat", "lon"),
            P(None, "lat", "lon"),
            P(),
            P(),
            P(),
            P("lat", "lon", None, None),
            P(None, "lat", "lon"),
            P("lat", "lon"),
        ),
        out_specs=(P(None, "lat", "lon"), P(), P(), P()),
        check_vma=False,
    )
```

```python
import functools

import jax
import jax.numpy as jnp
from jax import lax
from jax.experimental import pallas as pl
from jax.experimental.pallas import tpu as pltpu
from jax.sharding import PartitionSpec as P

MARGIN = 4
SLOTS = 4
LANES = 128
F32 = jnp.float32
BF16 = jnp.bfloat16
VMEM_LIMIT = 48 * 1024 * 1024


def vmem():
    return pl.BlockSpec(memory_space=pltpu.VMEM)


def smem():
    return pl.BlockSpec(memory_space=pltpu.SMEM)


def lane_ids(shape):
    return lax.broadcasted_iota(jnp.int32, shape, len(shape) - 1)


def roll(value, shift, axis):
    size = value.shape[axis]
    if isinstance(shift, int):
        shift = shift % size
        if shift == 0:
            return value
    return pltpu.roll(value, shift, axis)


def choose(odd, when_odd, when_even):
    return jnp.where(odd, when_odd, when_even)


def pack_kernel(
    counts, anchors_in, fields_in, cotangent_in, weights_in, center, first_out, second_out, canvas,
    fields, cotangent, weights, anchors, spread, sems,
):
    copies = []
    for index, (source, target) in enumerate(
        ((weights_in, weights), (fields_in, fields), (cotangent_in, cotangent), (anchors_in, anchors))
    ):
        copy = pltpu.make_async_copy(source, target, sems.at[index])
        copy.start()
        copies.append(copy)
    channels, rows, cols = fields.shape
    wide = cols + LANES
    odd = lax.rem(lax.axis_index("lat"), 2) == 1
    spread[...] = jnp.zeros_like(spread)
    copies[0].wait()
    copies[3].wait()
    for slot in range(SLOTS):

        @pl.when(slot < counts[0, 0])
        def _():
            row = anchors[0, 0, 0, slot]
            col = anchors[0, 0, 1, slot]
            values = weights[slot].astype(F32)
            values = jnp.concatenate([values, jnp.zeros((rows, LANES), F32)], axis=1)
            values = jnp.concatenate([values, jnp.zeros((2 * MARGIN, wide), F32)], axis=0)
            values = roll(values, lax.rem(col + (wide - MARGIN), wide), 1)
            values = roll(values, row, 0)
            spread[...] += values

    total = spread[...]
    canvas[...] = total
    copies[1].wait()
    copies[2].wait()
    both = []
    for source in (fields, cotangent):
        both.append(jnp.swapaxes(source[...].astype(F32), 0, 1))
    tile = jnp.concatenate(both, axis=1).astype(BF16)
    center[...] = tile
    half = total.shape[0] // 2
    pad = jnp.zeros((2 * channels - 2 * half, cols), F32)
    extras = []
    for part in (total[:half], total[half:]):
        beside = jnp.concatenate([part[:, cols:], jnp.zeros((half, cols - LANES), F32)], axis=1)
        extras.append(jnp.concatenate([part[:, :cols], beside, pad], axis=0).astype(BF16))
    top, bottom = tile[:MARGIN], tile[rows - MARGIN :]
    first_out[0:MARGIN] = choose(odd, top, bottom)
    first_out[MARGIN] = choose(odd, extras[0], extras[1])
    second_out[0:MARGIN] = choose(odd, bottom, top)
    second_out[MARGIN] = choose(odd, extras[1], extras[0])


def edge_kernel(center, first, second, canvas, edges, total_out):
    rows = center.shape[0]
    channels = center.shape[1] // 2
    cols = center.shape[2]
    height = rows + 2 * MARGIN
    half = height // 2
    odd = lax.rem(lax.axis_index("lat"), 2) == 1

    def stretch(block):
        block = block.astype(F32)
        return jnp.concatenate([block[:half], block[half:height, :LANES]], axis=1)

    upper = stretch(choose(odd, first[MARGIN], second[MARGIN]))
    lower = stretch(choose(odd, second[MARGIN], first[MARGIN]))
    total = canvas[...] + jnp.concatenate([upper, lower], axis=0)
    total_out[...] = total
    lanes = lane_ids((2 * channels, LANES))
    packed = jnp.zeros((2 * channels, LANES), F32)
    for row in range(height):
        if row < MARGIN:
            line = choose(odd, first[row], second[row])
        elif row < MARGIN + rows:
            line = center[row - MARGIN]
        else:
            line = choose(odd, second[row - MARGIN - rows], first[row - MARGIN - rows])
        line = line.astype(F32)
        low = jnp.where(lanes < MARGIN, line[:, :LANES], 0.0)
        high = jnp.where(lanes >= LANES - MARGIN, line[:, cols - LANES :], 0.0)
        packed = packed + roll(low, MARGIN * row, 1) + roll(high, -MARGIN * row, 1)
    edges[0 : 2 * channels] = packed.astype(BF16)
    margin = total[:, cols:]
    lanes = lane_ids(margin.shape)
    to_left = jnp.where(lanes < LANES // 2, total[:, :LANES], margin)
    to_right = jnp.where(lanes < LANES // 2, margin, total[:, cols - LANES : cols])
    edges[2 * channels : 2 * channels + height] = to_left.astype(BF16)
    edges[2 * channels + height : 2 * channels + 2 * height] = to_right.astype(BF16)


def dot(left, right):
    return jnp.dot(left, right, preferred_element_type=F32)


def dot_lanes(left, right):
    return lax.dot_general(left, right, (((1,), (1,)), ((), ())), preferred_element_type=F32)


def patch_kernel(
    anchors, counts, center, first, second, third, fourth, total_in, weights,
    w_in, w_mid, w_mid_back, w_out, w_out_back,
    send, keep, numer, den_out,
    grads, window, y_s, *sets,
):
    rows = center.shape[0]
    channels = center.shape[1] // 2
    cols = center.shape[2]
    wide = cols + LANES
    width = w_mid.shape[0] // 3
    full = rows * cols
    height = rows + 2 * MARGIN
    lanes = lane_ids((2 * channels, LANES))
    lat_odd = lax.rem(lax.axis_index("lat"), 2) == 1
    lon_odd = lax.rem(lax.axis_index("lon"), 2) == 1

    left = choose(lon_odd, third[...], fourth[...]).astype(F32)
    right = choose(lon_odd, fourth[...], third[...]).astype(F32)
    base = 2 * channels
    left_part = left[base + height : base + 2 * height]
    right_part = right[base : base + height]
    edge_lanes = lane_ids((height, LANES))
    low = edge_lanes < MARGIN
    high = edge_lanes >= LANES - MARGIN
    zero = jnp.zeros((height, LANES), F32)
    pieces = [jnp.where(low, left_part, zero)]
    for _ in range(cols // LANES - 2):
        pieces.append(zero)
    pieces.append(jnp.where(high, right_part, zero))
    pieces.append(jnp.where(high, left_part, zero) + jnp.where(low, right_part, zero))
    den = jnp.maximum(total_in[...] + jnp.concatenate(pieces, axis=1), 1.0)
    den_out[...] = den[MARGIN : MARGIN + rows, :cols]
    inverse = 1.0 / den

    left = left[:base]
    right = right[:base]
    for row in range(height):
        if row < MARGIN:
            body = choose(lat_odd, first[row], second[row])
        elif row < MARGIN + rows:
            body = center[row - MARGIN]
        else:
            body = choose(lat_odd, second[row - MARGIN - rows], first[row - MARGIN - rows])
        beside = jnp.where(
            lanes < LANES // 2, roll(right, -MARGIN * row, 1), roll(left, MARGIN * row, 1)
        )
        line = jnp.concatenate([body.astype(F32), beside], axis=1)
        scaled = line[channels:] * inverse[row : row + 1]
        window[row, 0:channels] = line[:channels]
        window[row, channels : 2 * channels] = scaled.astype(BF16).astype(F32)

    numer[...] = jnp.zeros_like(numer)
    grads[...] = jnp.zeros_like(grads)
    sets = (sets[: len(sets) // 2], sets[len(sets) // 2 :])
    for ref in sets[0][:5] + sets[1][:5]:
        ref[:, 0:cols] = jnp.zeros((ref.shape[0], cols), BF16)
        ref[:, cols + full : 2 * cols + full] = jnp.zeros((ref.shape[0], cols), BF16)

    def shifted(value, step):
        blocks = [value[:, at : at + LANES] for at in range(0, cols, LANES)]
        turned = [roll(block, step, 1) for block in blocks]
        ids = lane_ids(blocks[0].shape)
        zero = jnp.zeros_like(blocks[0])
        if step > 0:
            ends = [zero] + turned[:-1]
            at_end = ids == 0
        else:
            ends = turned[1:] + [zero]
            at_end = ids == LANES - 1
        return jnp.concatenate([jnp.where(at_end, end, own) for end, own in zip(ends, turned)], axis=1)

    def before(value):
        return shifted(value, 1)

    def after(value):
        return shifted(value, -1)

    def spread(ref, value, row, flip):
        count = value.shape[0]
        at = slice((row + 1) * cols, (row + 2) * cols)
        first, last = before(value), after(value)
        if flip:
            first, last = last, first
        ref[0:count, at] = first
        ref[count : 2 * count, at] = value
        ref[2 * count : 3 * count, at] = last

    def stack(ref, row, flip):
        starts = [(row + (2 - tap if flip else tap)) * cols for tap in range(3)]
        return jnp.concatenate([ref[:, start : start + cols] for start in starts], axis=0)

    def across(parts, flip):
        count = parts.shape[0] // 3
        first, last = parts[:count], parts[2 * count :]
        if flip:
            first, last = last, first
        return before(first) + parts[count : 2 * count] + after(last)

    def all_rows(ref, flip):
        starts = [(2 - tap if flip else tap) * cols for tap in range(3)]
        return jnp.concatenate([ref[:, start : start + full] for start in starts], axis=0)

    def weights_of(slot):
        return weights[slot].astype(F32) * (slot < counts[0, 0]).astype(F32)

    def first_part(slot, x_s, d_s, h_s, z_s, h2_s, slope_s, dh_s, dz_s):
        row0 = anchors[0, 0, 0, slot]
        col0 = anchors[0, 0, 1, slot]
        patch_weights = weights_of(slot)
        back_shift = lax.rem(wide + MARGIN - col0, wide)

        def cut(row):
            line = roll(window[row0 + row], back_shift, 1)[:, :cols]
            spread(x_s, line[:channels].astype(BF16), row, False)
            grad = line[channels:] * patch_weights[row : row + 1]
            spread(d_s, grad.astype(BF16), row, True)

        def conv_in(row):
            at = slice(row * cols, (row + 1) * cols)
            parts = dot(w_in[...], stack(x_s.at[0 : 2 * channels], row, False))
            z1 = parts[:width] + after(parts[width:])
            sig = 0.5 * jnp.tanh(0.5 * z1) + 0.5
            h1 = z1 * sig
            slope_s[:, at] = sig + h1 * (1.0 - sig)
            h_s[:, (row + 1) * cols : (row + 2) * cols] = h1.astype(BF16)

        def conv_mid(row):
            at = slice(row * cols, (row + 1) * cols)
            ahead = slice((row + 1) * cols, (row + 2) * cols)
            parts = dot(w_out_back[...], stack(d_s.at[0 : 2 * channels], row, True))
            dh2 = parts[:width] + before(parts[width:])
            z2 = across(dot(w_mid[...], stack(h_s, row, False)), False)
            sig = 0.5 * jnp.tanh(0.5 * z2) + 0.5
            added = z2 * sig
            h2_s[:, ahead] = (h_s[:, ahead].astype(F32) + added).astype(BF16)
            dz2 = (dh2 * (sig + added * (1.0 - sig))).astype(BF16)
            dh_s[:, at] = dh2
            spread(z_s, dz2, row, True)

        return [functools.partial(step, row) for step in (cut, conv_in, conv_mid) for row in range(rows)]

    def second_part(slot, x_s, d_s, h_s, z_s, h2_s, slope_s, dh_s, dz_s):
        row0 = anchors[0, 0, 0, slot]
        col0 = anchors[0, 0, 1, slot]
        patch_weights = weights_of(slot)
        inside = slice(cols, cols + full)
        small = 9 * channels

        def conv_back(row):
            at = slice(row * cols, (row + 1) * cols)
            back = across(dot(w_mid_back[...], stack(z_s.at[width : 2 * width], row, True)), True)
            dz_s[:, at] = ((dh_s[:, at] + back) * slope_s[:, at]).astype(BF16)

        def pair_out(pair):
            starts = [(2 * pair + 1 + at) * cols for at in range(2)]
            both = jnp.concatenate([h2_s[:, start : start + cols] for start in starts], axis=0)
            y_s[pair] = dot(w_out[...], both)

        def conv_out(row):
            terms = []
            for pair, at in ((row // 2, 1 + row % 2), (row // 2 + 2 * (row % 2) - 1, 3 - 3 * (row % 2))):
                if 0 <= pair < rows // 2:
                    terms.append(y_s[pair, at * 3 * channels : (at + 1) * 3 * channels])
            result = across(terms[0] + terms[1] if len(terms) > 1 else terms[0], False)
            result = result * patch_weights[row : row + 1]
            result = jnp.concatenate([result, jnp.zeros((channels, LANES), F32)], axis=1)
            numer[row0 + row] += roll(result, lax.rem(col0 + (wide - MARGIN), wide), 1)

        def grad_mid():
            part = dot_lanes(z_s[:, inside], all_rows(h_s, False))
            for tap in range(3):
                for tap_col in range(3):
                    start = small + (3 * tap + tap_col) * width
                    grads[start : start + width] += part[
                        tap_col * width : (tap_col + 1) * width, tap * width : (tap + 1) * width
                    ]

        def grad_out():
            start = small + 9 * width
            grads[start : start + small] += dot_lanes(all_rows(d_s, True), h2_s[:, inside])

        def grad_in():
            grads[0:small] += dot_lanes(all_rows(x_s, False), dz_s[...])

        backs = [functools.partial(conv_back, row) for row in range(rows)]
        outs = [functools.partial(pair_out, pair) for pair in range(rows // 2)]
        outs += [functools.partial(conv_out, row) for row in range(rows)]
        return [grad_mid, grad_out] + backs + [grad_in] + outs

    def merged(left, right):
        left = [((at + 0.5) / len(left), step) for at, step in enumerate(left)]
        right = [((at + 0.5) / len(right), step) for at, step in enumerate(right)]
        for _, step in sorted(left + right, key=lambda pair: pair[0]):
            step()

    for slot in range(SLOTS + 1):

        @pl.when(max(slot, 1) <= counts[0, 0])
        def _():
            ahead = first_part(slot, *sets[slot % 2]) if slot < SLOTS else []
            behind = second_part(slot - 1, *sets[(slot - 1) % 2]) if slot > 0 else []
            merged(behind, ahead)

    half = grads.shape[0] // 2
    odd_index = lax.rem(lax.axis_index("lat"), 2)
    send[0:half] = grads[pl.ds(pl.multiple_of((1 - odd_index) * half, half), half)].astype(BF16)
    keep[...] = grads[pl.ds(pl.multiple_of(odd_index * half, half), half)]
    lanes = lane_ids((channels, LANES))
    blocks = cols // LANES
    base = half
    upper = [numer[row] for row in range(MARGIN)]
    lower = [numer[MARGIN + rows + row] for row in range(MARGIN)]
    for when_odd, when_even in ((upper, lower), (lower, upper)):
        packed = jnp.zeros((channels, LANES), F32)
        for row in range(MARGIN):
            line = choose(lat_odd, when_odd[row], when_even[row])
            for block in range(blocks):
                send[base : base + channels] = line[:, block * LANES : (block + 1) * LANES].astype(BF16)
                base += channels
            low = jnp.where(lanes < MARGIN, line[:, cols:], 0.0)
            high = jnp.where(lanes >= LANES - MARGIN, line[:, cols:], 0.0)
            packed = packed + roll(low, MARGIN * row, 1) + roll(high, -MARGIN * row, 1)
        send[base : base + channels] = packed.astype(BF16)
        base += channels


def beside_kernel(numer, first, held, inner, edges):
    height, channels, wide = numer.shape
    cols = wide - LANES
    rows = height - 2 * MARGIN
    blocks = cols // LANES
    edge_rows = held.shape[0]
    base = first.shape[0] - 2 * edge_rows
    lanes = lane_ids((channels, LANES))
    lat = lax.axis_index("lat")
    odd = lax.rem(lat, 2) == 1
    inside = jnp.logical_and(lat > 0, lat < lax.axis_size("lat") - 1)
    packed = jnp.zeros((channels, LANES), F32)
    for row in range(rows):
        at = row % MARGIN
        parts = []
        for block in range(blocks + 1):
            start = (at * blocks + block if block < blocks else MARGIN * blocks) * channels
            near = first[base + start : base + start + channels].astype(F32)
            far = choose(inside, held[start : start + channels].astype(F32), 0.0)
            other = choose(odd, near, far) if row < MARGIN else choose(odd, far, near)
            if block == blocks:
                low = jnp.where(lanes < MARGIN, roll(other, -MARGIN * at, 1), 0.0)
                other = low + jnp.where(lanes >= LANES - MARGIN, roll(other, MARGIN * at, 1), 0.0)
            parts.append(numer[MARGIN + row, :, block * LANES : (block + 1) * LANES] + other)
        inner[row] = jnp.concatenate(parts[:-1], axis=1)
        low = jnp.where(lanes < MARGIN, parts[-1], 0.0)
        high = jnp.where(lanes >= LANES - MARGIN, parts[-1], 0.0)
        packed = packed + roll(low, MARGIN * row, 1) + roll(high, -MARGIN * row, 1)
    edges[...] = packed.astype(BF16)


def fold_kernel(inner, parts, den, blended):
    rows, channels, cols = inner.shape
    lanes = lane_ids((channels, LANES))
    lon, lon_size = lax.axis_index("lon"), lax.axis_size("lon")
    base = parts.shape[1] - channels
    left = parts[lax.rem(lon + lon_size - 1, lon_size), base : base + channels].astype(F32)
    right = parts[lax.rem(lon + 1, lon_size), base : base + channels].astype(F32)
    inverse = 1.0 / den[...]
    lines = []
    for row in range(rows):
        from_left = jnp.where(lanes < MARGIN, roll(left, -MARGIN * row, 1), 0.0)
        from_right = jnp.where(lanes >= LANES - MARGIN, roll(right, MARGIN * row, 1), 0.0)
        beside = [from_left]
        for _ in range(cols // LANES - 2):
            beside.append(jnp.zeros((channels, LANES), F32))
        beside.append(from_right)
        line = inner[row] + jnp.concatenate(beside, axis=1)
        lines.append((line * inverse[row : row + 1])[None])
    blended[...] = jnp.swapaxes(jnp.concatenate(lines, axis=0), 0, 1)


def split_kernel(own, other, grad_in, grad_mid, grad_out):
    taps, channels, width = grad_in.shape
    half = own.shape[0]
    odd = lax.rem(lax.axis_index("lat"), 2) == 1
    own, other = own[...], other[...]
    summed = (choose(odd, other, own), choose(odd, own, other))

    def rows_of(start, count):
        pieces = []
        stop = start + count
        if start < half:
            pieces.append(summed[0][start : min(stop, half)])
        if stop > half:
            pieces.append(summed[1][max(start, half) - half : stop - half])
        return jnp.concatenate(pieces, axis=0).astype(F32) if len(pieces) > 1 else pieces[0].astype(F32)

    for tap in range(taps):
        grad_in[tap] = rows_of(tap * channels, channels)
        grad_mid[tap] = rows_of(taps * channels + tap * width, width)
        grad_out[tap] = rows_of(taps * (channels + width) + tap * channels, channels)


def params():
    return pltpu.CompilerParams(vmem_limit_bytes=VMEM_LIMIT)


def swap(value, axis, first, wrap):
    size = lax.axis_size(axis)
    pairs = []
    for index in range(first, size, 2):
        other = (index + 1) % size
        if other > index or wrap:
            pairs.extend([(index, other), (other, index)])
    return lax.ppermute(value, axis, pairs)


def swap_lat(first, second):
    return swap(first, "lat", 0, False), swap(second, "lat", 1, False)


def swap_lon(edges):
    return swap(edges, "lon", 0, True), swap(edges, "lon", 1, True)


def exchange(value, axis, order):
    pairs = [(index, index ^ order[index % 2]) for index in range(lax.axis_size(axis))]
    return lax.ppermute(value, axis, pairs)


def order_bit(lat, order):
    step = jnp.where(lat % 2 == 0, order[0], order[1])
    return (lat // step) % 2


def halves(value, bit):
    half = value.shape[0] // 2
    own = lax.dynamic_slice_in_dim(value, bit * half, half, 0)
    other = lax.dynamic_slice_in_dim(value, (1 - bit) * half, half, 0)
    return own, other


def ordered(own, other, bit):
    return jnp.concatenate([jnp.where(bit == 0, own, other), jnp.where(bit == 0, other, own)], axis=0)


def two_taps(kernel):
    last = jnp.stack([jnp.zeros_like(kernel[:, :, 2]), kernel[:, :, 2]], axis=2)
    return jnp.concatenate([kernel[:, :, :2], last], axis=0).reshape(2 * kernel.shape[0], -1)


def shards(
    fields, cotangent, kernel_in, kernel_mid, kernel_out, patch_anchors, blend_weights, tile_counts
):
    channels, rows, cols = fields.shape
    taps, width, _ = kernel_in.shape
    patch_anchors = jnp.transpose(patch_anchors, (0, 1, 3, 2))
    height = rows + 2 * MARGIN
    wide = cols + LANES
    full = rows * cols
    padded = full + 2 * cols
    shape = jax.ShapeDtypeStruct
    center, first, second, canvas = pl.pallas_call(
        pack_kernel,
        out_shape=(
            shape((rows, 2 * channels, cols), BF16),
            shape((MARGIN + 1, 2 * channels, cols), BF16),
            shape((MARGIN + 1, 2 * channels, cols), BF16),
            shape((height, wide), F32),
        ),
        in_specs=[smem()] + [pl.BlockSpec(memory_space=pltpu.HBM)] * 4,
        out_specs=(vmem(),) * 4,
        scratch_shapes=[
            pltpu.VMEM(fields.shape, BF16),
            pltpu.VMEM(cotangent.shape, BF16),
            pltpu.VMEM(blend_weights.shape, jnp.int32),
            pltpu.SMEM(patch_anchors.shape, jnp.int32),
            pltpu.VMEM((height, wide), F32),
            pltpu.SemaphoreType.DMA((4,)),
        ],
        compiler_params=params(),
        name="pack",
    )(
        tile_counts,
        *(
            pltpu.with_memory_space_constraint(value, pltpu.HBM)
            for value in (patch_anchors, fields, cotangent, blend_weights)
        ),
    )
    first, second = swap_lat(first, second)
    kernel_in = kernel_in.reshape(3, 3, width, channels)
    kernel_mid = kernel_mid.reshape(3, 3, width, width)
    kernel_out = kernel_out.reshape(3, 3, channels, width)
    w_in = two_taps(jnp.transpose(kernel_in, (2, 0, 1, 3)))
    w_mid = jnp.transpose(kernel_mid, (1, 2, 0, 3)).reshape(3 * width, 3 * width)
    w_mid_back = jnp.transpose(kernel_mid, (1, 3, 0, 2)).reshape(3 * width, 3 * width)
    by_col = kernel_out.reshape(3, 3 * channels, width)
    none = jnp.zeros_like(by_col[0])
    w_out = jnp.concatenate(
        [
            jnp.concatenate([by_col[at - out + 2] if 0 <= at - out + 2 < 3 else none for at in range(2)], axis=1)
            for out in range(4)
        ],
        axis=0,
    )
    w_out_back = two_taps(jnp.transpose(kernel_out, (3, 0, 1, 2)))
    first, second, w_in, w_mid, w_mid_back, w_out, w_out_back = lax.optimization_barrier(
        (first, second, w_in, w_mid, w_mid_back, w_out, w_out_back)
    )
    edges, total = pl.pallas_call(
        edge_kernel,
        out_shape=(shape((2 * channels + 2 * height, LANES), BF16), shape((height, wide), F32)),
        in_specs=[vmem()] * 4,
        out_specs=(vmem(),) * 2,
        compiler_params=params(),
        name="edges",
    )(center, first, second, canvas)
    third, fourth = swap_lon(edges)

    lat_size, lon_size = lax.axis_size("lat"), lax.axis_size("lon")
    length = taps * (2 * channels + width)
    unit = 16 * lat_size
    length = (length + unit - 1) // unit * unit
    half = length // 2
    edge_rows = channels * (MARGIN * (cols // LANES) + 1)
    send, keep, numer, den = pl.pallas_call(
        patch_kernel,
        out_shape=(
            shape((half + 2 * edge_rows, LANES), BF16),
            shape((half, LANES), F32),
            shape((height, channels, wide), F32),
            shape((rows, cols), F32),
        ),
        in_specs=[smem(), smem()] + [vmem()] * 12,
        out_specs=(vmem(),) * 4,
        scratch_shapes=[
            pltpu.VMEM((length, LANES), F32),
            pltpu.VMEM((height, 2 * channels, wide), F32),
            pltpu.VMEM((rows // 2, 12 * channels, cols), F32),
        ]
        + 2
        * [
            pltpu.VMEM((3 * channels, padded), BF16),
            pltpu.VMEM((3 * channels, padded), BF16),
            pltpu.VMEM((width, padded), BF16),
            pltpu.VMEM((3 * width, padded), BF16),
            pltpu.VMEM((width, padded), BF16),
            pltpu.VMEM((width, full), F32),
            pltpu.VMEM((width, full), F32),
            pltpu.VMEM((width, full), BF16),
        ],
        compiler_params=params(),
        name="patches",
    )(
        patch_anchors, tile_counts, center, first, second, third, fourth, total, blend_weights,
        w_in, w_mid, w_mid_back, w_out, w_out_back,
    )

    lat = lax.axis_index("lat")
    even = lat % 2 == 0
    first = exchange(send, "lat", (1, 1))
    mine = keep + first[:half].astype(F32)
    held = first[half + edge_rows :]
    steps = [2 << bit for bit in range(lat_size.bit_length() - 2)]
    orders = list(zip(steps, steps[1:] + steps[:1]))
    for turn, order in enumerate(orders):
        own, other = halves(mine, order_bit(lat, order))
        payload = jnp.concatenate([other.astype(BF16), held], axis=0)
        payload = exchange(payload, "lat", order)
        count = own.shape[0]
        mine = own + payload[:count].astype(F32)
        moves = []
        for side in (0, 1):
            done = [orders[before][side] for before in range(turn)]
            move = jnp.bool_(True)
            for step in steps:
                if step < order[side]:
                    carries = 1 if (step in done) == (side == 1) else 0
                    move = jnp.logical_and(move, (lat // step) % 2 == carries)
            moves.append(move)
        held = jnp.where(jnp.where(even, moves[0], moves[1]), payload[count:], held)
    inner, edges = pl.pallas_call(
        beside_kernel,
        out_shape=(shape((rows, channels, cols), F32), shape((channels, LANES), BF16)),
        in_specs=[vmem()] * 3,
        out_specs=(vmem(),) * 2,
        compiler_params=params(),
        name="beside",
    )(numer, first, held)
    count = mine.shape[0]
    payload = jnp.concatenate([mine.astype(BF16), edges], axis=0)
    payload = jnp.broadcast_to(payload[None], (lon_size,) + payload.shape)
    payload = lax.all_to_all(payload, "lon", 0, 0)
    mine = jnp.sum(payload[:, :count].astype(F32), axis=0).astype(BF16)
    blended = pl.pallas_call(
        fold_kernel,
        out_shape=shape((channels, rows, cols), F32),
        in_specs=[vmem()] * 3,
        out_specs=vmem(),
        compiler_params=params(),
        name="fold",
    )(inner, payload, den)
    for order in reversed(orders):
        mine = ordered(mine, exchange(mine, "lat", order), order_bit(lat, order))
    grad_in, grad_mid, grad_out = pl.pallas_call(
        split_kernel,
        out_shape=(
            shape((taps, channels, width), F32),
            shape((taps, width, width), F32),
            shape((taps, channels, width), F32),
        ),
        in_specs=[vmem()] * 2,
        out_specs=(vmem(),) * 3,
        compiler_params=params(),
        name="split",
    )(mine, exchange(mine, "lat", (1, 1)))
    return blended, jnp.transpose(grad_in, (0, 2, 1)), grad_mid, grad_out


def solution(mesh):
    return jax.shard_map(
        shards,
        mesh=mesh,
        in_specs=(
            P(None, "lat", "lon"),
            P(None, "lat", "lon"),
            P(),
            P(),
            P(),
            P("lat", "lon", None, None),
            P(None, "lat", "lon"),
            P("lat", "lon"),
        ),
        out_specs=(P(None, "lat", "lon"), P(), P(), P()),
        check_vma=False,
    )
```

```python
import functools

import jax
import jax.numpy as jnp
from jax import lax
from jax.experimental import pallas as pl
from jax.experimental.pallas import tpu as pltpu
from jax.sharding import PartitionSpec as P

MARGIN = 4
SLOTS = 4
LANES = 128
F32 = jnp.float32
BF16 = jnp.bfloat16
VMEM_LIMIT = 48 * 1024 * 1024


def vmem():
    return pl.BlockSpec(memory_space=pltpu.VMEM)


def smem():
    return pl.BlockSpec(memory_space=pltpu.SMEM)


def lane_ids(shape):
    return lax.broadcasted_iota(jnp.int32, shape, len(shape) - 1)


def roll(value, shift, axis):
    size = value.shape[axis]
    if isinstance(shift, int):
        shift = shift % size
        if shift == 0:
            return value
    return pltpu.roll(value, shift, axis)


def choose(odd, when_odd, when_even):
    return jnp.where(odd, when_odd, when_even)


def pack_kernel(
    counts, anchors_in, fields_in, cotangent_in, weights_in, center, first_out, second_out, canvas,
    fields, cotangent, weights, anchors, spread, sems,
):
    copies = []
    for index, (source, target) in enumerate(
        ((weights_in, weights), (fields_in, fields), (cotangent_in, cotangent), (anchors_in, anchors))
    ):
        copy = pltpu.make_async_copy(source, target, sems.at[index])
        copy.start()
        copies.append(copy)
    channels, rows, cols = fields.shape
    wide = cols + LANES
    odd = lax.rem(lax.axis_index("lat"), 2) == 1
    spread[...] = jnp.zeros_like(spread)
    copies[0].wait()
    copies[3].wait()
    for slot in range(SLOTS):

        @pl.when(slot < counts[0, 0])
        def _():
            row = anchors[0, 0, 0, slot]
            col = anchors[0, 0, 1, slot]
            values = weights[slot].astype(F32)
            values = jnp.concatenate([values, jnp.zeros((rows, LANES), F32)], axis=1)
            values = jnp.concatenate([values, jnp.zeros((2 * MARGIN, wide), F32)], axis=0)
            values = roll(values, lax.rem(col + (wide - MARGIN), wide), 1)
            values = roll(values, row, 0)
            spread[...] += values

    total = spread[...]
    canvas[...] = total
    copies[1].wait()
    copies[2].wait()
    both = []
    for source in (fields, cotangent):
        both.append(jnp.swapaxes(source[...].astype(F32), 0, 1))
    tile = jnp.concatenate(both, axis=1).astype(BF16)
    center[...] = tile
    half = total.shape[0] // 2
    pad = jnp.zeros((2 * channels - 2 * half, cols), F32)
    extras = []
    for part in (total[:half], total[half:]):
        beside = jnp.concatenate([part[:, cols:], jnp.zeros((half, cols - LANES), F32)], axis=1)
        extras.append(jnp.concatenate([part[:, :cols], beside, pad], axis=0).astype(BF16))
    top, bottom = tile[:MARGIN], tile[rows - MARGIN :]
    first_out[0:MARGIN] = choose(odd, top, bottom)
    first_out[MARGIN] = choose(odd, extras[0], extras[1])
    second_out[0:MARGIN] = choose(odd, bottom, top)
    second_out[MARGIN] = choose(odd, extras[1], extras[0])


def edge_kernel(center, first, second, canvas, edges, total_out):
    rows = center.shape[0]
    channels = center.shape[1] // 2
    cols = center.shape[2]
    height = rows + 2 * MARGIN
    half = height // 2
    odd = lax.rem(lax.axis_index("lat"), 2) == 1

    def stretch(block):
        block = block.astype(F32)
        return jnp.concatenate([block[:half], block[half:height, :LANES]], axis=1)

    upper = stretch(choose(odd, first[MARGIN], second[MARGIN]))
    lower = stretch(choose(odd, second[MARGIN], first[MARGIN]))
    total = canvas[...] + jnp.concatenate([upper, lower], axis=0)
    total_out[...] = total
    lanes = lane_ids((2 * channels, LANES))
    packed = jnp.zeros((2 * channels, LANES), F32)
    for row in range(height):
        if row < MARGIN:
            line = choose(odd, first[row], second[row])
        elif row < MARGIN + rows:
            line = center[row - MARGIN]
        else:
            line = choose(odd, second[row - MARGIN - rows], first[row - MARGIN - rows])
        line = line.astype(F32)
        low = jnp.where(lanes < MARGIN, line[:, :LANES], 0.0)
        high = jnp.where(lanes >= LANES - MARGIN, line[:, cols - LANES :], 0.0)
        packed = packed + roll(low, MARGIN * row, 1) + roll(high, -MARGIN * row, 1)
    edges[0 : 2 * channels] = packed.astype(BF16)
    margin = total[:, cols:]
    lanes = lane_ids(margin.shape)
    to_left = jnp.where(lanes < LANES // 2, total[:, :LANES], margin)
    to_right = jnp.where(lanes < LANES // 2, margin, total[:, cols - LANES : cols])
    edges[2 * channels : 2 * channels + height] = to_left.astype(BF16)
    edges[2 * channels + height : 2 * channels + 2 * height] = to_right.astype(BF16)


def dot(left, right):
    return jnp.dot(left, right, preferred_element_type=F32)


def dot_lanes(left, right):
    return lax.dot_general(left, right, (((1,), (1,)), ((), ())), preferred_element_type=F32)


def patch_kernel(
    anchors, counts, center, first, second, third, fourth, total_in, weights,
    w_in, w_mid, w_mid_back, w_out, w_out_back,
    send, keep, numer, den_out,
    grads, window, *sets,
):
    rows = center.shape[0]
    channels = center.shape[1] // 2
    cols = center.shape[2]
    wide = cols + LANES
    width = w_in.shape[0]
    full = rows * cols
    height = rows + 2 * MARGIN
    lanes = lane_ids((2 * channels, LANES))
    lat_odd = lax.rem(lax.axis_index("lat"), 2) == 1
    lon_odd = lax.rem(lax.axis_index("lon"), 2) == 1

    left = choose(lon_odd, third[...], fourth[...]).astype(F32)
    right = choose(lon_odd, fourth[...], third[...]).astype(F32)
    base = 2 * channels
    left_part = left[base + height : base + 2 * height]
    right_part = right[base : base + height]
    edge_lanes = lane_ids((height, LANES))
    low = edge_lanes < MARGIN
    high = edge_lanes >= LANES - MARGIN
    zero = jnp.zeros((height, LANES), F32)
    pieces = [jnp.where(low, left_part, zero)]
    for _ in range(cols // LANES - 2):
        pieces.append(zero)
    pieces.append(jnp.where(high, right_part, zero))
    pieces.append(jnp.where(high, left_part, zero) + jnp.where(low, right_part, zero))
    den = jnp.maximum(total_in[...] + jnp.concatenate(pieces, axis=1), 1.0)
    den_out[...] = den[MARGIN : MARGIN + rows, :cols]
    inverse = 1.0 / den

    left = left[:base]
    right = right[:base]
    for row in range(height):
        if row < MARGIN:
            body = choose(lat_odd, first[row], second[row])
        elif row < MARGIN + rows:
            body = center[row - MARGIN]
        else:
            body = choose(lat_odd, second[row - MARGIN - rows], first[row - MARGIN - rows])
        beside = jnp.where(
            lanes < LANES // 2, roll(right, -MARGIN * row, 1), roll(left, MARGIN * row, 1)
        )
        line = jnp.concatenate([body.astype(F32), beside], axis=1)
        scaled = line[channels:] * inverse[row : row + 1]
        window[row, 0:channels] = line[:channels].astype(BF16)
        window[row, channels : 2 * channels] = scaled.astype(BF16)

    numer[...] = jnp.zeros_like(numer)
    grads[...] = jnp.zeros_like(grads)
    sets = (sets[: len(sets) // 2], sets[len(sets) // 2 :])
    for ref in sets[0][:5] + sets[1][:5]:
        ref[:, 0:cols] = jnp.zeros((ref.shape[0], cols), BF16)
        ref[:, cols + full : 2 * cols + full] = jnp.zeros((ref.shape[0], cols), BF16)

    def shifted(value, step):
        blocks = [value[:, at : at + LANES] for at in range(0, cols, LANES)]
        turned = [roll(block, step, 1) for block in blocks]
        ids = lane_ids(blocks[0].shape)
        zero = jnp.zeros_like(blocks[0])
        if step > 0:
            ends = [zero] + turned[:-1]
            at_end = ids == 0
        else:
            ends = turned[1:] + [zero]
            at_end = ids == LANES - 1
        return jnp.concatenate([jnp.where(at_end, end, own) for end, own in zip(ends, turned)], axis=1)

    def before(value):
        return shifted(value, 1)

    def after(value):
        return shifted(value, -1)

    def spread(ref, value, row, flip):
        count = value.shape[0]
        at = slice((row + 1) * cols, (row + 2) * cols)
        first, last = before(value), after(value)
        if flip:
            first, last = last, first
        ref[0:count, at] = first
        ref[count : 2 * count, at] = value
        ref[2 * count : 3 * count, at] = last

    def stack(ref, row, flip):
        starts = [(row + (2 - tap if flip else tap)) * cols for tap in range(3)]
        return jnp.concatenate([ref[:, start : start + cols] for start in starts], axis=0)

    def across(parts, flip):
        count = parts.shape[0] // 3
        first, last = parts[:count], parts[2 * count :]
        if flip:
            first, last = last, first
        return before(first) + parts[count : 2 * count] + after(last)

    def all_rows(ref, flip):
        starts = [(2 - tap if flip else tap) * cols for tap in range(3)]
        return jnp.concatenate([ref[:, start : start + full] for start in starts], axis=0)

    def weights_of(slot):
        return weights[slot].astype(F32) * (slot < counts[0, 0]).astype(F32)

    def first_part(slot, x_s, d_s, h_s, z_s, h2_s, slope_s, dh_s, dz_s):
        row0 = anchors[0, 0, 0, slot]
        col0 = anchors[0, 0, 1, slot]
        patch_weights = weights_of(slot)
        back_shift = lax.rem(wide + MARGIN - col0, wide)

        def cut(row):
            line = roll(window[row0 + row], back_shift, 1)[:, :cols]
            spread(x_s, line[:channels], row, False)
            grad = line[channels:].astype(F32) * patch_weights[row : row + 1]
            spread(d_s, grad.astype(BF16), row, True)

        def conv_in(row):
            at = slice(row * cols, (row + 1) * cols)
            z1 = dot(w_in[...], stack(x_s, row, False))
            sig = 0.5 * jnp.tanh(0.5 * z1) + 0.5
            h1 = z1 * sig
            slope_s[:, at] = sig + h1 * (1.0 - sig)
            spread(h_s, h1.astype(BF16), row, False)

        def conv_mid(row):
            at = slice(row * cols, (row + 1) * cols)
            ahead = slice((row + 1) * cols, (row + 2) * cols)
            dh2 = dot(w_out_back[...], stack(d_s, row, True))
            z2 = dot(w_mid[...], stack(h_s, row, False))
            sig = 0.5 * jnp.tanh(0.5 * z2) + 0.5
            added = z2 * sig
            h2_s[:, ahead] = (h_s[width : 2 * width, ahead].astype(F32) + added).astype(BF16)
            dz2 = (dh2 * (sig + added * (1.0 - sig))).astype(BF16)
            dh_s[:, at] = dh2
            spread(z_s, dz2, row, True)

        return [functools.partial(step, row) for step in (cut, conv_in, conv_mid) for row in range(rows)]

    def second_part(slot, x_s, d_s, h_s, z_s, h2_s, slope_s, dh_s, dz_s):
        row0 = anchors[0, 0, 0, slot]
        col0 = anchors[0, 0, 1, slot]
        patch_weights = weights_of(slot)
        inside = slice(cols, cols + full)
        small = 9 * channels

        def conv_back(row):
            at = slice(row * cols, (row + 1) * cols)
            back = dot(w_mid_back[...], stack(z_s, row, True))
            dz_s[:, at] = ((dh_s[:, at] + back) * slope_s[:, at]).astype(BF16)

        def conv_out(row):
            result = across(dot(w_out[...], stack(h2_s, row, False)), False)
            result = result * patch_weights[row : row + 1]
            result = jnp.concatenate([result, jnp.zeros((channels, LANES), F32)], axis=1)
            numer[row0 + row] += roll(result, lax.rem(col0 + (wide - MARGIN), wide), 1)

        def grad_mid():
            part = dot_lanes(z_s[:, inside], all_rows(h_s.at[width : 2 * width], False))
            for tap in range(3):
                for tap_col in range(3):
                    start = small + (3 * tap + tap_col) * width
                    grads[start : start + width] += part[
                        tap_col * width : (tap_col + 1) * width, tap * width : (tap + 1) * width
                    ]

        def grad_out():
            start = small + 9 * width
            grads[start : start + small] += dot_lanes(all_rows(d_s, True), h2_s[:, inside])

        def grad_in():
            grads[0:small] += dot_lanes(all_rows(x_s, False), dz_s[...])

        backs = [functools.partial(conv_back, row) for row in range(rows)]
        outs = [functools.partial(conv_out, row) for row in range(rows)]
        return [grad_mid, grad_out] + backs + [grad_in] + outs

    def merged(left, right):
        left = [((at + 0.5) / len(left), step) for at, step in enumerate(left)]
        right = [((at + 0.5) / len(right), step) for at, step in enumerate(right)]
        for _, step in sorted(left + right, key=lambda pair: pair[0]):
            step()

    for slot in range(SLOTS + 1):

        @pl.when(max(slot, 1) <= counts[0, 0])
        def _():
            ahead = first_part(slot, *sets[slot % 2]) if slot < SLOTS else []
            behind = second_part(slot - 1, *sets[(slot - 1) % 2]) if slot > 0 else []
            merged(behind, ahead)

    half = grads.shape[0] // 2
    odd_index = lax.rem(lax.axis_index("lat"), 2)
    send[0:half] = grads[pl.ds(pl.multiple_of((1 - odd_index) * half, half), half)].astype(BF16)
    keep[...] = grads[pl.ds(pl.multiple_of(odd_index * half, half), half)]
    lanes = lane_ids((channels, LANES))
    blocks = cols // LANES
    base = half
    upper = [numer[row] for row in range(MARGIN)]
    lower = [numer[MARGIN + rows + row] for row in range(MARGIN)]
    for when_odd, when_even in ((upper, lower), (lower, upper)):
        packed = jnp.zeros((channels, LANES), F32)
        for row in range(MARGIN):
            line = choose(lat_odd, when_odd[row], when_even[row])
            for block in range(blocks):
                send[base : base + channels] = line[:, block * LANES : (block + 1) * LANES].astype(BF16)
                base += channels
            low = jnp.where(lanes < MARGIN, line[:, cols:], 0.0)
            high = jnp.where(lanes >= LANES - MARGIN, line[:, cols:], 0.0)
            packed = packed + roll(low, MARGIN * row, 1) + roll(high, -MARGIN * row, 1)
        send[base : base + channels] = packed.astype(BF16)
        base += channels


def beside_kernel(numer, first, held, inner, edges):
    height, channels, wide = numer.shape
    cols = wide - LANES
    rows = height - 2 * MARGIN
    blocks = cols // LANES
    edge_rows = held.shape[0]
    base = first.shape[0] - 2 * edge_rows
    lanes = lane_ids((channels, LANES))
    lat = lax.axis_index("lat")
    odd = lax.rem(lat, 2) == 1
    inside = jnp.logical_and(lat > 0, lat < lax.axis_size("lat") - 1)
    packed = jnp.zeros((channels, LANES), F32)
    for row in range(rows):
        at = row % MARGIN
        parts = []
        for block in range(blocks + 1):
            start = (at * blocks + block if block < blocks else MARGIN * blocks) * channels
            near = first[base + start : base + start + channels].astype(F32)
            far = choose(inside, held[start : start + channels].astype(F32), 0.0)
            other = choose(odd, near, far) if row < MARGIN else choose(odd, far, near)
            if block == blocks:
                low = jnp.where(lanes < MARGIN, roll(other, -MARGIN * at, 1), 0.0)
                other = low + jnp.where(lanes >= LANES - MARGIN, roll(other, MARGIN * at, 1), 0.0)
            parts.append(numer[MARGIN + row, :, block * LANES : (block + 1) * LANES] + other)
        inner[row] = jnp.concatenate(parts[:-1], axis=1)
        low = jnp.where(lanes < MARGIN, parts[-1], 0.0)
        high = jnp.where(lanes >= LANES - MARGIN, parts[-1], 0.0)
        packed = packed + roll(low, MARGIN * row, 1) + roll(high, -MARGIN * row, 1)
    edges[...] = packed.astype(BF16)


def fold_kernel(inner, parts, den, blended):
    rows, channels, cols = inner.shape
    lanes = lane_ids((channels, LANES))
    lon, lon_size = lax.axis_index("lon"), lax.axis_size("lon")
    base = parts.shape[1] - channels
    left = parts[lax.rem(lon + lon_size - 1, lon_size), base : base + channels].astype(F32)
    right = parts[lax.rem(lon + 1, lon_size), base : base + channels].astype(F32)
    inverse = 1.0 / den[...]
    lines = []
    for row in range(rows):
        from_left = jnp.where(lanes < MARGIN, roll(left, -MARGIN * row, 1), 0.0)
        from_right = jnp.where(lanes >= LANES - MARGIN, roll(right, MARGIN * row, 1), 0.0)
        beside = [from_left]
        for _ in range(cols // LANES - 2):
            beside.append(jnp.zeros((channels, LANES), F32))
        beside.append(from_right)
        line = inner[row] + jnp.concatenate(beside, axis=1)
        lines.append((line * inverse[row : row + 1])[None])
    blended[...] = jnp.swapaxes(jnp.concatenate(lines, axis=0), 0, 1)


def split_kernel(own, other, grad_in, grad_mid, grad_out):
    taps, channels, width = grad_in.shape
    half = own.shape[0]
    odd = lax.rem(lax.axis_index("lat"), 2) == 1
    own, other = own[...], other[...]
    summed = (choose(odd, other, own), choose(odd, own, other))

    def rows_of(start, count):
        pieces = []
        stop = start + count
        if start < half:
            pieces.append(summed[0][start : min(stop, half)])
        if stop > half:
            pieces.append(summed[1][max(start, half) - half : stop - half])
        return jnp.concatenate(pieces, axis=0).astype(F32) if len(pieces) > 1 else pieces[0].astype(F32)

    for tap in range(taps):
        grad_in[tap] = rows_of(tap * channels, channels)
        grad_mid[tap] = rows_of(taps * channels + tap * width, width)
        grad_out[tap] = rows_of(taps * (channels + width) + tap * channels, channels)


def params():
    return pltpu.CompilerParams(vmem_limit_bytes=VMEM_LIMIT)


def swap(value, axis, first, wrap):
    size = lax.axis_size(axis)
    pairs = []
    for index in range(first, size, 2):
        other = (index + 1) % size
        if other > index or wrap:
            pairs.extend([(index, other), (other, index)])
    return lax.ppermute(value, axis, pairs)


def swap_lat(first, second):
    return swap(first, "lat", 0, False), swap(second, "lat", 1, False)


def swap_lon(edges):
    return swap(edges, "lon", 0, True), swap(edges, "lon", 1, True)


def exchange(value, axis, order):
    pairs = [(index, index ^ order[index % 2]) for index in range(lax.axis_size(axis))]
    return lax.ppermute(value, axis, pairs)


def order_bit(lat, order):
    step = jnp.where(lat % 2 == 0, order[0], order[1])
    return (lat // step) % 2


def halves(value, bit):
    half = value.shape[0] // 2
    own = lax.dynamic_slice_in_dim(value, bit * half, half, 0)
    other = lax.dynamic_slice_in_dim(value, (1 - bit) * half, half, 0)
    return own, other


def ordered(own, other, bit):
    return jnp.concatenate([jnp.where(bit == 0, own, other), jnp.where(bit == 0, other, own)], axis=0)


def shards(
    fields, cotangent, kernel_in, kernel_mid, kernel_out, patch_anchors, blend_weights, tile_counts
):
    channels, rows, cols = fields.shape
    taps, width, _ = kernel_in.shape
    patch_anchors = jnp.transpose(patch_anchors, (0, 1, 3, 2))
    height = rows + 2 * MARGIN
    wide = cols + LANES
    full = rows * cols
    padded = full + 2 * cols
    shape = jax.ShapeDtypeStruct
    center, first, second, canvas = pl.pallas_call(
        pack_kernel,
        out_shape=(
            shape((rows, 2 * channels, cols), BF16),
            shape((MARGIN + 1, 2 * channels, cols), BF16),
            shape((MARGIN + 1, 2 * channels, cols), BF16),
            shape((height, wide), F32),
        ),
        in_specs=[smem()] + [pl.BlockSpec(memory_space=pltpu.HBM)] * 4,
        out_specs=(vmem(),) * 4,
        scratch_shapes=[
            pltpu.VMEM(fields.shape, BF16),
            pltpu.VMEM(cotangent.shape, BF16),
            pltpu.VMEM(blend_weights.shape, jnp.int32),
            pltpu.SMEM(patch_anchors.shape, jnp.int32),
            pltpu.VMEM((height, wide), F32),
            pltpu.SemaphoreType.DMA((4,)),
        ],
        compiler_params=params(),
        name="pack",
    )(
        tile_counts,
        *(
            pltpu.with_memory_space_constraint(value, pltpu.HBM)
            for value in (patch_anchors, fields, cotangent, blend_weights)
        ),
    )
    first, second = swap_lat(first, second)
    w_in = jnp.transpose(kernel_in, (1, 0, 2)).reshape(width, taps * channels)
    kernel_mid = kernel_mid.reshape(3, 3, width, width)
    kernel_out = kernel_out.reshape(3, 3, channels, width)
    w_mid = jnp.transpose(kernel_mid, (2, 0, 1, 3)).reshape(width, taps * width)
    w_mid_back = jnp.transpose(kernel_mid, (3, 0, 1, 2)).reshape(width, taps * width)
    w_out = jnp.transpose(kernel_out, (1, 2, 0, 3)).reshape(3 * channels, 3 * width)
    w_out_back = jnp.transpose(kernel_out, (3, 0, 1, 2)).reshape(width, taps * channels)
    first, second, w_in, w_mid, w_mid_back, w_out, w_out_back = lax.optimization_barrier(
        (first, second, w_in, w_mid, w_mid_back, w_out, w_out_back)
    )
    edges, total = pl.pallas_call(
        edge_kernel,
        out_shape=(shape((2 * channels + 2 * height, LANES), BF16), shape((height, wide), F32)),
        in_specs=[vmem()] * 4,
        out_specs=(vmem(),) * 2,
        compiler_params=params(),
        name="edges",
    )(center, first, second, canvas)
    third, fourth = swap_lon(edges)

    lat_size, lon_size = lax.axis_size("lat"), lax.axis_size("lon")
    length = taps * (2 * channels + width)
    unit = 16 * lat_size
    length = (length + unit - 1) // unit * unit
    half = length // 2
    edge_rows = channels * (MARGIN * (cols // LANES) + 1)
    send, keep, numer, den = pl.pallas_call(
        patch_kernel,
        out_shape=(
            shape((half + 2 * edge_rows, LANES), BF16),
            shape((half, LANES), F32),
            shape((height, channels, wide), F32),
            shape((rows, cols), F32),
        ),
        in_specs=[smem(), smem()] + [vmem()] * 12,
        out_specs=(vmem(),) * 4,
        scratch_shapes=[
            pltpu.VMEM((length, LANES), F32),
            pltpu.VMEM((height, 2 * channels, wide), BF16),
        ]
        + 2
        * [
            pltpu.VMEM((3 * channels, padded), BF16),
            pltpu.VMEM((3 * channels, padded), BF16),
            pltpu.VMEM((3 * width, padded), BF16),
            pltpu.VMEM((3 * width, padded), BF16),
            pltpu.VMEM((width, padded), BF16),
            pltpu.VMEM((width, full), F32),
            pltpu.VMEM((width, full), F32),
            pltpu.VMEM((width, full), BF16),
        ],
        compiler_params=params(),
        name="patches",
    )(
        patch_anchors, tile_counts, center, first, second, third, fourth, total, blend_weights,
        w_in, w_mid, w_mid_back, w_out, w_out_back,
    )

    lat = lax.axis_index("lat")
    even = lat % 2 == 0
    first = exchange(send, "lat", (1, 1))
    mine = keep + first[:half].astype(F32)
    held = first[half + edge_rows :]
    steps = [2 << bit for bit in range(lat_size.bit_length() - 2)]
    orders = list(zip(steps, steps[1:] + steps[:1]))
    for turn, order in enumerate(orders):
        own, other = halves(mine, order_bit(lat, order))
        payload = jnp.concatenate([other.astype(BF16), held], axis=0)
        payload = exchange(payload, "lat", order)
        count = own.shape[0]
        mine = own + payload[:count].astype(F32)
        moves = []
        for side in (0, 1):
            done = [orders[before][side] for before in range(turn)]
            move = jnp.bool_(True)
            for step in steps:
                if step < order[side]:
                    carries = 1 if (step in done) == (side == 1) else 0
                    move = jnp.logical_and(move, (lat // step) % 2 == carries)
            moves.append(move)
        held = jnp.where(jnp.where(even, moves[0], moves[1]), payload[count:], held)
    inner, edges = pl.pallas_call(
        beside_kernel,
        out_shape=(shape((rows, channels, cols), F32), shape((channels, LANES), BF16)),
        in_specs=[vmem()] * 3,
        out_specs=(vmem(),) * 2,
        compiler_params=params(),
        name="beside",
    )(numer, first, held)
    count = mine.shape[0]
    payload = jnp.concatenate([mine.astype(BF16), edges], axis=0)
    payload = jnp.broadcast_to(payload[None], (lon_size,) + payload.shape)
    payload = lax.all_to_all(payload, "lon", 0, 0)
    mine = jnp.sum(payload[:, :count].astype(F32), axis=0).astype(BF16)
    blended = pl.pallas_call(
        fold_kernel,
        out_shape=shape((channels, rows, cols), F32),
        in_specs=[vmem()] * 3,
        out_specs=vmem(),
        compiler_params=params(),
        name="fold",
    )(inner, payload, den)
    for order in reversed(orders):
        mine = ordered(mine, exchange(mine, "lat", order), order_bit(lat, order))
    grad_in, grad_mid, grad_out = pl.pallas_call(
        split_kernel,
        out_shape=(
            shape((taps, channels, width), F32),
            shape((taps, width, width), F32),
            shape((taps, channels, width), F32),
        ),
        in_specs=[vmem()] * 2,
        out_specs=(vmem(),) * 3,
        compiler_params=params(),
        name="split",
    )(mine, exchange(mine, "lat", (1, 1)))
    return blended, jnp.transpose(grad_in, (0, 2, 1)), grad_mid, grad_out


def solution(mesh):
    return jax.shard_map(
        shards,
        mesh=mesh,
        in_specs=(
            P(None, "lat", "lon"),
            P(None, "lat", "lon"),
            P(),
            P(),
            P(),
            P("lat", "lon", None, None),
            P(None, "lat", "lon"),
            P("lat", "lon"),
        ),
        out_specs=(P(None, "lat", "lon"), P(), P(), P()),
        check_vma=False,
    )
```

```python
import functools

import jax
import jax.numpy as jnp
from jax import lax
from jax.experimental import pallas as pl
from jax.experimental.pallas import tpu as pltpu
from jax.sharding import PartitionSpec as P

MARGIN = 4
SLOTS = 4
LANES = 128
F32 = jnp.float32
BF16 = jnp.bfloat16
VMEM_LIMIT = 48 * 1024 * 1024


def vmem():
    return pl.BlockSpec(memory_space=pltpu.VMEM)


def smem():
    return pl.BlockSpec(memory_space=pltpu.SMEM)


def lane_ids(shape):
    return lax.broadcasted_iota(jnp.int32, shape, len(shape) - 1)


def roll(value, shift, axis):
    size = value.shape[axis]
    if isinstance(shift, int):
        shift = shift % size
        if shift == 0:
            return value
    return pltpu.roll(value, shift, axis)


def choose(odd, when_odd, when_even):
    return jnp.where(odd, when_odd, when_even)


def pack_kernel(
    counts, anchors_in, fields_in, cotangent_in, weights_in, center, first_out, second_out, canvas,
    fields, cotangent, weights, anchors, spread, sems,
):
    copies = []
    for index, (source, target) in enumerate(
        ((weights_in, weights), (fields_in, fields), (cotangent_in, cotangent), (anchors_in, anchors))
    ):
        copy = pltpu.make_async_copy(source, target, sems.at[index])
        copy.start()
        copies.append(copy)
    channels, rows, cols = fields.shape
    wide = cols + LANES
    odd = lax.rem(lax.axis_index("lat"), 2) == 1
    spread[...] = jnp.zeros_like(spread)
    copies[0].wait()
    copies[3].wait()
    for slot in range(SLOTS):

        @pl.when(slot < counts[0, 0])
        def _():
            row = anchors[0, 0, 0, slot]
            col = anchors[0, 0, 1, slot]
            values = weights[slot].astype(F32)
            values = jnp.concatenate([values, jnp.zeros((rows, LANES), F32)], axis=1)
            values = jnp.concatenate([values, jnp.zeros((2 * MARGIN, wide), F32)], axis=0)
            values = roll(values, lax.rem(col + (wide - MARGIN), wide), 1)
            values = roll(values, row, 0)
            spread[...] += values

    total = spread[...]
    canvas[...] = total
    copies[1].wait()
    copies[2].wait()
    both = []
    for source in (fields, cotangent):
        both.append(jnp.swapaxes(source[...].astype(F32), 0, 1))
    tile = jnp.concatenate(both, axis=1).astype(BF16)
    center[...] = tile
    half = total.shape[0] // 2
    extras = []
    for part in (total[:half], total[half:]):
        beside = jnp.concatenate([part[:, cols:], jnp.zeros((half, cols - LANES), F32)], axis=1)
        extras.append(jnp.concatenate([part[:, :cols], beside], axis=0).astype(BF16))
    flat = (MARGIN * 2 * channels, cols)
    top, bottom = tile[:MARGIN].reshape(flat), tile[rows - MARGIN :].reshape(flat)
    first_out[0 : flat[0]] = choose(odd, top, bottom)
    first_out[flat[0] :] = choose(odd, extras[0], extras[1])
    second_out[0 : flat[0]] = choose(odd, bottom, top)
    second_out[flat[0] :] = choose(odd, extras[1], extras[0])


def edge_kernel(center, first, second, canvas, edges, total_out):
    rows = center.shape[0]
    channels = center.shape[1] // 2
    cols = center.shape[2]
    height = rows + 2 * MARGIN
    half = height // 2
    odd = lax.rem(lax.axis_index("lat"), 2) == 1

    def stretch(block):
        block = block.astype(F32)
        return jnp.concatenate([block[:half], block[half:height, :LANES]], axis=1)

    base = MARGIN * 2 * channels
    upper = stretch(choose(odd, first[base:], second[base:]))
    lower = stretch(choose(odd, second[base:], first[base:]))
    total = canvas[...] + jnp.concatenate([upper, lower], axis=0)
    total_out[...] = total
    lanes = lane_ids((2 * channels, LANES))
    packed = jnp.zeros((2 * channels, LANES), F32)
    for row in range(height):
        at = slice(row % MARGIN * 2 * channels, (row % MARGIN + 1) * 2 * channels)
        if row < MARGIN:
            line = choose(odd, first[at], second[at])
        elif row < MARGIN + rows:
            line = center[row - MARGIN]
        else:
            line = choose(odd, second[at], first[at])
        line = line.astype(F32)
        low = jnp.where(lanes < MARGIN, line[:, :LANES], 0.0)
        high = jnp.where(lanes >= LANES - MARGIN, line[:, cols - LANES :], 0.0)
        packed = packed + roll(low, MARGIN * row, 1) + roll(high, -MARGIN * row, 1)
    edges[0 : 2 * channels] = packed.astype(BF16)
    margin = total[:, cols:]
    lanes = lane_ids(margin.shape)
    to_left = jnp.where(lanes < LANES // 2, total[:, :LANES], margin)
    to_right = jnp.where(lanes < LANES // 2, margin, total[:, cols - LANES : cols])
    edges[2 * channels : 2 * channels + height] = to_left.astype(BF16)
    edges[2 * channels + height : 2 * channels + 2 * height] = to_right.astype(BF16)


def dot(left, right):
    return jnp.dot(left, right, preferred_element_type=F32)


def dot_lanes(left, right):
    return lax.dot_general(left, right, (((1,), (1,)), ((), ())), preferred_element_type=F32)


def patch_kernel(
    anchors, counts, center, first, second, third, fourth, total_in, weights,
    w_in, w_mid, w_mid_back, w_out, w_out_back,
    send, keep, numer, den_out,
    grads, window, *sets,
):
    rows = center.shape[0]
    channels = center.shape[1] // 2
    cols = center.shape[2]
    wide = cols + LANES
    width = w_in.shape[0]
    full = rows * cols
    height = rows + 2 * MARGIN
    lanes = lane_ids((2 * channels, LANES))
    lat_odd = lax.rem(lax.axis_index("lat"), 2) == 1
    lon_odd = lax.rem(lax.axis_index("lon"), 2) == 1

    left = choose(lon_odd, third[...], fourth[...]).astype(F32)
    right = choose(lon_odd, fourth[...], third[...]).astype(F32)
    base = 2 * channels
    left_part = left[base + height : base + 2 * height]
    right_part = right[base : base + height]
    edge_lanes = lane_ids((height, LANES))
    low = edge_lanes < MARGIN
    high = edge_lanes >= LANES - MARGIN
    zero = jnp.zeros((height, LANES), F32)
    pieces = [jnp.where(low, left_part, zero)]
    for _ in range(cols // LANES - 2):
        pieces.append(zero)
    pieces.append(jnp.where(high, right_part, zero))
    pieces.append(jnp.where(high, left_part, zero) + jnp.where(low, right_part, zero))
    den = jnp.maximum(total_in[...] + jnp.concatenate(pieces, axis=1), 1.0)
    den_out[...] = den[MARGIN : MARGIN + rows, :cols]
    inverse = 1.0 / den

    left = left[:base]
    right = right[:base]
    for row in range(height):
        at = slice(row % MARGIN * base, (row % MARGIN + 1) * base)
        if row < MARGIN:
            body = choose(lat_odd, first[at], second[at])
        elif row < MARGIN + rows:
            body = center[row - MARGIN]
        else:
            body = choose(lat_odd, second[at], first[at])
        beside = jnp.where(
            lanes < LANES // 2, roll(right, -MARGIN * row, 1), roll(left, MARGIN * row, 1)
        )
        line = jnp.concatenate([body.astype(F32), beside], axis=1)
        scaled = line[channels:] * inverse[row : row + 1]
        window[row, 0:channels] = line[:channels].astype(BF16)
        window[row, channels : 2 * channels] = scaled.astype(BF16)

    numer[...] = jnp.zeros_like(numer)
    grads[...] = jnp.zeros_like(grads)
    sets = (sets[: len(sets) // 2], sets[len(sets) // 2 :])
    for ref in sets[0][:5] + sets[1][:5]:
        ref[:, 0:cols] = jnp.zeros((ref.shape[0], cols), BF16)
        ref[:, cols + full : 2 * cols + full] = jnp.zeros((ref.shape[0], cols), BF16)

    def shifted(value, step):
        blocks = [value[:, at : at + LANES] for at in range(0, cols, LANES)]
        turned = [roll(block, step, 1) for block in blocks]
        ids = lane_ids(blocks[0].shape)
        zero = jnp.zeros_like(blocks[0])
        if step > 0:
            ends = [zero] + turned[:-1]
            at_end = ids == 0
        else:
            ends = turned[1:] + [zero]
            at_end = ids == LANES - 1
        return jnp.concatenate([jnp.where(at_end, end, own) for end, own in zip(ends, turned)], axis=1)

    def before(value):
        return shifted(value, 1)

    def after(value):
        return shifted(value, -1)

    def spread(ref, value, row, flip):
        count = value.shape[0]
        at = slice((row + 1) * cols, (row + 2) * cols)
        first, last = before(value), after(value)
        if flip:
            first, last = last, first
        ref[0:count, at] = first
        ref[count : 2 * count, at] = value
        ref[2 * count : 3 * count, at] = last

    def stack(ref, row, flip):
        starts = [(row + (2 - tap if flip else tap)) * cols for tap in range(3)]
        return jnp.concatenate([ref[:, start : start + cols] for start in starts], axis=0)

    def across(parts, flip):
        count = parts.shape[0] // 3
        first, last = parts[:count], parts[2 * count :]
        if flip:
            first, last = last, first
        return before(first) + parts[count : 2 * count] + after(last)

    def all_rows(ref, flip):
        starts = [(2 - tap if flip else tap) * cols for tap in range(3)]
        return jnp.concatenate([ref[:, start : start + full] for start in starts], axis=0)

    def weights_of(slot):
        return weights[slot].astype(F32) * (slot < counts[0, 0]).astype(F32)

    def first_part(slot, x_s, d_s, h_s, z_s, h2_s, slope_s, dh_s, dz_s):
        row0 = anchors[0, 0, 0, slot]
        col0 = anchors[0, 0, 1, slot]
        patch_weights = weights_of(slot)
        back_shift = lax.rem(wide + MARGIN - col0, wide)

        def cut(row):
            line = roll(window[row0 + row], back_shift, 1)[:, :cols]
            spread(x_s, line[:channels], row, False)
            grad = line[channels:].astype(F32) * patch_weights[row : row + 1]
            spread(d_s, grad.astype(BF16), row, True)

        def conv_in(row):
            at = slice(row * cols, (row + 1) * cols)
            z1 = dot(w_in[...], stack(x_s, row, False))
            sig = 0.5 * jnp.tanh(0.5 * z1) + 0.5
            h1 = z1 * sig
            slope_s[:, at] = sig + h1 * (1.0 - sig)
            h_s[:, (row + 1) * cols : (row + 2) * cols] = h1.astype(BF16)

        def conv_mid(row):
            at = slice(row * cols, (row + 1) * cols)
            ahead = slice((row + 1) * cols, (row + 2) * cols)
            dh2 = dot(w_out_back[...], stack(d_s, row, True))
            z2 = across(dot(w_mid[...], stack(h_s, row, False)), False)
            sig = 0.5 * jnp.tanh(0.5 * z2) + 0.5
            added = z2 * sig
            h2_s[:, ahead] = (h_s[:, ahead].astype(F32) + added).astype(BF16)
            dz2 = (dh2 * (sig + added * (1.0 - sig))).astype(BF16)
            dh_s[:, at] = dh2
            spread(z_s, dz2, row, True)

        return [functools.partial(step, row) for step in (cut, conv_in, conv_mid) for row in range(rows)]

    def second_part(slot, x_s, d_s, h_s, z_s, h2_s, slope_s, dh_s, dz_s):
        row0 = anchors[0, 0, 0, slot]
        col0 = anchors[0, 0, 1, slot]
        patch_weights = weights_of(slot)
        inside = slice(cols, cols + full)
        small = 9 * channels

        def conv_back(row):
            at = slice(row * cols, (row + 1) * cols)
            back = dot(w_mid_back[...], stack(z_s, row, True))
            dz_s[:, at] = ((dh_s[:, at] + back) * slope_s[:, at]).astype(BF16)

        def conv_out(row):
            result = across(dot(w_out[...], stack(h2_s, row, False)), False)
            result = result * patch_weights[row : row + 1]
            result = jnp.concatenate([result, jnp.zeros((channels, LANES), F32)], axis=1)
            numer[row0 + row] += roll(result, lax.rem(col0 + (wide - MARGIN), wide), 1)

        def grad_mid():
            part = dot_lanes(z_s[:, inside], all_rows(h_s, False))
            for tap in range(3):
                for tap_col in range(3):
                    start = small + (3 * tap + tap_col) * width
                    grads[start : start + width] += part[
                        tap_col * width : (tap_col + 1) * width, tap * width : (tap + 1) * width
                    ]

        def grad_out():
            start = small + 9 * width
            grads[start : start + small] += dot_lanes(all_rows(d_s, True), h2_s[:, inside])

        def grad_in():
            grads[0:small] += dot_lanes(all_rows(x_s, False), dz_s[...])

        backs = [functools.partial(conv_back, row) for row in range(rows)]
        outs = [functools.partial(conv_out, row) for row in range(rows)]
        return [grad_mid, grad_out] + backs + [grad_in] + outs

    def merged(left, right):
        left = [((at + 0.5) / len(left), step) for at, step in enumerate(left)]
        right = [((at + 0.5) / len(right), step) for at, step in enumerate(right)]
        for _, step in sorted(left + right, key=lambda pair: pair[0]):
            step()

    for slot in range(SLOTS + 1):

        @pl.when(max(slot, 1) <= counts[0, 0])
        def _():
            ahead = first_part(slot, *sets[slot % 2]) if slot < SLOTS else []
            behind = second_part(slot - 1, *sets[(slot - 1) % 2]) if slot > 0 else []
            merged(behind, ahead)

    half = grads.shape[0] // 2
    odd_index = lax.rem(lax.axis_index("lat"), 2)
    send[0:half] = grads[pl.ds(pl.multiple_of((1 - odd_index) * half, half), half)].astype(BF16)
    keep[...] = grads[pl.ds(pl.multiple_of(odd_index * half, half), half)]
    lanes = lane_ids((channels, LANES))
    blocks = cols // LANES
    base = half
    upper = [numer[row] for row in range(MARGIN)]
    lower = [numer[MARGIN + rows + row] for row in range(MARGIN)]
    for when_odd, when_even in ((upper, lower), (lower, upper)):
        packed = jnp.zeros((channels, LANES), F32)
        for row in range(MARGIN):
            line = choose(lat_odd, when_odd[row], when_even[row])
            for block in range(blocks):
                send[base : base + channels] = line[:, block * LANES : (block + 1) * LANES].astype(BF16)
                base += channels
            low = jnp.where(lanes < MARGIN, line[:, cols:], 0.0)
            high = jnp.where(lanes >= LANES - MARGIN, line[:, cols:], 0.0)
            packed = packed + roll(low, MARGIN * row, 1) + roll(high, -MARGIN * row, 1)
        send[base : base + channels] = packed.astype(BF16)
        base += channels


def beside_kernel(numer, first, held, inner, edges):
    height, channels, wide = numer.shape
    cols = wide - LANES
    rows = height - 2 * MARGIN
    blocks = cols // LANES
    edge_rows = held.shape[0]
    base = first.shape[0] - 2 * edge_rows
    lanes = lane_ids((channels, LANES))
    lat = lax.axis_index("lat")
    odd = lax.rem(lat, 2) == 1
    inside = jnp.logical_and(lat > 0, lat < lax.axis_size("lat") - 1)
    packed = jnp.zeros((channels, LANES), F32)
    for row in range(rows):
        at = row % MARGIN
        parts = []
        for block in range(blocks + 1):
            start = (at * blocks + block if block < blocks else MARGIN * blocks) * channels
            near = first[base + start : base + start + channels].astype(F32)
            far = choose(inside, held[start : start + channels].astype(F32), 0.0)
            other = choose(odd, near, far) if row < MARGIN else choose(odd, far, near)
            if block == blocks:
                low = jnp.where(lanes < MARGIN, roll(other, -MARGIN * at, 1), 0.0)
                other = low + jnp.where(lanes >= LANES - MARGIN, roll(other, MARGIN * at, 1), 0.0)
            parts.append(numer[MARGIN + row, :, block * LANES : (block + 1) * LANES] + other)
        inner[row] = jnp.concatenate(parts[:-1], axis=1)
        low = jnp.where(lanes < MARGIN, parts[-1], 0.0)
        high = jnp.where(lanes >= LANES - MARGIN, parts[-1], 0.0)
        packed = packed + roll(low, MARGIN * row, 1) + roll(high, -MARGIN * row, 1)
    part = channels // 2
    lanes = lane_ids((part, LANES))
    quarter = LANES // 4
    rest = packed[part:]
    rest = jnp.where(lanes < 2 * quarter, roll(rest, quarter, 1), roll(rest, -quarter, 1))
    middle = jnp.logical_and(lanes >= quarter, lanes < 3 * quarter)
    edges[...] = jnp.where(middle, rest, packed[:part]).astype(BF16)


def fold_kernel(inner, parts, den, blended):
    rows, channels, cols = inner.shape
    lanes = lane_ids((channels, LANES))
    lon, lon_size = lax.axis_index("lon"), lax.axis_size("lon")
    quarter = LANES // 4
    part_lanes = lane_ids((channels // 2, LANES))

    def margins(index):
        part = parts[index, 0 : channels // 2].astype(F32)
        rest = jnp.where(part_lanes < 2 * quarter, roll(part, -quarter, 1), roll(part, quarter, 1))
        return jnp.concatenate([part, rest], axis=0)

    left = margins(lax.rem(lon + lon_size - 1, lon_size))
    right = margins(lax.rem(lon + 1, lon_size))
    inverse = 1.0 / den[...]
    lines = []
    for row in range(rows):
        from_left = jnp.where(lanes < MARGIN, roll(left, -MARGIN * row, 1), 0.0)
        from_right = jnp.where(lanes >= LANES - MARGIN, roll(right, MARGIN * row, 1), 0.0)
        beside = [from_left]
        for _ in range(cols // LANES - 2):
            beside.append(jnp.zeros((channels, LANES), F32))
        beside.append(from_right)
        line = inner[row] + jnp.concatenate(beside, axis=1)
        lines.append((line * inverse[row : row + 1])[None])
    blended[...] = jnp.swapaxes(jnp.concatenate(lines, axis=0), 0, 1)


def split_kernel(own, other, grad_in, grad_mid, grad_out):
    taps, channels, width = grad_in.shape
    half = own.shape[0]
    odd = lax.rem(lax.axis_index("lat"), 2) == 1
    own, other = own[...], other[...]
    summed = (choose(odd, other, own), choose(odd, own, other))

    def rows_of(start, count):
        pieces = []
        stop = start + count
        if start < half:
            pieces.append(summed[0][start : min(stop, half)])
        if stop > half:
            pieces.append(summed[1][max(start, half) - half : stop - half])
        return jnp.concatenate(pieces, axis=0).astype(F32) if len(pieces) > 1 else pieces[0].astype(F32)

    for tap in range(taps):
        grad_in[tap] = rows_of(tap * channels, channels)
        grad_mid[tap] = rows_of(taps * channels + tap * width, width)
        grad_out[tap] = rows_of(taps * (channels + width) + tap * channels, channels)


def params():
    return pltpu.CompilerParams(vmem_limit_bytes=VMEM_LIMIT)


def swap(value, axis, first, wrap):
    size = lax.axis_size(axis)
    pairs = []
    for index in range(first, size, 2):
        other = (index + 1) % size
        if other > index or wrap:
            pairs.extend([(index, other), (other, index)])
    return lax.ppermute(value, axis, pairs)


def swap_lat(first, second):
    return swap(first, "lat", 0, False), swap(second, "lat", 1, False)


def swap_lon(edges):
    return swap(edges, "lon", 0, True), swap(edges, "lon", 1, True)


def exchange(value, axis, order):
    pairs = [(index, index ^ order[index % 2]) for index in range(lax.axis_size(axis))]
    return lax.ppermute(value, axis, pairs)


def order_bit(lat, order):
    step = jnp.where(lat % 2 == 0, order[0], order[1])
    return (lat // step) % 2


def halves(value, bit):
    half = value.shape[0] // 2
    own = lax.dynamic_slice_in_dim(value, bit * half, half, 0)
    other = lax.dynamic_slice_in_dim(value, (1 - bit) * half, half, 0)
    return own, other


def ordered(own, other, bit):
    return jnp.concatenate([jnp.where(bit == 0, own, other), jnp.where(bit == 0, other, own)], axis=0)


def shards(
    fields, cotangent, kernel_in, kernel_mid, kernel_out, patch_anchors, blend_weights, tile_counts
):
    channels, rows, cols = fields.shape
    taps, width, _ = kernel_in.shape
    patch_anchors = jnp.transpose(patch_anchors, (0, 1, 3, 2))
    height = rows + 2 * MARGIN
    wide = cols + LANES
    full = rows * cols
    padded = full + 2 * cols
    shape = jax.ShapeDtypeStruct
    center, first, second, canvas = pl.pallas_call(
        pack_kernel,
        out_shape=(
            shape((rows, 2 * channels, cols), BF16),
            shape((MARGIN * 2 * channels + height, cols), BF16),
            shape((MARGIN * 2 * channels + height, cols), BF16),
            shape((height, wide), F32),
        ),
        in_specs=[smem()] + [pl.BlockSpec(memory_space=pltpu.HBM)] * 4,
        out_specs=(vmem(),) * 4,
        scratch_shapes=[
            pltpu.VMEM(fields.shape, BF16),
            pltpu.VMEM(cotangent.shape, BF16),
            pltpu.VMEM(blend_weights.shape, jnp.int32),
            pltpu.SMEM(patch_anchors.shape, jnp.int32),
            pltpu.VMEM((height, wide), F32),
            pltpu.SemaphoreType.DMA((4,)),
        ],
        compiler_params=params(),
        name="pack",
    )(
        tile_counts,
        *(
            pltpu.with_memory_space_constraint(value, pltpu.HBM)
            for value in (patch_anchors, fields, cotangent, blend_weights)
        ),
    )
    first, second = swap_lat(first, second)
    w_in = jnp.transpose(kernel_in, (1, 0, 2)).reshape(width, taps * channels)
    kernel_mid = kernel_mid.reshape(3, 3, width, width)
    kernel_out = kernel_out.reshape(3, 3, channels, width)
    w_mid = jnp.transpose(kernel_mid, (1, 2, 0, 3)).reshape(3 * width, 3 * width)
    w_mid_back = jnp.transpose(kernel_mid, (3, 0, 1, 2)).reshape(width, taps * width)
    w_out = jnp.transpose(kernel_out, (1, 2, 0, 3)).reshape(3 * channels, 3 * width)
    w_out_back = jnp.transpose(kernel_out, (3, 0, 1, 2)).reshape(width, taps * channels)
    first, second, w_in, w_mid, w_mid_back, w_out, w_out_back = lax.optimization_barrier(
        (first, second, w_in, w_mid, w_mid_back, w_out, w_out_back)
    )
    edges, total = pl.pallas_call(
        edge_kernel,
        out_shape=(shape((2 * channels + 2 * height, LANES), BF16), shape((height, wide), F32)),
        in_specs=[vmem()] * 4,
        out_specs=(vmem(),) * 2,
        compiler_params=params(),
        name="edges",
    )(center, first, second, canvas)
    third, fourth = swap_lon(edges)

    lat_size, lon_size = lax.axis_size("lat"), lax.axis_size("lon")
    length = taps * (2 * channels + width)
    unit = 8 * lat_size
    length = (length + unit - 1) // unit * unit
    half = length // 2
    edge_rows = channels * (MARGIN * (cols // LANES) + 1)
    send, keep, numer, den = pl.pallas_call(
        patch_kernel,
        out_shape=(
            shape((half + 2 * edge_rows, LANES), BF16),
            shape((half, LANES), F32),
            shape((height, channels, wide), F32),
            shape((rows, cols), F32),
        ),
        in_specs=[smem(), smem()] + [vmem()] * 12,
        out_specs=(vmem(),) * 4,
        scratch_shapes=[
            pltpu.VMEM((length, LANES), F32),
            pltpu.VMEM((height, 2 * channels, wide), BF16),
        ]
        + 2
        * [
            pltpu.VMEM((3 * channels, padded), BF16),
            pltpu.VMEM((3 * channels, padded), BF16),
            pltpu.VMEM((width, padded), BF16),
            pltpu.VMEM((3 * width, padded), BF16),
            pltpu.VMEM((width, padded), BF16),
            pltpu.VMEM((width, full), F32),
            pltpu.VMEM((width, full), F32),
            pltpu.VMEM((width, full), BF16),
        ],
        compiler_params=params(),
        name="patches",
    )(
        patch_anchors, tile_counts, center, first, second, third, fourth, total, blend_weights,
        w_in, w_mid, w_mid_back, w_out, w_out_back,
    )

    lat = lax.axis_index("lat")
    even = lat % 2 == 0
    first = exchange(send, "lat", (1, 1))
    mine = keep + first[:half].astype(F32)
    held = first[half + edge_rows :]
    steps = [2 << bit for bit in range(lat_size.bit_length() - 2)]
    orders = list(zip(steps, steps[1:] + steps[:1]))
    for turn, order in enumerate(orders):
        own, other = halves(mine, order_bit(lat, order))
        payload = jnp.concatenate([other.astype(BF16), held], axis=0)
        payload = exchange(payload, "lat", order)
        count = own.shape[0]
        mine = own + payload[:count].astype(F32)
        moves = []
        for side in (0, 1):
            done = [orders[before][side] for before in range(turn)]
            move = jnp.bool_(True)
            for step in steps:
                if step < order[side]:
                    carries = 1 if (step in done) == (side == 1) else 0
                    move = jnp.logical_and(move, (lat // step) % 2 == carries)
            moves.append(move)
        held = jnp.where(jnp.where(even, moves[0], moves[1]), payload[count:], held)
    inner, edges = pl.pallas_call(
        beside_kernel,
        out_shape=(shape((rows, channels, cols), F32), shape((channels // 2, LANES), BF16)),
        in_specs=[vmem()] * 3,
        out_specs=(vmem(),) * 2,
        compiler_params=params(),
        name="beside",
    )(numer, first, held)
    payload = jnp.concatenate([edges, mine.astype(BF16)], axis=0)
    payload = jnp.broadcast_to(payload[None], (lon_size,) + payload.shape)
    payload = lax.all_to_all(payload, "lon", 0, 0)
    mine = jnp.sum(payload[:, channels // 2 :].astype(F32), axis=0).astype(BF16)
    blended = pl.pallas_call(
        fold_kernel,
        out_shape=shape((channels, rows, cols), F32),
        in_specs=[vmem()] * 3,
        out_specs=vmem(),
        compiler_params=params(),
        name="fold",
    )(inner, payload, den)
    for order in reversed(orders):
        mine = ordered(mine, exchange(mine, "lat", order), order_bit(lat, order))
    grad_in, grad_mid, grad_out = pl.pallas_call(
        split_kernel,
        out_shape=(
            shape((taps, channels, width), F32),
            shape((taps, width, width), F32),
            shape((taps, channels, width), F32),
        ),
        in_specs=[vmem()] * 2,
        out_specs=(vmem(),) * 3,
        compiler_params=params(),
        name="split",
    )(mine, exchange(mine, "lat", (1, 1)))
    return blended, jnp.transpose(grad_in, (0, 2, 1)), grad_mid, grad_out


def solution(mesh):
    return jax.shard_map(
        shards,
        mesh=mesh,
        in_specs=(
            P(None, "lat", "lon"),
            P(None, "lat", "lon"),
            P(),
            P(),
            P(),
            P("lat", "lon", None, None),
            P(None, "lat", "lon"),
            P("lat", "lon"),
        ),
        out_specs=(P(None, "lat", "lon"), P(), P(), P()),
        check_vma=False,
    )
```

```python
import functools

import jax
import jax.numpy as jnp
from jax import lax
from jax.experimental import pallas as pl
from jax.experimental.pallas import tpu as pltpu
from jax.sharding import PartitionSpec as P

MARGIN = 4
SLOTS = 4
LANES = 128
F32 = jnp.float32
BF16 = jnp.bfloat16
VMEM_LIMIT = 48 * 1024 * 1024


def vmem():
    return pl.BlockSpec(memory_space=pltpu.VMEM)


def smem():
    return pl.BlockSpec(memory_space=pltpu.SMEM)


def lane_ids(shape):
    return lax.broadcasted_iota(jnp.int32, shape, len(shape) - 1)


def roll(value, shift, axis):
    size = value.shape[axis]
    if isinstance(shift, int):
        shift = shift % size
        if shift == 0:
            return value
    return pltpu.roll(value, shift, axis)


def choose(odd, when_odd, when_even):
    return jnp.where(odd, when_odd, when_even)


def pack_kernel(
    counts, anchors_in, fields_in, cotangent_in, weights_in, center, first_out, second_out, canvas,
    fields, cotangent, weights, anchors, spread, sems,
):
    copies = []
    for index, (source, target) in enumerate(
        ((weights_in, weights), (fields_in, fields), (cotangent_in, cotangent), (anchors_in, anchors))
    ):
        copy = pltpu.make_async_copy(source, target, sems.at[index])
        copy.start()
        copies.append(copy)
    channels, rows, cols = fields.shape
    wide = cols + LANES
    odd = lax.rem(lax.axis_index("lat"), 2) == 1
    spread[...] = jnp.zeros_like(spread)
    copies[0].wait()
    copies[3].wait()
    for slot in range(SLOTS):

        @pl.when(slot < counts[0, 0])
        def _():
            row = anchors[0, 0, 0, slot]
            col = anchors[0, 0, 1, slot]
            values = weights[slot].astype(F32)
            values = jnp.concatenate([values, jnp.zeros((rows, LANES), F32)], axis=1)
            values = jnp.concatenate([values, jnp.zeros((2 * MARGIN, wide), F32)], axis=0)
            values = roll(values, lax.rem(col + (wide - MARGIN), wide), 1)
            values = roll(values, row, 0)
            spread[...] += values

    total = spread[...]
    canvas[...] = total
    copies[1].wait()
    copies[2].wait()
    both = []
    for source in (fields, cotangent):
        both.append(jnp.swapaxes(source[...].astype(F32), 0, 1))
    tile = jnp.concatenate(both, axis=1).astype(BF16)
    center[...] = tile
    half = total.shape[0] // 2
    extras = []
    for part in (total[:half], total[half:]):
        beside = jnp.concatenate([part[:, cols:], jnp.zeros((half, cols - LANES), F32)], axis=1)
        extras.append(jnp.concatenate([part[:, :cols], beside], axis=0).astype(BF16))
    flat = (MARGIN * 2 * channels, cols)
    top, bottom = tile[:MARGIN].reshape(flat), tile[rows - MARGIN :].reshape(flat)
    first_out[0 : flat[0]] = choose(odd, top, bottom)
    first_out[flat[0] :] = choose(odd, extras[0], extras[1])
    second_out[0 : flat[0]] = choose(odd, bottom, top)
    second_out[flat[0] :] = choose(odd, extras[1], extras[0])


def edge_kernel(center, first, second, canvas, edges, total_out):
    rows = center.shape[0]
    channels = center.shape[1] // 2
    cols = center.shape[2]
    height = rows + 2 * MARGIN
    half = height // 2
    odd = lax.rem(lax.axis_index("lat"), 2) == 1

    def stretch(block):
        block = block.astype(F32)
        return jnp.concatenate([block[:half], block[half:height, :LANES]], axis=1)

    base = MARGIN * 2 * channels
    upper = stretch(choose(odd, first[base:], second[base:]))
    lower = stretch(choose(odd, second[base:], first[base:]))
    total = canvas[...] + jnp.concatenate([upper, lower], axis=0)
    total_out[...] = total
    lanes = lane_ids((2 * channels, LANES))
    packed = jnp.zeros((2 * channels, LANES), F32)
    for row in range(height):
        at = slice(row % MARGIN * 2 * channels, (row % MARGIN + 1) * 2 * channels)
        if row < MARGIN:
            line = choose(odd, first[at], second[at])
        elif row < MARGIN + rows:
            line = center[row - MARGIN]
        else:
            line = choose(odd, second[at], first[at])
        line = line.astype(F32)
        low = jnp.where(lanes < MARGIN, line[:, :LANES], 0.0)
        high = jnp.where(lanes >= LANES - MARGIN, line[:, cols - LANES :], 0.0)
        packed = packed + roll(low, MARGIN * row, 1) + roll(high, -MARGIN * row, 1)
    edges[0 : 2 * channels] = packed.astype(BF16)
    margin = total[:, cols:]
    lanes = lane_ids(margin.shape)
    to_left = jnp.where(lanes < LANES // 2, total[:, :LANES], margin)
    to_right = jnp.where(lanes < LANES // 2, margin, total[:, cols - LANES : cols])
    edges[2 * channels : 2 * channels + height] = to_left.astype(BF16)
    edges[2 * channels + height : 2 * channels + 2 * height] = to_right.astype(BF16)


def dot(left, right):
    return jnp.dot(left, right, preferred_element_type=F32)


def dot_lanes(left, right):
    return lax.dot_general(left, right, (((1,), (1,)), ((), ())), preferred_element_type=F32)


def patch_kernel(
    anchors, counts, center, first, second, third, fourth, total_in, weights,
    w_in, w_mid, w_mid_back, w_out, w_out_back,
    send, keep, numer, den_out,
    grads, window, *sets,
):
    rows = center.shape[0]
    channels = center.shape[1] // 2
    cols = center.shape[2]
    wide = cols + LANES
    width = w_in.shape[0]
    full = rows * cols
    height = rows + 2 * MARGIN
    lanes = lane_ids((2 * channels, LANES))
    lat_odd = lax.rem(lax.axis_index("lat"), 2) == 1
    lon_odd = lax.rem(lax.axis_index("lon"), 2) == 1

    left = choose(lon_odd, third[...], fourth[...]).astype(F32)
    right = choose(lon_odd, fourth[...], third[...]).astype(F32)
    base = 2 * channels
    left_part = left[base + height : base + 2 * height]
    right_part = right[base : base + height]
    edge_lanes = lane_ids((height, LANES))
    low = edge_lanes < MARGIN
    high = edge_lanes >= LANES - MARGIN
    zero = jnp.zeros((height, LANES), F32)
    pieces = [jnp.where(low, left_part, zero)]
    for _ in range(cols // LANES - 2):
        pieces.append(zero)
    pieces.append(jnp.where(high, right_part, zero))
    pieces.append(jnp.where(high, left_part, zero) + jnp.where(low, right_part, zero))
    den = jnp.maximum(total_in[...] + jnp.concatenate(pieces, axis=1), 1.0)
    den_out[...] = den[MARGIN : MARGIN + rows, :cols]
    inverse = 1.0 / den

    left = left[:base]
    right = right[:base]
    for row in range(height):
        at = slice(row % MARGIN * base, (row % MARGIN + 1) * base)
        if row < MARGIN:
            body = choose(lat_odd, first[at], second[at])
        elif row < MARGIN + rows:
            body = center[row - MARGIN]
        else:
            body = choose(lat_odd, second[at], first[at])
        beside = jnp.where(
            lanes < LANES // 2, roll(right, -MARGIN * row, 1), roll(left, MARGIN * row, 1)
        )
        line = jnp.concatenate([body.astype(F32), beside], axis=1)
        scaled = line[channels:] * inverse[row : row + 1]
        window[row, 0:channels] = line[:channels].astype(BF16)
        window[row, channels : 2 * channels] = scaled.astype(BF16)

    numer[...] = jnp.zeros_like(numer)
    grads[...] = jnp.zeros_like(grads)
    sets = (sets[: len(sets) // 2], sets[len(sets) // 2 :])
    for ref in sets[0][:5] + sets[1][:5]:
        ref[:, 0:cols] = jnp.zeros((ref.shape[0], cols), BF16)
        ref[:, cols + full : 2 * cols + full] = jnp.zeros((ref.shape[0], cols), BF16)

    def shifted(value, step):
        blocks = [value[:, at : at + LANES] for at in range(0, cols, LANES)]
        turned = [roll(block, step, 1) for block in blocks]
        ids = lane_ids(blocks[0].shape)
        zero = jnp.zeros_like(blocks[0])
        if step > 0:
            ends = [zero] + turned[:-1]
            at_end = ids == 0
        else:
            ends = turned[1:] + [zero]
            at_end = ids == LANES - 1
        return jnp.concatenate([jnp.where(at_end, end, own) for end, own in zip(ends, turned)], axis=1)

    def before(value):
        return shifted(value, 1)

    def after(value):
        return shifted(value, -1)

    def spread(ref, value, row, flip):
        count = value.shape[0]
        at = slice((row + 1) * cols, (row + 2) * cols)
        first, last = before(value), after(value)
        if flip:
            first, last = last, first
        ref[0:count, at] = first
        ref[count : 2 * count, at] = value
        ref[2 * count : 3 * count, at] = last

    def stack(ref, row, flip):
        starts = [(row + (2 - tap if flip else tap)) * cols for tap in range(3)]
        return jnp.concatenate([ref[:, start : start + cols] for start in starts], axis=0)

    def across(parts, flip):
        count = parts.shape[0] // 3
        first, last = parts[:count], parts[2 * count :]
        if flip:
            first, last = last, first
        return before(first) + parts[count : 2 * count] + after(last)

    def all_rows(ref, flip):
        starts = [(2 - tap if flip else tap) * cols for tap in range(3)]
        return jnp.concatenate([ref[:, start : start + full] for start in starts], axis=0)

    def weights_of(slot):
        return weights[slot].astype(F32) * (slot < counts[0, 0]).astype(F32)

    def first_part(slot, x_s, d_s, h_s, z_s, h2_s, slope_s, dh_s, dz_s):
        row0 = anchors[0, 0, 0, slot]
        col0 = anchors[0, 0, 1, slot]
        patch_weights = weights_of(slot)
        back_shift = lax.rem(wide + MARGIN - col0, wide)

        def cut(row):
            line = roll(window[row0 + row], back_shift, 1)[:, :cols]
            spread(x_s, line[:channels], row, False)
            grad = line[channels:].astype(F32) * patch_weights[row : row + 1]
            spread(d_s, grad.astype(BF16), row, True)

        def conv_in(row):
            at = slice(row * cols, (row + 1) * cols)
            z1 = dot(w_in[...], stack(x_s, row, False))
            sig = 0.5 * jnp.tanh(0.5 * z1) + 0.5
            h1 = z1 * sig
            slope_s[:, at] = sig + h1 * (1.0 - sig)
            h_s[:, (row + 1) * cols : (row + 2) * cols] = h1.astype(BF16)

        def conv_mid(row):
            at = slice(row * cols, (row + 1) * cols)
            ahead = slice((row + 1) * cols, (row + 2) * cols)
            dh2 = dot(w_out_back[...], stack(d_s, row, True))
            z2 = across(dot(w_mid[...], stack(h_s, row, False)), False)
            sig = 0.5 * jnp.tanh(0.5 * z2) + 0.5
            added = z2 * sig
            h2_s[:, ahead] = (h_s[:, ahead].astype(F32) + added).astype(BF16)
            dz2 = (dh2 * (sig + added * (1.0 - sig))).astype(BF16)
            dh_s[:, at] = dh2
            spread(z_s, dz2, row, True)

        return [functools.partial(step, row) for step in (cut, conv_in, conv_mid) for row in range(rows)]

    def second_part(slot, x_s, d_s, h_s, z_s, h2_s, slope_s, dh_s, dz_s):
        row0 = anchors[0, 0, 0, slot]
        col0 = anchors[0, 0, 1, slot]
        patch_weights = weights_of(slot)
        inside = slice(cols, cols + full)
        small = 9 * channels

        def conv_back(row):
            at = slice(row * cols, (row + 1) * cols)
            back = dot(w_mid_back[...], stack(z_s, row, True))
            dz_s[:, at] = ((dh_s[:, at] + back) * slope_s[:, at]).astype(BF16)

        def conv_out(row):
            result = across(dot(w_out[...], stack(h2_s, row, False)), False)
            result = result * patch_weights[row : row + 1]
            result = jnp.concatenate([result, jnp.zeros((channels, LANES), F32)], axis=1)
            numer[row0 + row] += roll(result, lax.rem(col0 + (wide - MARGIN), wide), 1)

        def grad_mid(taps):
            both = jnp.concatenate([h_s[:, tap * cols : tap * cols + full] for tap in taps], axis=0)
            part = dot_lanes(z_s[:, inside], both)
            for at, tap in enumerate(taps):
                for tap_col in range(3):
                    start = small + (3 * tap + tap_col) * width
                    grads[start : start + width] += part[
                        tap_col * width : (tap_col + 1) * width, at * width : (at + 1) * width
                    ]

        def grad_out():
            start = small + 9 * width
            grads[start : start + small] += dot_lanes(all_rows(d_s, True), h2_s[:, inside])

        def grad_in():
            grads[0:small] += dot_lanes(all_rows(x_s, False), dz_s[...])

        steps = [(0.02 + 0.04 * row, functools.partial(conv_back, row)) for row in range(rows)]
        steps += [(0.33 + 0.08 * row, functools.partial(conv_out, row)) for row in range(rows)]
        steps.append((0.41, functools.partial(grad_mid, (0, 1))))
        steps.append((0.53, grad_in))
        steps.append((0.68, functools.partial(grad_mid, (2,))))
        steps.append((0.82, grad_out))
        return steps

    def run(slot):
        steps = []
        if slot < SLOTS:
            ahead = first_part(slot, *sets[slot % 2])
            steps += [((at + 0.5) / len(ahead), step) for at, step in enumerate(ahead)]
        if slot > 0:
            steps += second_part(slot - 1, *sets[(slot - 1) % 2])
        for _, step in sorted(steps, key=lambda pair: pair[0]):
            step()

    @pl.when(counts[0, 0] == SLOTS)
    def _():
        for slot in range(SLOTS + 1):
            run(slot)

    @pl.when(counts[0, 0] < SLOTS)
    def _():
        for slot in range(SLOTS):
            pl.when(max(slot, 1) <= counts[0, 0])(functools.partial(run, slot))

    half = grads.shape[0] // 2
    odd_index = lax.rem(lax.axis_index("lat"), 2)
    send[0:half] = grads[pl.ds(pl.multiple_of((1 - odd_index) * half, half), half)].astype(BF16)
    keep[...] = grads[pl.ds(pl.multiple_of(odd_index * half, half), half)]
    lanes = lane_ids((channels, LANES))
    blocks = cols // LANES
    base = half
    upper = [numer[row] for row in range(MARGIN)]
    lower = [numer[MARGIN + rows + row] for row in range(MARGIN)]
    for when_odd, when_even in ((upper, lower), (lower, upper)):
        packed = jnp.zeros((channels, LANES), F32)
        for row in range(MARGIN):
            line = choose(lat_odd, when_odd[row], when_even[row])
            for block in range(blocks):
                send[base : base + channels] = line[:, block * LANES : (block + 1) * LANES].astype(BF16)
                base += channels
            low = jnp.where(lanes < MARGIN, line[:, cols:], 0.0)
            high = jnp.where(lanes >= LANES - MARGIN, line[:, cols:], 0.0)
            packed = packed + roll(low, MARGIN * row, 1) + roll(high, -MARGIN * row, 1)
        send[base : base + channels] = packed.astype(BF16)
        base += channels


def beside_kernel(numer, first, held, inner, edges):
    height, channels, wide = numer.shape
    cols = wide - LANES
    rows = height - 2 * MARGIN
    blocks = cols // LANES
    edge_rows = held.shape[0]
    base = first.shape[0] - 2 * edge_rows
    lanes = lane_ids((channels, LANES))
    lat = lax.axis_index("lat")
    odd = lax.rem(lat, 2) == 1
    inside = jnp.logical_and(lat > 0, lat < lax.axis_size("lat") - 1)
    packed = jnp.zeros((channels, LANES), F32)
    for row in range(rows):
        at = row % MARGIN
        parts = []
        for block in range(blocks + 1):
            start = (at * blocks + block if block < blocks else MARGIN * blocks) * channels
            near = first[base + start : base + start + channels].astype(F32)
            far = choose(inside, held[start : start + channels].astype(F32), 0.0)
            other = choose(odd, near, far) if row < MARGIN else choose(odd, far, near)
            if block == blocks:
                low = jnp.where(lanes < MARGIN, roll(other, -MARGIN * at, 1), 0.0)
                other = low + jnp.where(lanes >= LANES - MARGIN, roll(other, MARGIN * at, 1), 0.0)
            parts.append(numer[MARGIN + row, :, block * LANES : (block + 1) * LANES] + other)
        inner[row] = jnp.concatenate(parts[:-1], axis=1)
        low = jnp.where(lanes < MARGIN, parts[-1], 0.0)
        high = jnp.where(lanes >= LANES - MARGIN, parts[-1], 0.0)
        packed = packed + roll(low, MARGIN * row, 1) + roll(high, -MARGIN * row, 1)
    part = channels // 2
    lanes = lane_ids((part, LANES))
    quarter = LANES // 4
    rest = packed[part:]
    rest = jnp.where(lanes < 2 * quarter, roll(rest, quarter, 1), roll(rest, -quarter, 1))
    middle = jnp.logical_and(lanes >= quarter, lanes < 3 * quarter)
    edges[...] = jnp.where(middle, rest, packed[:part]).astype(BF16)


def fold_kernel(inner, parts, den, blended):
    rows, channels, cols = inner.shape
    lanes = lane_ids((channels, LANES))
    lon, lon_size = lax.axis_index("lon"), lax.axis_size("lon")
    quarter = LANES // 4
    part_lanes = lane_ids((channels // 2, LANES))

    def margins(index):
        part = parts[index, 0 : channels // 2].astype(F32)
        rest = jnp.where(part_lanes < 2 * quarter, roll(part, -quarter, 1), roll(part, quarter, 1))
        return jnp.concatenate([part, rest], axis=0)

    left = margins(lax.rem(lon + lon_size - 1, lon_size))
    right = margins(lax.rem(lon + 1, lon_size))
    inverse = 1.0 / den[...]
    lines = []
    for row in range(rows):
        from_left = jnp.where(lanes < MARGIN, roll(left, -MARGIN * row, 1), 0.0)
        from_right = jnp.where(lanes >= LANES - MARGIN, roll(right, MARGIN * row, 1), 0.0)
        beside = [from_left]
        for _ in range(cols // LANES - 2):
            beside.append(jnp.zeros((channels, LANES), F32))
        beside.append(from_right)
        line = inner[row] + jnp.concatenate(beside, axis=1)
        lines.append((line * inverse[row : row + 1])[None])
    blended[...] = jnp.swapaxes(jnp.concatenate(lines, axis=0), 0, 1)


def split_kernel(own, other, grad_in, grad_mid, grad_out):
    taps, channels, width = grad_in.shape
    half = own.shape[0]
    odd = lax.rem(lax.axis_index("lat"), 2) == 1
    own, other = own[...], other[...]
    summed = (choose(odd, other, own), choose(odd, own, other))

    def rows_of(start, count):
        pieces = []
        stop = start + count
        if start < half:
            pieces.append(summed[0][start : min(stop, half)])
        if stop > half:
            pieces.append(summed[1][max(start, half) - half : stop - half])
        return jnp.concatenate(pieces, axis=0).astype(F32) if len(pieces) > 1 else pieces[0].astype(F32)

    for tap in range(taps):
        grad_in[tap] = rows_of(tap * channels, channels)
        grad_mid[tap] = rows_of(taps * channels + tap * width, width)
        grad_out[tap] = rows_of(taps * (channels + width) + tap * channels, channels)


def params():
    return pltpu.CompilerParams(vmem_limit_bytes=VMEM_LIMIT)


def swap(value, axis, first, wrap):
    size = lax.axis_size(axis)
    pairs = []
    for index in range(first, size, 2):
        other = (index + 1) % size
        if other > index or wrap:
            pairs.extend([(index, other), (other, index)])
    return lax.ppermute(value, axis, pairs)


def swap_lat(first, second):
    return swap(first, "lat", 0, False), swap(second, "lat", 1, False)


def swap_lon(edges):
    return swap(edges, "lon", 0, True), swap(edges, "lon", 1, True)


def exchange(value, axis, order):
    pairs = [(index, index ^ order[index % 2]) for index in range(lax.axis_size(axis))]
    return lax.ppermute(value, axis, pairs)


def order_bit(lat, order):
    step = jnp.where(lat % 2 == 0, order[0], order[1])
    return (lat // step) % 2


def halves(value, bit):
    half = value.shape[0] // 2
    own = lax.dynamic_slice_in_dim(value, bit * half, half, 0)
    other = lax.dynamic_slice_in_dim(value, (1 - bit) * half, half, 0)
    return own, other


def ordered(own, other, bit):
    return jnp.concatenate([jnp.where(bit == 0, own, other), jnp.where(bit == 0, other, own)], axis=0)


def shards(
    fields, cotangent, kernel_in, kernel_mid, kernel_out, patch_anchors, blend_weights, tile_counts
):
    channels, rows, cols = fields.shape
    taps, width, _ = kernel_in.shape
    patch_anchors = jnp.transpose(patch_anchors, (0, 1, 3, 2))
    height = rows + 2 * MARGIN
    wide = cols + LANES
    full = rows * cols
    padded = full + 2 * cols
    shape = jax.ShapeDtypeStruct
    center, first, second, canvas = pl.pallas_call(
        pack_kernel,
        out_shape=(
            shape((rows, 2 * channels, cols), BF16),
            shape((MARGIN * 2 * channels + height, cols), BF16),
            shape((MARGIN * 2 * channels + height, cols), BF16),
            shape((height, wide), F32),
        ),
        in_specs=[smem()] + [pl.BlockSpec(memory_space=pltpu.HBM)] * 4,
        out_specs=(vmem(),) * 4,
        scratch_shapes=[
            pltpu.VMEM(fields.shape, BF16),
            pltpu.VMEM(cotangent.shape, BF16),
            pltpu.VMEM(blend_weights.shape, jnp.int32),
            pltpu.SMEM(patch_anchors.shape, jnp.int32),
            pltpu.VMEM((height, wide), F32),
            pltpu.SemaphoreType.DMA((4,)),
        ],
        compiler_params=params(),
        name="pack",
    )(
        tile_counts,
        *(
            pltpu.with_memory_space_constraint(value, pltpu.HBM)
            for value in (patch_anchors, fields, cotangent, blend_weights)
        ),
    )
    first, second = swap_lat(first, second)
    w_in = jnp.transpose(kernel_in, (1, 0, 2)).reshape(width, taps * channels)
    kernel_mid = kernel_mid.reshape(3, 3, width, width)
    kernel_out = kernel_out.reshape(3, 3, channels, width)
    w_mid = jnp.transpose(kernel_mid, (1, 2, 0, 3)).reshape(3 * width, 3 * width)
    w_mid_back = jnp.transpose(kernel_mid, (3, 0, 1, 2)).reshape(width, taps * width)
    w_out = jnp.transpose(kernel_out, (1, 2, 0, 3)).reshape(3 * channels, 3 * width)
    w_out_back = jnp.transpose(kernel_out, (3, 0, 1, 2)).reshape(width, taps * channels)
    first, second, w_in, w_mid, w_mid_back, w_out, w_out_back = lax.optimization_barrier(
        (first, second, w_in, w_mid, w_mid_back, w_out, w_out_back)
    )
    edges, total = pl.pallas_call(
        edge_kernel,
        out_shape=(shape((2 * channels + 2 * height, LANES), BF16), shape((height, wide), F32)),
        in_specs=[vmem()] * 4,
        out_specs=(vmem(),) * 2,
        compiler_params=params(),
        name="edges",
    )(center, first, second, canvas)
    third, fourth = swap_lon(edges)

    lat_size, lon_size = lax.axis_size("lat"), lax.axis_size("lon")
    length = taps * (2 * channels + width)
    unit = 8 * lat_size
    length = (length + unit - 1) // unit * unit
    half = length // 2
    edge_rows = channels * (MARGIN * (cols // LANES) + 1)
    send, keep, numer, den = pl.pallas_call(
        patch_kernel,
        out_shape=(
            shape((half + 2 * edge_rows, LANES), BF16),
            shape((half, LANES), F32),
            shape((height, channels, wide), F32),
            shape((rows, cols), F32),
        ),
        in_specs=[smem(), smem()] + [vmem()] * 12,
        out_specs=(vmem(),) * 4,
        scratch_shapes=[
            pltpu.VMEM((length, LANES), F32),
            pltpu.VMEM((height, 2 * channels, wide), BF16),
        ]
        + 2
        * [
            pltpu.VMEM((3 * channels, padded), BF16),
            pltpu.VMEM((3 * channels, padded), BF16),
            pltpu.VMEM((width, padded), BF16),
            pltpu.VMEM((3 * width, padded), BF16),
            pltpu.VMEM((width, padded), BF16),
            pltpu.VMEM((width, full), F32),
            pltpu.VMEM((width, full), F32),
            pltpu.VMEM((width, full), BF16),
        ],
        compiler_params=params(),
        name="patches",
    )(
        patch_anchors, tile_counts, center, first, second, third, fourth, total, blend_weights,
        w_in, w_mid, w_mid_back, w_out, w_out_back,
    )

    lat = lax.axis_index("lat")
    even = lat % 2 == 0
    first = exchange(send, "lat", (1, 1))
    mine = keep + first[:half].astype(F32)
    held = first[half + edge_rows :]
    steps = [2 << bit for bit in range(lat_size.bit_length() - 2)]
    orders = list(zip(steps, steps[1:] + steps[:1]))
    for turn, order in enumerate(orders):
        own, other = halves(mine, order_bit(lat, order))
        payload = jnp.concatenate([other.astype(BF16), held], axis=0)
        payload = exchange(payload, "lat", order)
        count = own.shape[0]
        mine = own + payload[:count].astype(F32)
        moves = []
        for side in (0, 1):
            done = [orders[before][side] for before in range(turn)]
            move = jnp.bool_(True)
            for step in steps:
                if step < order[side]:
                    carries = 1 if (step in done) == (side == 1) else 0
                    move = jnp.logical_and(move, (lat // step) % 2 == carries)
            moves.append(move)
        held = jnp.where(jnp.where(even, moves[0], moves[1]), payload[count:], held)
    inner, edges = pl.pallas_call(
        beside_kernel,
        out_shape=(shape((rows, channels, cols), F32), shape((channels // 2, LANES), BF16)),
        in_specs=[vmem()] * 3,
        out_specs=(vmem(),) * 2,
        compiler_params=params(),
        name="beside",
    )(numer, first, held)
    payload = jnp.concatenate([edges, mine.astype(BF16)], axis=0)
    payload = jnp.broadcast_to(payload[None], (lon_size,) + payload.shape)
    payload = lax.all_to_all(payload, "lon", 0, 0)
    mine = jnp.sum(payload[:, channels // 2 :].astype(F32), axis=0).astype(BF16)
    blended = pl.pallas_call(
        fold_kernel,
        out_shape=shape((channels, rows, cols), F32),
        in_specs=[vmem()] * 3,
        out_specs=vmem(),
        compiler_params=params(),
        name="fold",
    )(inner, payload, den)
    for order in reversed(orders):
        mine = ordered(mine, exchange(mine, "lat", order), order_bit(lat, order))
    grad_in, grad_mid, grad_out = pl.pallas_call(
        split_kernel,
        out_shape=(
            shape((taps, channels, width), F32),
            shape((taps, width, width), F32),
            shape((taps, channels, width), F32),
        ),
        in_specs=[vmem()] * 2,
        out_specs=(vmem(),) * 3,
        compiler_params=params(),
        name="split",
    )(mine, exchange(mine, "lat", (1, 1)))
    return blended, jnp.transpose(grad_in, (0, 2, 1)), grad_mid, grad_out


def solution(mesh):
    return jax.shard_map(
        shards,
        mesh=mesh,
        in_specs=(
            P(None, "lat", "lon"),
            P(None, "lat", "lon"),
            P(),
            P(),
            P(),
            P("lat", "lon", None, None),
            P(None, "lat", "lon"),
            P("lat", "lon"),
        ),
        out_specs=(P(None, "lat", "lon"), P(), P(), P()),
        check_vma=False,
    )
```

```python
import functools

import jax
import jax.numpy as jnp
from jax import lax
from jax.experimental import pallas as pl
from jax.experimental.pallas import tpu as pltpu
from jax.sharding import PartitionSpec as P

MARGIN = 4
SLOTS = 4
LANES = 128
F32 = jnp.float32
BF16 = jnp.bfloat16
VMEM_LIMIT = 48 * 1024 * 1024


def vmem():
    return pl.BlockSpec(memory_space=pltpu.VMEM)


def smem():
    return pl.BlockSpec(memory_space=pltpu.SMEM)


def lane_ids(shape):
    return lax.broadcasted_iota(jnp.int32, shape, len(shape) - 1)


def roll(value, shift, axis):
    size = value.shape[axis]
    if isinstance(shift, int):
        shift = shift % size
        if shift == 0:
            return value
    return pltpu.roll(value, shift, axis)


def choose(odd, when_odd, when_even):
    return jnp.where(odd, when_odd, when_even)


def pack_kernel(
    counts, anchors_in, fields_in, cotangent_in, weights_in, center, first_out, second_out, canvas,
    fields, cotangent, weights, anchors, spread, sems,
):
    copies = []
    for index, (source, target) in enumerate(
        ((weights_in, weights), (fields_in, fields), (cotangent_in, cotangent), (anchors_in, anchors))
    ):
        copy = pltpu.make_async_copy(source, target, sems.at[index])
        copy.start()
        copies.append(copy)
    channels, rows, cols = fields.shape
    wide = cols + LANES
    odd = lax.rem(lax.axis_index("lat"), 2) == 1
    spread[...] = jnp.zeros_like(spread)
    copies[0].wait()
    copies[3].wait()
    for slot in range(SLOTS):

        @pl.when(slot < counts[0, 0])
        def _():
            row = anchors[0, 0, 0, slot]
            col = anchors[0, 0, 1, slot]
            values = weights[slot].astype(F32)
            values = jnp.concatenate([values, jnp.zeros((rows, LANES), F32)], axis=1)
            values = jnp.concatenate([values, jnp.zeros((2 * MARGIN, wide), F32)], axis=0)
            values = roll(values, lax.rem(col + (wide - MARGIN), wide), 1)
            values = roll(values, row, 0)
            spread[...] += values

    total = spread[...]
    canvas[...] = total
    copies[1].wait()
    copies[2].wait()
    both = []
    for source in (fields, cotangent):
        both.append(jnp.swapaxes(source[...].astype(F32), 0, 1))
    tile = jnp.concatenate(both, axis=1).astype(BF16)
    center[...] = tile
    half = total.shape[0] // 2
    extras = []
    for part in (total[:half], total[half:]):
        beside = jnp.concatenate([part[:, cols:], jnp.zeros((half, cols - LANES), F32)], axis=1)
        extras.append(jnp.concatenate([part[:, :cols], beside], axis=0).astype(BF16))
    flat = (MARGIN * 2 * channels, cols)
    top, bottom = tile[:MARGIN].reshape(flat), tile[rows - MARGIN :].reshape(flat)
    first_out[0 : flat[0]] = choose(odd, top, bottom)
    first_out[flat[0] :] = choose(odd, extras[0], extras[1])
    second_out[0 : flat[0]] = choose(odd, bottom, top)
    second_out[flat[0] :] = choose(odd, extras[1], extras[0])


def edge_kernel(center, first, second, canvas, edges, total_out):
    rows = center.shape[0]
    channels = center.shape[1] // 2
    cols = center.shape[2]
    height = rows + 2 * MARGIN
    half = height // 2
    odd = lax.rem(lax.axis_index("lat"), 2) == 1

    def stretch(block):
        block = block.astype(F32)
        return jnp.concatenate([block[:half], block[half:height, :LANES]], axis=1)

    base = MARGIN * 2 * channels
    upper = stretch(choose(odd, first[base:], second[base:]))
    lower = stretch(choose(odd, second[base:], first[base:]))
    total = canvas[...] + jnp.concatenate([upper, lower], axis=0)
    total_out[...] = total
    lanes = lane_ids((2 * channels, LANES))
    packed = jnp.zeros((2 * channels, LANES), F32)
    for row in range(height):
        at = slice(row % MARGIN * 2 * channels, (row % MARGIN + 1) * 2 * channels)
        if row < MARGIN:
            line = choose(odd, first[at], second[at])
        elif row < MARGIN + rows:
            line = center[row - MARGIN]
        else:
            line = choose(odd, second[at], first[at])
        line = line.astype(F32)
        low = jnp.where(lanes < MARGIN, line[:, :LANES], 0.0)
        high = jnp.where(lanes >= LANES - MARGIN, line[:, cols - LANES :], 0.0)
        packed = packed + roll(low, MARGIN * row, 1) + roll(high, -MARGIN * row, 1)
    edges[0 : 2 * channels] = packed.astype(BF16)
    margin = total[:, cols:]
    lanes = lane_ids(margin.shape)
    to_left = jnp.where(lanes < LANES // 2, total[:, :LANES], margin)
    to_right = jnp.where(lanes < LANES // 2, margin, total[:, cols - LANES : cols])
    edges[2 * channels : 2 * channels + height] = to_left.astype(BF16)
    edges[2 * channels + height : 2 * channels + 2 * height] = to_right.astype(BF16)


def dot(left, right):
    return jnp.dot(left, right, preferred_element_type=F32)


def dot_lanes(left, right):
    return lax.dot_general(left, right, (((1,), (1,)), ((), ())), preferred_element_type=F32)


def patch_kernel(
    anchors, counts, center, first, second, third, fourth, total_in, weights,
    w_in, w_mid, w_mid_back, w_out, w_out_back,
    send, keep, numer, den_out,
    grads, window, *sets,
):
    rows = center.shape[0]
    channels = center.shape[1] // 2
    cols = center.shape[2]
    wide = cols + LANES
    width = w_in.shape[0]
    full = rows * cols
    height = rows + 2 * MARGIN
    lanes = lane_ids((2 * channels, LANES))
    lat_odd = lax.rem(lax.axis_index("lat"), 2) == 1
    lon_odd = lax.rem(lax.axis_index("lon"), 2) == 1

    left = choose(lon_odd, third[...], fourth[...]).astype(F32)
    right = choose(lon_odd, fourth[...], third[...]).astype(F32)
    base = 2 * channels
    left_part = left[base + height : base + 2 * height]
    right_part = right[base : base + height]
    edge_lanes = lane_ids((height, LANES))
    low = edge_lanes < MARGIN
    high = edge_lanes >= LANES - MARGIN
    zero = jnp.zeros((height, LANES), F32)
    pieces = [jnp.where(low, left_part, zero)]
    for _ in range(cols // LANES - 2):
        pieces.append(zero)
    pieces.append(jnp.where(high, right_part, zero))
    pieces.append(jnp.where(high, left_part, zero) + jnp.where(low, right_part, zero))
    den = jnp.maximum(total_in[...] + jnp.concatenate(pieces, axis=1), 1.0)
    den_out[...] = den[MARGIN : MARGIN + rows, :cols]
    inverse = 1.0 / den

    left = left[:base]
    right = right[:base]
    for row in range(height):
        at = slice(row % MARGIN * base, (row % MARGIN + 1) * base)
        if row < MARGIN:
            body = choose(lat_odd, first[at], second[at])
        elif row < MARGIN + rows:
            body = center[row - MARGIN]
        else:
            body = choose(lat_odd, second[at], first[at])
        beside = jnp.where(
            lanes < LANES // 2, roll(right, -MARGIN * row, 1), roll(left, MARGIN * row, 1)
        )
        line = jnp.concatenate([body.astype(F32), beside], axis=1)
        scaled = line[channels:] * inverse[row : row + 1]
        window[row, 0:channels] = line[:channels].astype(BF16)
        window[row, channels : 2 * channels] = scaled.astype(BF16)

    numer[...] = jnp.zeros_like(numer)
    grads[...] = jnp.zeros_like(grads)
    sets = (sets[: len(sets) // 2], sets[len(sets) // 2 :])
    for ref in sets[0][:5] + sets[1][:5]:
        ref[:, 0:cols] = jnp.zeros((ref.shape[0], cols), BF16)
        ref[:, cols + full : 2 * cols + full] = jnp.zeros((ref.shape[0], cols), BF16)

    def shifted(value, step):
        blocks = [value[:, at : at + LANES] for at in range(0, cols, LANES)]
        turned = [roll(block, step, 1) for block in blocks]
        ids = lane_ids(blocks[0].shape)
        zero = jnp.zeros_like(blocks[0])
        if step > 0:
            ends = [zero] + turned[:-1]
            at_end = ids == 0
        else:
            ends = turned[1:] + [zero]
            at_end = ids == LANES - 1
        return jnp.concatenate([jnp.where(at_end, end, own) for end, own in zip(ends, turned)], axis=1)

    def before(value):
        return shifted(value, 1)

    def after(value):
        return shifted(value, -1)

    def spread(ref, value, row, flip):
        count = value.shape[0]
        at = slice((row + 1) * cols, (row + 2) * cols)
        first, last = before(value), after(value)
        if flip:
            first, last = last, first
        ref[0:count, at] = first
        ref[count : 2 * count, at] = value
        ref[2 * count : 3 * count, at] = last

    def stack(ref, row, flip):
        starts = [(row + (2 - tap if flip else tap)) * cols for tap in range(3)]
        return jnp.concatenate([ref[:, start : start + cols] for start in starts], axis=0)

    def across(parts, flip):
        count = parts.shape[0] // 3
        first, last = parts[:count], parts[2 * count :]
        if flip:
            first, last = last, first
        return before(first) + parts[count : 2 * count] + after(last)

    def all_rows(ref, flip):
        starts = [(2 - tap if flip else tap) * cols for tap in range(3)]
        return jnp.concatenate([ref[:, start : start + full] for start in starts], axis=0)

    def weights_of(slot):
        return weights[slot].astype(F32) * (slot < counts[0, 0]).astype(F32)

    def first_part(slot, x_s, d_s, h_s, z_s, h2_s, slope_s, dh_s, dz_s):
        row0 = anchors[0, 0, 0, slot]
        col0 = anchors[0, 0, 1, slot]
        patch_weights = weights_of(slot)
        back_shift = lax.rem(wide + MARGIN - col0, wide)

        def cut(row):
            line = roll(window[row0 + row], back_shift, 1)[:, :cols]
            spread(x_s, line[:channels], row, False)
            grad = line[channels:].astype(F32) * patch_weights[row : row + 1]
            spread(d_s, grad.astype(BF16), row, True)

        def conv_in(row):
            at = slice(row * cols, (row + 1) * cols)
            z1 = dot(w_in[...], stack(x_s, row, False))
            sig = 0.5 * jnp.tanh(0.5 * z1) + 0.5
            h1 = z1 * sig
            slope_s[:, at] = sig + h1 * (1.0 - sig)
            spread(h_s, h1.astype(BF16), row, False)

        def conv_mid(row):
            at = slice(row * cols, (row + 1) * cols)
            ahead = slice((row + 1) * cols, (row + 2) * cols)
            dh2 = dot(w_out_back[...], stack(d_s, row, True))
            z2 = dot(w_mid[...], stack(h_s, row, False))
            sig = 0.5 * jnp.tanh(0.5 * z2) + 0.5
            added = z2 * sig
            h2_s[:, ahead] = (h_s[width : 2 * width, ahead].astype(F32) + added).astype(BF16)
            dz2 = (dh2 * (sig + added * (1.0 - sig))).astype(BF16)
            dh_s[:, at] = dh2
            spread(z_s, dz2, row, True)

        return [functools.partial(step, row) for step in (cut, conv_in, conv_mid) for row in range(rows)]

    def second_part(slot, x_s, d_s, h_s, z_s, h2_s, slope_s, dh_s, dz_s):
        row0 = anchors[0, 0, 0, slot]
        col0 = anchors[0, 0, 1, slot]
        patch_weights = weights_of(slot)
        inside = slice(cols, cols + full)
        small = 9 * channels

        def conv_back(row):
            at = slice(row * cols, (row + 1) * cols)
            back = dot(w_mid_back[...], stack(z_s, row, True))
            dz_s[:, at] = ((dh_s[:, at] + back) * slope_s[:, at]).astype(BF16)

        def conv_out(row):
            result = across(dot(w_out[...], stack(h2_s, row, False)), False)
            result = result * patch_weights[row : row + 1]
            result = jnp.concatenate([result, jnp.zeros((channels, LANES), F32)], axis=1)
            numer[row0 + row] += roll(result, lax.rem(col0 + (wide - MARGIN), wide), 1)

        def grad_mid():
            part = dot_lanes(z_s[:, inside], all_rows(h_s.at[width : 2 * width], False))
            for tap in range(3):
                for tap_col in range(3):
                    start = small + (3 * tap + tap_col) * width
                    grads[start : start + width] += part[
                        tap_col * width : (tap_col + 1) * width, tap * width : (tap + 1) * width
                    ]

        def grad_out():
            start = small + 9 * width
            grads[start : start + small] += dot_lanes(all_rows(d_s, True), h2_s[:, inside])

        def grad_in():
            grads[0:small] += dot_lanes(all_rows(x_s, False), dz_s[...])

        backs = [functools.partial(conv_back, row) for row in range(rows)]
        outs = [functools.partial(conv_out, row) for row in range(rows)]
        return [grad_mid, grad_out] + backs + [grad_in] + outs

    def run(slot):
        steps = []
        if slot > 0:
            behind = second_part(slot - 1, *sets[(slot - 1) % 2])
            steps += [((at + 0.5) / len(behind), step) for at, step in enumerate(behind)]
        if slot < SLOTS:
            ahead = first_part(slot, *sets[slot % 2])
            steps += [((at + 0.5) / len(ahead), step) for at, step in enumerate(ahead)]
        for _, step in sorted(steps, key=lambda pair: pair[0]):
            step()

    @pl.when(counts[0, 0] == SLOTS)
    def _():
        for slot in range(SLOTS + 1):
            run(slot)

    @pl.when(counts[0, 0] < SLOTS)
    def _():
        for slot in range(SLOTS):
            pl.when(max(slot, 1) <= counts[0, 0])(functools.partial(run, slot))

    half = grads.shape[0] // 2
    odd_index = lax.rem(lax.axis_index("lat"), 2)
    send[0:half] = grads[pl.ds(pl.multiple_of((1 - odd_index) * half, half), half)].astype(BF16)
    keep[...] = grads[pl.ds(pl.multiple_of(odd_index * half, half), half)]
    lanes = lane_ids((channels, LANES))
    blocks = cols // LANES
    base = half
    upper = [numer[row] for row in range(MARGIN)]
    lower = [numer[MARGIN + rows + row] for row in range(MARGIN)]
    for when_odd, when_even in ((upper, lower), (lower, upper)):
        packed = jnp.zeros((channels, LANES), F32)
        for row in range(MARGIN):
            line = choose(lat_odd, when_odd[row], when_even[row])
            for block in range(blocks):
                send[base : base + channels] = line[:, block * LANES : (block + 1) * LANES].astype(BF16)
                base += channels
            low = jnp.where(lanes < MARGIN, line[:, cols:], 0.0)
            high = jnp.where(lanes >= LANES - MARGIN, line[:, cols:], 0.0)
            packed = packed + roll(low, MARGIN * row, 1) + roll(high, -MARGIN * row, 1)
        send[base : base + channels] = packed.astype(BF16)
        base += channels


def beside_kernel(numer, first, held, inner, edges):
    height, channels, wide = numer.shape
    cols = wide - LANES
    rows = height - 2 * MARGIN
    blocks = cols // LANES
    edge_rows = held.shape[0]
    base = first.shape[0] - 2 * edge_rows
    lanes = lane_ids((channels, LANES))
    lat = lax.axis_index("lat")
    odd = lax.rem(lat, 2) == 1
    inside = jnp.logical_and(lat > 0, lat < lax.axis_size("lat") - 1)
    packed = jnp.zeros((channels, LANES), F32)
    for row in range(rows):
        at = row % MARGIN
        parts = []
        for block in range(blocks + 1):
            start = (at * blocks + block if block < blocks else MARGIN * blocks) * channels
            near = first[base + start : base + start + channels].astype(F32)
            far = choose(inside, held[start : start + channels].astype(F32), 0.0)
            other = choose(odd, near, far) if row < MARGIN else choose(odd, far, near)
            if block == blocks:
                low = jnp.where(lanes < MARGIN, roll(other, -MARGIN * at, 1), 0.0)
                other = low + jnp.where(lanes >= LANES - MARGIN, roll(other, MARGIN * at, 1), 0.0)
            parts.append(numer[MARGIN + row, :, block * LANES : (block + 1) * LANES] + other)
        inner[row] = jnp.concatenate(parts[:-1], axis=1)
        low = jnp.where(lanes < MARGIN, parts[-1], 0.0)
        high = jnp.where(lanes >= LANES - MARGIN, parts[-1], 0.0)
        packed = packed + roll(low, MARGIN * row, 1) + roll(high, -MARGIN * row, 1)
    part = channels // 2
    lanes = lane_ids((part, LANES))
    quarter = LANES // 4
    rest = packed[part:]
    rest = jnp.where(lanes < 2 * quarter, roll(rest, quarter, 1), roll(rest, -quarter, 1))
    middle = jnp.logical_and(lanes >= quarter, lanes < 3 * quarter)
    edges[...] = jnp.where(middle, rest, packed[:part]).astype(BF16)


def fold_kernel(inner, parts, den, blended):
    rows, channels, cols = inner.shape
    lanes = lane_ids((channels, LANES))
    lon, lon_size = lax.axis_index("lon"), lax.axis_size("lon")
    quarter = LANES // 4
    part_lanes = lane_ids((channels // 2, LANES))

    def margins(index):
        part = parts[index, 0 : channels // 2].astype(F32)
        rest = jnp.where(part_lanes < 2 * quarter, roll(part, -quarter, 1), roll(part, quarter, 1))
        return jnp.concatenate([part, rest], axis=0)

    left = margins(lax.rem(lon + lon_size - 1, lon_size))
    right = margins(lax.rem(lon + 1, lon_size))
    inverse = 1.0 / den[...]
    lines = []
    for row in range(rows):
        from_left = jnp.where(lanes < MARGIN, roll(left, -MARGIN * row, 1), 0.0)
        from_right = jnp.where(lanes >= LANES - MARGIN, roll(right, MARGIN * row, 1), 0.0)
        beside = [from_left]
        for _ in range(cols // LANES - 2):
            beside.append(jnp.zeros((channels, LANES), F32))
        beside.append(from_right)
        line = inner[row] + jnp.concatenate(beside, axis=1)
        lines.append((line * inverse[row : row + 1])[None])
    blended[...] = jnp.swapaxes(jnp.concatenate(lines, axis=0), 0, 1)


def split_kernel(own, other, grad_in, grad_mid, grad_out):
    taps, channels, width = grad_in.shape
    half = own.shape[0]
    odd = lax.rem(lax.axis_index("lat"), 2) == 1
    own, other = own[...], other[...]
    summed = (choose(odd, other, own), choose(odd, own, other))

    def rows_of(start, count):
        pieces = []
        stop = start + count
        if start < half:
            pieces.append(summed[0][start : min(stop, half)])
        if stop > half:
            pieces.append(summed[1][max(start, half) - half : stop - half])
        return jnp.concatenate(pieces, axis=0).astype(F32) if len(pieces) > 1 else pieces[0].astype(F32)

    for tap in range(taps):
        grad_in[tap] = rows_of(tap * channels, channels)
        grad_mid[tap] = rows_of(taps * channels + tap * width, width)
        grad_out[tap] = rows_of(taps * (channels + width) + tap * channels, channels)


def params():
    return pltpu.CompilerParams(vmem_limit_bytes=VMEM_LIMIT)


def swap(value, axis, first, wrap):
    size = lax.axis_size(axis)
    pairs = []
    for index in range(first, size, 2):
        other = (index + 1) % size
        if other > index or wrap:
            pairs.extend([(index, other), (other, index)])
    return lax.ppermute(value, axis, pairs)


def swap_lat(first, second):
    return swap(first, "lat", 0, False), swap(second, "lat", 1, False)


def swap_lon(edges):
    return swap(edges, "lon", 0, True), swap(edges, "lon", 1, True)


def exchange(value, axis, order):
    pairs = [(index, index ^ order[index % 2]) for index in range(lax.axis_size(axis))]
    return lax.ppermute(value, axis, pairs)


def order_bit(lat, order):
    step = jnp.where(lat % 2 == 0, order[0], order[1])
    return (lat // step) % 2


def halves(value, bit):
    half = value.shape[0] // 2
    own = lax.dynamic_slice_in_dim(value, bit * half, half, 0)
    other = lax.dynamic_slice_in_dim(value, (1 - bit) * half, half, 0)
    return own, other


def ordered(own, other, bit):
    return jnp.concatenate([jnp.where(bit == 0, own, other), jnp.where(bit == 0, other, own)], axis=0)


def shards(
    fields, cotangent, kernel_in, kernel_mid, kernel_out, patch_anchors, blend_weights, tile_counts
):
    channels, rows, cols = fields.shape
    taps, width, _ = kernel_in.shape
    patch_anchors = jnp.transpose(patch_anchors, (0, 1, 3, 2))
    height = rows + 2 * MARGIN
    wide = cols + LANES
    full = rows * cols
    padded = full + 2 * cols
    shape = jax.ShapeDtypeStruct
    center, first, second, canvas = pl.pallas_call(
        pack_kernel,
        out_shape=(
            shape((rows, 2 * channels, cols), BF16),
            shape((MARGIN * 2 * channels + height, cols), BF16),
            shape((MARGIN * 2 * channels + height, cols), BF16),
            shape((height, wide), F32),
        ),
        in_specs=[smem()] + [pl.BlockSpec(memory_space=pltpu.HBM)] * 4,
        out_specs=(vmem(),) * 4,
        scratch_shapes=[
            pltpu.VMEM(fields.shape, BF16),
            pltpu.VMEM(cotangent.shape, BF16),
            pltpu.VMEM(blend_weights.shape, jnp.int32),
            pltpu.SMEM(patch_anchors.shape, jnp.int32),
            pltpu.VMEM((height, wide), F32),
            pltpu.SemaphoreType.DMA((4,)),
        ],
        compiler_params=params(),
        name="pack",
    )(
        tile_counts,
        *(
            pltpu.with_memory_space_constraint(value, pltpu.HBM)
            for value in (patch_anchors, fields, cotangent, blend_weights)
        ),
    )
    first, second = swap_lat(first, second)
    w_in = jnp.transpose(kernel_in, (1, 0, 2)).reshape(width, taps * channels)
    kernel_mid = kernel_mid.reshape(3, 3, width, width)
    kernel_out = kernel_out.reshape(3, 3, channels, width)
    w_mid = jnp.transpose(kernel_mid, (2, 0, 1, 3)).reshape(width, taps * width)
    w_mid_back = jnp.transpose(kernel_mid, (3, 0, 1, 2)).reshape(width, taps * width)
    w_out = jnp.transpose(kernel_out, (1, 2, 0, 3)).reshape(3 * channels, 3 * width)
    w_out_back = jnp.transpose(kernel_out, (3, 0, 1, 2)).reshape(width, taps * channels)
    first, second, w_in, w_mid, w_mid_back, w_out, w_out_back = lax.optimization_barrier(
        (first, second, w_in, w_mid, w_mid_back, w_out, w_out_back)
    )
    edges, total = pl.pallas_call(
        edge_kernel,
        out_shape=(shape((2 * channels + 2 * height, LANES), BF16), shape((height, wide), F32)),
        in_specs=[vmem()] * 4,
        out_specs=(vmem(),) * 2,
        compiler_params=params(),
        name="edges",
    )(center, first, second, canvas)
    third, fourth = swap_lon(edges)

    lat_size, lon_size = lax.axis_size("lat"), lax.axis_size("lon")
    length = taps * (2 * channels + width)
    unit = 8 * lat_size
    length = (length + unit - 1) // unit * unit
    half = length // 2
    edge_rows = channels * (MARGIN * (cols // LANES) + 1)
    send, keep, numer, den = pl.pallas_call(
        patch_kernel,
        out_shape=(
            shape((half + 2 * edge_rows, LANES), BF16),
            shape((half, LANES), F32),
            shape((height, channels, wide), F32),
            shape((rows, cols), F32),
        ),
        in_specs=[smem(), smem()] + [vmem()] * 12,
        out_specs=(vmem(),) * 4,
        scratch_shapes=[
            pltpu.VMEM((length, LANES), F32),
            pltpu.VMEM((height, 2 * channels, wide), BF16),
        ]
        + 2
        * [
            pltpu.VMEM((3 * channels, padded), BF16),
            pltpu.VMEM((3 * channels, padded), BF16),
            pltpu.VMEM((3 * width, padded), BF16),
            pltpu.VMEM((3 * width, padded), BF16),
            pltpu.VMEM((width, padded), BF16),
            pltpu.VMEM((width, full), F32),
            pltpu.VMEM((width, full), F32),
            pltpu.VMEM((width, full), BF16),
        ],
        compiler_params=params(),
        name="patches",
    )(
        patch_anchors, tile_counts, center, first, second, third, fourth, total, blend_weights,
        w_in, w_mid, w_mid_back, w_out, w_out_back,
    )

    lat = lax.axis_index("lat")
    even = lat % 2 == 0
    first = exchange(send, "lat", (1, 1))
    mine = keep + first[:half].astype(F32)
    held = first[half + edge_rows :]
    steps = [2 << bit for bit in range(lat_size.bit_length() - 2)]
    orders = list(zip(steps, steps[1:] + steps[:1]))
    for turn, order in enumerate(orders):
        own, other = halves(mine, order_bit(lat, order))
        payload = jnp.concatenate([other.astype(BF16), held], axis=0)
        payload = exchange(payload, "lat", order)
        count = own.shape[0]
        mine = own + payload[:count].astype(F32)
        moves = []
        for side in (0, 1):
            done = [orders[before][side] for before in range(turn)]
            move = jnp.bool_(True)
            for step in steps:
                if step < order[side]:
                    carries = 1 if (step in done) == (side == 1) else 0
                    move = jnp.logical_and(move, (lat // step) % 2 == carries)
            moves.append(move)
        held = jnp.where(jnp.where(even, moves[0], moves[1]), payload[count:], held)
    inner, edges = pl.pallas_call(
        beside_kernel,
        out_shape=(shape((rows, channels, cols), F32), shape((channels // 2, LANES), BF16)),
        in_specs=[vmem()] * 3,
        out_specs=(vmem(),) * 2,
        compiler_params=params(),
        name="beside",
    )(numer, first, held)
    payload = jnp.concatenate([edges, mine.astype(BF16)], axis=0)
    payload = jnp.broadcast_to(payload[None], (lon_size,) + payload.shape)
    payload = lax.all_to_all(payload, "lon", 0, 0)
    mine = jnp.sum(payload[:, channels // 2 :].astype(F32), axis=0).astype(BF16)
    blended = pl.pallas_call(
        fold_kernel,
        out_shape=shape((channels, rows, cols), F32),
        in_specs=[vmem()] * 3,
        out_specs=vmem(),
        compiler_params=params(),
        name="fold",
    )(inner, payload, den)
    for order in reversed(orders):
        mine = ordered(mine, exchange(mine, "lat", order), order_bit(lat, order))
    grad_in, grad_mid, grad_out = pl.pallas_call(
        split_kernel,
        out_shape=(
            shape((taps, channels, width), F32),
            shape((taps, width, width), F32),
            shape((taps, channels, width), F32),
        ),
        in_specs=[vmem()] * 2,
        out_specs=(vmem(),) * 3,
        compiler_params=params(),
        name="split",
    )(mine, exchange(mine, "lat", (1, 1)))
    return blended, jnp.transpose(grad_in, (0, 2, 1)), grad_mid, grad_out


def solution(mesh):
    return jax.shard_map(
        shards,
        mesh=mesh,
        in_specs=(
            P(None, "lat", "lon"),
            P(None, "lat", "lon"),
            P(),
            P(),
            P(),
            P("lat", "lon", None, None),
            P(None, "lat", "lon"),
            P("lat", "lon"),
        ),
        out_specs=(P(None, "lat", "lon"), P(), P(), P()),
        check_vma=False,
    )
```

```python
import functools

import jax
import jax.numpy as jnp
from jax import lax
from jax.experimental import pallas as pl
from jax.experimental.pallas import tpu as pltpu
from jax.sharding import PartitionSpec as P

MARGIN = 4
SLOTS = 4
LANES = 128
F32 = jnp.float32
BF16 = jnp.bfloat16
VMEM_LIMIT = 48 * 1024 * 1024


def vmem():
    return pl.BlockSpec(memory_space=pltpu.VMEM)


def smem():
    return pl.BlockSpec(memory_space=pltpu.SMEM)


def lane_ids(shape):
    return lax.broadcasted_iota(jnp.int32, shape, len(shape) - 1)


def roll(value, shift, axis):
    size = value.shape[axis]
    if isinstance(shift, int):
        shift = shift % size
        if shift == 0:
            return value
    return pltpu.roll(value, shift, axis)


def choose(odd, when_odd, when_even):
    return jnp.where(odd, when_odd, when_even)


def pack_kernel(
    counts, anchors_in, fields_in, cotangent_in, weights_in, center, first_out, second_out, canvas,
    fields, cotangent, weights, anchors, spread, sems,
):
    copies = []
    for index, (source, target) in enumerate(
        ((weights_in, weights), (fields_in, fields), (cotangent_in, cotangent), (anchors_in, anchors))
    ):
        copy = pltpu.make_async_copy(source, target, sems.at[index])
        copy.start()
        copies.append(copy)
    channels, rows, cols = fields.shape
    wide = cols + LANES
    odd = lax.rem(lax.axis_index("lat"), 2) == 1
    spread[...] = jnp.zeros_like(spread)
    copies[0].wait()
    copies[3].wait()
    for slot in range(SLOTS):

        @pl.when(slot < counts[0, 0])
        def _():
            row = anchors[0, 0, 0, slot]
            col = anchors[0, 0, 1, slot]
            values = weights[slot].astype(F32)
            values = jnp.concatenate([values, jnp.zeros((rows, LANES), F32)], axis=1)
            values = jnp.concatenate([values, jnp.zeros((2 * MARGIN, wide), F32)], axis=0)
            values = roll(values, lax.rem(col + (wide - MARGIN), wide), 1)
            values = roll(values, row, 0)
            spread[...] += values

    total = spread[...]
    canvas[...] = total
    copies[1].wait()
    copies[2].wait()
    both = []
    for source in (fields, cotangent):
        both.append(jnp.swapaxes(source[...].astype(F32), 0, 1))
    tile = jnp.concatenate(both, axis=1).astype(BF16)
    center[...] = tile
    half = total.shape[0] // 2
    extras = []
    for part in (total[:half], total[half:]):
        beside = jnp.concatenate([part[:, cols:], jnp.zeros((half, cols - LANES), F32)], axis=1)
        extras.append(jnp.concatenate([part[:, :cols], beside], axis=0).astype(BF16))
    flat = (MARGIN * 2 * channels, cols)
    top, bottom = tile[:MARGIN].reshape(flat), tile[rows - MARGIN :].reshape(flat)
    first_out[0 : flat[0]] = choose(odd, top, bottom)
    first_out[flat[0] :] = choose(odd, extras[0], extras[1])
    second_out[0 : flat[0]] = choose(odd, bottom, top)
    second_out[flat[0] :] = choose(odd, extras[1], extras[0])


def edge_kernel(center, first, second, canvas, edges, total_out):
    rows = center.shape[0]
    channels = center.shape[1] // 2
    cols = center.shape[2]
    height = rows + 2 * MARGIN
    half = height // 2
    odd = lax.rem(lax.axis_index("lat"), 2) == 1

    def stretch(block):
        block = block.astype(F32)
        return jnp.concatenate([block[:half], block[half:height, :LANES]], axis=1)

    base = MARGIN * 2 * channels
    upper = stretch(choose(odd, first[base:], second[base:]))
    lower = stretch(choose(odd, second[base:], first[base:]))
    total = canvas[...] + jnp.concatenate([upper, lower], axis=0)
    total_out[...] = total
    lanes = lane_ids((2 * channels, LANES))
    packed = jnp.zeros((2 * channels, LANES), F32)
    for row in range(height):
        at = slice(row % MARGIN * 2 * channels, (row % MARGIN + 1) * 2 * channels)
        if row < MARGIN:
            line = choose(odd, first[at], second[at])
        elif row < MARGIN + rows:
            line = center[row - MARGIN]
        else:
            line = choose(odd, second[at], first[at])
        line = line.astype(F32)
        low = jnp.where(lanes < MARGIN, line[:, :LANES], 0.0)
        high = jnp.where(lanes >= LANES - MARGIN, line[:, cols - LANES :], 0.0)
        packed = packed + roll(low, MARGIN * row, 1) + roll(high, -MARGIN * row, 1)
    edges[0 : 2 * channels] = packed.astype(BF16)
    margin = total[:, cols:]
    lanes = lane_ids(margin.shape)
    to_left = jnp.where(lanes < LANES // 2, total[:, :LANES], margin)
    to_right = jnp.where(lanes < LANES // 2, margin, total[:, cols - LANES : cols])
    edges[2 * channels : 2 * channels + height] = to_left.astype(BF16)
    edges[2 * channels + height : 2 * channels + 2 * height] = to_right.astype(BF16)


def dot(left, right):
    return jnp.dot(left, right, preferred_element_type=F32)


def dot_lanes(left, right):
    return lax.dot_general(left, right, (((1,), (1,)), ((), ())), preferred_element_type=F32)


def patch_kernel(
    anchors, counts, center, first, second, third, fourth, total_in, weights,
    w_in, w_mid, w_mid_back, w_out, w_out_back,
    send, keep, numer, den_out,
    grads, window, *sets,
):
    rows = center.shape[0]
    channels = center.shape[1] // 2
    cols = center.shape[2]
    wide = cols + LANES
    width = w_in.shape[0]
    full = rows * cols
    height = rows + 2 * MARGIN
    lanes = lane_ids((2 * channels, LANES))
    lat_odd = lax.rem(lax.axis_index("lat"), 2) == 1
    lon_odd = lax.rem(lax.axis_index("lon"), 2) == 1

    left = choose(lon_odd, third[...], fourth[...]).astype(F32)
    right = choose(lon_odd, fourth[...], third[...]).astype(F32)
    base = 2 * channels
    left_part = left[base + height : base + 2 * height]
    right_part = right[base : base + height]
    edge_lanes = lane_ids((height, LANES))
    low = edge_lanes < MARGIN
    high = edge_lanes >= LANES - MARGIN
    zero = jnp.zeros((height, LANES), F32)
    pieces = [jnp.where(low, left_part, zero)]
    for _ in range(cols // LANES - 2):
        pieces.append(zero)
    pieces.append(jnp.where(high, right_part, zero))
    pieces.append(jnp.where(high, left_part, zero) + jnp.where(low, right_part, zero))
    den = jnp.maximum(total_in[...] + jnp.concatenate(pieces, axis=1), 1.0)
    den_out[...] = den[MARGIN : MARGIN + rows, :cols]
    inverse = 1.0 / den

    sets = (sets[: len(sets) // 2], sets[len(sets) // 2 :])

    def prepare():
        left_edge = left[:base]
        right_edge = right[:base]
        for row in range(height):
            at = slice(row % MARGIN * base, (row % MARGIN + 1) * base)
            if row < MARGIN:
                body = choose(lat_odd, first[at], second[at])
            elif row < MARGIN + rows:
                body = center[row - MARGIN]
            else:
                body = choose(lat_odd, second[at], first[at])
            beside = jnp.where(
                lanes < LANES // 2, roll(right_edge, -MARGIN * row, 1), roll(left_edge, MARGIN * row, 1)
            )
            line = jnp.concatenate([body.astype(F32), beside], axis=1)
            scaled = line[channels:] * inverse[row : row + 1]
            window[row, 0:channels] = line[:channels].astype(BF16)
            window[row, channels : 2 * channels] = scaled.astype(BF16)
        numer[...] = jnp.zeros_like(numer)
        used = 9 * (2 * channels + width)
        if used < grads.shape[0]:
            grads[used:] = jnp.zeros((grads.shape[0] - used, LANES), F32)
        for ref in sets[0][:5] + sets[1][:5]:
            ref[:, 0:cols] = jnp.zeros((ref.shape[0], cols), BF16)
            ref[:, cols + full : 2 * cols + full] = jnp.zeros((ref.shape[0], cols), BF16)

    def shifted(value, step):
        blocks = [value[:, at : at + LANES] for at in range(0, cols, LANES)]
        turned = [roll(block, step, 1) for block in blocks]
        ids = lane_ids(blocks[0].shape)
        zero = jnp.zeros_like(blocks[0])
        if step > 0:
            ends = [zero] + turned[:-1]
            at_end = ids == 0
        else:
            ends = turned[1:] + [zero]
            at_end = ids == LANES - 1
        return jnp.concatenate([jnp.where(at_end, end, own) for end, own in zip(ends, turned)], axis=1)

    def before(value):
        return shifted(value, 1)

    def after(value):
        return shifted(value, -1)

    def spread(ref, value, row, flip):
        count = value.shape[0]
        at = slice((row + 1) * cols, (row + 2) * cols)
        first, last = before(value), after(value)
        if flip:
            first, last = last, first
        ref[0:count, at] = first
        ref[count : 2 * count, at] = value
        ref[2 * count : 3 * count, at] = last

    def stack(ref, row, flip):
        starts = [(row + (2 - tap if flip else tap)) * cols for tap in range(3)]
        return jnp.concatenate([ref[:, start : start + cols] for start in starts], axis=0)

    def across(parts, flip):
        count = parts.shape[0] // 3
        first, last = parts[:count], parts[2 * count :]
        if flip:
            first, last = last, first
        return before(first) + parts[count : 2 * count] + after(last)

    def all_rows(ref, flip):
        starts = [(2 - tap if flip else tap) * cols for tap in range(3)]
        return jnp.concatenate([ref[:, start : start + full] for start in starts], axis=0)

    def weights_of(slot):
        return weights[slot].astype(F32) * (slot < counts[0, 0]).astype(F32)

    def first_part(slot, x_s, d_s, h_s, z_s, h2_s, slope_s, dh_s, dz_s):
        row0 = anchors[0, 0, 0, slot]
        col0 = anchors[0, 0, 1, slot]
        patch_weights = weights_of(slot)
        back_shift = lax.rem(wide + MARGIN - col0, wide)

        def cut(row):
            line = roll(window[row0 + row], back_shift, 1)[:, :cols]
            spread(x_s, line[:channels], row, False)
            grad = line[channels:].astype(F32) * patch_weights[row : row + 1]
            spread(d_s, grad.astype(BF16), row, True)

        def conv_in(row):
            at = slice(row * cols, (row + 1) * cols)
            z1 = dot(w_in[...], stack(x_s, row, False))
            sig = 0.5 * jnp.tanh(0.5 * z1) + 0.5
            h1 = z1 * sig
            slope_s[:, at] = sig + h1 * (1.0 - sig)
            spread(h_s, h1.astype(BF16), row, False)

        def conv_mid(row):
            at = slice(row * cols, (row + 1) * cols)
            ahead = slice((row + 1) * cols, (row + 2) * cols)
            dh2 = dot(w_out_back[...], stack(d_s, row, True))
            z2 = dot(w_mid[...], stack(h_s, row, False))
            sig = 0.5 * jnp.tanh(0.5 * z2) + 0.5
            added = z2 * sig
            h2_s[:, ahead] = (h_s[width : 2 * width, ahead].astype(F32) + added).astype(BF16)
            dz2 = (dh2 * (sig + added * (1.0 - sig))).astype(BF16)
            dh_s[:, at] = dh2
            spread(z_s, dz2, row, True)

        return [functools.partial(step, row) for step in (cut, conv_in, conv_mid) for row in range(rows)]

    def second_part(slot, x_s, d_s, h_s, z_s, h2_s, slope_s, dh_s, dz_s):
        row0 = anchors[0, 0, 0, slot]
        col0 = anchors[0, 0, 1, slot]
        patch_weights = weights_of(slot)
        inside = slice(cols, cols + full)
        small = 9 * channels

        def add(start, part):
            at = slice(start, start + part.shape[0])
            grads[at] = part if slot == 0 else grads[at] + part

        def conv_back(row):
            at = slice(row * cols, (row + 1) * cols)
            back = dot(w_mid_back[...], stack(z_s, row, True))
            dz_s[:, at] = ((dh_s[:, at] + back) * slope_s[:, at]).astype(BF16)

        def conv_out(row):
            result = across(dot(w_out[...], stack(h2_s, row, False)), False)
            result = result * patch_weights[row : row + 1]
            result = jnp.concatenate([result, jnp.zeros((channels, LANES), F32)], axis=1)
            numer[row0 + row] += roll(result, lax.rem(col0 + (wide - MARGIN), wide), 1)

        def grad_mid():
            part = dot_lanes(z_s[:, inside], all_rows(h_s.at[width : 2 * width], False))
            for tap in range(3):
                for tap_col in range(3):
                    start = small + (3 * tap + tap_col) * width
                    add(start, part[tap_col * width : (tap_col + 1) * width, tap * width : (tap + 1) * width])

        def grad_out():
            start = small + 9 * width
            add(start, dot_lanes(all_rows(d_s, True), h2_s[:, inside]))

        def grad_in():
            add(0, dot_lanes(all_rows(x_s, False), dz_s[...]))

        backs = [functools.partial(conv_back, row) for row in range(rows)]
        outs = [functools.partial(conv_out, row) for row in range(rows)]
        return [grad_mid, grad_out] + backs + [grad_in] + outs

    def run(slot):
        steps = []
        if slot > 0:
            behind = second_part(slot - 1, *sets[(slot - 1) % 2])
            steps += [((at + 0.5) / len(behind), step) for at, step in enumerate(behind)]
        if slot < SLOTS:
            ahead = first_part(slot, *sets[slot % 2])
            steps += [((at + 0.5) / len(ahead), step) for at, step in enumerate(ahead)]
        for _, step in sorted(steps, key=lambda pair: pair[0]):
            step()

    def finish():
        half = grads.shape[0] // 2
        odd_index = lax.rem(lax.axis_index("lat"), 2)
        send[0:half] = grads[pl.ds(pl.multiple_of((1 - odd_index) * half, half), half)].astype(BF16)
        keep[...] = grads[pl.ds(pl.multiple_of(odd_index * half, half), half)]
        lanes = lane_ids((channels, LANES))
        blocks = cols // LANES
        base = half
        upper = [numer[row] for row in range(MARGIN)]
        lower = [numer[MARGIN + rows + row] for row in range(MARGIN)]
        for when_odd, when_even in ((upper, lower), (lower, upper)):
            packed = jnp.zeros((channels, LANES), F32)
            for row in range(MARGIN):
                line = choose(lat_odd, when_odd[row], when_even[row])
                for block in range(blocks):
                    send[base : base + channels] = line[:, block * LANES : (block + 1) * LANES].astype(BF16)
                    base += channels
                low = jnp.where(lanes < MARGIN, line[:, cols:], 0.0)
                high = jnp.where(lanes >= LANES - MARGIN, line[:, cols:], 0.0)
                packed = packed + roll(low, MARGIN * row, 1) + roll(high, -MARGIN * row, 1)
            send[base : base + channels] = packed.astype(BF16)
            base += channels

    @pl.when(counts[0, 0] == SLOTS)
    def _():
        prepare()
        for slot in range(SLOTS + 1):
            run(slot)
        finish()

    @pl.when(counts[0, 0] < SLOTS)
    def _():
        prepare()

        @pl.when(counts[0, 0] == 0)
        def _():
            grads[...] = jnp.zeros_like(grads)

        for slot in range(SLOTS):
            pl.when(max(slot, 1) <= counts[0, 0])(functools.partial(run, slot))
        finish()


def beside_kernel(numer, first, held, inner, edges):
    height, channels, wide = numer.shape
    cols = wide - LANES
    rows = height - 2 * MARGIN
    blocks = cols // LANES
    edge_rows = held.shape[0]
    base = first.shape[0] - 2 * edge_rows
    lanes = lane_ids((channels, LANES))
    lat = lax.axis_index("lat")
    odd = lax.rem(lat, 2) == 1
    inside = jnp.logical_and(lat > 0, lat < lax.axis_size("lat") - 1)
    packed = jnp.zeros((channels, LANES), F32)
    for row in range(rows):
        at = row % MARGIN
        parts = []
        for block in range(blocks + 1):
            start = (at * blocks + block if block < blocks else MARGIN * blocks) * channels
            near = first[base + start : base + start + channels].astype(F32)
            far = choose(inside, held[start : start + channels].astype(F32), 0.0)
            other = choose(odd, near, far) if row < MARGIN else choose(odd, far, near)
            if block == blocks:
                low = jnp.where(lanes < MARGIN, roll(other, -MARGIN * at, 1), 0.0)
                other = low + jnp.where(lanes >= LANES - MARGIN, roll(other, MARGIN * at, 1), 0.0)
            parts.append(numer[MARGIN + row, :, block * LANES : (block + 1) * LANES] + other)
        inner[row] = jnp.concatenate(parts[:-1], axis=1)
        low = jnp.where(lanes < MARGIN, parts[-1], 0.0)
        high = jnp.where(lanes >= LANES - MARGIN, parts[-1], 0.0)
        packed = packed + roll(low, MARGIN * row, 1) + roll(high, -MARGIN * row, 1)
    part = channels // 2
    lanes = lane_ids((part, LANES))
    quarter = LANES // 4
    rest = packed[part:]
    rest = jnp.where(lanes < 2 * quarter, roll(rest, quarter, 1), roll(rest, -quarter, 1))
    middle = jnp.logical_and(lanes >= quarter, lanes < 3 * quarter)
    edges[...] = jnp.where(middle, rest, packed[:part]).astype(BF16)


def fold_kernel(inner, parts, den, blended):
    rows, channels, cols = inner.shape
    lanes = lane_ids((channels, LANES))
    lon, lon_size = lax.axis_index("lon"), lax.axis_size("lon")
    quarter = LANES // 4
    part_lanes = lane_ids((channels // 2, LANES))

    def margins(index):
        part = parts[index, 0 : channels // 2].astype(F32)
        rest = jnp.where(part_lanes < 2 * quarter, roll(part, -quarter, 1), roll(part, quarter, 1))
        return jnp.concatenate([part, rest], axis=0)

    left = margins(lax.rem(lon + lon_size - 1, lon_size))
    right = margins(lax.rem(lon + 1, lon_size))
    inverse = 1.0 / den[...]
    lines = []
    for row in range(rows):
        from_left = jnp.where(lanes < MARGIN, roll(left, -MARGIN * row, 1), 0.0)
        from_right = jnp.where(lanes >= LANES - MARGIN, roll(right, MARGIN * row, 1), 0.0)
        beside = [from_left]
        for _ in range(cols // LANES - 2):
            beside.append(jnp.zeros((channels, LANES), F32))
        beside.append(from_right)
        line = inner[row] + jnp.concatenate(beside, axis=1)
        lines.append((line * inverse[row : row + 1])[None])
    blended[...] = jnp.swapaxes(jnp.concatenate(lines, axis=0), 0, 1)


def split_kernel(own, other, grad_in, grad_mid, grad_out):
    taps, channels, width = grad_in.shape
    half = own.shape[0]
    odd = lax.rem(lax.axis_index("lat"), 2) == 1
    own, other = own[...], other[...]
    summed = (choose(odd, other, own), choose(odd, own, other))

    def rows_of(start, count):
        pieces = []
        stop = start + count
        if start < half:
            pieces.append(summed[0][start : min(stop, half)])
        if stop > half:
            pieces.append(summed[1][max(start, half) - half : stop - half])
        return jnp.concatenate(pieces, axis=0).astype(F32) if len(pieces) > 1 else pieces[0].astype(F32)

    for tap in range(taps):
        grad_in[tap] = rows_of(tap * channels, channels)
        grad_mid[tap] = rows_of(taps * channels + tap * width, width)
        grad_out[tap] = rows_of(taps * (channels + width) + tap * channels, channels)


def params():
    return pltpu.CompilerParams(vmem_limit_bytes=VMEM_LIMIT)


def swap(value, axis, first, wrap):
    size = lax.axis_size(axis)
    pairs = []
    for index in range(first, size, 2):
        other = (index + 1) % size
        if other > index or wrap:
            pairs.extend([(index, other), (other, index)])
    return lax.ppermute(value, axis, pairs)


def swap_lat(first, second):
    return swap(first, "lat", 0, False), swap(second, "lat", 1, False)


def swap_lon(edges):
    return swap(edges, "lon", 0, True), swap(edges, "lon", 1, True)


def exchange(value, axis, order):
    pairs = [(index, index ^ order[index % 2]) for index in range(lax.axis_size(axis))]
    return lax.ppermute(value, axis, pairs)


def order_bit(lat, order):
    step = jnp.where(lat % 2 == 0, order[0], order[1])
    return (lat // step) % 2


def halves(value, bit):
    half = value.shape[0] // 2
    own = lax.dynamic_slice_in_dim(value, bit * half, half, 0)
    other = lax.dynamic_slice_in_dim(value, (1 - bit) * half, half, 0)
    return own, other


def ordered(own, other, bit):
    return jnp.concatenate([jnp.where(bit == 0, own, other), jnp.where(bit == 0, other, own)], axis=0)


def shards(
    fields, cotangent, kernel_in, kernel_mid, kernel_out, patch_anchors, blend_weights, tile_counts
):
    channels, rows, cols = fields.shape
    taps, width, _ = kernel_in.shape
    patch_anchors = jnp.transpose(patch_anchors, (0, 1, 3, 2))
    height = rows + 2 * MARGIN
    wide = cols + LANES
    full = rows * cols
    padded = full + 2 * cols
    shape = jax.ShapeDtypeStruct
    center, first, second, canvas = pl.pallas_call(
        pack_kernel,
        out_shape=(
            shape((rows, 2 * channels, cols), BF16),
            shape((MARGIN * 2 * channels + height, cols), BF16),
            shape((MARGIN * 2 * channels + height, cols), BF16),
            shape((height, wide), F32),
        ),
        in_specs=[smem()] + [pl.BlockSpec(memory_space=pltpu.HBM)] * 4,
        out_specs=(vmem(),) * 4,
        scratch_shapes=[
            pltpu.VMEM(fields.shape, BF16),
            pltpu.VMEM(cotangent.shape, BF16),
            pltpu.VMEM(blend_weights.shape, jnp.int32),
            pltpu.SMEM(patch_anchors.shape, jnp.int32),
            pltpu.VMEM((height, wide), F32),
            pltpu.SemaphoreType.DMA((4,)),
        ],
        compiler_params=params(),
        name="pack",
    )(
        tile_counts,
        *(
            pltpu.with_memory_space_constraint(value, pltpu.HBM)
            for value in (patch_anchors, fields, cotangent, blend_weights)
        ),
    )
    first, second = swap_lat(first, second)
    w_in = jnp.transpose(kernel_in, (1, 0, 2)).reshape(width, taps * channels)
    kernel_mid = kernel_mid.reshape(3, 3, width, width)
    kernel_out = kernel_out.reshape(3, 3, channels, width)
    w_mid = jnp.transpose(kernel_mid, (2, 0, 1, 3)).reshape(width, taps * width)
    w_mid_back = jnp.transpose(kernel_mid, (3, 0, 1, 2)).reshape(width, taps * width)
    w_out = jnp.transpose(kernel_out, (1, 2, 0, 3)).reshape(3 * channels, 3 * width)
    w_out_back = jnp.transpose(kernel_out, (3, 0, 1, 2)).reshape(width, taps * channels)
    first, second, w_in, w_mid, w_mid_back, w_out, w_out_back = lax.optimization_barrier(
        (first, second, w_in, w_mid, w_mid_back, w_out, w_out_back)
    )
    edges, total = pl.pallas_call(
        edge_kernel,
        out_shape=(shape((2 * channels + 2 * height, LANES), BF16), shape((height, wide), F32)),
        in_specs=[vmem()] * 4,
        out_specs=(vmem(),) * 2,
        compiler_params=params(),
        name="edges",
    )(center, first, second, canvas)
    third, fourth = swap_lon(edges)

    lat_size, lon_size = lax.axis_size("lat"), lax.axis_size("lon")
    length = taps * (2 * channels + width)
    unit = 8 * lat_size
    length = (length + unit - 1) // unit * unit
    half = length // 2
    edge_rows = channels * (MARGIN * (cols // LANES) + 1)
    send, keep, numer, den = pl.pallas_call(
        patch_kernel,
        out_shape=(
            shape((half + 2 * edge_rows, LANES), BF16),
            shape((half, LANES), F32),
            shape((height, channels, wide), F32),
            shape((rows, cols), F32),
        ),
        in_specs=[smem(), smem()] + [vmem()] * 12,
        out_specs=(vmem(),) * 4,
        scratch_shapes=[
            pltpu.VMEM((length, LANES), F32),
            pltpu.VMEM((height, 2 * channels, wide), BF16),
        ]
        + 2
        * [
            pltpu.VMEM((3 * channels, padded), BF16),
            pltpu.VMEM((3 * channels, padded), BF16),
            pltpu.VMEM((3 * width, padded), BF16),
            pltpu.VMEM((3 * width, padded), BF16),
            pltpu.VMEM((width, padded), BF16),
            pltpu.VMEM((width, full), F32),
            pltpu.VMEM((width, full), F32),
            pltpu.VMEM((width, full), BF16),
        ],
        compiler_params=params(),
        name="patches",
    )(
        patch_anchors, tile_counts, center, first, second, third, fourth, total, blend_weights,
        w_in, w_mid, w_mid_back, w_out, w_out_back,
    )

    lat = lax.axis_index("lat")
    even = lat % 2 == 0
    first = exchange(send, "lat", (1, 1))
    mine = keep + first[:half].astype(F32)
    held = first[half + edge_rows :]
    steps = [2 << bit for bit in range(lat_size.bit_length() - 2)]
    orders = list(zip(steps, steps[1:] + steps[:1]))
    for turn, order in enumerate(orders):
        own, other = halves(mine, order_bit(lat, order))
        payload = jnp.concatenate([other.astype(BF16), held], axis=0)
        payload = exchange(payload, "lat", order)
        count = own.shape[0]
        mine = own + payload[:count].astype(F32)
        moves = []
        for side in (0, 1):
            done = [orders[before][side] for before in range(turn)]
            move = jnp.bool_(True)
            for step in steps:
                if step < order[side]:
                    carries = 1 if (step in done) == (side == 1) else 0
                    move = jnp.logical_and(move, (lat // step) % 2 == carries)
            moves.append(move)
        held = jnp.where(jnp.where(even, moves[0], moves[1]), payload[count:], held)
    inner, edges = pl.pallas_call(
        beside_kernel,
        out_shape=(shape((rows, channels, cols), F32), shape((channels // 2, LANES), BF16)),
        in_specs=[vmem()] * 3,
        out_specs=(vmem(),) * 2,
        compiler_params=params(),
        name="beside",
    )(numer, first, held)
    payload = jnp.concatenate([edges, mine.astype(BF16)], axis=0)
    payload = jnp.broadcast_to(payload[None], (lon_size,) + payload.shape)
    payload = lax.all_to_all(payload, "lon", 0, 0)
    mine = jnp.sum(payload[:, channels // 2 :].astype(F32), axis=0).astype(BF16)
    blended = pl.pallas_call(
        fold_kernel,
        out_shape=shape((channels, rows, cols), F32),
        in_specs=[vmem()] * 3,
        out_specs=vmem(),
        compiler_params=params(),
        name="fold",
    )(inner, payload, den)
    for order in reversed(orders):
        mine = ordered(mine, exchange(mine, "lat", order), order_bit(lat, order))
    grad_in, grad_mid, grad_out = pl.pallas_call(
        split_kernel,
        out_shape=(
            shape((taps, channels, width), F32),
            shape((taps, width, width), F32),
            shape((taps, channels, width), F32),
        ),
        in_specs=[vmem()] * 2,
        out_specs=(vmem(),) * 3,
        compiler_params=params(),
        name="split",
    )(mine, exchange(mine, "lat", (1, 1)))
    return blended, jnp.transpose(grad_in, (0, 2, 1)), grad_mid, grad_out


def solution(mesh):
    return jax.shard_map(
        shards,
        mesh=mesh,
        in_specs=(
            P(None, "lat", "lon"),
            P(None, "lat", "lon"),
            P(),
            P(),
            P(),
            P("lat", "lon", None, None),
            P(None, "lat", "lon"),
            P("lat", "lon"),
        ),
        out_specs=(P(None, "lat", "lon"), P(), P(), P()),
        check_vma=False,
    )
```

```python
import functools

import jax
import jax.numpy as jnp
from jax import lax
from jax.experimental import pallas as pl
from jax.experimental.pallas import tpu as pltpu
from jax.sharding import PartitionSpec as P

MARGIN = 4
SLOTS = 4
LANES = 128
F32 = jnp.float32
BF16 = jnp.bfloat16
VMEM_LIMIT = 48 * 1024 * 1024


def vmem():
    return pl.BlockSpec(memory_space=pltpu.VMEM)


def smem():
    return pl.BlockSpec(memory_space=pltpu.SMEM)


def lane_ids(shape):
    return lax.broadcasted_iota(jnp.int32, shape, len(shape) - 1)


def roll(value, shift, axis):
    size = value.shape[axis]
    if isinstance(shift, int):
        shift = shift % size
        if shift == 0:
            return value
    return pltpu.roll(value, shift, axis)


def choose(odd, when_odd, when_even):
    return jnp.where(odd, when_odd, when_even)


def pack_kernel(
    counts, anchors_in, fields_in, cotangent_in, weights_in, center, first_out, second_out, canvas,
    fields, cotangent, weights, anchors, spread, sems,
):
    copies = []
    for index, (source, target) in enumerate(
        ((weights_in, weights), (fields_in, fields), (cotangent_in, cotangent), (anchors_in, anchors))
    ):
        copy = pltpu.make_async_copy(source, target, sems.at[index])
        copy.start()
        copies.append(copy)
    channels, rows, cols = fields.shape
    wide = cols + LANES
    odd = lax.rem(lax.axis_index("lat"), 2) == 1
    spread[...] = jnp.zeros_like(spread)
    copies[0].wait()
    copies[3].wait()
    for slot in range(SLOTS):

        @pl.when(slot < counts[0, 0])
        def _():
            row = anchors[0, 0, 0, slot]
            col = anchors[0, 0, 1, slot]
            values = weights[slot].astype(F32)
            values = jnp.concatenate([values, jnp.zeros((rows, LANES), F32)], axis=1)
            values = jnp.concatenate([values, jnp.zeros((2 * MARGIN, wide), F32)], axis=0)
            values = roll(values, lax.rem(col + (wide - MARGIN), wide), 1)
            values = roll(values, row, 0)
            spread[...] += values

    total = spread[...]
    canvas[...] = total
    copies[1].wait()
    copies[2].wait()
    both = []
    for source in (fields, cotangent):
        both.append(jnp.swapaxes(source[...].astype(F32), 0, 1))
    tile = jnp.concatenate(both, axis=1).astype(BF16)
    center[...] = tile
    half = total.shape[0] // 2
    extras = []
    for part in (total[:half], total[half:]):
        beside = jnp.concatenate([part[:, cols:], jnp.zeros((half, cols - LANES), F32)], axis=1)
        extras.append(jnp.concatenate([part[:, :cols], beside], axis=0).astype(BF16))
    flat = (MARGIN * 2 * channels, cols)
    top, bottom = tile[:MARGIN].reshape(flat), tile[rows - MARGIN :].reshape(flat)
    first_out[0 : flat[0]] = choose(odd, top, bottom)
    first_out[flat[0] :] = choose(odd, extras[0], extras[1])
    second_out[0 : flat[0]] = choose(odd, bottom, top)
    second_out[flat[0] :] = choose(odd, extras[1], extras[0])


def edge_kernel(center, first, second, canvas, edges, total_out):
    rows = center.shape[0]
    channels = center.shape[1] // 2
    cols = center.shape[2]
    height = rows + 2 * MARGIN
    half = height // 2
    odd = lax.rem(lax.axis_index("lat"), 2) == 1

    def stretch(block):
        block = block.astype(F32)
        return jnp.concatenate([block[:half], block[half:height, :LANES]], axis=1)

    base = MARGIN * 2 * channels
    upper = stretch(choose(odd, first[base:], second[base:]))
    lower = stretch(choose(odd, second[base:], first[base:]))
    total = canvas[...] + jnp.concatenate([upper, lower], axis=0)
    total_out[...] = total
    lanes = lane_ids((2 * channels, LANES))
    packed = jnp.zeros((2 * channels, LANES), F32)
    for row in range(height):
        at = slice(row % MARGIN * 2 * channels, (row % MARGIN + 1) * 2 * channels)
        if row < MARGIN:
            line = choose(odd, first[at], second[at])
        elif row < MARGIN + rows:
            line = center[row - MARGIN]
        else:
            line = choose(odd, second[at], first[at])
        line = line.astype(F32)
        low = jnp.where(lanes < MARGIN, line[:, :LANES], 0.0)
        high = jnp.where(lanes >= LANES - MARGIN, line[:, cols - LANES :], 0.0)
        packed = packed + roll(low, MARGIN * row, 1) + roll(high, -MARGIN * row, 1)
    edges[0 : 2 * channels] = packed.astype(BF16)
    margin = total[:, cols:]
    lanes = lane_ids(margin.shape)
    to_left = jnp.where(lanes < LANES // 2, total[:, :LANES], margin)
    to_right = jnp.where(lanes < LANES // 2, margin, total[:, cols - LANES : cols])
    edges[2 * channels : 2 * channels + height] = to_left.astype(BF16)
    edges[2 * channels + height : 2 * channels + 2 * height] = to_right.astype(BF16)


def dot(left, right):
    return jnp.dot(left, right, preferred_element_type=F32)


def dot_lanes(left, right):
    return lax.dot_general(left, right, (((1,), (1,)), ((), ())), preferred_element_type=F32)


def patch_kernel(
    anchors, counts, center, first, second, third, fourth, total_in, weights,
    w_in, w_mid, w_mid_back, w_out, w_out_back,
    send, keep, numer, den_out,
    grads, window, *sets,
):
    rows = center.shape[0]
    channels = center.shape[1] // 2
    cols = center.shape[2]
    wide = cols + LANES
    width = w_in.shape[0]
    full = rows * cols
    height = rows + 2 * MARGIN
    lanes = lane_ids((2 * channels, LANES))
    lat_odd = lax.rem(lax.axis_index("lat"), 2) == 1
    lon_odd = lax.rem(lax.axis_index("lon"), 2) == 1

    left = choose(lon_odd, third[...], fourth[...]).astype(F32)
    right = choose(lon_odd, fourth[...], third[...]).astype(F32)
    base = 2 * channels
    left_part = left[base + height : base + 2 * height]
    right_part = right[base : base + height]
    edge_lanes = lane_ids((height, LANES))
    low = edge_lanes < MARGIN
    high = edge_lanes >= LANES - MARGIN
    zero = jnp.zeros((height, LANES), F32)
    pieces = [jnp.where(low, left_part, zero)]
    for _ in range(cols // LANES - 2):
        pieces.append(zero)
    pieces.append(jnp.where(high, right_part, zero))
    pieces.append(jnp.where(high, left_part, zero) + jnp.where(low, right_part, zero))
    den = jnp.maximum(total_in[...] + jnp.concatenate(pieces, axis=1), 1.0)
    den_out[...] = den[MARGIN : MARGIN + rows, :cols]
    inverse = 1.0 / den

    left = left[:base]
    right = right[:base]
    for row in range(height):
        at = slice(row % MARGIN * base, (row % MARGIN + 1) * base)
        if row < MARGIN:
            body = choose(lat_odd, first[at], second[at])
        elif row < MARGIN + rows:
            body = center[row - MARGIN]
        else:
            body = choose(lat_odd, second[at], first[at])
        beside = jnp.where(
            lanes < LANES // 2, roll(right, -MARGIN * row, 1), roll(left, MARGIN * row, 1)
        )
        line = jnp.concatenate([body.astype(F32), beside], axis=1)
        scaled = line[channels:] * inverse[row : row + 1]
        window[row, 0:channels] = line[:channels].astype(BF16)
        window[row, channels : 2 * channels] = scaled.astype(BF16)

    numer[...] = jnp.zeros_like(numer)
    grads[...] = jnp.zeros_like(grads)
    sets = (sets[: len(sets) // 2], sets[len(sets) // 2 :])
    for ref in sets[0][:5] + sets[1][:5]:
        ref[:, 0:cols] = jnp.zeros((ref.shape[0], cols), BF16)
        ref[:, cols + full : 2 * cols + full] = jnp.zeros((ref.shape[0], cols), BF16)

    def shifted(value, step):
        blocks = [value[:, at : at + LANES] for at in range(0, cols, LANES)]
        turned = [roll(block, step, 1) for block in blocks]
        ids = lane_ids(blocks[0].shape)
        zero = jnp.zeros_like(blocks[0])
        if step > 0:
            ends = [zero] + turned[:-1]
            at_end = ids == 0
        else:
            ends = turned[1:] + [zero]
            at_end = ids == LANES - 1
        return jnp.concatenate([jnp.where(at_end, end, own) for end, own in zip(ends, turned)], axis=1)

    def before(value):
        return shifted(value, 1)

    def after(value):
        return shifted(value, -1)

    def spread(ref, value, row, flip):
        count = value.shape[0]
        at = slice((row + 1) * cols, (row + 2) * cols)
        first, last = before(value), after(value)
        if flip:
            first, last = last, first
        ref[0:count, at] = first
        ref[count : 2 * count, at] = value
        ref[2 * count : 3 * count, at] = last

    def stack(ref, row, flip):
        starts = [(row + (2 - tap if flip else tap)) * cols for tap in range(3)]
        return jnp.concatenate([ref[:, start : start + cols] for start in starts], axis=0)

    def across(parts, flip):
        count = parts.shape[0] // 3
        first, last = parts[:count], parts[2 * count :]
        if flip:
            first, last = last, first
        return before(first) + parts[count : 2 * count] + after(last)

    def all_rows(ref, flip):
        starts = [(2 - tap if flip else tap) * cols for tap in range(3)]
        return jnp.concatenate([ref[:, start : start + full] for start in starts], axis=0)

    def weights_of(slot):
        return weights[slot].astype(F32) * (slot < counts[0, 0]).astype(F32)

    def first_part(slot, x_s, d_s, h_s, z_s, h2_s, slope_s, dh_s, dz_s):
        row0 = anchors[0, 0, 0, slot]
        col0 = anchors[0, 0, 1, slot]
        patch_weights = weights_of(slot)
        back_shift = lax.rem(wide + MARGIN - col0, wide)

        def cut(row):
            line = roll(window[row0 + row], back_shift, 1)[:, :cols]
            spread(x_s, line[:channels], row, False)
            grad = line[channels:].astype(F32) * patch_weights[row : row + 1]
            spread(d_s, grad.astype(BF16), row, True)

        def conv_in(row):
            at = slice(row * cols, (row + 1) * cols)
            z1 = dot(w_in[...], stack(x_s, row, False))
            sig = 0.5 * jnp.tanh(0.5 * z1) + 0.5
            h1 = z1 * sig
            slope_s[:, at] = sig + h1 * (1.0 - sig)
            spread(h_s, h1.astype(BF16), row, False)

        def conv_mid(row):
            at = slice(row * cols, (row + 1) * cols)
            ahead = slice((row + 1) * cols, (row + 2) * cols)
            dh2 = dot(w_out_back[...], stack(d_s, row, True))
            z2 = dot(w_mid[...], stack(h_s, row, False))
            sig = 0.5 * jnp.tanh(0.5 * z2) + 0.5
            added = z2 * sig
            h2_s[:, ahead] = (h_s[width : 2 * width, ahead].astype(F32) + added).astype(BF16)
            dz2 = (dh2 * (sig + added * (1.0 - sig))).astype(BF16)
            dh_s[:, at] = dh2
            spread(z_s, dz2, row, True)

        return [functools.partial(step, row) for step in (cut, conv_in, conv_mid) for row in range(rows)]

    def second_part(slot, x_s, d_s, h_s, z_s, h2_s, slope_s, dh_s, dz_s):
        row0 = anchors[0, 0, 0, slot]
        col0 = anchors[0, 0, 1, slot]
        patch_weights = weights_of(slot)
        inside = slice(cols, cols + full)
        small = 9 * channels

        def conv_back(row):
            at = slice(row * cols, (row + 1) * cols)
            back = dot(w_mid_back[...], stack(z_s, row, True))
            dz_s[:, at] = ((dh_s[:, at] + back) * slope_s[:, at]).astype(BF16)

        def conv_out(row):
            result = across(dot(w_out[...], stack(h2_s, row, False)), False)
            result = result * patch_weights[row : row + 1]
            result = jnp.concatenate([result, jnp.zeros((channels, LANES), F32)], axis=1)
            numer[row0 + row] += roll(result, lax.rem(col0 + (wide - MARGIN), wide), 1)

        def grad_mid():
            part = dot_lanes(z_s[:, inside], all_rows(h_s.at[width : 2 * width], False))
            for tap in range(3):
                for tap_col in range(3):
                    start = small + (3 * tap + tap_col) * width
                    grads[start : start + width] += part[
                        tap_col * width : (tap_col + 1) * width, tap * width : (tap + 1) * width
                    ]

        def grad_out():
            start = small + 9 * width
            grads[start : start + small] += dot_lanes(all_rows(d_s, True), h2_s[:, inside])

        def grad_in():
            grads[0:small] += dot_lanes(all_rows(x_s, False), dz_s[...])

        backs = [functools.partial(conv_back, row) for row in range(rows)]
        outs = [functools.partial(conv_out, row) for row in range(rows)]
        return [grad_mid, grad_out] + backs + [grad_in] + outs

    def run(slot):
        steps = []
        if slot > 0:
            behind = second_part(slot - 1, *sets[(slot - 1) % 2])
            steps += [((at + 0.5) / len(behind), step) for at, step in enumerate(behind)]
        if slot < SLOTS:
            ahead = first_part(slot, *sets[slot % 2])
            steps += [((at + 0.5) / len(ahead), step) for at, step in enumerate(ahead)]
        for _, step in sorted(steps, key=lambda pair: pair[0]):
            step()

    @pl.when(counts[0, 0] == SLOTS)
    def _():
        for slot in range(SLOTS + 1):
            run(slot)

    @pl.when(counts[0, 0] < SLOTS)
    def _():
        def one_slot(slot, carry):
            for step in first_part(slot, *sets[0]) + second_part(slot, *sets[0]):
                step()
            return carry

        lax.fori_loop(0, counts[0, 0], one_slot, 0)

    half = grads.shape[0] // 2
    odd_index = lax.rem(lax.axis_index("lat"), 2)
    send[0:half] = grads[pl.ds(pl.multiple_of((1 - odd_index) * half, half), half)].astype(BF16)
    keep[...] = grads[pl.ds(pl.multiple_of(odd_index * half, half), half)]
    lanes = lane_ids((channels, LANES))
    blocks = cols // LANES
    base = half
    upper = [numer[row] for row in range(MARGIN)]
    lower = [numer[MARGIN + rows + row] for row in range(MARGIN)]
    for when_odd, when_even in ((upper, lower), (lower, upper)):
        packed = jnp.zeros((channels, LANES), F32)
        for row in range(MARGIN):
            line = choose(lat_odd, when_odd[row], when_even[row])
            for block in range(blocks):
                send[base : base + channels] = line[:, block * LANES : (block + 1) * LANES].astype(BF16)
                base += channels
            low = jnp.where(lanes < MARGIN, line[:, cols:], 0.0)
            high = jnp.where(lanes >= LANES - MARGIN, line[:, cols:], 0.0)
            packed = packed + roll(low, MARGIN * row, 1) + roll(high, -MARGIN * row, 1)
        send[base : base + channels] = packed.astype(BF16)
        base += channels


def beside_kernel(numer, first, held, inner, edges):
    height, channels, wide = numer.shape
    cols = wide - LANES
    rows = height - 2 * MARGIN
    blocks = cols // LANES
    edge_rows = held.shape[0]
    base = first.shape[0] - 2 * edge_rows
    lanes = lane_ids((channels, LANES))
    lat = lax.axis_index("lat")
    odd = lax.rem(lat, 2) == 1
    inside = jnp.logical_and(lat > 0, lat < lax.axis_size("lat") - 1)
    packed = jnp.zeros((channels, LANES), F32)
    for row in range(rows):
        at = row % MARGIN
        parts = []
        for block in range(blocks + 1):
            start = (at * blocks + block if block < blocks else MARGIN * blocks) * channels
            near = first[base + start : base + start + channels].astype(F32)
            far = choose(inside, held[start : start + channels].astype(F32), 0.0)
            other = choose(odd, near, far) if row < MARGIN else choose(odd, far, near)
            if block == blocks:
                low = jnp.where(lanes < MARGIN, roll(other, -MARGIN * at, 1), 0.0)
                other = low + jnp.where(lanes >= LANES - MARGIN, roll(other, MARGIN * at, 1), 0.0)
            parts.append(numer[MARGIN + row, :, block * LANES : (block + 1) * LANES] + other)
        inner[row] = jnp.concatenate(parts[:-1], axis=1)
        low = jnp.where(lanes < MARGIN, parts[-1], 0.0)
        high = jnp.where(lanes >= LANES - MARGIN, parts[-1], 0.0)
        packed = packed + roll(low, MARGIN * row, 1) + roll(high, -MARGIN * row, 1)
    part = channels // 2
    lanes = lane_ids((part, LANES))
    quarter = LANES // 4
    rest = packed[part:]
    rest = jnp.where(lanes < 2 * quarter, roll(rest, quarter, 1), roll(rest, -quarter, 1))
    middle = jnp.logical_and(lanes >= quarter, lanes < 3 * quarter)
    edges[...] = jnp.where(middle, rest, packed[:part]).astype(BF16)


def fold_kernel(inner, parts, den, blended):
    rows, channels, cols = inner.shape
    lanes = lane_ids((channels, LANES))
    lon, lon_size = lax.axis_index("lon"), lax.axis_size("lon")
    quarter = LANES // 4
    part_lanes = lane_ids((channels // 2, LANES))

    def margins(index):
        part = parts[index, 0 : channels // 2].astype(F32)
        rest = jnp.where(part_lanes < 2 * quarter, roll(part, -quarter, 1), roll(part, quarter, 1))
        return jnp.concatenate([part, rest], axis=0)

    left = margins(lax.rem(lon + lon_size - 1, lon_size))
    right = margins(lax.rem(lon + 1, lon_size))
    inverse = 1.0 / den[...]
    lines = []
    for row in range(rows):
        from_left = jnp.where(lanes < MARGIN, roll(left, -MARGIN * row, 1), 0.0)
        from_right = jnp.where(lanes >= LANES - MARGIN, roll(right, MARGIN * row, 1), 0.0)
        beside = [from_left]
        for _ in range(cols // LANES - 2):
            beside.append(jnp.zeros((channels, LANES), F32))
        beside.append(from_right)
        line = inner[row] + jnp.concatenate(beside, axis=1)
        lines.append((line * inverse[row : row + 1])[None])
    blended[...] = jnp.swapaxes(jnp.concatenate(lines, axis=0), 0, 1)


def split_kernel(own, other, grad_in, grad_mid, grad_out):
    taps, channels, width = grad_in.shape
    half = own.shape[0]
    odd = lax.rem(lax.axis_index("lat"), 2) == 1
    own, other = own[...], other[...]
    summed = (choose(odd, other, own), choose(odd, own, other))

    def rows_of(start, count):
        pieces = []
        stop = start + count
        if start < half:
            pieces.append(summed[0][start : min(stop, half)])
        if stop > half:
            pieces.append(summed[1][max(start, half) - half : stop - half])
        return jnp.concatenate(pieces, axis=0).astype(F32) if len(pieces) > 1 else pieces[0].astype(F32)

    for tap in range(taps):
        grad_in[tap] = rows_of(tap * channels, channels)
        grad_mid[tap] = rows_of(taps * channels + tap * width, width)
        grad_out[tap] = rows_of(taps * (channels + width) + tap * channels, channels)


def params():
    return pltpu.CompilerParams(vmem_limit_bytes=VMEM_LIMIT)


def swap(value, axis, first, wrap):
    size = lax.axis_size(axis)
    pairs = []
    for index in range(first, size, 2):
        other = (index + 1) % size
        if other > index or wrap:
            pairs.extend([(index, other), (other, index)])
    return lax.ppermute(value, axis, pairs)


def swap_lat(first, second):
    return swap(first, "lat", 0, False), swap(second, "lat", 1, False)


def swap_lon(edges):
    return swap(edges, "lon", 0, True), swap(edges, "lon", 1, True)


def exchange(value, axis, order):
    pairs = [(index, index ^ order[index % 2]) for index in range(lax.axis_size(axis))]
    return lax.ppermute(value, axis, pairs)


def order_bit(lat, order):
    step = jnp.where(lat % 2 == 0, order[0], order[1])
    return (lat // step) % 2


def halves(value, bit):
    half = value.shape[0] // 2
    own = lax.dynamic_slice_in_dim(value, bit * half, half, 0)
    other = lax.dynamic_slice_in_dim(value, (1 - bit) * half, half, 0)
    return own, other


def ordered(own, other, bit):
    return jnp.concatenate([jnp.where(bit == 0, own, other), jnp.where(bit == 0, other, own)], axis=0)


def shards(
    fields, cotangent, kernel_in, kernel_mid, kernel_out, patch_anchors, blend_weights, tile_counts
):
    channels, rows, cols = fields.shape
    taps, width, _ = kernel_in.shape
    patch_anchors = jnp.transpose(patch_anchors, (0, 1, 3, 2))
    height = rows + 2 * MARGIN
    wide = cols + LANES
    full = rows * cols
    padded = full + 2 * cols
    shape = jax.ShapeDtypeStruct
    center, first, second, canvas = pl.pallas_call(
        pack_kernel,
        out_shape=(
            shape((rows, 2 * channels, cols), BF16),
            shape((MARGIN * 2 * channels + height, cols), BF16),
            shape((MARGIN * 2 * channels + height, cols), BF16),
            shape((height, wide), F32),
        ),
        in_specs=[smem()] + [pl.BlockSpec(memory_space=pltpu.HBM)] * 4,
        out_specs=(vmem(),) * 4,
        scratch_shapes=[
            pltpu.VMEM(fields.shape, BF16),
            pltpu.VMEM(cotangent.shape, BF16),
            pltpu.VMEM(blend_weights.shape, jnp.int32),
            pltpu.SMEM(patch_anchors.shape, jnp.int32),
            pltpu.VMEM((height, wide), F32),
            pltpu.SemaphoreType.DMA((4,)),
        ],
        compiler_params=params(),
        name="pack",
    )(
        tile_counts,
        *(
            pltpu.with_memory_space_constraint(value, pltpu.HBM)
            for value in (patch_anchors, fields, cotangent, blend_weights)
        ),
    )
    first, second = swap_lat(first, second)
    w_in = jnp.transpose(kernel_in, (1, 0, 2)).reshape(width, taps * channels)
    kernel_mid = kernel_mid.reshape(3, 3, width, width)
    kernel_out = kernel_out.reshape(3, 3, channels, width)
    w_mid = jnp.transpose(kernel_mid, (2, 0, 1, 3)).reshape(width, taps * width)
    w_mid_back = jnp.transpose(kernel_mid, (3, 0, 1, 2)).reshape(width, taps * width)
    w_out = jnp.transpose(kernel_out, (1, 2, 0, 3)).reshape(3 * channels, 3 * width)
    w_out_back = jnp.transpose(kernel_out, (3, 0, 1, 2)).reshape(width, taps * channels)
    first, second, w_in, w_mid, w_mid_back, w_out, w_out_back = lax.optimization_barrier(
        (first, second, w_in, w_mid, w_mid_back, w_out, w_out_back)
    )
    edges, total = pl.pallas_call(
        edge_kernel,
        out_shape=(shape((2 * channels + 2 * height, LANES), BF16), shape((height, wide), F32)),
        in_specs=[vmem()] * 4,
        out_specs=(vmem(),) * 2,
        compiler_params=params(),
        name="edges",
    )(center, first, second, canvas)
    third, fourth = swap_lon(edges)

    lat_size, lon_size = lax.axis_size("lat"), lax.axis_size("lon")
    length = taps * (2 * channels + width)
    unit = 8 * lat_size
    length = (length + unit - 1) // unit * unit
    half = length // 2
    edge_rows = channels * (MARGIN * (cols // LANES) + 1)
    send, keep, numer, den = pl.pallas_call(
        patch_kernel,
        out_shape=(
            shape((half + 2 * edge_rows, LANES), BF16),
            shape((half, LANES), F32),
            shape((height, channels, wide), F32),
            shape((rows, cols), F32),
        ),
        in_specs=[smem(), smem()] + [vmem()] * 12,
        out_specs=(vmem(),) * 4,
        scratch_shapes=[
            pltpu.VMEM((length, LANES), F32),
            pltpu.VMEM((height, 2 * channels, wide), BF16),
        ]
        + 2
        * [
            pltpu.VMEM((3 * channels, padded), BF16),
            pltpu.VMEM((3 * channels, padded), BF16),
            pltpu.VMEM((3 * width, padded), BF16),
            pltpu.VMEM((3 * width, padded), BF16),
            pltpu.VMEM((width, padded), BF16),
            pltpu.VMEM((width, full), F32),
            pltpu.VMEM((width, full), F32),
            pltpu.VMEM((width, full), BF16),
        ],
        compiler_params=params(),
        name="patches",
    )(
        patch_anchors, tile_counts, center, first, second, third, fourth, total, blend_weights,
        w_in, w_mid, w_mid_back, w_out, w_out_back,
    )

    lat = lax.axis_index("lat")
    even = lat % 2 == 0
    first = exchange(send, "lat", (1, 1))
    mine = keep + first[:half].astype(F32)
    held = first[half + edge_rows :]
    steps = [2 << bit for bit in range(lat_size.bit_length() - 2)]
    orders = list(zip(steps, steps[1:] + steps[:1]))
    for turn, order in enumerate(orders):
        own, other = halves(mine, order_bit(lat, order))
        payload = jnp.concatenate([other.astype(BF16), held], axis=0)
        payload = exchange(payload, "lat", order)
        count = own.shape[0]
        mine = own + payload[:count].astype(F32)
        moves = []
        for side in (0, 1):
            done = [orders[before][side] for before in range(turn)]
            move = jnp.bool_(True)
            for step in steps:
                if step < order[side]:
                    carries = 1 if (step in done) == (side == 1) else 0
                    move = jnp.logical_and(move, (lat // step) % 2 == carries)
            moves.append(move)
        held = jnp.where(jnp.where(even, moves[0], moves[1]), payload[count:], held)
    inner, edges = pl.pallas_call(
        beside_kernel,
        out_shape=(shape((rows, channels, cols), F32), shape((channels // 2, LANES), BF16)),
        in_specs=[vmem()] * 3,
        out_specs=(vmem(),) * 2,
        compiler_params=params(),
        name="beside",
    )(numer, first, held)
    payload = jnp.concatenate([edges, mine.astype(BF16)], axis=0)
    payload = jnp.broadcast_to(payload[None], (lon_size,) + payload.shape)
    payload = lax.all_to_all(payload, "lon", 0, 0)
    mine = jnp.sum(payload[:, channels // 2 :].astype(F32), axis=0).astype(BF16)
    blended = pl.pallas_call(
        fold_kernel,
        out_shape=shape((channels, rows, cols), F32),
        in_specs=[vmem()] * 3,
        out_specs=vmem(),
        compiler_params=params(),
        name="fold",
    )(inner, payload, den)
    for order in reversed(orders):
        mine = ordered(mine, exchange(mine, "lat", order), order_bit(lat, order))
    grad_in, grad_mid, grad_out = pl.pallas_call(
        split_kernel,
        out_shape=(
            shape((taps, channels, width), F32),
            shape((taps, width, width), F32),
            shape((taps, channels, width), F32),
        ),
        in_specs=[vmem()] * 2,
        out_specs=(vmem(),) * 3,
        compiler_params=params(),
        name="split",
    )(mine, exchange(mine, "lat", (1, 1)))
    return blended, jnp.transpose(grad_in, (0, 2, 1)), grad_mid, grad_out


def solution(mesh):
    return jax.shard_map(
        shards,
        mesh=mesh,
        in_specs=(
            P(None, "lat", "lon"),
            P(None, "lat", "lon"),
            P(),
            P(),
            P(),
            P("lat", "lon", None, None),
            P(None, "lat", "lon"),
            P("lat", "lon"),
        ),
        out_specs=(P(None, "lat", "lon"), P(), P(), P()),
        check_vma=False,
    )
```
